32 devices in a mesh: ctx: 2 (over y), exp: 4 (over z), dp: 4 (over x, core).
Axes of the slice: x: 2, y: 2, z: 4, core: 2. Of those that a mesh axis runs over, the one named last changes fastest.
Arguments:
- block_in: bfloat16 [16, 256, 1024], P(('exp', 'dp'), 'ctx'), may hold values from -6 to 6
- seg_ids: int32 [16, 256], P(('exp', 'dp')), may hold values from 0 to 6, as said below
- routes: int32 [16, 256, 2], P(('exp', 'dp'), 'ctx'), may hold values from 0 to 3, all different within a row; in each aligned block of 128 rows (0 to 127, 128 to 255, ..., all dimensions but the last counted through in order) at most 96 rows name the same one
- gates: float32 [16, 256, 2], P(('exp', 'dp'), 'ctx'), may hold values from 0.25 to 1
- buckets: int32 [256], replicated, may hold values from 0 to 31, as said below
- norm_attn: float32 [1024], replicated, may hold values from 0.5 to 1.5
- norm_ffn: float32 [1024], replicated, may hold values from 0.5 to 1.5
- w_query: bfloat16 [1024, 1024], replicated, may hold values from -0.1875 to 0.1875
- w_key: bfloat16 [1024, 1024], replicated, may hold values from -0.1875 to 0.1875
- w_value: bfloat16 [1024, 1024], replicated, may hold values from -0.1875 to 0.1875
- w_out_attn: bfloat16 [1024, 1024], replicated, may hold values from -1.5 to 1.5
- rel_bias: float32 [512], replicated, may hold values from -4 to 4
- clip_level: float32 [16], replicated, may hold values from 2 to 6
- w_in: bfloat16 [4, 1024, 5632], P('exp'), may hold values from -0.1875 to 0.1875
- w_down: bfloat16 [4, 2816, 1024], P('exp'), may hold values from -0.109375 to 0.109375
- cotangent: bfloat16 [16, 256, 1024], P(('exp', 'dp'), 'ctx'), may hold values from -6 to 6
Outputs:
- block_out: bfloat16 [16, 256, 1024], P(('exp', 'dp'), 'ctx')
- grad_in: float32 [16, 256, 1024], P(('exp', 'dp'), 'ctx')
- grad_norm_attn: float32 [1024], P(('ctx', 'exp', 'dp'))
- grad_norm_ffn: float32 [1024], P(('ctx', 'exp', 'dp'))
- grad_query: float32 [1024, 1024], P(('ctx', 'exp', 'dp'))
- grad_key: float32 [1024, 1024], P(('ctx', 'exp', 'dp'))
- grad_value: float32 [1024, 1024], P(('ctx', 'exp', 'dp'))
- grad_out_attn: float32 [1024, 1024], P(('ctx', 'exp', 'dp'))
- grad_rel_bias: float32 [512], P(('ctx', 'exp', 'dp'))
- grad_w_in: float32 [4, 1024, 5632], P('exp', ('ctx', 'dp'))
- grad_w_down: float32 [4, 2816, 1024], P('exp', ('ctx', 'dp'))
- clipped_query: float32 [1024, 1024], replicated
- clipped_key: float32 [1024, 1024], replicated
- clip_factor: float32 [16], replicated
The draws below stay inside these ranges and needn't reach their ends.
Inputs may be any that keep to these rules, and one draw needn't show every extreme that they name: `seg_ids`: numbers never fall along a sequence; the first document ends and the last begins within the first and the last 128 positions; between them one document covers the sequence. In the 128 rows of one device no expert is named by more than 96 routes. `buckets`: never falls as the distance grows; 0 at distance 0 and 31 at the largest distance.
All inputs are finite; a program needn't handle non-finite values.
Results may differ from the reference program's by a relative error of at most 0.012.
The reference program's roundings to bfloat16 on the way count: a program that leaves them out, or rounds other values in their place, can miss the bound.
Values may be sent and summed in bfloat16 or wider, within the bound.
No kernel may reach another device: no remote copies, remote signals or barrier semaphores. Data moves between devices by JAX's collectives and lax.ppermute only.
A program may use at most 192 MiB of HBM per device.

```python
import math
import jax
import jax.numpy as jnp
import numpy as np
from jax import lax

D = 1024
FF = 2816
HDIM = 64
NB = 32
H = 16
TOP = 2
DOCS = 3
TOK_DEV = 128
EXPERTS = 4
SEQS = 16
LEN = 256
CAP = 96
N_CTX = 2


def draw_seg_ids(key, part):
    lower_bounds = jax.random.randint(jax.random.fold_in(key, 1), (SEQS, DOCS), 1, TOK_DEV)
    upper_bounds = jax.random.randint(jax.random.fold_in(key, 2), (SEQS, DOCS), LEN - TOK_DEV + 1, LEN)
    bounds = jnp.concatenate([lower_bounds, upper_bounds], axis=1).astype(jnp.int32)
    positions = jnp.arange(LEN, dtype=jnp.int32)
    return jnp.sum((bounds[:, None, :] <= positions[None, :, None]).astype(jnp.int32), axis=2).astype(jnp.int32)


def draw_buckets(key, part):
    steps_up = (jax.random.randint(jax.random.fold_in(key, 3), (LEN,), 0, 3) == 0).astype(jnp.int32)
    positions = jnp.arange(LEN, dtype=jnp.int32)
    climb = jnp.cumsum(jnp.where(positions == 0, 0, steps_up))
    return jnp.where(positions == LEN - 1, NB - 1, jnp.minimum(climb, NB - 1)).astype(jnp.int32)


def level_of(rng, shape, cuts, least, largest):
    factor_of, own = 1.0, jax.random.fold_in(rng, 6)
    for axis_at, blocks in cuts:
        draws = jnp.exp(jax.random.uniform(jax.random.fold_in(own, axis_at), (blocks,), jnp.float32, least / len(cuts), largest / len(cuts)))
        factor_of = factor_of * jnp.repeat(draws, shape[axis_at] // blocks).reshape([-1 if axis == axis_at else 1 for axis in range(len(shape))])
    return factor_of


def shared_out(key, own, number, rows, amount, top, limit, skew):
    ranking = jax.random.permutation(key, amount)
    crowded, usual = shares(amount, rows * top, limit, skew, True), shares(amount, rows * top, limit, skew, False)
    places = jnp.arange(amount)

    def named(tallies, offset_by):
        used = int((tallies > 0).sum())
        fixed = max(1, used // 4)
        moved = fixed + (places - fixed + offset_by * (used - fixed)) % max(1, amount - fixed)
        return jnp.zeros((amount,), jnp.int32).at[ranking[jnp.where(places < fixed, places, moved)]].set(jnp.asarray(tallies, jnp.int32))

    tallies = jnp.where(number % 4 == 0, named(crowded, number // 4), named(usual, number - number // 4 - 1))
    mixed = jax.random.permutation(jax.random.fold_in(own, 3), amount)
    giver, receiver = mixed[0:amount // 2 * 2:2], mixed[1:amount // 2 * 2:2]
    slack = jnp.minimum(tallies[giver] - 1, limit - tallies[receiver]) // 2
    slack = jnp.where((giver == ranking[0]) | (receiver == ranking[0]) | (tallies[receiver] == 0), 0, jnp.maximum(slack, 0))
    moved = jax.random.randint(jax.random.fold_in(own, 4), (amount // 2,), 0, 1 << 20) % (slack + 1)
    tallies = tallies.at[giver].add(-moved).at[receiver].add(moved)
    items = jnp.searchsorted(jnp.cumsum(tallies), jnp.arange(rows * top), side="right").astype(jnp.int32)
    table = items.reshape(top, rows).T
    table = table[jax.random.permutation(jax.random.fold_in(own, 1), rows)]
    offset_by = jax.random.randint(jax.random.fold_in(own, 2), (rows, 1), 0, top)
    return jnp.take_along_axis(table, (jnp.arange(top)[None, :] + offset_by) % top, axis=1)


def shares(count, total, limit, skew, full):
    portions = [(1 << 20) // math.isqrt(grade ** skew) + 1 for grade in range(1, count + 1)]
    largest = limit if full else min(limit, max(-(-total // count), total * portions[0] // sum(portions)))
    least = 1 if total - largest >= count - 1 else 0
    given, spare = [largest] + [least] * (count - 1), total - largest - least * (count - 1)
    while spare > 0:
        free = [i for i in range(1, count) if given[i] < largest] or [i for i in range(1, count) if given[i] < limit]
        mass, left = sum([portions[i] for i in free]), spare
        for i in free:
            extra = min(limit - given[i], max(1, left * portions[i] // mass), spare)
            given[i] = given[i] + extra
            spare = spare - extra
    return np.array(given)


def bell_draw(rng, dims, scale, reach, cuts=(), kind=jnp.bfloat16):
    array = jax.random.normal(rng, dims, jnp.float32) * scale
    if len(cuts) > 0:
        array = level_of(rng, dims, cuts, -0.22, 0.18) * array
    return jnp.clip(array, min=-reach, max=reach).astype(kind)


def setup_inputs(seed: int = 0) -> dict:
    splits = jax.random.split(jax.random.key(seed), 17)
    block_in = bell_draw(splits[0], (SEQS, LEN, D), 1.0, 6.0, ((0, 16), (1, 2)))
    seg_ids = draw_seg_ids(jax.random.fold_in(splits[16], 71), 0)
    routes_keys = jax.random.split(jax.random.fold_in(splits[2], 1), SEQS * LEN // TOK_DEV)
    routes_turns = jax.random.permutation(jax.random.fold_in(splits[2], 3), SEQS * LEN // TOK_DEV)
    routes = jax.vmap(lambda own, number: shared_out(jax.random.fold_in(splits[2], 2), own, number, TOK_DEV, EXPERTS, TOP, CAP, 2))(routes_keys, routes_turns).reshape((SEQS, LEN, TOP))
    gates = jnp.clip(0.25 + 0.75 * jax.random.uniform(splits[3], (SEQS, LEN, TOP), jnp.float32) ** level_of(splits[3], (SEQS, LEN, TOP), ((0, 16), (1, 2)), -0.2, 0.2), 0.25, 1.0)
    buckets = draw_buckets(jax.random.fold_in(splits[16], 71), 0)
    norm_attn = jnp.clip(1.0 + 0.1 * jax.random.normal(splits[5], (D,), jnp.float32), 0.5, 1.5)
    norm_ffn = jnp.clip(1.0 + 0.1 * jax.random.normal(splits[6], (D,), jnp.float32), 0.5, 1.5)
    w_query = bell_draw(splits[7], (D, D), D ** -0.5, 0.1875)
    w_key = bell_draw(splits[8], (D, D), D ** -0.5, 0.1875)
    w_value = bell_draw(splits[9], (D, D), D ** -0.5, 0.1875)
    w_out_attn = bell_draw(splits[10], (D, D), (D // 64) ** -0.5, 1.5)
    rel_bias = bell_draw(splits[11], (NB * H,), 1.0, 4.0, (), jnp.float32)
    clip_level = jnp.clip(jax.random.uniform(splits[12], (H,), jnp.float32, 2.0, 6.0), 2.0, 6.0)
    w_in = bell_draw(splits[13], (EXPERTS, D, 2 * FF), D ** -0.5, 0.1875, ((0, 4),))
    w_down = bell_draw(splits[14], (EXPERTS, FF, D), FF ** -0.5, 0.109375, ((0, 4),))
    cotangent = bell_draw(splits[15], (SEQS, LEN, D), 1.0, 6.0, ((0, 16), (1, 2)))
    return dict(block_in=block_in, seg_ids=seg_ids, routes=routes, gates=gates, buckets=buckets, norm_attn=norm_attn, norm_ffn=norm_ffn, w_query=w_query, w_key=w_key, w_value=w_value, w_out_attn=w_out_attn, rel_bias=rel_bias, clip_level=clip_level, w_in=w_in, w_down=w_down, cotangent=cotangent)


EPSILON = 1e-06
FULL_PRECISION = lax.Precision.HIGHEST

@jax.custom_vjp
def reduced_precision_cast(v):
    return lax.optimization_barrier(v.astype(jnp.bfloat16)).astype(jnp.float32)

@jax.custom_vjp
def reduced_precision_backward(v):
    return v

def low_keep(v):
    return (reduced_precision_cast(v), None)

def low_pass(kept, grad):
    return (grad,)

def back_keep(v):
    return (v, None)

def back_low(kept, grad):
    return (reduced_precision_cast(grad),)
reduced_precision_cast.defvjp(low_keep, low_pass)
reduced_precision_backward.defvjp(back_keep, back_low)

def rms_norm(block_inputs, scale_gain):
    return block_inputs * lax.rsqrt(lax.optimization_barrier(jnp.mean(block_inputs * block_inputs, axis=-1, keepdims=True)) + EPSILON) * scale_gain

def route_slots(block_routes):
    flat_routes = block_routes.reshape(-1)
    one_hot = (flat_routes[:, None] == jnp.arange(EXPERTS, dtype=jnp.int32)[None, :]).astype(jnp.int32)
    running = jnp.cumsum(one_hot, axis=0) - 1
    return (flat_routes, lax.optimization_barrier(jnp.sum(running * one_hot, axis=1)).astype(jnp.int32))

def reference(block_in, seg_ids, routes, gates, buckets, norm_attn, norm_ffn, w_query, w_key, w_value, w_out_attn, rel_bias, clip_level, w_in, w_down, cotangent):
    blocks = SEQS * N_CTX
    score_scale = HDIM ** (-0.5)
    positions = jnp.arange(LEN, dtype=jnp.int32)
    distance = jnp.clip(positions[:, None] - positions[None, :], 0, LEN - 1).astype(jnp.int32)
    causal = positions[None, :] <= positions[:, None]
    flat_routes, slot_index = jax.vmap(route_slots)(routes.reshape(blocks, TOK_DEV, TOP))

    def forward(block_inputs, gain_attn, gain_ffn, weight_query, weight_key, weight_value, output_weight, bias_flat, weight_in, weight_down):
        normalized_rows = reduced_precision_cast(rms_norm(block_inputs, gain_attn))

        def project(weight_matrix):
            return reduced_precision_cast(reduced_precision_backward(jnp.einsum('yzx,xi->yzi', normalized_rows, weight_matrix, precision=FULL_PRECISION)))
        queries = project(weight_query)
        key_rows = project(weight_key)
        value_rows = project(weight_value)
        bias_all = jnp.transpose(bias_flat.reshape(NB, H)[buckets[distance]], (2, 0, 1))

        def one_sequence(items):
            seq_query, seq_key, seq_value, seq_docs = items
            q_heads = seq_query.reshape(LEN, H, HDIM)
            k_heads = seq_key.reshape(LEN, H, HDIM)
            v_heads = seq_value.reshape(LEN, H, HDIM)
            raw_logits = reduced_precision_backward(jnp.einsum('qhd,khd->hqk', q_heads, k_heads, precision=FULL_PRECISION) * score_scale)
            allowed = causal & (seq_docs[:, None] == seq_docs[None, :])
            peak_vals = lax.optimization_barrier(jnp.max(jnp.where(allowed[None], raw_logits, -1e+30), axis=(1, 2)))
            scores = jnp.where(allowed[None], raw_logits + bias_all, -1e+30)
            row_max = lax.optimization_barrier(jnp.max(scores, axis=-1, keepdims=True))
            exp_scores = jnp.exp(scores - row_max)
            probs_full = exp_scores / lax.optimization_barrier(jnp.sum(exp_scores, axis=-1, keepdims=True))
            mixed = jnp.einsum('hqk,khd->qhd', reduced_precision_cast(probs_full), v_heads, precision=FULL_PRECISION)
            return (mixed.reshape(LEN, D), peak_vals)
        attention_output, peaks = lax.map(jax.checkpoint(one_sequence), (queries, key_rows, value_rows, seg_ids))
        attention_output = reduced_precision_cast(reduced_precision_backward(attention_output))
        residual_after_attention = block_inputs + reduced_precision_backward(jnp.einsum('yzx,xi->yzi', attention_output, output_weight, precision=FULL_PRECISION))
        sent_rows = reduced_precision_cast(rms_norm(residual_after_attention, gain_ffn)).reshape(blocks, TOK_DEV, D)
        copies = jnp.stack([reduced_precision_backward(sent_rows) for route_num in range(TOP)], axis=2).reshape(blocks, TOK_DEV * TOP, D)

        def fill(rows_here, route_here, slot_here):
            return jnp.zeros((EXPERTS, CAP, D), jnp.float32).at[route_here, slot_here].set(rows_here)
        buffers = jax.vmap(fill)(copies, flat_routes, slot_index)
        per_expert = jnp.transpose(buffers, (1, 0, 2, 3)).reshape(EXPERTS, blocks * CAP, D)

        def expert_pass(items):
            expert_rows, first_weight, second_weight = items
            gate_up = reduced_precision_backward(jnp.dot(expert_rows, first_weight, precision=FULL_PRECISION))
            hidden = reduced_precision_cast(jax.nn.gelu(gate_up[:, :FF], approximate=True) * gate_up[:, FF:])
            return reduced_precision_cast(reduced_precision_backward(jnp.dot(hidden, second_weight, precision=FULL_PRECISION)))
        expert_out = lax.map(jax.checkpoint(expert_pass), (per_expert, weight_in, weight_down))
        returned = jnp.transpose(expert_out.reshape(EXPERTS, blocks, CAP, D), (1, 0, 2, 3))

        def pick(buffer_here, route_here, slot_here):
            return buffer_here[route_here, slot_here]
        picked = jax.vmap(pick)(returned, flat_routes, slot_index).reshape(SEQS, LEN, TOP, D)
        result = residual_after_attention + lax.optimization_barrier(jnp.sum(gates[..., None] * picked, axis=2))
        return (result, peaks)
    result, pull_back, peaks = jax.vjp(forward, block_in.astype(jnp.float32), norm_attn, norm_ffn, w_query.astype(jnp.float32), w_key.astype(jnp.float32), w_value.astype(jnp.float32), w_out_attn.astype(jnp.float32), rel_bias, w_in.astype(jnp.float32), w_down.astype(jnp.float32), has_aux=True)
    grads = pull_back(cotangent.astype(jnp.float32))
    peak_all = lax.optimization_barrier(jnp.max(peaks, axis=0))
    factor = clip_level / jnp.maximum(peak_all, clip_level)
    column_scale = jnp.repeat(jnp.sqrt(factor), HDIM)
    clipped_query = w_query.astype(jnp.float32) * column_scale[None, :]
    clipped_key = w_key.astype(jnp.float32) * column_scale[None, :]
    return (result.astype(jnp.bfloat16), grads[0], grads[1], grads[2], grads[3], grads[4], grads[5], grads[6], grads[7], grads[8], grads[9], clipped_query, clipped_key, factor)
```

```python
import functools

import jax
import jax.numpy as jnp
from jax import lax
from jax.experimental import pallas as pl
from jax.experimental.pallas import tpu as pltpu
from jax.sharding import PartitionSpec as P

HDIM = 64
NB = 32
PAIR = 2 * HDIM
EPSILON = 1e-06
FULL_PRECISION = lax.Precision.HIGHEST
LOW = jnp.bfloat16
FULL = jnp.float32
OUTSIDE = -1e30
GELU_SCALE = 0.7978845608028654
GELU_CUBE = 0.044715


def rms_norm(rows, gain):
    return rows * lax.rsqrt(jnp.mean(rows * rows, axis=-1, keepdims=True) + EPSILON) * gain


def dot_rows(left, right):
    return lax.dot_general(left, right, (((1,), (0,)), ((), ())), preferred_element_type=FULL)


def dot_back(left, right):
    return lax.dot_general(left, right, (((1,), (1,)), ((), ())), preferred_element_type=FULL)


def transpose_dot(left, right):
    return lax.dot_general(left, right, (((0,), (0,)), ((), ())), preferred_element_type=FULL)


def shifted(array, axis, shift):
    size = lax.axis_size(axis)
    return lax.ppermute(array, axis, [(i, (i + shift) % size) for i in range(size)])


def swapped(array, axis, bit):
    size = lax.axis_size(axis)
    return lax.ppermute(array, axis, [(i, i ^ bit) for i in range(size)])


def across_all(array, combine):
    for axis in ("dp", "ctx", "exp"):
        bit = 1
        while bit < lax.axis_size(axis):
            array = combine(array, swapped(array, axis, bit))
            bit *= 2
    return array


def bias_kernel(by_lane_ref, bias_ref):
    rows, keys = bias_ref.shape[1:]
    width = by_lane_ref.shape[2]
    for half in range(2):
        line = jnp.broadcast_to(by_lane_ref[0, half : half + 1, :], (rows, width))
        turned = pltpu.roll(line, keys + 1, 1, stride=1, stride_axis=0)
        bias_ref[half] = turned[:, :keys]


def bias_tiles(by_lane, rows, keys):
    heads, width = by_lane.shape
    return pl.pallas_call(
        bias_kernel,
        grid=(heads // 2,),
        in_specs=[pl.BlockSpec((1, 2, width), lambda g: (g, 0, 0))],
        out_specs=pl.BlockSpec((2, rows, keys), lambda g: (g, 0, 0)),
        out_shape=jax.ShapeDtypeStruct((heads, rows, keys), FULL),
        cost_estimate=pl.CostEstimate(
            flops=heads * rows * keys * 4, bytes_accessed=heads * rows * keys * 4, transcendentals=0
        ),
        name="bias_tiles",
    )(by_lane.reshape(heads // 2, 2, width))


def half_lanes(half, shape):
    lane = lax.broadcasted_iota(jnp.int32, shape, 1)
    return lane < HDIM if half == 0 else lane >= HDIM


def attention_kernel(q_ref, k_ref, v_ref, bias_ref, mask_ref, out_ref, probs_ref, peak_ref):
    queries, keys, values, mask = q_ref[...], k_ref[...], v_ref[...], mask_ref[...]
    parts = []
    for half in range(2):
        own = half_lanes(half, queries.shape)
        raw = dot_back(jnp.where(own, queries, jnp.zeros_like(queries)), keys) * HDIM**-0.5 + mask
        top = jnp.max(raw, axis=0, keepdims=True)
        best = top[:, :128]
        for start in range(128, top.shape[1], 128):
            best = jnp.maximum(best, top[:, start : start + 128])
        peak_ref[0, half : half + 1, :] = best
        scores = raw + bias_ref[half]
        raised = jnp.exp(scores - jnp.max(scores, axis=1, keepdims=True))
        probs = raised / jnp.sum(raised, axis=1, keepdims=True)
        probs_ref[half] = probs
        parts.append(dot_rows(probs.astype(LOW), values))
    out_ref[...] = jnp.where(half_lanes(0, parts[0].shape), parts[0], parts[1]).astype(LOW)


def attention(queries, keys, values, bias, mask):
    rows, width = queries.shape
    length = keys.shape[0]
    pairs = width // PAIR
    heads = pairs * 2
    column = lambda size: pl.BlockSpec((size, PAIR), lambda g: (0, g))
    tile = pl.BlockSpec((2, rows, length), lambda g: (g, 0, 0))
    return pl.pallas_call(
        attention_kernel,
        grid=(pairs,),
        in_specs=[
            column(rows),
            column(length),
            column(length),
            tile,
            pl.BlockSpec((rows, length), lambda g: (0, 0)),
        ],
        out_specs=[column(rows), tile, pl.BlockSpec((1, 8, 128), lambda g: (g, 0, 0))],
        out_shape=[
            jax.ShapeDtypeStruct((rows, width), LOW),
            jax.ShapeDtypeStruct((heads, rows, length), FULL),
            jax.ShapeDtypeStruct((pairs, 8, 128), FULL),
        ],
        cost_estimate=pl.CostEstimate(
            flops=heads * rows * length * 512,
            bytes_accessed=heads * rows * length * 8,
            transcendentals=heads * rows * length,
        ),
        compiler_params=pltpu.CompilerParams(vmem_limit_bytes=32 * 2**20),
        name="attention",
    )(queries, keys, values, bias, mask)


def attention_back_kernel(
    q_ref, k_ref, v_ref, probs_ref, grad_ref, dq_ref, dk_ref, dv_ref, lines_ref
):
    queries, keys, values, grad = q_ref[...], k_ref[...], v_ref[...], grad_ref[...]
    rows, length = probs_ref.shape[1:]
    scale = HDIM**-0.5
    dq, dk, dv = [], [], []
    for half in range(2):
        own = half_lanes(half, grad.shape)
        dp = dot_back(jnp.where(own, grad, jnp.zeros_like(grad)), values)
        probs = probs_ref[half]
        ds = probs * (dp - jnp.sum(probs * dp, axis=1, keepdims=True))
        ds_low = ds.astype(LOW)
        dq.append(dot_rows(ds_low, keys))
        dk.append(transpose_dot(ds_low, queries))
        dv.append(transpose_dot(probs.astype(LOW), grad))
        wide = jnp.concatenate([ds, jnp.zeros((rows, rows), FULL)], axis=1)
        total = wide[rows - 8 :, :]
        for start in range(0, rows - 8, 8):
            total = total + pltpu.roll(wide[start : start + 8, :], rows - 8 - start, 1)
        line = lax.broadcasted_iota(jnp.int32, total.shape, 0)
        for bit in (1, 2, 4):
            total = jnp.where(((7 - line) & bit) != 0, pltpu.roll(total, bit, 1), total)
        lines_ref[0, half : half + 1, :] = jnp.sum(total, axis=0, keepdims=True)
    first = half_lanes(0, dq[0].shape)
    dq_ref[...] = (jnp.where(first, dq[0], dq[1]) * scale).astype(LOW)
    first = half_lanes(0, dk[0].shape)
    dk_ref[...] = (jnp.where(first, dk[0], dk[1]) * scale).astype(LOW)
    dv_ref[...] = jnp.where(first, dv[0], dv[1]).astype(LOW)


def attention_back(queries, keys, values, probs, grad):
    rows, width = queries.shape
    length = keys.shape[0]
    pairs = width // PAIR
    heads = pairs * 2
    column = lambda size: pl.BlockSpec((size, PAIR), lambda g: (0, g))
    dq, dk, dv, lines = pl.pallas_call(
        attention_back_kernel,
        grid=(pairs,),
        in_specs=[
            column(rows),
            column(length),
            column(length),
            pl.BlockSpec((2, rows, length), lambda g: (g, 0, 0)),
            column(rows),
        ],
        out_specs=[
            column(rows),
            column(length),
            column(length),
            pl.BlockSpec((1, 8, length + rows), lambda g: (g, 0, 0)),
        ],
        out_shape=[
            jax.ShapeDtypeStruct((rows, width), LOW),
            jax.ShapeDtypeStruct((length, width), LOW),
            jax.ShapeDtypeStruct((length, width), LOW),
            jax.ShapeDtypeStruct((pairs, 8, length + rows), FULL),
        ],
        cost_estimate=pl.CostEstimate(
            flops=heads * rows * length * 1024,
            bytes_accessed=heads * rows * length * 4,
            transcendentals=0,
        ),
        compiler_params=pltpu.CompilerParams(vmem_limit_bytes=32 * 2**20),
        name="attention_back",
    )(queries, keys, values, probs, grad)
    return dq, dk, dv, lines[:, :2, :].reshape(heads, length + rows)


def expert_kernel(
    rows_ref,
    grad_ref,
    gate_w_ref,
    up_w_ref,
    down_w_ref,
    out_ref,
    back_ref,
    gate_g_ref,
    up_g_ref,
    down_g_ref,
    out_sum,
    back_sum,
    turned,
):
    step = pl.program_id(0)

    @pl.when(step == 0)
    def _():
        turned[...] = rows_ref[...].T
        out_sum[...] = jnp.zeros_like(out_sum)
        back_sum[...] = jnp.zeros_like(back_sum)

    rows, grad = rows_ref[...], grad_ref[...]
    gate_w, up_w, down_w = gate_w_ref[0], up_w_ref[0], down_w_ref[0]
    gate = dot_rows(rows, gate_w)
    up = dot_rows(rows, up_w)
    dhid = dot_back(grad, down_w)
    square = gate * gate
    curve = jnp.tanh(GELU_SCALE * gate * (1.0 + GELU_CUBE * square))
    upper = 0.5 * (1.0 + curve)
    gelu = gate * upper
    slope = upper + 0.5 * gate * (1.0 - curve * curve) * (
        GELU_SCALE * (1.0 + 3.0 * GELU_CUBE * square)
    )
    hid = (gelu * up).astype(LOW)
    dgate = (dhid * up * slope).astype(LOW)
    dup = (dhid * gelu).astype(LOW)
    out_sum[...] += dot_rows(hid, down_w)
    back_sum[...] += dot_back(dgate, gate_w) + dot_back(dup, up_w)
    down_g_ref[...] = transpose_dot(hid, grad).astype(LOW)
    flipped = turned[...]
    gate_g_ref[...] = dot_rows(flipped, dgate).astype(LOW)
    up_g_ref[...] = dot_rows(flipped, dup).astype(LOW)

    @pl.when(step == pl.num_programs(0) - 1)
    def _():
        out_ref[...] = out_sum[...].astype(LOW)
        back_ref[...] = back_sum[...].astype(LOW)


def expert(rows, grad, w_in, w_down):
    count, width = rows.shape
    hidden = w_down.shape[1]
    part = 256
    steps = hidden // part
    whole = pl.BlockSpec((count, width), lambda i: (0, 0))
    return pl.pallas_call(
        expert_kernel,
        grid=(steps,),
        in_specs=[
            whole,
            whole,
            pl.BlockSpec((1, width, part), lambda i: (0, 0, i)),
            pl.BlockSpec((1, width, part), lambda i: (0, 0, i + steps)),
            pl.BlockSpec((1, part, width), lambda i: (0, i, 0)),
        ],
        out_specs=[
            whole,
            whole,
            pl.BlockSpec((width, part), lambda i: (0, i)),
            pl.BlockSpec((width, part), lambda i: (0, i)),
            pl.BlockSpec((part, width), lambda i: (i, 0)),
        ],
        out_shape=[
            jax.ShapeDtypeStruct((count, width), LOW),
            jax.ShapeDtypeStruct((count, width), LOW),
            jax.ShapeDtypeStruct((width, hidden), LOW),
            jax.ShapeDtypeStruct((width, hidden), LOW),
            jax.ShapeDtypeStruct((hidden, width), LOW),
        ],
        scratch_shapes=[
            pltpu.VMEM((count, width), FULL),
            pltpu.VMEM((count, width), FULL),
            pltpu.VMEM((width, count), LOW),
        ],
        cost_estimate=pl.CostEstimate(
            flops=18 * count * width * hidden,
            bytes_accessed=12 * width * hidden,
            transcendentals=count * hidden,
        ),
        compiler_params=pltpu.CompilerParams(vmem_limit_bytes=48 * 2**20),
        name="expert",
    )(rows, grad, w_in, w_in, w_down)


def place():
    dp = lax.axis_index("dp")
    return lax.axis_index("ctx"), lax.axis_index("exp"), dp // 2, dp % 2


def pick(array, index, axis):
    return lax.dynamic_index_in_dim(array, index, axis, keepdims=False)


def plus(left, right):
    return left.astype(FULL) + right.astype(FULL)


def scatter_plane(core_sum, y, x):
    get, cols = core_sum
    first, second = slice(0, cols // 2), slice(cols // 2, cols)
    a = swapped(get(None, 1 - x, first).astype(LOW), "dp", 2)
    b = swapped(get(1 - y, None, second).astype(LOW), "ctx", 1)
    a_send = plus(get(1 - y, 1 - (1 - x), first), pick(a, 1 - y, 0))
    b_send = plus(get(y, 1 - x, second), pick(b, 1 - x, 0))
    a2 = swapped(a_send.astype(LOW), "ctx", 1)
    b2 = swapped(b_send.astype(LOW), "dp", 2)
    a_out = plus(get(y, x, first), pick(a, y, 0)) + a2.astype(FULL)
    b_out = plus(get(y, x, second), pick(b, x, 0)) + b2.astype(FULL)
    return jnp.concatenate([a_out, b_out], axis=-1)


def chip_sum(grads, core):
    received = swapped(pick(grads, 1 - core, 2), "dp", 1)
    kept = pick(grads, core, 2)

    def get(cut_y, cut_x, cols):
        left, right = kept[..., cols], received[..., cols]
        if cut_x is not None:
            left, right = pick(left, cut_x, 1), pick(right, cut_x, 1)
        if cut_y is not None:
            left, right = pick(left, cut_y, 0), pick(right, cut_y, 0)
        return plus(left, right)

    return get, grads.shape[-1]


def scatter_experts(grads):
    y, _, x, core = place()
    rows, cols = grads.shape
    return scatter_plane(chip_sum(grads.reshape(2, 2, 2, rows // 8, cols), core), y, x)


def scatter_line(blocks):
    z = lax.axis_index("exp")
    size = blocks.shape[0]
    total = pick(blocks, z, 0).astype(FULL)
    for shift in range(1, size):
        out = pick(blocks, (z + shift) % size, 0).astype(LOW)
        total = total + shifted(out, "exp", shift).astype(FULL)
    return total


def scatter_shared(plane_first, line_first):
    y, _, x, core = place()
    width = plane_first[0].shape[-1]
    rows = plane_first[0].shape[0] // 32

    def over_chip(pair):
        both = jnp.stack([grads.reshape(2, 4, 2, 2, rows, width) for grads in pair])
        received = swapped(pick(both, 1 - core, 4), "dp", 1)
        return plus(pick(both, core, 4), received)

    line = over_chip(line_first)
    line = jnp.moveaxis(line, 2, 0)
    line = scatter_line(line)
    line_low = line.astype(FULL)

    plane = over_chip(plane_first)
    plane = plane.transpose(1, 3, 2, 4, 0, 5).reshape(2, 2, 4 * rows, 2 * width)

    def getter(array):
        def get(cut_y, cut_x, cols):
            cut = array[..., cols]
            if cut_x is not None:
                cut = pick(cut, cut_x, 1)
            if cut_y is not None:
                cut = pick(cut, cut_y, 0)
            return cut

        return get, array.shape[-1]

    plane = scatter_plane(getter(plane), y, x).reshape(4, rows, 2 * width)
    plane = scatter_line(plane)
    line = scatter_plane(
        getter(line_low.transpose(1, 2, 3, 0, 4).reshape(2, 2, rows, 2 * width)), y, x
    )
    return plane[:, :width], plane[:, width:], line[:, :width], line[:, width:]


def local(
    block_in,
    seg_ids,
    routes,
    gates,
    buckets,
    norm_attn,
    norm_ffn,
    w_query,
    w_key,
    w_value,
    w_out_attn,
    rel_bias,
    clip_level,
    w_in,
    w_down,
    cotangent,
):
    tokens, width = block_in.shape[1:]
    heads = width // HDIM
    n_ctx, experts, n_dp = (lax.axis_size(axis) for axis in ("ctx", "exp", "dp"))
    length = n_ctx * tokens
    ctx, z = lax.axis_index("ctx"), lax.axis_index("exp")
    place_all = (ctx * experts + z) * n_dp + lax.axis_index("dp")
    top_count = routes.shape[-1]
    capacity = tokens * top_count * 3 // (2 * experts)

    backs = list(range(n_ctx - 1, 0, -1))
    earlier = [
        lax.ppermute(block_in[0], "ctx", [(i, i + back) for i in range(n_ctx - back)])
        for back in backs
    ]

    routes_own, gates_own = routes[0], gates[0]
    relative = jnp.arange(experts, dtype=jnp.int32)
    hits = (routes_own - z) % experts
    names = hits[:, :, None] == relative[None, None, :]
    named = jnp.any(names, axis=1)
    before = jnp.tril(jnp.ones((tokens, tokens), FULL), -1)
    slot = jnp.dot(before, named.astype(FULL)).astype(jnp.int32)
    slots = jnp.arange(capacity, dtype=jnp.int32)
    spread = (slot.T[:, None, :] == slots[None, :, None]) & named.T[:, None, :]
    gate_of = jnp.sum(jnp.where(names, gates_own[:, :, None], 0.0), axis=1)
    spread_flat = spread.reshape(experts * capacity, tokens)
    spread_low = spread_flat.astype(LOW)
    slot_gate = jnp.sum(
        jnp.where(spread, gate_of.T[:, None, :], 0.0), axis=2
    ).reshape(experts * capacity, 1)
    grad_mix = cotangent[0]
    grad_out = (slot_gate * dot_rows(spread_low, grad_mix)).astype(LOW)

    def to_experts(rows):
        blocks = rows.reshape(experts, capacity, width)
        return jnp.concatenate(
            [blocks[0]] + [shifted(blocks[k], "exp", k) for k in range(1, experts)], axis=0
        )

    def from_experts(rows):
        blocks = rows.reshape(experts, capacity, width)
        return jnp.concatenate(
            [blocks[0]] + [shifted(blocks[k], "exp", experts - k) for k in range(1, experts)],
            axis=0,
        )

    expert_grad = to_experts(grad_out)

    lane_bucket = jnp.concatenate(
        [buckets[::-1], jnp.broadcast_to(buckets[:1], (tokens,))]
    )
    bucket_hot = (lane_bucket[None, :] == jnp.arange(NB, dtype=jnp.int32)[:, None]).astype(FULL)
    by_lane = lax.dot_general(
        rel_bias.reshape(NB, heads), bucket_hot, (((0,), (0,)), ((), ())), precision=FULL_PRECISION
    )
    bias = bias_tiles(by_lane, tokens, length)
    seg_all = seg_ids[0]
    seg_own = lax.dynamic_slice_in_dim(seg_all, ctx * tokens, tokens)
    seg_keys = jnp.concatenate(
        [
            jnp.where(
                ctx >= back,
                lax.dynamic_slice_in_dim(seg_all, jnp.maximum(ctx - back, 0) * tokens, tokens),
                -1,
            )
            for back in backs + [0]
        ]
    )
    at_row = jnp.arange(tokens, dtype=jnp.int32)[:, None] + (length - tokens)
    at_key = jnp.arange(length, dtype=jnp.int32)[None, :]
    allowed = (at_key <= at_row) & (seg_own[:, None] == seg_keys[None, :])
    mask = jnp.where(allowed, 0.0, OUTSIDE).astype(FULL)

    own_rows = block_in[0].astype(FULL)
    all_rows = jnp.concatenate([rows.astype(FULL) for rows in earlier] + [own_rows], axis=0)
    normed_own = rms_norm(own_rows, norm_attn).astype(LOW)
    normed_all = jnp.concatenate(
        [rms_norm(rows.astype(FULL), norm_attn).astype(LOW) for rows in earlier] + [normed_own],
        axis=0,
    )
    queries = dot_rows(normed_own, w_query).astype(LOW)
    keys = dot_rows(normed_all, w_key).astype(LOW)
    values = dot_rows(normed_all, w_value).astype(LOW)
    attended, probs, peak_lanes = attention(queries, keys, values, bias, mask)
    peak = across_all(jnp.max(peak_lanes[:, :2, :], axis=-1).reshape(heads), jnp.maximum)
    after = own_rows + dot_rows(attended, w_out_attn)

    sent_f32, ffn_pull = jax.vjp(rms_norm, after, norm_ffn)
    sent = sent_f32.astype(LOW)
    expert_rows = to_experts(dot_rows(spread_low, sent).astype(LOW))
    out_rows, back_rows, grad_gate, grad_up, grad_down = expert(
        expert_rows, expert_grad, w_in, w_down
    )
    back_home = from_experts(back_rows)
    out_home = from_experts(out_rows)
    if (n_ctx, n_dp) == (2, 4):
        expert_second = scatter_experts(grad_down)
        expert_first = jnp.concatenate(
            [scatter_experts(grad_gate), scatter_experts(grad_up)], axis=-1
        )
    else:
        grad_first = jnp.concatenate([grad_gate, grad_up], axis=-1).astype(FULL)
        expert_first, expert_second = (
            lax.psum_scatter(grads, ("ctx", "dp"), scatter_dimension=0, tiled=True)
            for grads in (grad_first, grad_down.astype(FULL))
        )

    by_route = jnp.concatenate(
        [
            (spread & (hits[:, route] == relative[:, None])[:, None, :]).reshape(-1, tokens)
            for route in range(top_count)
        ],
        axis=1,
    ).astype(LOW)
    picked = transpose_dot(by_route, out_home).reshape(top_count, tokens, width)
    mixed = after + sum(
        gates_own[:, route : route + 1] * picked[route] for route in range(top_count)
    )

    grad_sent = transpose_dot(spread_low, back_home)
    grad_after, grad_gain_ffn = ffn_pull(grad_sent)
    grad_after = grad_after + grad_mix.astype(FULL)
    grad_branch = grad_after.astype(LOW)
    grad_wo = transpose_dot(attended, grad_branch).astype(LOW)
    grad_attended = dot_back(grad_branch, w_out_attn).astype(LOW)

    dq, dk, dv, lines = attention_back(queries, keys, values, probs, grad_attended)
    grad_table = lax.dot_general(
        bucket_hot, lines, (((1,), (1,)), ((), ())), precision=FULL_PRECISION
    ).reshape(-1)
    grad_wq = transpose_dot(normed_own, dq).astype(LOW)
    grad_wk = transpose_dot(normed_all, dk).astype(LOW)
    grad_wv = transpose_dot(normed_all, dv).astype(LOW)
    grad_normed = dot_back(dk, w_key) + dot_back(dv, w_value)
    grad_normed_own = grad_normed[length - tokens :] + dot_back(dq, w_query)
    scaled = all_rows * lax.rsqrt(jnp.mean(all_rows * all_rows, axis=-1, keepdims=True) + EPSILON)
    grad_gain_attn = jnp.sum(
        scaled * jnp.concatenate([grad_normed[: length - tokens], grad_normed_own], axis=0), axis=0
    )
    for at, back in enumerate(backs):
        term = grad_normed[at * tokens : (at + 1) * tokens].astype(LOW)
        returned = lax.ppermute(term, "ctx", [(i + back, i) for i in range(n_ctx - back)])
        grad_normed_own = grad_normed_own + returned.astype(FULL)
    _, norm_pull = jax.vjp(lambda rows: rms_norm(rows, norm_attn), own_rows)
    grad_input = grad_after + norm_pull(grad_normed_own)[0]

    devices = n_ctx * experts * n_dp
    small = across_all(jnp.concatenate([grad_gain_attn, grad_gain_ffn, grad_table]), jnp.add)
    own_gain = width // devices
    own_table = grad_table.shape[0] // devices
    small_attn = lax.dynamic_slice_in_dim(small, place_all * own_gain, own_gain)
    small_ffn = lax.dynamic_slice_in_dim(small, width + place_all * own_gain, own_gain)
    small_table = lax.dynamic_slice_in_dim(small, 2 * width + place_all * own_table, own_table)
    if (n_ctx, experts, n_dp) == (2, 4, 4):
        shared_o, shared_q, shared_k, shared_v = scatter_shared(
            (grad_wo, grad_wq), (grad_wk, grad_wv)
        )
    else:
        shared_q, shared_k, shared_v, shared_o = (
            lax.psum_scatter(
                grads.astype(FULL), ("ctx", "exp", "dp"), scatter_dimension=0, tiled=True
            )
            for grads in (grad_wq, grad_wk, grad_wv, grad_wo)
        )

    factor = clip_level / jnp.maximum(peak, clip_level)
    column_scale = jnp.repeat(jnp.sqrt(factor), HDIM)
    clipped_query = w_query.astype(FULL) * column_scale[None, :]
    clipped_key = w_key.astype(FULL) * column_scale[None, :]
    return (
        mixed.astype(LOW)[None],
        grad_input[None],
        small_attn,
        small_ffn,
        shared_q,
        shared_k,
        shared_v,
        shared_o,
        small_table,
        expert_first[None],
        expert_second[None],
        clipped_query,
        clipped_key,
        factor,
    )


def solution(mesh):
    tokens = P(("exp", "dp"), "ctx", None)
    everywhere = P(("ctx", "exp", "dp"))
    by_rows = P(("ctx", "exp", "dp"), None)
    by_expert = P("exp", None, None)
    expert_rows = P("exp", ("ctx", "dp"), None)
    in_specs = (tokens, P(("exp", "dp"), None), tokens, tokens) + (P(),) * 9
    in_specs = in_specs + (by_expert, by_expert, tokens)
    out_specs = (tokens, tokens, everywhere, everywhere) + (by_rows,) * 4
    out_specs = out_specs + (everywhere, expert_rows, expert_rows, P(), P(), P())
    return jax.shard_map(local, mesh=mesh, in_specs=in_specs, out_specs=out_specs, check_vma=False)
```

```python
import functools

import jax
import jax.numpy as jnp
from jax import lax
from jax.experimental import pallas as pl
from jax.experimental.pallas import tpu as pltpu
from jax.sharding import PartitionSpec as P

HDIM = 64
NB = 32
GROUP = 4
LANES = 128
EPSILON = 1e-06
FULL_PRECISION = lax.Precision.HIGHEST
LOW = jnp.bfloat16
FULL = jnp.float32
OUTSIDE = -1e30
GELU_SCALE = 0.7978845608028654
GELU_CUBE = 0.044715


def rms_norm(rows, gain):
    return rows * lax.rsqrt(jnp.mean(rows * rows, axis=-1, keepdims=True) + EPSILON) * gain


def dot_rows(left, right):
    return lax.dot_general(left, right, (((1,), (0,)), ((), ())), preferred_element_type=FULL)


def dot_back(left, right):
    return lax.dot_general(left, right, (((1,), (1,)), ((), ())), preferred_element_type=FULL)


def transpose_dot(left, right):
    return lax.dot_general(left, right, (((0,), (0,)), ((), ())), preferred_element_type=FULL)


def swapped(array, axis, bit):
    size = lax.axis_size(axis)
    return lax.ppermute(array, axis, [(i, i ^ bit) for i in range(size)])


def over_experts(blocks):
    return lax.all_to_all(blocks, "exp", split_axis=0, concat_axis=0, tiled=True)


MICROSECOND = 1.15e9


def call(
    body, name, inputs, outputs, us, grid=(1,), token=None, prefetch=(), scratch=(), vmem=12,
    near_in=(), near_out=(),
):
    n_pre, n_in, n_out = len(prefetch), len(inputs), len(outputs)
    held = [] if token is None else [token]

    def kernel(*refs):
        split = n_pre + n_in
        outs = split + len(held)
        refs[outs + n_out][...] = jnp.zeros((8, LANES), FULL)
        body(*refs[:split], *refs[outs : outs + n_out], *refs[outs + n_out + 1 :])

    where = lambda at, near: pltpu.VMEM if at in near else pltpu.HBM
    arrays = [
        pltpu.with_memory_space_constraint(array, where(at, near_in))
        for at, (array, _) in enumerate(inputs)
    ]
    held = [pltpu.with_memory_space_constraint(array, pltpu.HBM) for array in held]
    results = pl.pallas_call(
        kernel,
        grid_spec=pltpu.PrefetchScalarGridSpec(
            num_scalar_prefetch=n_pre,
            grid=grid,
            in_specs=[spec for _, spec in inputs]
            + [pl.BlockSpec(memory_space=pl.ANY)] * len(held),
            out_specs=[spec for _, _, spec in outputs]
            + [pl.BlockSpec((8, LANES), lambda *_: (0, 0))],
            scratch_shapes=list(scratch),
        ),
        out_shape=[
            where(at, near_out)(shape, dtype) for at, (shape, dtype, _) in enumerate(outputs)
        ]
        + [pltpu.HBM((8, LANES), FULL)],
        cost_estimate=pl.CostEstimate(
            flops=int(us * MICROSECOND), bytes_accessed=1, transcendentals=0
        ),
        compiler_params=pltpu.CompilerParams(vmem_limit_bytes=vmem * 2**20),
        name=name,
    )(*prefetch, *arrays, *held)
    return list(results[:-1]), results[-1]


def whole(array):
    return array, pl.BlockSpec(array.shape, lambda *_: (0,) * array.ndim)


def whole_out(shape, dtype):
    return shape, dtype, pl.BlockSpec(shape, lambda *_: (0,) * len(shape))


def hold(token, *arrays):
    anywhere = pl.BlockSpec(memory_space=pl.ANY)
    return pl.pallas_call(
        lambda *refs: None,
        in_specs=[anywhere] * (len(arrays) + 1),
        out_specs=[anywhere] * len(arrays),
        out_shape=[jax.ShapeDtypeStruct(array.shape, array.dtype) for array in arrays],
        input_output_aliases={at + 1: at for at in range(len(arrays))},
        cost_estimate=pl.CostEstimate(flops=1, bytes_accessed=1, transcendentals=0),
        name="hold",
    )(token, *arrays)


def eye(size):
    rows = lax.broadcasted_iota(jnp.int32, (size, size), 0)
    return rows == lax.broadcasted_iota(jnp.int32, (size, size), 1)


def to_column(row):
    size = row.shape[1]
    return jnp.sum(jnp.where(eye(size), row, jnp.zeros_like(row)), 1, keepdims=True)


def front_kernel(
    at_ref, routes_ref, gates_ref, grad_ref, seg_ref, spread_ref, pick_ref, out_ref, mask_ref
):
    top, tokens = routes_ref.shape
    experts, capacity, _ = out_ref.shape
    routes = [routes_ref[r : r + 1, :] for r in range(top)]
    gates = [gates_ref[r : r + 1, :] for r in range(top)]
    before = lax.broadcasted_iota(jnp.int32, (tokens, tokens), 0)
    before = before < lax.broadcasted_iota(jnp.int32, (tokens, tokens), 1)
    slots = lax.broadcasted_iota(jnp.int32, (capacity, tokens), 0).astype(FULL)
    for e in range(experts):
        part = pl.ds(e * capacity, capacity)
        hits = [jnp.where(route == e, 1.0, 0.0) for route in routes]
        named = functools.reduce(jnp.add, hits)
        slot = jnp.sum(jnp.where(before, to_column(named), 0.0), 0, keepdims=True)
        place = (slots == slot).astype(FULL)
        spread = place * named
        gate = functools.reduce(jnp.add, [hit * g for hit, g in zip(hits, gates)])
        spread_low = spread.astype(LOW)
        spread_ref[part, :] = spread_low
        for r in range(top):
            pick_ref[part, pl.ds(r * tokens, tokens)] = (place * hits[r]).astype(LOW)
        slot_gate = jnp.sum(spread * gate, 1, keepdims=True)
        out_ref[e] = (slot_gate * dot_rows(spread_low, grad_ref[...])).astype(LOW)
    length = mask_ref.shape[1]
    ctx = at_ref[0]
    seg = jnp.broadcast_to(seg_ref[...].astype(FULL), (8, length))
    keys = pltpu.roll(seg, length - (ctx + 1) * tokens, 1)[:1, :]
    at_row = lax.broadcasted_iota(jnp.int32, (tokens, length), 0) + (length - tokens)
    at_key = lax.broadcasted_iota(jnp.int32, (tokens, length), 1)
    own = jnp.sum(jnp.where(at_row == at_key, keys, 0.0), 1, keepdims=True)
    allowed = (at_key <= at_row) & (own == keys) & (at_key >= length - (ctx + 1) * tokens)
    mask_ref[...] = jnp.where(allowed, 0.0, OUTSIDE)


def front(at, routes, gates, grad, seg, experts, capacity):
    top, tokens = routes.shape
    slots = experts * capacity
    return call(
        front_kernel,
        "front",
        [whole(routes), whole(gates), whole(grad), whole(seg)],
        [
            whole_out((slots, tokens), LOW),
            whole_out((slots, top * tokens), LOW),
            whole_out((experts, capacity, grad.shape[1]), LOW),
            whole_out((tokens, seg.shape[1]), FULL),
        ],
        prefetch=(at,),
        us=1.5,
    near_out=(0, 3),
        )


def bias_kernel(buckets_ref, table_ref, hot_ref, bias_ref, by_lane):
    group, rows, keys = bias_ref.shape
    width = hot_ref.shape[1]
    step = pl.program_id(0)

    @pl.when(step == 0)
    def _():
        buckets = buckets_ref[...].astype(FULL)
        column = jnp.sum(jnp.where(eye(keys), buckets, 0.0), 1, keepdims=True)
        distance = lax.broadcasted_iota(jnp.int32, (keys, width), 0)
        lane = lax.broadcasted_iota(jnp.int32, (keys, width), 1)
        turned = jnp.sum(jnp.where(distance + lane == keys - 1, column, 0.0), 0, keepdims=True)
        bucket = lax.broadcasted_iota(jnp.int32, (NB, width), 0).astype(FULL)
        hot = jnp.where(bucket == turned, 1.0, 0.0)
        hot_ref[...] = hot
        lines = lax.dot_general(
            table_ref[...], hot, (((0,), (0,)), ((), ())), precision=FULL_PRECISION,
            preferred_element_type=FULL,
        )
        by_lane[...] = lines

    for at in range(group):
        line = jnp.broadcast_to(by_lane[pl.ds(step * group + at, 1), :], (8, width))
        line = pltpu.roll(line, keys + 1, 1, stride=1, stride_axis=0)
        for start in range(0, rows, 8):
            moved = line if start == 0 else pltpu.roll(line, start, 1)
            bias_ref[at, pl.ds(start, 8), :] = moved[:, :keys]


def bias_tiles(buckets, table, rows):
    heads, keys = table.shape[1], buckets.shape[1]
    width = keys + rows
    return call(
        bias_kernel,
        "bias_tiles",
        [whole(buckets), whole(table)],
        [
            whole_out((NB, width), FULL),
            ((heads, rows, keys), FULL, pl.BlockSpec((GROUP, rows, keys), lambda g: (g, 0, 0))),
        ],
        grid=(heads // GROUP,),
        scratch=[pltpu.VMEM((heads, width), FULL)],
        us=2.5,
        near_out=(1,),
    )


def half_lanes(half, shape):
    lane = lax.broadcasted_iota(jnp.int32, shape, 1)
    return lane < HDIM if half == 0 else lane >= HDIM


def attention_kernel(q_ref, k_ref, v_ref, bias_ref, mask_ref, out_ref, probs_ref, peak_ref):
    mask = mask_ref[...]
    for pair in range(GROUP // 2):
        lanes = pl.ds(pair * LANES, LANES)
        queries, keys, values = q_ref[:, lanes], k_ref[:, lanes], v_ref[:, lanes]
        parts = []
        for half in range(2):
            at = 2 * pair + half
            own = half_lanes(half, queries.shape)
            raw = dot_back(jnp.where(own, queries, jnp.zeros_like(queries)), keys)
            raw = raw * HDIM**-0.5 + mask
            top = jnp.max(raw, axis=0, keepdims=True)
            best = top[:, :LANES]
            for start in range(LANES, top.shape[1], LANES):
                best = jnp.maximum(best, top[:, start : start + LANES])
            peak_ref[0, at : at + 1, :] = best
            scores = raw + bias_ref[at]
            raised = jnp.exp(scores - jnp.max(scores, axis=1, keepdims=True))
            probs = raised * (1.0 / jnp.sum(raised, axis=1, keepdims=True))
            probs_ref[at] = probs
            parts.append(dot_rows(probs.astype(LOW), values))
        first = half_lanes(0, parts[0].shape)
        out_ref[:, lanes] = jnp.where(first, parts[0], parts[1]).astype(LOW)


def column_spec(size):
    return pl.BlockSpec((size, GROUP * HDIM), lambda g: (0, g))


def attention(queries, keys, values, bias, mask):
    rows, width = queries.shape
    length = keys.shape[0]
    heads = width // HDIM
    groups = heads // GROUP
    tile = pl.BlockSpec((GROUP, rows, length), lambda g: (g, 0, 0))
    (out, probs, peak), _ = call(
        attention_kernel,
        "attention",
        [
            (queries, column_spec(rows)),
            (keys, column_spec(length)),
            (values, column_spec(length)),
            (bias, tile),
            whole(mask),
        ],
        [
            ((rows, width), LOW, column_spec(rows)),
            ((heads, rows, length), FULL, tile),
            ((groups, 8, LANES), FULL, pl.BlockSpec((1, 8, LANES), lambda g: (g, 0, 0))),
        ],
        grid=(groups,),
        near_in=(0, 1, 2, 3, 4),
        near_out=(0, 1),
        us=4.5,
    )
    return out, probs, peak


def attention_back_kernel(q_ref, k_ref, v_ref, probs_ref, grad_ref, dq_ref, dk_ref, dv_ref, lines_ref):
    rows, length = probs_ref.shape[1:]
    scale = HDIM**-0.5
    for pair in range(GROUP // 2):
        lanes = pl.ds(pair * LANES, LANES)
        queries, keys, values, grad = (ref[:, lanes] for ref in (q_ref, k_ref, v_ref, grad_ref))
        dq, dk, dv = [], [], []
        for half in range(2):
            at = 2 * pair + half
            own = half_lanes(half, grad.shape)
            dp = dot_back(jnp.where(own, grad, jnp.zeros_like(grad)), values)
            probs = probs_ref[at]
            ds = probs * (dp - jnp.sum(probs * dp, axis=1, keepdims=True))
            ds_low = ds.astype(LOW)
            dq.append(dot_rows(ds_low, keys))
            dk.append(transpose_dot(ds_low, queries))
            dv.append(transpose_dot(probs.astype(LOW), grad))
            wide = jnp.concatenate([ds, jnp.zeros((rows, rows), FULL)], axis=1)
            total = wide[rows - 8 :, :]
            for start in range(0, rows - 8, 8):
                total = total + pltpu.roll(wide[start : start + 8, :], rows - 8 - start, 1)
            line = lax.broadcasted_iota(jnp.int32, total.shape, 0)
            for bit in (1, 2, 4):
                total = jnp.where(((7 - line) & bit) != 0, pltpu.roll(total, bit, 1), total)
            lines_ref[0, at : at + 1, :] = jnp.sum(total, axis=0, keepdims=True)
        first = half_lanes(0, dq[0].shape)
        dq_ref[:, lanes] = (jnp.where(first, dq[0], dq[1]) * scale).astype(LOW)
        first = half_lanes(0, dk[0].shape)
        dk_ref[:, lanes] = (jnp.where(first, dk[0], dk[1]) * scale).astype(LOW)
        dv_ref[:, lanes] = jnp.where(first, dv[0], dv[1]).astype(LOW)


def packed_back_kernel(
    q_ref, k_ref, v_ref, probs_ref, grad_ref, branch_ref, hot_ref, gain_ref, out_ref, lines_ref, small
):
    rows, length = probs_ref.shape[1:]
    ends = [0, rows, rows + length, rows + 2 * length, 2 * rows + 2 * length]
    parts = [out_ref.at[pl.ds(a, b - a), :] for a, b in zip(ends, ends[1:])]
    attention_back_kernel(q_ref, k_ref, v_ref, probs_ref, grad_ref, *parts[:3], lines_ref)
    parts[3][...] = branch_ref[...]
    step = pl.program_id(0)
    devices, width = small.shape[0], gain_ref.shape[1]
    own = width // devices

    @pl.when(step == 0)
    def _():
        device = lax.broadcasted_iota(jnp.int32, (devices, width), 0)
        feature = lax.broadcasted_iota(jnp.int32, (devices, width), 1)
        spread = jnp.where(feature // own == device, gain_ref[...], 0.0)
        feature = lax.broadcasted_iota(jnp.int32, (width, LANES), 0)
        lane = lax.broadcasted_iota(jnp.int32, (width, LANES), 1)
        small[...] = jnp.dot(
            spread, jnp.where(feature % own == lane, 1.0, 0.0), precision=FULL_PRECISION,
            preferred_element_type=FULL,
        )

    head = lax.broadcasted_iota(jnp.int32, (8, LANES), 0)
    lane = lax.broadcasted_iota(jnp.int32, (8, LANES), 1)
    lines = jnp.where(lax.broadcasted_iota(jnp.int32, lines_ref.shape[1:], 0) < GROUP, lines_ref[0], 0.0)
    table = lax.dot_general(
        hot_ref[...], lines, (((1,), (1,)), ((), ())), precision=FULL_PRECISION,
        preferred_element_type=FULL,
    )
    to_lane = jnp.where(lane == TABLE_LANE + step * GROUP + head, 1.0, 0.0)
    small[...] += jnp.dot(table, to_lane, precision=FULL_PRECISION, preferred_element_type=FULL)
    out_ref[pl.ds(ends[4], devices), :] = jnp.zeros((devices, out_ref.shape[1]), LOW)
    out_ref[pl.ds(ends[4], devices), :LANES] = small[...].astype(LOW)


def attention_back(queries, keys, values, probs, grad, token, packed=None):
    rows, width = queries.shape
    length = keys.shape[0]
    heads = width // HDIM
    groups = heads // GROUP
    lines = (
        (groups, 8, length + rows), FULL, pl.BlockSpec((1, 8, length + rows), lambda g: (g, 0, 0))
    )
    inputs = [
        (queries, column_spec(rows)),
        (keys, column_spec(length)),
        (values, column_spec(length)),
        (probs, pl.BlockSpec((GROUP, rows, length), lambda g: (g, 0, 0))),
        (grad, column_spec(rows)),
    ]
    if packed is None:
        outs, token = call(
            attention_back_kernel,
            "attention_back",
            inputs,
            [((size, width), LOW, column_spec(size)) for size in (rows, length, length)] + [lines],
            grid=(groups,),
            token=token,
            us=6.6,
        )
        return *outs, token
    branch, hot, gain, devices = packed
    total = 2 * rows + 2 * length + devices
    (out, _), token = call(
        packed_back_kernel,
        "attention_back",
        inputs + [(branch, column_spec(rows)), whole(hot), whole(gain)],
        [((total, width), LOW, column_spec(total)), lines],
        grid=(groups,),
        token=token,
        scratch=[pltpu.VMEM((devices, LANES), FULL)],
        near_in=(0, 1, 2, 3, 4, 5),
        near_out=(0,),
        us=7,
    )
    return out, token


def expert_part(rows, grad, gate_w, up_w, down_w):
    gate = dot_rows(rows, gate_w)
    up = dot_rows(rows, up_w)
    dhid = dot_back(grad, down_w)
    square = gate * gate
    curve = jnp.tanh(GELU_SCALE * gate * (1.0 + GELU_CUBE * square))
    upper = 0.5 * (1.0 + curve)
    gelu = gate * upper
    slope = upper + 0.5 * gate * (1.0 - curve * curve) * (
        GELU_SCALE * (1.0 + 3.0 * GELU_CUBE * square)
    )
    hid = (gelu * up).astype(LOW)
    dgate = (dhid * up * slope).astype(LOW)
    dup = (dhid * gelu).astype(LOW)
    return hid, dgate, dup, dot_rows(hid, down_w), dot_back(dgate, gate_w) + dot_back(dup, up_w)


def expert_kernel(
    rows_ref, grad_ref, gate_w_ref, up_w_ref, down_w_ref,
    out_ref, back_ref, dgate_ref, dup_ref, hid_ref, turned_ref, out_sum, back_sum,
):
    step = pl.program_id(0)

    @pl.when(step == 0)
    def _():
        out_sum[...] = jnp.zeros_like(out_sum)
        back_sum[...] = jnp.zeros_like(back_sum)

    hid, dgate, dup, out_more, back_more = expert_part(
        rows_ref[...], grad_ref[...], gate_w_ref[0], up_w_ref[0], down_w_ref[0]
    )
    dgate_ref[...] = dgate
    dup_ref[...] = dup
    hid_ref[...] = hid.T
    out_sum[...] += out_more
    back_sum[...] += back_more

    @pl.when(step == pl.num_programs(0) - 1)
    def _():
        out_ref[...] = out_sum[...].astype(LOW)
        back_ref[...] = back_sum[...].astype(LOW)
        turned_ref[...] = rows_ref[...].T


def expert(rows, grad, w_in, w_down, token):
    count, width = rows.shape
    hidden = w_down.shape[1]
    part = 256
    steps = hidden // part
    return call(
        expert_kernel,
        "expert",
        [
            whole(rows),
            whole(grad),
            (w_in, pl.BlockSpec((1, width, part), lambda i: (0, 0, i))),
            (w_in, pl.BlockSpec((1, width, part), lambda i: (0, 0, i + steps))),
            (w_down, pl.BlockSpec((1, part, width), lambda i: (0, i, 0))),
        ],
        [
            whole_out((count, width), LOW),
            whole_out((count, width), LOW),
            ((count, hidden), LOW, pl.BlockSpec((count, part), lambda i: (0, i))),
            ((count, hidden), LOW, pl.BlockSpec((count, part), lambda i: (0, i))),
            ((hidden, count), LOW, pl.BlockSpec((part, count), lambda i: (i, 0))),
            whole_out((width, count), LOW),
        ],
        grid=(steps,),
        token=token,
        scratch=[pltpu.VMEM((count, width), FULL), pltpu.VMEM((count, width), FULL)],
        vmem=24,
        us=20,
    )


PART = 256


def halves_kernel(*refs):
    x_refs, g_refs, w_refs = refs[1:3], refs[3:5], refs[5:11]
    out_keep, out_send, back_keep, back_send, dgate_ref, dup_ref, a_ref, b_ref, turned_ref = refs[11:20]
    out_sum, back_sum = refs[20:]
    step, last = pl.program_id(0), pl.num_programs(0) - 1
    count = x_refs[0].shape[0]

    @pl.when(step == 0)
    def _():
        out_sum[...] = jnp.zeros_like(out_sum)
        back_sum[...] = jnp.zeros_like(back_sum)

    def part(units):
        blocks = units // LANES
        gate_w = jnp.concatenate([ref[0] for ref in w_refs[0:blocks]], axis=1)
        up_w = jnp.concatenate([ref[0] for ref in w_refs[2 : 2 + blocks]], axis=1)
        down_w = jnp.concatenate([ref[0] for ref in w_refs[4 : 4 + blocks]], axis=0)
        down_g = None
        for half in range(2):
            rows = pl.ds(half * count, count)
            hid, dgate, dup, out_more, back_more = expert_part(
                x_refs[half][...], g_refs[half][...], gate_w, up_w, down_w
            )
            dgate_ref[rows, pl.ds(0, units)] = dgate
            dup_ref[rows, pl.ds(0, units)] = dup
            more = transpose_dot(hid, g_refs[half][...])
            down_g = more if half == 0 else down_g + more
            out_sum[rows, :] += out_more
            back_sum[rows, :] += back_more
        width = down_g.shape[1] // 2
        a_ref[pl.ds(0, units), :] = down_g[:, :width].astype(LOW)
        b_ref[pl.ds(0, units), :] = down_g[:, width:].astype(LOW)

    @pl.when(step < last)
    def _():
        part(PART)

    @pl.when(step == last)
    def _():
        part(PART // 2)
        own, other = pl.ds(0, count), pl.ds(count, count)
        back_keep[...] = back_sum[own, :]
        back_send[...] = back_sum[other, :].astype(LOW)
        out_keep[...] = out_sum[own, :]
        out_send[...] = out_sum[other, :].astype(LOW)
        for half in range(2):
            turned_ref[:, pl.ds(half * count, count)] = x_refs[half][...].T


def expert_halves(at, rows, grads, w_in, w_down, token):
    count, width = rows[0].shape
    hidden = w_down.shape[1]
    units = hidden // (2 * LANES)
    steps = (units + 1) // 2

    def block(step, at, second):
        return at[2] * units + jnp.minimum(2 * step + second, units - 1)

    column = lambda first, second: pl.BlockSpec(
        (1, width, LANES), lambda i, at: (0, 0, first + block(i, at, second))
    )
    row = lambda second: pl.BlockSpec((1, LANES, width), lambda i, at: (0, block(i, at, second), 0))
    shape = (count, width)
    return call(
        halves_kernel,
        "expert_halves",
        [whole(array) for array in (*rows, *grads)]
        + [(w_in, column(first, second)) for first in (0, 2 * units) for second in range(2)]
        + [(w_down, row(second)) for second in range(2)],
        [
            whole_out(shape, FULL),
            whole_out(shape, LOW),
            whole_out(shape, FULL),
            whole_out(shape, LOW),
            ((2 * count, steps * PART), LOW, pl.BlockSpec((2 * count, PART), lambda i, at: (0, i))),
            ((2 * count, steps * PART), LOW, pl.BlockSpec((2 * count, PART), lambda i, at: (0, i))),
            ((hidden // 2, width // 2), LOW, pl.BlockSpec((PART, width // 2), lambda i, at: (i, 0))),
            ((hidden // 2, width // 2), LOW, pl.BlockSpec((PART, width // 2), lambda i, at: (i, 0))),
            whole_out((width, 2 * count), LOW),
        ],
        grid=(steps,),
        token=token,
        prefetch=(at,),
        scratch=[pltpu.VMEM((2 * count, width), FULL)] * 2,
        vmem=40,
        near_in=(0, 1, 2, 3),
        near_out=(2, 3, 4, 5, 6, 7, 8),
        us=24,
    )


def join_kernel(kept_ref, got_ref, out_ref):
    out_ref[...] = (kept_ref[...] + got_ref[...].astype(FULL)).astype(LOW).reshape(out_ref.shape)


def join(kept, got, shape, token):
    (out,), token = call(
        join_kernel,
        "join",
        [whole(kept), whole(got)],
        [whole_out(shape, LOW)],
        token=token,
        near_in=(0, 1),
        near_out=(0,),
        us=1,
    )
    return out, token


def join_peak_kernel(kept_ref, got_ref, peak_ref, out_ref):
    blocks, size, width = out_ref.shape
    rows = kept_ref.shape[0] // blocks
    best = jnp.concatenate([peak_ref[g, :GROUP, :] for g in range(peak_ref.shape[0])], axis=0)
    best = jnp.broadcast_to(jnp.max(best, axis=1, keepdims=True), (size - rows, LANES))
    upper = best.astype(LOW)
    lower = (best - upper.astype(FULL)).astype(LOW)
    for block in range(blocks):
        part = pl.ds(block * rows, rows)
        total = kept_ref[part, :] + got_ref[part, :].astype(FULL)
        out_ref[block, :rows, :] = total.astype(LOW)
        out_ref[block, rows:, :] = jnp.zeros((size - rows, width), LOW)
        out_ref[block, rows:, :LANES] = upper
        out_ref[block, rows:, LANES : 2 * LANES] = lower


def join_peak(kept, got, peak, blocks, token):
    rows, width = kept.shape
    heads = peak.shape[0] * GROUP
    (out,), token = call(
        join_peak_kernel,
        "join_peak",
        [whole(kept), whole(got), whole(peak)],
        [whole_out((blocks, rows // blocks + heads, width), LOW)],
        token=token,
        us=1.5,
    )
    return out, token


def larger_kernel(one_ref, two_ref, out_ref):
    out_ref[...] = jnp.maximum(one_ref[...], two_ref[...])


def larger(one, two, token):
    (out,), token = call(
        larger_kernel,
        "larger",
        [whole(one), whole(two)],
        [whole_out(one.shape, FULL)],
        token=token,
        near_in=(0, 1),
        near_out=(0,),
        us=0.5,
    )
    return out, token


def place():
    dp = lax.axis_index("dp")
    return lax.axis_index("ctx"), lax.axis_index("exp"), dp // 2, dp % 2


def pick_block(blocks, index):
    return lax.dynamic_index_in_dim(blocks, index, 0, keepdims=False)


def to_down_plane(array):
    pairs = [
        ((1 - core) * 4 + x * 2 + core, core * 4 + x * 2 + core)
        for core in range(2)
        for x in range(2)
    ]
    return lax.ppermute(array, ("ctx", "dp"), pairs)


def in_down_plane(array):
    pairs = [
        (core * 4 + x * 2 + core, core * 4 + (1 - x) * 2 + core)
        for core in range(2)
        for x in range(2)
    ]
    return lax.ppermute(array, ("ctx", "dp"), pairs)


def in_kernel(
    at_ref, rows_ref, gate_ref, up_ref, a_send_ref, a_keep_ref, b_send_ref, b_keep_ref
):
    size = a_send_ref.shape[1]
    right = jnp.concatenate([gate_ref[...], up_ref[...]], axis=1)
    for block in range(4):
        ry, rx = block // 2, block % 2
        chip = (at_ref[0] ^ ry) * 2 + (at_ref[1] ^ rx)
        both = dot_rows(rows_ref[pl.ds(chip * size, size), :], right)
        a, b = both[:, :LANES], both[:, LANES:]
        (a_send_ref if rx else a_keep_ref)[ry] = a.astype(LOW)
        (b_send_ref if ry else b_keep_ref)[rx] = b.astype(LOW)


def in_terms(at, rows, gate, up, hidden, token):
    width, count = rows.shape
    size = width // 4
    right = pl.BlockSpec((count, LANES), lambda i, at: (0, i))
    spec = pl.BlockSpec((2, size, LANES), lambda i, at: (0, 0, i))
    shape = (2, size, hidden // 2)
    return call(
        in_kernel,
        "in_terms",
        [whole(rows), (gate, right), (up, right)],
        [(shape, LOW, spec)] * 4,
        grid=(hidden // (2 * LANES),),
        token=token,
        prefetch=(at,),
        near_in=(0, 1, 2),
        near_out=(0, 2),
        us=6,
    )


def plane_first(parts):
    a_send, a_keep, b_send, b_keep = parts
    return swapped(a_send, "dp", 2), a_keep, swapped(b_send, "ctx", 1), b_keep


def second_kernel(a_ref, a_keep_ref, b_ref, b_keep_ref, a_send_ref, b_send_ref):
    a_send_ref[...] = (a_keep_ref[...].astype(FULL) + a_ref[...].astype(FULL)).astype(LOW)
    b_send_ref[...] = (b_keep_ref[...].astype(FULL) + b_ref[...].astype(FULL)).astype(LOW)


def second_terms(parts, token, cuts, us):
    inputs = []
    for part, axis in zip(parts, cuts):
        if axis is None:
            inputs.append(whole(part))
        else:
            shape = part.shape[:axis] + (None,) + part.shape[axis + 1 :]
            index = tuple(int(at == axis) for at in range(part.ndim))
            inputs.append((part, pl.BlockSpec(shape, lambda *_, index=index: index)))
    shapes = [
        tuple(size for size in spec.block_shape if size is not None)
        for _, spec in (inputs[0], inputs[2])
    ]
    return call(
        second_kernel,
        "second_terms",
        inputs,
        [whole_out(shape, LOW) for shape in shapes],
        token=token,
        us=us,
    )


def plane_second(parts, token, axis=0, us=1.5):
    (a_send, b_send), token = second_terms(parts, token, (axis,) * 4, us)
    return (parts, swapped(a_send, "ctx", 1), swapped(b_send, "dp", 2)), token


def plane_last(parts, axis=0):
    (a, a_keep, b, b_keep), a2, b2 = parts
    cut = lambda array: lax.index_in_dim(array, 0, axis, keepdims=False).astype(FULL)
    return cut(a_keep) + cut(a) + a2.astype(FULL), cut(b_keep) + cut(b) + b2.astype(FULL)


def down_last_kernel(
    at_ref, a_ref, a_keep_ref, b_ref, b_keep_ref, a2_ref, b2_ref, keep_ref, send_ref
):
    half = a_ref.shape[1]
    a, b = (
        sum(ref[...].astype(FULL) for ref in refs)
        for refs in ((a_keep_ref, a_ref, a2_ref), (b_keep_ref, b_ref, b2_ref))
    )

    @pl.when(pl.program_id(0) == 0)
    def _():
        send_ref[:, :half] = a.astype(LOW)
        send_ref[:, half:] = b.astype(LOW)

    @pl.when(pl.program_id(0) == 1)
    def _():
        keep_ref[:, :half] = a
        keep_ref[:, half:] = b


def down_last(at, parts, a2, b2, token):
    _, size, half = a2.shape
    core = lambda i, at: at[2] ^ (1 - i)
    three = pl.BlockSpec((None, size, half), lambda i, at: (core(i, at), 0, 0))
    four = pl.BlockSpec((None, None, size, half), lambda i, at: (0, core(i, at), 0, 0))
    shape = (size, 2 * half)
    (keep, send), token = call(
        down_last_kernel,
        "down_last",
        [(parts[0], three), (parts[1], three), (parts[2], four), (parts[3], four)]
        + [(a2, three), (b2, three)],
        [whole_out(shape, FULL), whole_out(shape, LOW)],
        grid=(2,),
        token=token,
        prefetch=(at,),
        us=3,
    )
    return keep, send, token


def choose_kernel(at_ref, keep_ref, got_ref, out_ref):
    mine = at_ref[0] == at_ref[2]
    out_ref[0] = jnp.where(mine, keep_ref[...], got_ref[...].astype(FULL))


def choose(at, keep, got, token):
    size, width = keep.shape
    rows = pl.BlockSpec((size // 2, width), lambda i, at: (i, 0))
    (out,), token = call(
        choose_kernel,
        "choose",
        [(keep, rows), (got, rows)],
        [((1, size, width), FULL, pl.BlockSpec((1, size // 2, width), lambda i, at: (0, i, 0)))],
        grid=(2,),
        token=token,
        prefetch=(at,),
        us=2,
    )
    return out, token


def in_last_kernel(
    at_ref, a_ref, a_keep_ref, b_ref, b_keep_ref, a2_ref, b2_ref, keep_ref, send_ref
):
    a, b = (
        sum(ref[...].astype(FULL) for ref in refs)
        for refs in ((a_keep_ref, a_ref, a2_ref), (b_keep_ref, b_ref, b2_ref))
    )

    @pl.when(pl.program_id(0) == 0)
    def _():
        send_ref[0] = a.astype(LOW)
        send_ref[1] = b.astype(LOW)

    @pl.when(pl.program_id(0) == 1)
    def _():
        keep_ref[0] = a
        keep_ref[1] = b


def in_last(at, parts, token):
    firsts, a2, b2 = parts
    rows, half = a2.shape
    size = rows // 2
    core = lambda i, at: at[2] ^ (1 - i)
    first = pl.BlockSpec((None, size, half), lambda i, at: (0, core(i, at), 0))
    second = pl.BlockSpec((size, half), lambda i, at: (core(i, at), 0))
    shape = (2, size, half)
    (keep, send), token = call(
        in_last_kernel,
        "in_last",
        [(part, first) for part in firsts] + [(a2, second), (b2, second)],
        [whole_out(shape, FULL), whole_out(shape, LOW)],
        grid=(2,),
        token=token,
        prefetch=(at,),
        us=4,
        vmem=16,
    )
    return keep, send, token


def in_end_kernel(at_ref, keep_ref, got_ref, out_ref):
    half = keep_ref.shape[2]
    for part in range(2):
        for first, value in (
            (at_ref[2], keep_ref[part]),
            (1 - at_ref[2], got_ref[part].astype(FULL)),
        ):
            start = pl.multiple_of((part * 2 + first) * half, LANES)
            out_ref[0, :, pl.ds(start, half)] = value


def in_end(at, keep, got, token):
    _, rows, half = keep.shape
    size = rows // 4
    spec = pl.BlockSpec((2, size, half), lambda i, at: (0, i, 0))
    (out,), token = call(
        in_end_kernel,
        "in_end",
        [(keep, spec), (got, spec)],
        [((1, rows, 4 * half), FULL, pl.BlockSpec((1, size, 4 * half), lambda i, at: (0, i, 0)))],
        grid=(4,),
        token=token,
        prefetch=(at,),
        us=2.5,
    )
    return out, token


EXTRA = 16
TABLE_LANE = 32


def turn_kernel(at_ref, own_ref, other_ref, out_ref, turned):
    count = own_ref.shape[0]
    turned[:, :count] = own_ref[...].T
    turned[:, count:] = other_ref[...].T
    size = out_ref.shape[0] // 16
    for to in range(16):
        device = device_at(to % 4, to // 4, at_ref)
        out_ref[pl.ds(to * size, size), :] = turned[pl.ds(device * size, size), :]


def device_at(block, z, at_ref):
    return (
        (at_ref[0] ^ (block // 2)) * 16 + z * 4 + (at_ref[1] ^ (block % 2)) * 2 + at_ref[2]
    )


def line_at(step, at):
    return at[3] ^ (step // 2) ^ (2 * (step % 2))


def turn(at, own, other, token):
    count, width = own.shape
    (out,), token = call(
        turn_kernel,
        "turn",
        [whole(own), whole(other)],
        [whole_out((width // 2, 2 * count), LOW)],
        token=token,
        prefetch=(at,),
        scratch=[pltpu.VMEM((width, 2 * count), LOW)],
        us=2,
        near_in=(0, 1),
        near_out=(0,),
    )
    return out, token


def shared_kernel(
    at_ref, left_ref, own_ref, other_ref,
    a_send_ref, a_keep_ref, b_send_ref, b_keep_ref, line_send_ref, line_keep_ref,
):
    step = pl.program_id(0)
    rows, count = left_ref.shape[0], left_ref.shape[1] // 2
    width = own_ref.shape[1]
    tokens = count // 3
    left = left_ref[...]

    def product(columns, start, length):
        return dot_rows(left[:, columns : columns + length], own_ref[start : start + length, :]) + (
            dot_rows(
                left[:, count + columns : count + columns + length],
                other_ref[start : start + length, :],
            )
        )

    total = [
        product(2 * tokens, 5 * tokens, tokens),
        product(tokens, 0, tokens),
        product(0, tokens, 2 * tokens),
        product(0, 3 * tokens, 2 * tokens),
    ]
    size = rows // 4
    first_lane = width - GROUP * HDIM
    small = own_ref[6 * tokens :, first_lane : first_lane + LANES].astype(FULL)
    small = small + other_ref[6 * tokens :, first_lane : first_lane + LANES].astype(FULL)
    place = lax.broadcasted_iota(jnp.int32, small.shape, 0)
    extras = []
    for block in range(4):
        device = device_at(block, line_at(step, at_ref), at_ref)
        row = jnp.sum(jnp.where(place == device, small, 0.0), 0, keepdims=True)
        extras.append(jnp.broadcast_to(row, (EXTRA, LANES)))
    for r in range(2):
        a_keep_ref[0, r] = total[0][(2 * r) * size : (2 * r + 1) * size]
        a_send_ref[0, r] = total[0][(2 * r + 1) * size : (2 * r + 2) * size].astype(LOW)
        b_keep_ref[0, r, :size, :] = total[1][r * size : (r + 1) * size]
        b_send_ref[0, r, :size, :] = total[1][(2 + r) * size : (3 + r) * size].astype(LOW)
        b_keep_ref[0, r, size:, :] = jnp.zeros((EXTRA, width), FULL)
        b_send_ref[0, r, size:, :] = jnp.zeros((EXTRA, width), LOW)
        b_keep_ref[0, r, size:, :LANES] = extras[r]
        b_send_ref[0, r, size:, :LANES] = extras[2 + r].astype(LOW)

    @pl.when(step < 2)
    def _():
        line_keep_ref[0, 0] = total[2]
        line_keep_ref[0, 1] = total[3]

    @pl.when(step >= 2)
    def _():
        line_send_ref[0, 0] = total[2].astype(LOW)
        line_send_ref[0, 1] = total[3].astype(LOW)


def shared_terms(at, left, own, other, experts, token):
    rows, count = left.shape
    width = own.shape[1]
    size = rows // experts
    a_shape, b_shape = ((experts, 2, size // 4 + extra, width) for extra in (0, EXTRA))
    cut = lambda shape: pl.BlockSpec((1, *shape[1:]), lambda i, at: (line_at(i, at), 0, 0, 0))
    line_shape = (2, 2, size, width)
    line = lambda index: pl.BlockSpec((1, *line_shape[1:]), lambda i, at: (index(i), 0, 0, 0))
    outs, token = call(
        shared_kernel,
        "shared_terms",
        [
            (left, pl.BlockSpec((size, count), lambda i, at: (line_at(i, at), 0))),
            whole(own),
            whole(other),
        ],
        [
            (a_shape, LOW, cut(a_shape)),
            (a_shape, FULL, cut(a_shape)),
            (b_shape, LOW, cut(b_shape)),
            (b_shape, FULL, cut(b_shape)),
            (line_shape, LOW, line(lambda i: i // 3)),
            (line_shape, FULL, line(lambda i: (i + 1) // 2 - i // 3)),
        ],
        grid=(experts,),
        token=token,
        prefetch=(at,),
        vmem=24,
        near_in=(0, 1, 2),
        near_out=(0, 2, 4),
        us=4,
    )
    return outs[:4], outs[4:], token


def line_second_kernel(got_ref, keep_ref, out_ref):
    out_ref[...] = (keep_ref[...] + got_ref[...].astype(FULL)).astype(LOW)


def line_second(got, keep, token):
    spec = pl.BlockSpec((None, *got.shape[1:]), lambda *_: (1, 0, 0, 0))
    (out,), token = call(
        line_second_kernel,
        "line_second",
        [(got, spec), (keep, spec)],
        [whole_out(got.shape[1:], LOW)],
        token=token,
        us=1,
    )
    return out, token


def line_last_kernel(
    got_ref, keep_ref, second_ref, a_send_ref, a_keep_ref, b_send_ref, b_keep_ref
):
    size = a_send_ref.shape[1]
    total = keep_ref[...] + got_ref[...].astype(FULL) + second_ref[...].astype(FULL)
    for r in range(2):
        a_keep_ref[r] = total[0, (2 * r) * size : (2 * r + 1) * size]
        a_send_ref[r] = total[0, (2 * r + 1) * size : (2 * r + 2) * size].astype(LOW)
        b_keep_ref[r] = total[1, r * size : (r + 1) * size]
        b_send_ref[r] = total[1, (2 + r) * size : (3 + r) * size].astype(LOW)


def line_last(got, keep, second, token):
    _, rows, width = second.shape
    shape = (2, rows // 4, width)
    spec = pl.BlockSpec((None, *got.shape[1:]), lambda *_: (0, 0, 0, 0))
    return call(
        line_last_kernel,
        "line_last",
        [(got, spec), (keep, spec), whole(second)],
        [whole_out(shape, dtype) for dtype in (LOW, FULL, LOW, FULL)],
        token=token,
        us=1,
    )


def back_kernel(
    spread_ref, rows_ref, after_ref, gain_ref, grad_ref, weights_ref,
    total_ref, branch_ref, attended_ref, gain_grad_ref,
):
    rows = after_ref[...]
    inverse = lax.rsqrt(jnp.mean(rows * rows, axis=1, keepdims=True) + EPSILON)
    scaled = rows * inverse
    grad = transpose_dot(spread_ref[...], rows_ref[...])
    gain_grad_ref[...] = jnp.sum(scaled * grad, axis=0, keepdims=True)
    grad = grad * gain_ref[...]
    along = jnp.mean(scaled * grad, axis=1, keepdims=True)
    total = grad_ref[...].astype(FULL) + inverse * (grad - scaled * along)
    total_ref[...] = total
    branch = total.astype(LOW)
    branch_ref[...] = branch
    attended_ref[...] = dot_back(branch, weights_ref[...]).astype(LOW)


def back_to_attention(spread, rows, after, gain, grad, weights, token):
    shape = after.shape
    inputs = (spread, rows, after, gain, grad, weights)
    return call(
        back_kernel,
        "back",
        [whole(array) for array in inputs],
        [
            whole_out(shape, FULL),
            whole_out(shape, LOW),
            whole_out(shape, LOW),
            whole_out((1, shape[1]), FULL),
        ],
        token=token,
        vmem=16,
        us=3,
        near_in=(0, 1, 2, 5),
        near_out=(1, 2),
    )


def mix_kernel(pick_ref, rows_ref, gates_ref, after_ref, out_ref, peak_ref):
    top, tokens = gates_ref.shape
    blocks = rows_ref.shape[0]
    size = pick_ref.shape[0] // blocks
    total = after_ref[...]
    gates = [to_column(gates_ref[r : r + 1, :]) for r in range(top)]
    for block in range(blocks):
        rows = rows_ref[block, :size, :]
        for r in range(top):
            pick = pick_ref[pl.ds(block * size, size), pl.ds(r * tokens, tokens)]
            total = total + gates[r] * transpose_dot(pick, rows)
    out_ref[0] = total.astype(LOW)
    if rows_ref.shape[1] > size:
        peaks = [
            rows_ref[block, size:, :LANES].astype(FULL)
            + rows_ref[block, size:, LANES : 2 * LANES].astype(FULL)
            for block in range(blocks)
        ]
        peak_ref[...] = functools.reduce(jnp.maximum, peaks)


def mix(pick, rows, gates, after, token):
    (out, peak), token = call(
        mix_kernel,
        "mix",
        [whole(pick), whole(rows), whole(gates), whole(after)],
        [whole_out((1, *after.shape), LOW), whole_out((16, LANES), FULL)],
        token=token,
        near_in=(1,),
        us=2.5,
    )
    return out, peak, token


def local(
    block_in,
    seg_ids,
    routes,
    gates,
    buckets,
    norm_attn,
    norm_ffn,
    w_query,
    w_key,
    w_value,
    w_out_attn,
    rel_bias,
    clip_level,
    w_in,
    w_down,
    cotangent,
):
    tokens, width = block_in.shape[1:]
    heads = width // HDIM
    n_ctx, experts, n_dp = (lax.axis_size(axis) for axis in ("ctx", "exp", "dp"))
    fast = (n_ctx, experts, n_dp) == (2, 4, 4)
    devices = n_ctx * experts * n_dp
    length = n_ctx * tokens
    hidden = w_down.shape[1]
    y, z, x, core = place()
    place_all = (y * experts + z) * n_dp + lax.axis_index("dp")
    top_count = routes.shape[-1]
    capacity = tokens * top_count * 3 // (2 * experts)
    at = jnp.stack([y, x, core, z])

    backs = list(range(n_ctx - 1, 0, -1))
    earlier = [
        lax.ppermute(block_in[0], "ctx", [(i, (i + back) % n_ctx) for i in range(n_ctx)])
        for back in backs
    ]

    (spread, pick, grad_out, mask), _ = front(
        at, routes[0].T, gates[0].T, cotangent[0], seg_ids, experts, capacity
    )
    expert_grad = over_experts(grad_out).reshape(-1, width)
    (bucket_hot, bias), _ = bias_tiles(
        buckets.reshape(1, length), rel_bias.reshape(NB, heads), tokens
    )

    own_rows = block_in[0].astype(FULL)
    normed_own = rms_norm(own_rows, norm_attn).astype(LOW)
    normed_all = jnp.concatenate(
        [rms_norm(rows.astype(FULL), norm_attn).astype(LOW) for rows in earlier] + [normed_own],
        axis=0,
    )
    queries = dot_rows(normed_own, w_query).astype(LOW)
    keys = dot_rows(normed_all, w_key).astype(LOW)
    values = dot_rows(normed_all, w_value).astype(LOW)
    attended, probs, peak_lanes = attention(queries, keys, values, bias, mask)
    after = own_rows + dot_rows(attended, w_out_attn)

    sent = rms_norm(after, norm_ffn).astype(LOW)
    sent_rows = dot_rows(spread, sent).astype(LOW).reshape(experts, capacity, width)
    expert_rows = over_experts(sent_rows).reshape(-1, width)
    own_gain, own_table = width // devices, NB * heads // devices
    token = None
    if fast:
        beside = jnp.concatenate([normed_all, attended], axis=0)
        left, token = turn(at, beside, swapped(beside, "dp", 1), token)
        peak, token = larger(peak_lanes, swapped(peak_lanes, "dp", 1), token)
        peak, token = larger(peak, swapped(peak, "dp", 2), token)
        peak, token = larger(peak, swapped(peak, "ctx", 1), token)
        both_rows = expert_rows, swapped(expert_rows, "dp", 1)
        both_grads = expert_grad, swapped(expert_grad, "dp", 1)
        outs, token = expert_halves(at, both_rows, both_grads, w_in, w_down, token)
        out_keep, out_send, back_keep, back_send, dgate, dup, down_a, down_b, rows_turned = outs
        back_got = swapped(back_send, "dp", 1)
        down_a = down_a.reshape(2, 2, hidden // 8, width // 2)
        down_b = down_b.reshape(2, 2, hidden // 8, width // 2)
        down_by_x = jnp.stack([pick_block(down_b, x), pick_block(down_b, 1 - x)])
        down = (
            swapped(pick_block(down_a, 1 - x), "dp", 2),
            pick_block(down_a, x),
            to_down_plane(down_by_x),
            down_by_x,
        )
        back_rows, token = join(back_keep, back_got, (experts, capacity, width), token)
    else:
        (out_rows, back_rows, dgate, dup, hid_turned, rows_turned), token = expert(
            expert_rows, expert_grad, w_in, w_down, token
        )
        back_rows = back_rows.reshape(experts, capacity, width)
        expert_first, expert_second = (
            lax.psum_scatter(grads, ("ctx", "dp"), scatter_dimension=0, tiled=True)[None]
            for grads in (
                dot_rows(rows_turned, jnp.concatenate([dgate, dup], axis=1)),
                dot_rows(hid_turned, expert_grad),
            )
        )
    back_home = over_experts(back_rows).reshape(-1, width)
    if fast:
        first, token = in_terms(at, rows_turned, dgate, dup, hidden, token)
        first = plane_first(first)

    (grad_after, grad_branch, grad_attended, grad_gain_ffn), token = back_to_attention(
        spread, back_home, after, norm_ffn.reshape(1, width), cotangent[0], w_out_attn, token
    )
    if fast:
        packed, token = attention_back(
            queries, keys, values, probs, grad_attended, token,
            (grad_branch, bucket_hot, grad_gain_ffn, devices),
        )
        packed_got = swapped(packed, "dp", 1)
        (a_send, b_send), token = second_terms(down, token, (None, None, 0, 0), 20)
        down_more = to_down_plane(a_send), in_down_plane(b_send)
        out_got = swapped(out_send, "dp", 1)
        plane_2, line, token = shared_terms(at, left, packed, packed_got, experts, token)
        line_send, line_keep = line
        line_got = swapped(line_send, "exp", 1)
        plane_2 = plane_first(plane_2)
        out_rows, token = join_peak(out_keep, out_got, peak, experts, token)
        out_home = over_experts(out_rows)
        first, token = plane_second(first, token, us=3)
        keep, send, token = down_last(at, down, *down_more, token)
        down_got = swapped(send, "dp", 1)
        line_send, token = line_second(line_got, line_keep, token)
        line_more = swapped(line_send, "exp", 2)
        expert_second, token = choose(at, keep, down_got, token)
        mixed, peak, token = mix(pick, out_home, gates[0].T, after, token)
        peak = peak[:, 0]
        packed, = hold(token, packed)
        dq = packed[:tokens]
        dk = packed[tokens : tokens + length]
        dv = packed[tokens + length : tokens + 2 * length]
    else:
        dq, dk, dv, lines, token = attention_back(
            queries, keys, values, probs, grad_attended, token
        )
        lines = lines[:, :GROUP, :].reshape(heads, length + tokens)
        grad_table = lax.dot_general(
            bucket_hot, lines, (((1,), (1,)), ((), ())), precision=FULL_PRECISION
        ).reshape(-1)
        out_home = over_experts(out_rows.reshape(experts, capacity, width))
        mixed, _, _ = mix(pick, out_home, gates[0].T, after, token)
        peak = jnp.max(peak_lanes[:, :GROUP, :], axis=-1).reshape(heads)
        peak = lax.pmax(peak, ("ctx", "exp", "dp"))

    grad_normed = dot_back(dk, w_key) + dot_back(dv, w_value)
    grad_normed_own = grad_normed[length - tokens :] + dot_back(dq, w_query)
    for block, back in enumerate(backs):
        term = grad_normed[block * tokens : (block + 1) * tokens].astype(LOW)
        returned = lax.ppermute(term, "ctx", [((i + back) % n_ctx, i) for i in range(n_ctx)])
        grad_normed_own = grad_normed_own + returned.astype(FULL)
    _, norm_pull = jax.vjp(lambda rows: rms_norm(rows, norm_attn), own_rows)
    grad_input = grad_after + norm_pull(grad_normed_own)[0]

    factor = clip_level / jnp.maximum(peak, clip_level)
    column_scale = jnp.repeat(jnp.sqrt(factor), HDIM)
    clipped_query = w_query.astype(FULL) * column_scale[None, :]
    clipped_key = w_key.astype(FULL) * column_scale[None, :]

    if fast:
        plane_2, token = plane_second(plane_2, token, axis=1)
        line, token = line_last(line_got, line_keep, line_more, token)
        line = plane_first(line)
        keep, send, token = in_last(at, first, token)
        in_got = swapped(send, "dp", 1)
        plane_o, plane_q = plane_last(plane_2, axis=1)
        total = jnp.concatenate([plane_o, plane_q], axis=1).astype(LOW)
        total = over_experts(total).astype(FULL).sum(axis=0)
        shared_o, shared_q = total[:own_gain], total[own_gain : 2 * own_gain]
        small = total[2 * own_gain]
        small_ffn, small_table = small[:own_gain], small[TABLE_LANE : TABLE_LANE + own_table]
        line, token = plane_second(line, token)
        expert_first, token = in_end(at, keep, in_got, token)
        shared_k, shared_v = plane_last(line)
    else:
        shared_q, shared_k, shared_v, shared_o = (
            lax.psum_scatter(grads, ("ctx", "exp", "dp"), scatter_dimension=0, tiled=True)
            for grads in (
                transpose_dot(normed_own, dq),
                transpose_dot(normed_all, dk),
                transpose_dot(normed_all, dv),
                transpose_dot(attended, grad_branch),
            )
        )
        small_ffn, small_table = (
            lax.dynamic_slice_in_dim(lax.psum(array, ("ctx", "exp", "dp")), place_all * own, own)
            for array, own in ((grad_gain_ffn[0], own_gain), (grad_table, own_table))
        )
    pairs = ((shared_q, w_query), (shared_k, w_key), (shared_v, w_value))
    row_sums = sum(
        jnp.sum(
            grads * lax.dynamic_slice_in_dim(weights, place_all * own_gain, own_gain).astype(FULL),
            axis=1,
        )
        for grads, weights in pairs
    )
    small_attn = row_sums / lax.dynamic_slice_in_dim(norm_attn, place_all * own_gain, own_gain)

    return (
        mixed,
        grad_input[None],
        small_attn,
        small_ffn,
        shared_q,
        shared_k,
        shared_v,
        shared_o,
        small_table,
        expert_first,
        expert_second,
        clipped_query,
        clipped_key,
        factor,
    )


def solution(mesh):
    tokens = P(("exp", "dp"), "ctx", None)
    everywhere = P(("ctx", "exp", "dp"))
    by_rows = P(("ctx", "exp", "dp"), None)
    by_expert = P("exp", None, None)
    expert_rows = P("exp", ("ctx", "dp"), None)
    in_specs = (tokens, P(("exp", "dp"), None), tokens, tokens) + (P(),) * 9
    in_specs = in_specs + (by_expert, by_expert, tokens)
    out_specs = (tokens, tokens, everywhere, everywhere) + (by_rows,) * 4
    out_specs = out_specs + (everywhere, expert_rows, expert_rows, P(), P(), P())
    return jax.shard_map(local, mesh=mesh, in_specs=in_specs, out_specs=out_specs, check_vma=False)
```

```python
import functools

import jax
import jax.numpy as jnp
from jax import lax
from jax.experimental import pallas as pl
from jax.experimental.pallas import tpu as pltpu
from jax.sharding import PartitionSpec as P

HDIM = 64
NB = 32
GROUP = 4
LANES = 128
EPSILON = 1e-06
FULL_PRECISION = lax.Precision.HIGHEST
LOW = jnp.bfloat16
FULL = jnp.float32
OUTSIDE = -1e30
GELU_SCALE = 0.7978845608028654
GELU_CUBE = 0.044715


def rms_norm(rows, gain):
    return rows * lax.rsqrt(jnp.mean(rows * rows, axis=-1, keepdims=True) + EPSILON) * gain


def dot_rows(left, right):
    return lax.dot_general(left, right, (((1,), (0,)), ((), ())), preferred_element_type=FULL)


def dot_back(left, right):
    return lax.dot_general(left, right, (((1,), (1,)), ((), ())), preferred_element_type=FULL)


def transpose_dot(left, right):
    return lax.dot_general(left, right, (((0,), (0,)), ((), ())), preferred_element_type=FULL)


def swapped(array, axis, bit):
    size = lax.axis_size(axis)
    return lax.ppermute(array, axis, [(i, i ^ bit) for i in range(size)])


def shifted(array, axis, shift):
    size = lax.axis_size(axis)
    return lax.ppermute(array, axis, [(i, (i + shift) % size) for i in range(size)])


def to_experts(blocks):
    return [blocks[0]] + [shifted(blocks[k], "exp", k) for k in range(1, len(blocks))]


def from_experts(blocks):
    return [blocks[0]] + [shifted(blocks[k], "exp", len(blocks) - k) for k in range(1, len(blocks))]


def over_experts(blocks):
    return lax.all_to_all(blocks, "exp", split_axis=0, concat_axis=0, tiled=True)


MICROSECOND = 1.15e9


def call(
    body, name, inputs, outputs, us, grid=None, token=None, prefetch=(), scratch=(), vmem=6,
    near_in=(), near_out=(), far_in=(), far_out=(), fetch=(),
    part_in=None,
):
    part_in = dict(part_in or {})
    far_in = tuple(far_in) + tuple(part_in)
    inputs = list(inputs) + [(array, None) for array in fetch]
    outputs = list(outputs) + [whole_out(array.shape, array.dtype) for array in fetch]
    n_pre, n_in, n_out = len(prefetch), len(inputs), len(outputs)
    held = [] if token is None else [token]
    n_far, n_scratch = len(far_in) + len(far_out), len(scratch)

    def kernel(*refs):
        split = n_pre + n_in
        outs = split + len(held)
        rest = refs[outs + n_out + 1 :]
        ins_here, outs_here = list(refs[:split]), list(refs[outs : outs + n_out])
        copies = []
        for number, at in enumerate(far_in):
            here = rest[n_scratch + number]
            source = refs[n_pre + at].at[part_in[at]] if at in part_in else refs[n_pre + at]
            copies.append(pltpu.make_async_copy(source, here, rest[-1].at[number]))
            ins_here[n_pre + at] = here
        for copy in copies:
            copy.start()
        fetches = [
            pltpu.make_async_copy(ins_here.pop(), outs_here.pop(), rest[-1].at[n_far + number])
            for number in range(len(fetch))
        ]
        for copy in fetches:
            copy.start()
        for copy in copies:
            copy.wait()
        copies = []
        for number, at in enumerate(far_out, len(far_in)):
            here = rest[n_scratch + number]
            copies.append(pltpu.make_async_copy(here, refs[outs + at], rest[-1].at[number]))
            outs_here[at] = here
        body(*ins_here, *outs_here, *rest[:n_scratch])
        for copy in fetches:
            copy.wait()
        for copy in copies:
            copy.start()
        for copy in copies:
            copy.wait()

    where = lambda at, near: pltpu.VMEM if at in near else pltpu.HBM
    arrays = [array for array, _ in inputs]
    shapes = [(shape, dtype) for shape, dtype, _ in outputs]
    anywhere = pl.BlockSpec(memory_space=pl.ANY)
    if grid is None:
        near = pl.BlockSpec(memory_space=pltpu.VMEM)
        far = [at in far_in or spec is None for at, (_, spec) in enumerate(inputs)]
        far_results = [at in far_out or spec is None for at, (_, _, spec) in enumerate(outputs)]
        left = lambda at: tuple(
            size if axis >= len(part_in.get(at, ())) else len(range(size)[part_in[at][axis]])
            for axis, size in enumerate(arrays[at].shape)
            if axis >= len(part_in.get(at, ())) or isinstance(part_in[at][axis], slice)
        )
        buffers = [pltpu.VMEM(left(at), arrays[at].dtype) for at in far_in]
        buffers += [pltpu.VMEM(*shapes[at]) for at in far_out]
        n_sems = n_far + len(fetch)
        buffers += [pltpu.SemaphoreType.DMA((n_sems,))] if n_sems else []
        form = dict(
            in_specs=[pl.BlockSpec(memory_space=pltpu.SMEM)] * n_pre
            + [anywhere if away else near for away in far]
            + [anywhere] * len(held),
            out_specs=[anywhere if away else near for away in far_results] + [anywhere],
            scratch_shapes=list(scratch) + buffers,
        )
        arrays = [
            pltpu.with_memory_space_constraint(array, pltpu.HBM) if away else array
            for array, away in zip(arrays, far)
        ]
        shapes = [
            pltpu.HBM(*one) if away else jax.ShapeDtypeStruct(*one)
            for away, one in zip(far_results, shapes)
        ]
    else:
        form = dict(
            grid_spec=pltpu.PrefetchScalarGridSpec(
                num_scalar_prefetch=n_pre,
                grid=grid,
                in_specs=[spec for _, spec in inputs] + [anywhere] * len(held),
                out_specs=[spec for _, _, spec in outputs] + [anywhere],
                scratch_shapes=list(scratch),
            )
        )
        arrays = [
            pltpu.with_memory_space_constraint(array, where(at, near_in))
            for at, array in enumerate(arrays)
        ]
        shapes = [where(at, near_out)(*one) for at, one in enumerate(shapes)]
    held = [pltpu.with_memory_space_constraint(array, pltpu.HBM) for array in held]
    results = pl.pallas_call(
        kernel,
        out_shape=shapes + [pltpu.HBM((8, LANES), FULL)],
        cost_estimate=pl.CostEstimate(
            flops=int(us * MICROSECOND), bytes_accessed=1, transcendentals=0
        ),
        compiler_params=pltpu.CompilerParams(vmem_limit_bytes=vmem * 2**20),
        name=name,
        **form,
    )(*prefetch, *arrays, *held)
    return list(results[:-1]), results[-1]


def whole(array):
    return array, pl.BlockSpec(array.shape, lambda *_: (0,) * array.ndim)


def whole_out(shape, dtype):
    return shape, dtype, pl.BlockSpec(shape, lambda *_: (0,) * len(shape))


def hold(token, *arrays):
    anywhere = pl.BlockSpec(memory_space=pl.ANY)
    return pl.pallas_call(
        lambda *refs: None,
        in_specs=[anywhere] * (len(arrays) + 1),
        out_specs=[anywhere] * len(arrays),
        out_shape=[jax.ShapeDtypeStruct(array.shape, array.dtype) for array in arrays],
        input_output_aliases={at + 1: at for at in range(len(arrays))},
        cost_estimate=pl.CostEstimate(flops=1, bytes_accessed=1, transcendentals=0),
        name="hold",
    )(token, *arrays)


def pass_kernel(*refs):
    half = len(refs) // 2
    for ref, out_ref in zip(refs[:half], refs[half:]):
        out_ref[...] = ref[...]


def pass_on(token, *arrays):
    return call(
        pass_kernel,
        "pass_on",
        [whole(array) for array in arrays],
        [whole_out(array.shape, array.dtype) for array in arrays],
        token=token,
        us=1,
    )


def eye(size):
    rows = lax.broadcasted_iota(jnp.int32, (size, size), 0)
    return rows == lax.broadcasted_iota(jnp.int32, (size, size), 1)


def to_column(row):
    size = row.shape[1]
    return jnp.sum(jnp.where(eye(size), row, jnp.zeros_like(row)), 1, keepdims=True)


def front_kernel(
    at_ref, routes_ref, gates_ref, grad_ref, seg_ref, rows_ref,
    spread_ref, pick_ref, mask_ref, copy_ref, *out_refs,
):
    top, tokens = routes_ref.shape
    experts, capacity = len(out_refs), out_refs[0].shape[0]
    routes = [routes_ref[r : r + 1, :] for r in range(top)]
    gates = [gates_ref[r : r + 1, :] for r in range(top)]
    before = lax.broadcasted_iota(jnp.int32, (tokens, tokens), 0)
    before = before < lax.broadcasted_iota(jnp.int32, (tokens, tokens), 1)
    slots = lax.broadcasted_iota(jnp.int32, (capacity, tokens), 0).astype(FULL)
    for e in range(experts):
        part = pl.ds(e * capacity, capacity)
        name = lax.rem(at_ref[3] + e, experts)
        hits = [jnp.where(route == name, 1.0, 0.0) for route in routes]
        named = functools.reduce(jnp.add, hits)
        slot = jnp.sum(jnp.where(before, to_column(named), 0.0), 0, keepdims=True)
        place = (slots == slot).astype(FULL)
        spread = place * named
        gate = functools.reduce(jnp.add, [hit * g for hit, g in zip(hits, gates)])
        spread_low = spread.astype(LOW)
        spread_ref[part, :] = spread_low
        for r in range(top):
            pick_ref[part, pl.ds(r * tokens, tokens)] = (place * hits[r]).astype(LOW)
        slot_gate = jnp.sum(spread * gate, 1, keepdims=True)
        out_refs[e][...] = (slot_gate * dot_rows(spread_low, grad_ref[...])).astype(LOW)
    length = mask_ref.shape[1]
    ctx = at_ref[0]
    seg = jnp.broadcast_to(seg_ref[...].astype(FULL), (8, length))
    keys = pltpu.roll(seg, length - (ctx + 1) * tokens, 1)[:1, :]
    at_row = lax.broadcasted_iota(jnp.int32, (tokens, length), 0) + (length - tokens)
    at_key = lax.broadcasted_iota(jnp.int32, (tokens, length), 1)
    own = jnp.sum(jnp.where(at_row == at_key, keys, 0.0), 1, keepdims=True)
    allowed = (at_key <= at_row) & (own == keys) & (at_key >= length - (ctx + 1) * tokens)
    mask_ref[...] = jnp.where(allowed, 0.0, OUTSIDE)
    copy_ref[...] = rows_ref[...]


def front(at, routes, gates, grad, seg, rows, experts, capacity):
    top, tokens = routes.shape
    slots = experts * capacity
    return call(
        front_kernel,
        "front",
        [whole(array) for array in (routes, gates, grad, seg, rows)],
        [
            whole_out((slots, tokens), LOW),
            whole_out((slots, top * tokens), LOW),
            whole_out((tokens, seg.shape[1]), FULL),
            whole_out(rows.shape, LOW),
        ]
        + [whole_out((capacity, grad.shape[1]), LOW)] * experts,
        prefetch=(at,),
        far_in=(0, 1, 2, 3, 4),
        far_out=(1,),
        us=1.5,
    )


def bias_kernel(buckets_ref, table_ref, hot_ref, bias_ref):
    heads, rows, keys = bias_ref.shape
    width = hot_ref.shape[1]
    buckets = buckets_ref[...].astype(FULL)
    column = jnp.sum(jnp.where(eye(keys), buckets, 0.0), 1, keepdims=True)
    distance = lax.broadcasted_iota(jnp.int32, (keys, width), 0)
    lane = lax.broadcasted_iota(jnp.int32, (keys, width), 1)
    turned = jnp.sum(jnp.where(distance + lane == keys - 1, column, 0.0), 0, keepdims=True)
    bucket = lax.broadcasted_iota(jnp.int32, (NB, width), 0).astype(FULL)
    hot = jnp.where(bucket == turned, 1.0, 0.0)
    hot_ref[...] = hot
    by_lane = lax.dot_general(
        table_ref[...], hot, (((0,), (0,)), ((), ())), precision=FULL_PRECISION,
        preferred_element_type=FULL,
    )
    for head in range(heads):
        line = jnp.broadcast_to(by_lane[head : head + 1, :], (8, width))
        line = pltpu.roll(line, keys + 1, 1, stride=1, stride_axis=0)
        for start in range(0, rows, 8):
            moved = line if start == 0 else pltpu.roll(line, start, 1)
            bias_ref[head, pl.ds(start, 8), :] = moved[:, :keys]


def bias_tiles(buckets, table, rows, fetch):
    heads, keys = table.shape[1], buckets.shape[1]
    return call(
        bias_kernel,
        "bias_tiles",
        [whole(buckets), whole(table)],
        [whole_out((NB, keys + rows), FULL), whole_out((heads, rows, keys), FULL)],
        us=2.5,
        vmem=16,
        fetch=fetch,
    )


def half_lanes(half, shape):
    lane = lax.broadcasted_iota(jnp.int32, shape, 1)
    return lane < HDIM if half == 0 else lane >= HDIM


def attention_kernel(q_ref, k_ref, v_ref, bias_ref, mask_ref, out_ref, probs_ref, peak_ref):
    groups = peak_ref.shape[0]

    def group(step, _):
        mask = mask_ref[...]
        for pair in range(GROUP // 2):
            lanes = pair_lanes(step, pair)
            queries, keys, values = q_ref[:, lanes], k_ref[:, lanes], v_ref[:, lanes]
            parts = []
            for half in range(2):
                at = 2 * pair + half
                own = half_lanes(half, queries.shape)
                raw = dot_back(jnp.where(own, queries, jnp.zeros_like(queries)), keys)
                raw = raw * HDIM**-0.5 + mask
                top = jnp.max(raw, axis=0, keepdims=True)
                best = top[:, :LANES]
                for start in range(LANES, top.shape[1], LANES):
                    best = jnp.maximum(best, top[:, start : start + LANES])
                peak_ref[step, at : at + 1, :] = best
                scores = raw + bias_ref[step * GROUP + at]
                raised = jnp.exp(scores - jnp.max(scores, axis=1, keepdims=True))
                probs = raised * (1.0 / jnp.sum(raised, axis=1, keepdims=True))
                probs_low = probs.astype(LOW)
                probs_ref[step * GROUP + at] = probs_low
                parts.append(dot_rows(probs_low, values))
            first = half_lanes(0, parts[0].shape)
            out_ref[:, lanes] = jnp.where(first, parts[0], parts[1]).astype(LOW)
        return 0

    lax.fori_loop(0, groups, group, 0)


def pair_lanes(step, pair):
    return pl.ds(pl.multiple_of(step * GROUP * HDIM + pair * LANES, LANES), LANES)


def attention(queries, keys, values, bias, mask, fetch):
    rows, width = queries.shape
    length = keys.shape[0]
    heads = width // HDIM
    (out, probs, peak, *fetched), _ = call(
        attention_kernel,
        "attention",
        [whole(array) for array in (queries, keys, values, bias, mask)],
        [
            whole_out((rows, width), LOW),
            whole_out((heads, rows, length), LOW),
            whole_out((heads // GROUP, 8, LANES), FULL),
        ],
        us=4.5,
        vmem=10,
        far_out=(1,),
        fetch=fetch,
    )
    return out, probs, peak, *fetched


def attention_back_kernel(
    q_ref, k_ref, v_ref, probs_ref, grad_ref, dq_ref, dk_ref, dv_ref, lines_ref
):
    groups = lines_ref.shape[0]
    rows, length = probs_ref.shape[1:]
    scale = HDIM**-0.5

    def group(step, _):
        for pair in range(GROUP // 2):
            lanes = pair_lanes(step, pair)
            queries, keys, values, grad = (
                ref[:, lanes] for ref in (q_ref, k_ref, v_ref, grad_ref)
            )
            dq, dk, dv = [], [], []
            for half in range(2):
                at = 2 * pair + half
                own = half_lanes(half, grad.shape)
                dp = dot_back(jnp.where(own, grad, jnp.zeros_like(grad)), values)
                probs_low = probs_ref[step * GROUP + at]
                probs = probs_low.astype(FULL)
                ds = probs * (dp - jnp.sum(probs * dp, axis=1, keepdims=True))
                ds_low = ds.astype(LOW)
                dq.append(dot_rows(ds_low, keys))
                dk.append(transpose_dot(ds_low, queries))
                dv.append(transpose_dot(probs_low, grad))
                wide = jnp.concatenate([ds, jnp.zeros((rows, rows), FULL)], axis=1)
                total = wide[rows - 8 :, :]
                for start in range(0, rows - 8, 8):
                    total = total + pltpu.roll(wide[start : start + 8, :], rows - 8 - start, 1)
                line = lax.broadcasted_iota(jnp.int32, total.shape, 0)
                for bit in (1, 2, 4):
                    total = jnp.where(((7 - line) & bit) != 0, pltpu.roll(total, bit, 1), total)
                lines_ref[step, at : at + 1, :] = jnp.sum(total, axis=0, keepdims=True)
            first = half_lanes(0, dq[0].shape)
            dq_ref[:, lanes] = (jnp.where(first, dq[0], dq[1]) * scale).astype(LOW)
            first = half_lanes(0, dk[0].shape)
            dk_ref[:, lanes] = (jnp.where(first, dk[0], dk[1]) * scale).astype(LOW)
            dv_ref[:, lanes] = jnp.where(first, dv[0], dv[1]).astype(LOW)
        return 0

    lax.fori_loop(0, groups, group, 0)


def packed_back_kernel(
    q_ref, k_ref, v_ref, probs_ref, grad_ref, branch_ref, hot_ref, gain_ref, out_ref, lines_ref
):
    rows, length = probs_ref.shape[1:]
    ends = [0, rows, rows + length, rows + 2 * length, 2 * rows + 2 * length]
    parts = [out_ref.at[pl.ds(a, b - a), :] for a, b in zip(ends, ends[1:])]
    attention_back_kernel(q_ref, k_ref, v_ref, probs_ref, grad_ref, *parts[:3], lines_ref)
    parts[3][...] = branch_ref[...]
    groups = lines_ref.shape[0]
    width = gain_ref.shape[1]
    devices = out_ref.shape[0] - ends[4]
    own, turns = width // devices, LANES * devices // width
    device = lax.broadcasted_iota(jnp.int32, (devices, width), 0)
    feature = lax.broadcasted_iota(jnp.int32, (devices, width), 1)
    spread = jnp.where(feature // own == device, gain_ref[...], 0.0)
    folded = functools.reduce(
        jnp.add, [spread[:, start : start + LANES] for start in range(0, width, LANES)]
    )
    device = lax.broadcasted_iota(jnp.int32, folded.shape, 0)
    small = folded
    for turn_by in range(1, turns):
        moved = pltpu.roll(folded, LANES - turn_by * own, 1)
        small = jnp.where(device % turns == turn_by, moved, small)
    lines = jnp.concatenate([lines_ref[g, :GROUP, :] for g in range(groups)], axis=0)
    blank = jnp.zeros((LANES - TABLE_LANE - lines.shape[0], lines.shape[1]), FULL)
    lines = jnp.concatenate([jnp.zeros((TABLE_LANE, lines.shape[1]), FULL), lines, blank], axis=0)
    upper = lines.astype(LOW)
    lower = (lines - upper.astype(FULL)).astype(LOW)
    hot = hot_ref[...].astype(LOW)
    small = small + dot_back(hot, upper) + dot_back(hot, lower)
    out_ref[pl.ds(ends[4], devices), :LANES] = small.astype(LOW)


def attention_back(queries, keys, values, probs, grad, token, packed=None):
    rows, width = queries.shape
    length = keys.shape[0]
    heads = width // HDIM
    lines = whole_out((heads // GROUP, 8, length + rows), FULL)
    inputs = [whole(array) for array in (queries, keys, values, probs, grad)]
    if packed is None:
        outs, token = call(
            attention_back_kernel,
            "attention_back",
            inputs,
            [whole_out((size, width), LOW) for size in (rows, length, length)] + [lines],
            token=token,
            us=6.6,
            vmem=16,
        )
        return *outs, token
    branch, hot, gain, devices = packed
    (out, _), token = call(
        packed_back_kernel,
        "attention_back",
        inputs + [whole(branch), whole(hot), whole(gain)],
        [whole_out((2 * rows + 2 * length + devices, width), LOW), lines],
        token=token,
        us=7,
        vmem=16,
        far_in=(0, 1, 2, 3, 6),
    )
    return out, token


def post_kernel(attended_ref, weights_ref, rows_ref, gain_ref, spread_ref, after_ref, *out_refs):
    after = rows_ref[...].astype(FULL) + dot_rows(attended_ref[...], weights_ref[...])
    after_ref[...] = after
    sent = rms_norm(after, gain_ref[...]).astype(LOW)
    size = out_refs[0].shape[0]
    for at, out_ref in enumerate(out_refs):
        out_ref[...] = dot_rows(spread_ref[pl.ds(at * size, size), :], sent).astype(LOW)


def after_attention(attended, weights, rows, gain, spread, experts):
    tokens, width = rows.shape
    (after, *sent), _ = call(
        post_kernel,
        "post",
        [whole(array) for array in (attended, weights, rows, gain, spread)],
        [whole_out((tokens, width), FULL)]
        + [whole_out((spread.shape[0] // experts, width), LOW)] * experts,
        far_out=(0,),
        us=2,
    )
    return after, sent


def gather_kernel(*refs):
    size = refs[0].shape[0]
    for at, ref in enumerate(refs[:-1]):
        refs[-1][pl.ds(at * size, size), :] = ref[...]


def side_by_side(blocks, token):
    size, width = blocks[0].shape
    (out,), token = call(
        gather_kernel,
        "gather",
        [whole(block) for block in blocks],
        [whole_out((len(blocks) * size, width), LOW)],
        token=token,
        us=1,
    )
    return out, token


def expert_part(gate, up, dhid):
    square = gate * gate
    curve = jnp.tanh(GELU_SCALE * gate * (1.0 + GELU_CUBE * square))
    upper = 0.5 * (1.0 + curve)
    gelu = gate * upper
    slope = upper + 0.5 * gate * (1.0 - curve * curve) * (
        GELU_SCALE * (1.0 + 3.0 * GELU_CUBE * square)
    )
    hid = (gelu * up).astype(LOW)
    dgate = (dhid * up * slope).astype(LOW)
    dup = (dhid * gelu).astype(LOW)
    return hid, dgate, dup


def expert_kernel(
    rows_ref, grad_ref, gate_w_ref, up_w_ref, down_w_ref,
    out_ref, back_ref, dgate_ref, dup_ref, hid_ref, turned_ref, out_sum, back_sum,
):
    step = pl.program_id(0)

    @pl.when(step == 0)
    def _():
        out_sum[...] = jnp.zeros_like(out_sum)
        back_sum[...] = jnp.zeros_like(back_sum)

    rows, grad = rows_ref[...], grad_ref[...]
    gate_w, up_w, down_w = gate_w_ref[0], up_w_ref[0], down_w_ref[0]
    hid, dgate, dup = expert_part(
        dot_rows(rows, gate_w), dot_rows(rows, up_w), dot_back(grad, down_w)
    )
    dgate_ref[...] = dgate
    dup_ref[...] = dup
    hid_ref[...] = hid.T
    out_sum[...] += dot_rows(hid, down_w)
    back_sum[...] += dot_back(dgate, gate_w) + dot_back(dup, up_w)

    @pl.when(step == pl.num_programs(0) - 1)
    def _():
        out_ref[...] = out_sum[...].astype(LOW)
        back_ref[...] = back_sum[...].astype(LOW)
        turned_ref[...] = rows_ref[...].T


def expert(rows, grad, w_in, w_down, token):
    count, width = rows.shape
    hidden = w_down.shape[1]
    part = 256
    steps = hidden // part
    return call(
        expert_kernel,
        "expert",
        [
            whole(rows),
            whole(grad),
            (w_in, pl.BlockSpec((1, width, part), lambda i: (0, 0, i))),
            (w_in, pl.BlockSpec((1, width, part), lambda i: (0, 0, i + steps))),
            (w_down, pl.BlockSpec((1, part, width), lambda i: (0, i, 0))),
        ],
        [
            whole_out((count, width), LOW),
            whole_out((count, width), LOW),
            ((count, hidden), LOW, pl.BlockSpec((count, part), lambda i: (0, i))),
            ((count, hidden), LOW, pl.BlockSpec((count, part), lambda i: (0, i))),
            ((hidden, count), LOW, pl.BlockSpec((part, count), lambda i: (i, 0))),
            whole_out((width, count), LOW),
        ],
        grid=(steps,),
        token=token,
        scratch=[pltpu.VMEM((count, width), FULL), pltpu.VMEM((count, width), FULL)],
        vmem=24,
        us=20,
    )


CHUNK = 512
EXPERT_VMEM = 40


def halves_kernel(
    at_ref, x0_ref, x1_ref, g0_ref, g1_ref, w_in_ref, w_down_ref,
    back_keep, back_send, dgate_ref, dup_ref, turned_ref, hid_out, down_out, a_send, a_keep, b_ref,
    both_w, du, turned, hid_ref, down_ref, a_sum, sems, out_sems,
):
    count, width = x0_ref.shape
    half = down_ref.shape[0]
    full, rest = half // CHUNK, half % CHUNK
    first = pl.multiple_of(at_ref[2] * half, LANES)

    def copies(i, units):
        start = pl.multiple_of(i * CHUNK, LANES)
        pairs = []
        for piece in range(4):
            rows = pl.ds(piece * (width // 4), width // 4)
            for part in range(2):
                one = pl.ds(pl.multiple_of(first + start + 2 * part * half, LANES), units)
                two = pl.ds(pl.multiple_of(start + part * half, LANES), units)
                pairs.append((w_in_ref.at[0, rows, one], both_w.at[rows, two]))
            size = units // 4
            one = pl.ds(pl.multiple_of(first + start + piece * size, 16), size)
            two = pl.ds(pl.multiple_of(start + piece * size, 16), size)
            pairs.append((w_down_ref.at[0, one, :], down_ref.at[two, :]))
        return [
            pltpu.make_async_copy(one, two, sems.at[i, at]) for at, (one, two) in enumerate(pairs)
        ]

    def results(i, units):
        copies = []
        for part, ref in enumerate((dgate_ref, dup_ref)):
            one = pl.ds(pl.multiple_of(part * half + i * CHUNK, LANES), units)
            two = pl.ds(pl.multiple_of(i * CHUNK, LANES), units)
            copies.append(pltpu.make_async_copy(du.at[:, one], ref.at[:, two], out_sems.at[i, part]))
        return copies

    sizes = [CHUNK] * full + ([rest] if rest else [])
    for i, units in enumerate(sizes):
        for copy in copies(i, units):
            copy.start()

    turned[:, :count] = x0_ref[...].T
    turned[:, count:] = x1_ref[...].T
    turned_copy = pltpu.make_async_copy(turned, turned_ref, out_sems.at[len(sizes), 0])
    turned_copy.start()

    def chunk(i, units):
        for copy in copies(i, units):
            copy.wait()
        start = pl.multiple_of(i * CHUNK, LANES)
        columns = pl.ds(start, units)
        other = pl.ds(pl.multiple_of(start + half, LANES), units)
        gate_w, up_w, down_w = both_w[:, columns], both_w[:, other], down_ref[columns, :]
        for side, (x_ref, g_ref) in enumerate(((x0_ref, g0_ref), (x1_ref, g1_ref))):
            rows = pl.ds(side * count, count)
            x = x_ref[...]
            hid, dgate, dup = expert_part(
                dot_rows(x, gate_w), dot_rows(x, up_w), dot_back(g_ref[...], down_w)
            )
            hid_ref[rows, columns] = hid
            du[rows, columns] = dgate
            du[rows, other] = dup
        for copy in results(i, units):
            copy.start()

    def step(i, _):
        chunk(i, CHUNK)
        return 0

    lax.fori_loop(0, full, step, 0)
    if rest:
        chunk(full, rest)
    kept = [
        pltpu.make_async_copy(ref, out, out_sems.at[len(sizes) + 1, at])
        for at, (ref, out) in enumerate(((hid_ref, hid_out), (down_ref, down_out)))
    ]
    for copy in kept:
        copy.start()
    terms = transpose_dot(hid_ref[:count, :], g0_ref[...])
    terms = terms + transpose_dot(hid_ref[count:, :], g1_ref[...])
    middle, size = width // 2, half // 2
    b_ref[...] = terms[:, middle:].astype(LOW)
    a_sum[...] = terms[:, :middle].astype(LOW)
    a_keep[...] = a_sum[pl.ds(pl.multiple_of(at_ref[1] * size, 16), size), :]
    a_send[...] = a_sum[pl.ds(pl.multiple_of((1 - at_ref[1]) * size, 16), size), :]
    back_send[...] = dot_back(du[count:, :], both_w[...]).astype(LOW)
    back_keep[...] = dot_back(du[:count, :], both_w[...])
    turned_copy.wait()
    for copy in kept:
        copy.wait()
    for i, units in enumerate(sizes):
        for copy in results(i, units):
            copy.wait()


def expert_halves(at, rows, grads, w_in, w_down, token):
    count, width = rows[0].shape
    half = w_down.shape[1] // 2
    chunks = pl.cdiv(half, CHUNK)
    return call(
        halves_kernel,
        "expert_halves",
        [whole(array) for array in (*rows, *grads)] + [(w_in, None), (w_down, None)],
        [
            whole_out((count, width), FULL),
            whole_out((count, width), LOW),
            ((2 * count, half), LOW, None),
            ((2 * count, half), LOW, None),
            ((width, 2 * count), LOW, None),
            ((2 * count, half), LOW, None),
            ((half, width), LOW, None),
            whole_out((half // 2, width // 2), LOW),
            whole_out((half // 2, width // 2), LOW),
            whole_out((half, width // 2), LOW),
        ],
        token=token,
        prefetch=(at,),
        scratch=[
            pltpu.VMEM((width, 2 * half), LOW),
            pltpu.VMEM((2 * count, 2 * half), LOW),
            pltpu.VMEM((width, 2 * count), LOW),
            pltpu.VMEM((2 * count, half), LOW),
            pltpu.VMEM((half, width), LOW),
            pltpu.VMEM((half, width // 2), LOW),
            pltpu.SemaphoreType.DMA((chunks, 12)),
            pltpu.SemaphoreType.DMA((chunks + 2, 2)),
        ],
        vmem=EXPERT_VMEM,
        us=20,
        far_out=(7, 8, 9),
    )


def results_kernel(hid_ref, down_ref, keep_ref, send_ref):
    count = keep_ref.shape[0]
    send_ref[...] = dot_rows(hid_ref[count:, :], down_ref[...]).astype(LOW)
    keep_ref[...] = dot_rows(hid_ref[:count, :], down_ref[...]).astype(LOW)


def expert_results(hid, down_w, token):
    shape = (hid.shape[0] // 2, down_w.shape[1])
    (keep, send), token = call(
        results_kernel,
        "expert_results",
        [whole(hid), whole(down_w)],
        [whole_out(shape, LOW)] * 2,
        token=token,
        far_in=(0, 1),
        far_out=(0, 1),
        vmem=16,
        us=0.01,
    )
    return keep, send, token


def block_of(at_ref, k, blocks):
    return lax.rem(at_ref[3] + (blocks - k), blocks)


def join_kernel(at_ref, kept_ref, got_ref, out_ref):
    blocks, size, _ = out_ref.shape
    for k in range(blocks):
        rows = pl.ds(k * size, size)
        total = kept_ref[rows, :] + got_ref[rows, :].astype(FULL)
        out_ref[block_of(at_ref, k, blocks)] = total.astype(LOW)


def join(at, kept, got, blocks, token):
    rows, width = kept.shape
    (out,), token = call(
        join_kernel,
        "join",
        [whole(kept), whole(got)],
        [whole_out((blocks, rows // blocks, width), LOW)],
        token=token,
        prefetch=(at,),
        far_out=(0,),
        us=1,
    )
    return out, token


def join_peak_kernel(at_ref, kept_ref, got_ref, peak_ref, out_ref):
    blocks, size, width = out_ref.shape
    rows = kept_ref.shape[0] // blocks
    best = jnp.concatenate([peak_ref[g, :GROUP, :] for g in range(peak_ref.shape[0])], axis=0)
    best = jnp.broadcast_to(jnp.max(best, axis=1, keepdims=True), (size - rows, LANES))
    upper = best.astype(LOW)
    lower = (best - upper.astype(FULL)).astype(LOW)
    for k in range(blocks):
        part = pl.ds(k * rows, rows)
        to = block_of(at_ref, k, blocks)
        total = kept_ref[part, :].astype(FULL) + got_ref[part, :].astype(FULL)
        out_ref[to, :rows, :] = total.astype(LOW)
        out_ref[to, rows:, :] = jnp.zeros((size - rows, width), LOW)
        out_ref[to, rows:, :LANES] = upper
        out_ref[to, rows:, LANES : 2 * LANES] = lower


def join_peak(at, kept, got, peak, blocks, token):
    rows, width = kept.shape
    heads = peak.shape[0] * GROUP
    (out,), token = call(
        join_peak_kernel,
        "join_peak",
        [whole(kept), whole(got), whole(peak)],
        [whole_out((blocks, rows // blocks + heads, width), LOW)],
        token=token,
        prefetch=(at,),
        far_out=(0,),
        us=0.01,
        far_in=(0,),
    )
    return out, token


def larger_kernel(one_ref, two_ref, out_ref):
    out_ref[...] = jnp.maximum(one_ref[...], two_ref[...])


def larger(one, two, token):
    (out,), token = call(
        larger_kernel,
        "larger",
        [whole(one), whole(two)],
        [whole_out(one.shape, FULL)],
        token=token,
        us=0.5,
    )
    return out, token


def place():
    dp = lax.axis_index("dp")
    return lax.axis_index("ctx"), lax.axis_index("exp"), dp // 2, dp % 2


def to_down_plane(array):
    pairs = [
        ((1 - core) * 4 + x * 2 + core, core * 4 + x * 2 + core)
        for core in range(2)
        for x in range(2)
    ]
    return lax.ppermute(array, ("ctx", "dp"), pairs)


def in_down_plane(array):
    pairs = [
        (core * 4 + x * 2 + core, core * 4 + (1 - x) * 2 + core)
        for core in range(2)
        for x in range(2)
    ]
    return lax.ppermute(array, ("ctx", "dp"), pairs)


def in_kernel(
    at_ref, turned_ref, gate_ref, up_ref, *refs,
):
    out_refs, turned, near, results, sems, out_sems = refs[:4], *refs[4:]
    half = gate_ref.shape[1]
    starts = list(range(0, half, CHUNK))
    loads = []
    for at, (ref, to) in enumerate(((gate_ref, near.at[0]), (up_ref, near.at[1]))):
        for i, start in enumerate(starts):
            columns = pl.ds(start, min(CHUNK, half - start))
            loads.append(
                pltpu.make_async_copy(ref.at[:, columns], to.at[:, columns], sems.at[at, i])
            )
    whole_load = pltpu.make_async_copy(turned_ref, turned, sems.at[2, 0])
    whole_load.start()
    for i in range(len(starts)):
        loads[i].start()
        loads[len(starts) + i].start()
    whole_load.wait()
    size = turned.shape[0] // 4
    stores = []
    for i, start in enumerate(starts):
        columns = pl.ds(start, min(CHUNK, half - start))
        loads[i].wait()
        loads[len(starts) + i].wait()
        for block in range(4):
            ry, rx = block // 2, block % 2
            chip = (at_ref[0] ^ ry) * 2 + (at_ref[1] ^ rx)
            rows = turned[pl.ds(pl.multiple_of(chip * size, size), size), :]
            a, b = 1 - rx, 2 + 1 - ry
            results[a, ry, :, columns] = dot_rows(rows, near[0, :, columns]).astype(LOW)
            results[b, rx, :, columns] = dot_rows(rows, near[1, :, columns]).astype(LOW)
        for at, ref in enumerate(out_refs):
            copy = pltpu.make_async_copy(
                results.at[at, :, :, columns], ref.at[:, :, columns], out_sems.at[at, i]
            )
            copy.start()
            stores.append(copy)
    for copy in stores:
        copy.wait()


def in_terms(at, turned, gate, up, token):
    width, count = turned.shape
    half = gate.shape[1]
    shape = (2, width // 4, half)
    chunks = pl.cdiv(half, CHUNK)
    return call(
        in_kernel,
        "in_terms",
        [(turned, None), (gate, None), (up, None)],
        [(shape, LOW, None)] * 4,
        token=token,
        prefetch=(at,),
        scratch=[
            pltpu.VMEM((width, count), LOW),
            pltpu.VMEM((2, count, half), LOW),
            pltpu.VMEM((4, *shape), LOW),
            pltpu.SemaphoreType.DMA((3, chunks)),
            pltpu.SemaphoreType.DMA((4, chunks)),
        ],
        vmem=20,
        us=0.01,
    )


def plane_first(parts):
    a_send, a_keep, b_send, b_keep = parts
    return swapped(a_send, "dp", 2), a_keep, swapped(b_send, "ctx", 1), b_keep


def second_kernel(*refs):
    (a_ref, a_keep_ref, b_ref, b_keep_ref), (a_send_ref, b_send_ref) = refs[:4], refs[-2:]
    rows = a_ref.shape[0]
    total = a_keep_ref[...].astype(FULL) + a_ref[...].astype(FULL)
    a_send_ref[pl.ds(0, rows), :] = total.astype(LOW)
    b_send_ref[...] = (b_keep_ref[...].astype(FULL) + b_ref[...].astype(FULL)).astype(LOW)
    for beside in refs[4:-2]:
        more, width = beside.shape
        a_send_ref[pl.ds(rows, more), pl.ds(0, width)] = beside[...]


def plane_second(parts, token, beside=()):
    extra = sum(part.shape[0] for part in beside)
    (_, a_rows, a_width), (_, b_rows, b_width) = parts[0].shape, parts[2].shape
    (a_send, b_send), token = call(
        second_kernel,
        "second_terms",
        [whole(part) for part in (*parts, *beside)],
        [whole_out((a_rows + extra, a_width), LOW), whole_out((b_rows, b_width), LOW)],
        token=token,
        us=15,
        far_in=tuple(range(4, 4 + len(beside))),
        part_in={at: (1,) for at in range(4)},
        far_out=(0, 1),
        vmem=10,
    )
    return a_send, b_send, token


def down_second_kernel(at_ref, a_ref, a_keep_ref, b_ref, b_keep_ref, a_send_ref, b_send_ref):
    size = b_send_ref.shape[0]
    rows = pl.ds(pl.multiple_of((1 - at_ref[1]) * size, 16), size)
    a_send_ref[...] = (a_keep_ref[...].astype(FULL) + a_ref[...].astype(FULL)).astype(LOW)
    b_send_ref[...] = (b_keep_ref[rows, :].astype(FULL) + b_ref[rows, :].astype(FULL)).astype(LOW)


def down_second(at, parts, token, us):
    shape = parts[0].shape
    (a_send, b_send), token = call(
        down_second_kernel,
        "down_second",
        [whole(part) for part in parts],
        [whole_out(shape, LOW)] * 2,
        token=token,
        prefetch=(at,),
        us=us,
        far_out=(0, 1),
    )
    return a_send, b_send, token


def sum_kernel(one_ref, two_ref, three_ref, out_ref):
    out_ref[...] = sum(ref[...].astype(FULL) for ref in (one_ref, two_ref, three_ref)).astype(LOW)


def plane_sum(got, kept, more, token):
    (out,), token = call(
        sum_kernel,
        "plane_sum",
        [whole(got), whole(kept), whole(more)],
        [whole_out(more.shape, LOW)],
        token=token,
        far_in=(2,),
        part_in={0: (0,), 1: (0,)},
        far_out=(0,),
        us=15,
    )
    return out, token


def pair_last_kernel(a_ref, a_keep_ref, a2_ref, b_ref, out_ref):
    blocks = out_ref.shape[0]
    a = sum(ref[...].astype(FULL) for ref in (a_keep_ref, a_ref, a2_ref))
    size = b_ref.shape[0] // blocks
    for z in range(blocks):
        here = slice(z * size, (z + 1) * size)
        out_ref[z, :size, :] = a[here].astype(LOW)
        small = jnp.broadcast_to(a[blocks * size + z : blocks * size + z + 1], (EXTRA, a.shape[1]))
        out_ref[z, size : size + EXTRA, :] = small.astype(LOW)
        out_ref[z, size + EXTRA :, :] = b_ref[here, :]


def pair_last(got, kept, more, b, blocks, token):
    rows, width = b.shape
    own = slice(0, rows + EXTRA)
    (out,), token = call(
        pair_last_kernel,
        "pair_last",
        [whole(got), whole(kept), whole(more), whole(b)],
        [whole_out((blocks, 2 * rows // blocks + EXTRA, width), LOW)],
        token=token,
        far_in=(3,),
        part_in={0: (0,), 1: (0,), 2: (own,)},
        far_out=(0,),
        us=15,
        vmem=12,
    )
    return out, token


def down_last_kernel(
    at_ref, a_ref, a_keep_ref, b_ref, b_keep_ref, a2_ref, b2_ref, keep_ref, send_ref
):
    size, width = keep_ref.shape
    half = width // 2
    for out_ref, core in ((send_ref, 1 - at_ref[2]), (keep_ref, at_ref[2])):
        rows = pl.ds(pl.multiple_of(core * size, 16), size)
        there = pl.ds(pl.multiple_of((at_ref[1] * 2 + core) * size, 16), size)
        for first, refs in (
            (0, ((a_ref, rows), (a_keep_ref, rows), (a2_ref, rows))),
            (half, ((b_ref, there), (b_keep_ref, there), (b2_ref, rows))),
        ):
            total = sum(ref[cut, :].astype(FULL) for ref, cut in refs)
            out_ref[:, first : first + half] = total.astype(out_ref.dtype)


def down_last(at, parts, a2, b2, token):
    rows, half = a2.shape
    shape = (rows // 2, 2 * half)
    (keep, send), token = call(
        down_last_kernel,
        "down_last",
        [whole(array) for array in (*parts, a2, b2)],
        [whole_out(shape, FULL), whole_out(shape, LOW)],
        token=token,
        prefetch=(at,),
        us=15,
        far_out=(0, 1),
    )
    return keep, send, token


def choose_kernel(at_ref, keep_ref, got_ref, out_ref):
    mine = at_ref[0] == at_ref[2]
    out_ref[0] = jnp.where(mine, keep_ref[...], got_ref[...].astype(FULL))


def choose(at, keep, got, token):
    size, width = keep.shape
    rows = pl.BlockSpec((size // 2, width), lambda i, at: (i, 0))
    (out,), token = call(
        choose_kernel,
        "choose",
        [(keep, rows), (got, rows)],
        [((1, size, width), FULL, pl.BlockSpec((1, size // 2, width), lambda i, at: (0, i, 0)))],
        grid=(2,),
        token=token,
        prefetch=(at,),
        us=15,
    )
    return out, token


def in_last_kernel(
    at_ref, a_ref, a_keep_ref, b_ref, b_keep_ref, a2_ref, b2_ref, keep_ref, send_ref
):
    size = keep_ref.shape[1]
    for out_ref, core in ((send_ref, 1 - at_ref[2]), (keep_ref, at_ref[2])):
        rows = pl.ds(pl.multiple_of(core * size, 16), size)
        for part, refs in enumerate(((a_ref, a_keep_ref, a2_ref), (b_ref, b_keep_ref, b2_ref))):
            total = sum(ref[rows, :].astype(FULL) for ref in refs)
            out_ref[part] = total.astype(out_ref.dtype)


def in_last(at, parts, a2, b2, token):
    rows, half = b2.shape
    shape = (2, rows // 2, half)
    (keep, send), token = call(
        in_last_kernel,
        "in_last",
        [whole(array) for array in (*parts, a2, b2)],
        [whole_out(shape, FULL), whole_out(shape, LOW)],
        token=token,
        prefetch=(at,),
        us=15,
        far_in=(4, 5),
        part_in={at: (0,) for at in range(4)},
        far_out=(0, 1),
        vmem=16,
    )
    return keep, send, token


def in_end_kernel(at_ref, keep_ref, got_ref, out_ref):
    half = keep_ref.shape[2]
    for part in range(2):
        for first, value in (
            (at_ref[2], keep_ref[part]),
            (1 - at_ref[2], got_ref[part].astype(FULL)),
        ):
            start = pl.multiple_of((part * 2 + first) * half, LANES)
            out_ref[0, :, pl.ds(start, half)] = value


def in_end(at, keep, got, token):
    _, rows, half = keep.shape
    size = rows // 2
    spec = pl.BlockSpec((2, size, half), lambda i, at: (0, i, 0))
    (out,), token = call(
        in_end_kernel,
        "in_end",
        [(keep, spec), (got, spec)],
        [((1, rows, 4 * half), FULL, pl.BlockSpec((1, size, 4 * half), lambda i, at: (0, i, 0)))],
        grid=(2,),
        token=token,
        prefetch=(at,),
        us=15,
        vmem=12,
    )
    return out, token


EXTRA = 16
TABLE_LANE = 32


def turn_kernel(at_ref, *refs):
    out_ref, turned = refs[-2:]
    start = 0
    for ref in refs[:-2]:
        turned[:, start : start + ref.shape[0]] = ref[...].T
        start += ref.shape[0]
    size = out_ref.shape[0] // 16
    for to in range(16):
        device = device_at(to % 4, to // 4, at_ref)
        out_ref[pl.ds(to * size, size), :] = turned[pl.ds(device * size, size), :]


def device_at(block, z, at_ref):
    return (
        (at_ref[0] ^ (block // 2)) * 16 + z * 4 + (at_ref[1] ^ (block % 2)) * 2 + at_ref[2]
    )


def turn(at, parts, token):
    count, width = sum(part.shape[0] for part in parts), parts[0].shape[1]
    (out,), token = call(
        turn_kernel,
        "turn",
        [whole(part) for part in parts],
        [whole_out((width // 2, count), LOW)],
        token=token,
        prefetch=(at,),
        scratch=[pltpu.VMEM((width, count), LOW)],
        us=2,
        far_out=(0,),
    )
    return out, token


def shared_kernel(
    at_ref, left_ref, own_ref, other_ref, a_send_ref, a_keep_ref, b_send_ref, b_keep_ref, *, experts
):
    rows, count = left_ref.shape[0] // experts, left_ref.shape[1] // 2
    width = own_ref.shape[1]
    tokens = count // 3
    size = rows // 4
    small = own_ref[6 * tokens :, :LANES].astype(FULL) + other_ref[6 * tokens :, :LANES].astype(FULL)
    place = lax.broadcasted_iota(jnp.int32, small.shape, 0)
    for z in range(experts):
        left = left_ref[pl.ds(z * rows, rows), :]

        def product(columns, start, length):
            right = slice(start, start + length)
            one = left[:, columns : columns + length]
            two = left[:, count + columns : count + columns + length]
            total = dot_rows(one, own_ref[right, :]) + dot_rows(two, other_ref[right, :])
            return total.astype(LOW)

        a_terms = product(2 * tokens, 5 * tokens, tokens), product(tokens, 0, tokens)
        b_terms = product(0, tokens, 2 * tokens), product(0, 3 * tokens, 2 * tokens)
        for block in range(4):
            ry, rx = block // 2, block % 2
            a_ref = (a_send_ref if rx else a_keep_ref).at[ry]
            b_ref = (b_send_ref if ry else b_keep_ref).at[rx]
            here = slice(block * size, (block + 1) * size)
            for at in range(2):
                to = pl.ds((2 * z + at) * size, size)
                a_ref[to, :] = a_terms[at][here]
                b_ref[to, :] = b_terms[at][here]
    line = lax.broadcasted_iota(jnp.int32, (EXTRA, LANES), 0)
    for block in range(4):
        ry, rx = block // 2, block % 2
        a_ref = (a_send_ref if rx else a_keep_ref).at[ry]
        rows_here = jnp.zeros((EXTRA, LANES), FULL)
        for z in range(experts):
            row = jnp.where(place == device_at(block, z, at_ref), small, 0.0)
            rows_here = jnp.where(line == z, jnp.sum(row, 0, keepdims=True), rows_here)
        a_ref[2 * size * experts :, :] = jnp.zeros((EXTRA, width), LOW)
        a_ref[2 * size * experts :, :LANES] = rows_here.astype(LOW)


def shared_terms(at, left, own, other, experts, token):
    rows = left.shape[0]
    width = own.shape[1]
    b_shape = (2, rows // 2, width)
    a_shape = (2, rows // 2 + EXTRA, width)
    return call(
        functools.partial(shared_kernel, experts=experts),
        "shared_terms",
        [whole(array) for array in (left, own, other)],
        [whole_out(shape, LOW) for shape in (a_shape, a_shape, b_shape, b_shape)],
        token=token,
        prefetch=(at,),
        us=0.01,
        far_in=(0,),
        far_out=(0, 1, 2, 3),
        vmem=16,
    )


def rows_kernel(
    place_ref, plane_ref, w_query_ref, w_key_ref, w_value_ref, gain_ref,
    query_ref, key_ref, value_ref, out_ref, gain_grad_ref, ffn_ref, table_ref,
    near_query, near_key, near_value, sems,
):
    rows = query_ref.shape[0]
    at = pl.ds(pl.multiple_of(place_ref[0] * rows, rows), rows)
    pairs = ((w_query_ref, near_query), (w_key_ref, near_key), (w_value_ref, near_value))
    copies = [
        pltpu.make_async_copy(ref.at[at, :], near, sems.at[number])
        for number, (ref, near) in enumerate(pairs)
    ]
    for copy in copies:
        copy.start()
    total = sum(plane_ref[block].astype(FULL) for block in range(plane_ref.shape[0]))
    out_ref[...] = total[:rows]
    query = total[rows : 2 * rows]
    key, value = (
        total[start + EXTRA : start + EXTRA + rows] for start in (2 * rows, 3 * rows)
    )
    query_ref[...] = query
    key_ref[...] = key
    value_ref[...] = value
    small = total[2 * rows : 2 * rows + 1, :LANES]
    ffn_ref[...] = small
    table_ref[...] = pltpu.roll(jnp.broadcast_to(small, (8, LANES)), LANES - TABLE_LANE, 1)[:1]
    for copy in copies:
        copy.wait()
    sums = query * near_query[...].astype(FULL) + key * near_key[...].astype(FULL)
    sums = jnp.sum(sums + value * near_value[...].astype(FULL), axis=1, keepdims=True)
    lane = lax.broadcasted_iota(jnp.int32, (rows, LANES), 1)
    line = lax.broadcasted_iota(jnp.int32, (rows, LANES), 0)
    spread = jnp.sum(jnp.where(lane == line, sums, 0.0), 0, keepdims=True)
    device = place_ref[0]
    block = gain_ref[pl.ds(device * rows // LANES, 1), :]
    gain = pltpu.roll(jnp.broadcast_to(block, (8, LANES)), LANES - device * rows % LANES, 1)[:1]
    gain_grad_ref[...] = spread / gain


def last_rows(place_all, plane, rows, weights, gain, token):
    width = plane.shape[2]
    small = whole_out((1, LANES), FULL)
    outs, token = call(
        rows_kernel,
        "last_rows",
        [whole(plane)] + [(array, None) for array in weights] + [whole(gain.reshape(-1, LANES))],
        [whole_out((rows, width), FULL)] * 4 + [small] * 3,
        token=token,
        prefetch=(place_all.reshape(1),),
        scratch=[pltpu.VMEM((rows, width), LOW)] * 3 + [pltpu.SemaphoreType.DMA((3,))],
        us=15,
    )
    return outs, token


def clip_kernel(query_ref, key_ref, peak_ref, level_ref, query_out, key_out, factor_ref):
    heads = peak_ref.shape[0]
    width = query_ref.shape[1]
    level = jnp.sum(jnp.where(eye(heads), level_ref[...], 0.0), 1, keepdims=True)
    factor = level / jnp.maximum(peak_ref[:, :1], level)
    factor_ref[...] = jnp.broadcast_to(factor, (heads, LANES))
    head = lax.broadcasted_iota(jnp.int32, (heads, width), 0)
    lane = lax.broadcasted_iota(jnp.int32, (heads, width), 1)
    scale = jnp.sum(jnp.where(lane // HDIM == head, jnp.sqrt(factor), 0.0), 0, keepdims=True)
    query_out[...] = query_ref[...].astype(FULL) * scale
    key_out[...] = key_ref[...].astype(FULL) * scale


def clip(w_query, w_key, peak, level, token):
    rows, width = w_query.shape
    spec = pl.BlockSpec((rows // 4, width), lambda i: (i, 0))
    outs, token = call(
        clip_kernel,
        "clip",
        [(w_query, spec), (w_key, spec), whole(peak), whole(level.reshape(1, -1))],
        [((rows, width), FULL, spec)] * 2 + [whole_out(peak.shape, FULL)],
        grid=(4,),
        token=token,
        us=0.01,
        vmem=16,
    )
    return outs, token


def normed_kernel(
    packed_ref, w_query_ref, w_key_ref, w_value_ref, own_ref, other_ref, near, sems
):
    copies = [
        pltpu.make_async_copy(ref, near.at[at], sems.at[at])
        for at, ref in enumerate((w_key_ref, w_value_ref, w_query_ref))
    ]
    for copy in copies:
        copy.start()
    tokens = own_ref.shape[0]
    dq, dk, dv = (
        packed_ref[pl.ds(start * tokens, size * tokens), :]
        for start, size in ((0, 1), (1, 2), (3, 2))
    )
    copies[0].wait()
    total = dot_back(dk, near[0])
    copies[1].wait()
    total = total + dot_back(dv, near[1])
    other_ref[...] = total[:tokens].astype(LOW)
    copies[2].wait()
    own_ref[...] = total[tokens:] + dot_back(dq, near[2])


def normed_grads(packed, weights, tokens, token):
    width = packed.shape[1]
    (own, other), token = call(
        normed_kernel,
        "normed_grads",
        [whole(packed)] + [(array, None) for array in weights],
        [whole_out((tokens, width), FULL), whole_out((tokens, width), LOW)],
        token=token,
        scratch=[pltpu.VMEM((3, width, width), LOW), pltpu.SemaphoreType.DMA((3,))],
        far_in=(0,),
        far_out=(0, 1),
        us=0.01,
        vmem=14,
    )
    return own, other, token


def input_kernel(rows_ref, gain_ref, own_ref, got_ref, past_ref, out_ref):
    rows = rows_ref[...].astype(FULL)
    inverse = lax.rsqrt(jnp.mean(rows * rows, axis=1, keepdims=True) + EPSILON)
    scaled = rows * inverse
    grad = (own_ref[...] + got_ref[...].astype(FULL)) * gain_ref[...]
    along = jnp.mean(scaled * grad, axis=1, keepdims=True)
    out_ref[0] = past_ref[...] + inverse * (grad - scaled * along)


def input_grads(rows, gain, own, got, past, token):
    tokens, width = rows.shape
    start = got.shape[0] - tokens
    (out,), token = call(
        input_kernel,
        "input_grads",
        [whole(array) for array in (rows, gain, own, got, past)],
        [whole_out((1, tokens, width), FULL)],
        token=token,
        far_in=(0, 1, 2, 4),
        part_in={3: (slice(start, start + tokens), slice(0, width))},
        far_out=(0,),
        us=0.01,
    )
    return out, token


def back_kernel(
    at_ref, spread_ref, rows_ref, after_ref, gain_ref, grad_ref, weights_ref,
    total_ref, branch_ref, attended_ref, gain_grad_ref,
):
    rows = after_ref[...]
    inverse = lax.rsqrt(jnp.mean(rows * rows, axis=1, keepdims=True) + EPSILON)
    scaled = rows * inverse
    blocks, size, _ = rows_ref.shape
    grad = sum(
        transpose_dot(spread_ref[pl.ds(k * size, size), :], rows_ref[lax.rem(at_ref[3] + k, blocks)])
        for k in range(blocks)
    )
    gain_grad_ref[...] = jnp.sum(scaled * grad, axis=0, keepdims=True)
    grad = grad * gain_ref[...]
    along = jnp.mean(scaled * grad, axis=1, keepdims=True)
    total = grad_ref[...].astype(FULL) + inverse * (grad - scaled * along)
    total_ref[...] = total
    branch = total.astype(LOW)
    branch_ref[...] = branch
    attended_ref[...] = dot_back(branch, weights_ref[...]).astype(LOW)


def back_to_attention(at, spread, rows, after, gain, grad, weights, token):
    shape = after.shape
    inputs = (spread, rows, after, gain, grad, weights)
    return call(
        back_kernel,
        "back",
        [whole(array) for array in inputs],
        [
            whole_out(shape, FULL),
            whole_out(shape, LOW),
            whole_out(shape, LOW),
            whole_out((1, shape[1]), FULL),
        ],
        token=token,
        vmem=16,
        us=0.01,
        far_in=(0, 2, 4, 5),
        prefetch=(at,),
    )


def mix_kernel(at_ref, pick_ref, rows_ref, gates_ref, after_ref, out_ref, peak_ref):
    top, tokens = gates_ref.shape
    blocks = rows_ref.shape[0]
    size = pick_ref.shape[0] // blocks
    total = after_ref[...]
    gates = [to_column(gates_ref[r : r + 1, :]) for r in range(top)]
    for block in range(blocks):
        rows = rows_ref[lax.rem(at_ref[3] + block, blocks), :size, :]
        for r in range(top):
            pick = pick_ref[pl.ds(block * size, size), pl.ds(r * tokens, tokens)]
            total = total + gates[r] * transpose_dot(pick, rows)
    out_ref[0] = total.astype(LOW)
    if rows_ref.shape[1] > size:
        peaks = [
            rows_ref[block, size:, :LANES].astype(FULL)
            + rows_ref[block, size:, LANES : 2 * LANES].astype(FULL)
            for block in range(blocks)
        ]
        peak_ref[...] = functools.reduce(jnp.maximum, peaks)


def mix(at, pick, rows, gates, after, token):
    (out, peak), token = call(
        mix_kernel,
        "mix",
        [whole(pick), whole(rows), whole(gates), whole(after)],
        [whole_out((1, *after.shape), LOW), whole_out((16, LANES), FULL)],
        token=token,
        us=0.01,
        far_in=(0, 3),
        prefetch=(at,),
    )
    return out, peak, token


def local(
    block_in,
    seg_ids,
    routes,
    gates,
    buckets,
    norm_attn,
    norm_ffn,
    w_query,
    w_key,
    w_value,
    w_out_attn,
    rel_bias,
    clip_level,
    w_in,
    w_down,
    cotangent,
):
    tokens, width = block_in.shape[1:]
    heads = width // HDIM
    n_ctx, experts, n_dp = (lax.axis_size(axis) for axis in ("ctx", "exp", "dp"))
    fast = (n_ctx, experts, n_dp) == (2, 4, 4)
    devices = n_ctx * experts * n_dp
    length = n_ctx * tokens
    y, z, x, core = place()
    place_all = (y * experts + z) * n_dp + lax.axis_index("dp")
    top_count = routes.shape[-1]
    capacity = tokens * top_count * 3 // (2 * experts)
    at = jnp.stack([y, x, core, z])

    (spread, pick, mask, rows_copy, *grad_out), token = front(
        at, routes[0].T, gates[0].T, cotangent[0], seg_ids, block_in[0], experts, capacity
    )
    backs = list(range(n_ctx - 1, 0, -1))
    earlier = [
        lax.ppermute(block_in[0], "ctx", [(i, (i + back) % n_ctx) for i in range(n_ctx)])
        for back in backs
    ]
    grad_blocks = to_experts(grad_out)
    (bucket_hot, bias, w_key_near, w_value_near), _ = bias_tiles(
        buckets.reshape(1, length), rel_bias.reshape(NB, heads), tokens, (w_key, w_value)
    )

    own_rows = block_in[0].astype(FULL)
    normed_own = rms_norm(own_rows, norm_attn).astype(LOW)
    normed_all = jnp.concatenate(
        [rms_norm(rows.astype(FULL), norm_attn).astype(LOW) for rows in earlier] + [normed_own],
        axis=0,
    )
    queries = dot_rows(normed_own, w_query).astype(LOW)
    keys = dot_rows(normed_all, w_key_near).astype(LOW)
    values = dot_rows(normed_all, w_value_near).astype(LOW)
    attended, probs, peak_lanes, w_out_near = attention(
        queries, keys, values, bias, mask, (w_out_attn,)
    )
    after, sent = after_attention(
        attended, w_out_near, rows_copy, norm_ffn.reshape(1, width), spread, experts
    )

    row_blocks = to_experts(sent)
    own_gain, own_table = width // devices, NB * heads // devices
    if fast:
        expert_grad, token = side_by_side(grad_blocks, token)
        parts = (normed_all, attended)
        parts = parts + tuple(swapped(part, "dp", 1) for part in parts)
        left, token = turn(at, parts, token)
        peak, token = larger(peak_lanes, swapped(peak_lanes, "dp", 1), token)
        peak, token = larger(peak, swapped(peak, "dp", 2), token)
        peak, token = larger(peak, swapped(peak, "ctx", 1), token)
        expert_rows, token = side_by_side(row_blocks, token)
        both_rows = expert_rows, swapped(expert_rows, "dp", 1)
        both_grads = expert_grad, swapped(expert_grad, "dp", 1)
        outs, token = expert_halves(at, both_rows, both_grads, w_in, w_down, token)
        back_keep, back_send, dgate, dup, rows_turned, hid, down_w, *down = outs
        back_got = swapped(back_send, "dp", 1)
        down = swapped(down[0], "dp", 2), down[1], to_down_plane(down[2]), down[2]
        back_rows, token = join(at, back_keep, back_got, experts, token)
        back_home = over_experts(back_rows)
        first, token = in_terms(at, rows_turned, dgate, dup, token)
        first = plane_first(first)
        out_keep, out_send, token = expert_results(hid, down_w, token)
    else:
        expert_rows = jnp.concatenate(row_blocks, axis=0)
        expert_grad = jnp.concatenate(grad_blocks, axis=0)
        (out_rows, back_rows, dgate, dup, hid_turned, rows_turned), token = expert(
            expert_rows, expert_grad, w_in, w_down, token
        )
        expert_first, expert_second = (
            lax.psum_scatter(grads, ("ctx", "dp"), scatter_dimension=0, tiled=True)[None]
            for grads in (
                dot_rows(rows_turned, jnp.concatenate([dgate, dup], axis=1)),
                dot_rows(hid_turned, expert_grad),
            )
        )
        back_home, out_home = (
            jnp.stack(from_experts(list(rows.reshape(experts, capacity, width))))
            for rows in (back_rows, out_rows)
        )

    home = at if fast else jnp.zeros_like(at)
    (grad_after, grad_branch, grad_attended, grad_gain_ffn), token = back_to_attention(
        home, spread, back_home, after, norm_ffn.reshape(1, width), cotangent[0], w_out_attn, token
    )
    if fast:
        packed, token = attention_back(
            queries, keys, values, probs, grad_attended, token,
            (grad_branch, bucket_hot, grad_gain_ffn, devices),
        )
        packed_got = swapped(packed, "dp", 1)
        down_a, down_b, token = down_second(at, down, token, 20)
        plane_2, token = shared_terms(at, left, packed, packed_got, experts, token)
        plane_2 = plane_first(plane_2)
        out_send, = hold(token, out_send)
        out_got = swapped(out_send, "dp", 1)
        out_rows, token = join_peak(at, out_keep, out_got, peak, experts, token)
        out_home = over_experts(out_rows)
        normed_own_grad, normed_other_grad, token = normed_grads(
            packed, (w_query, w_key, w_value), tokens, token
        )
        in_a, in_b, token = plane_second(first, token)
        down_a, down_b = hold(token, down_a, down_b)
        down_a, down_b = to_down_plane(down_a), in_down_plane(down_b)
    else:
        dq, dk, dv, lines, token = attention_back(
            queries, keys, values, probs, grad_attended, token
        )
        lines = lines[:, :GROUP, :].reshape(heads, length + tokens)
        grad_table = lax.dot_general(
            bucket_hot, lines, (((1,), (1,)), ((), ())), precision=FULL_PRECISION
        ).reshape(-1)
        mixed, _, _ = mix(home, pick, out_home, gates[0].T, after, token)
        peak = jnp.max(peak_lanes[:, :GROUP, :], axis=-1).reshape(heads)
        peak = lax.pmax(peak, ("ctx", "exp", "dp"))
        peak = jnp.broadcast_to(peak[:, None], (heads, LANES))
        clipped, _ = clip(w_query, w_key, peak, clip_level, token)

        grad_normed = dot_back(dk, w_key) + dot_back(dv, w_value)
        grad_normed_own = grad_normed[length - tokens :] + dot_back(dq, w_query)
        for block, back in enumerate(backs):
            term = grad_normed[block * tokens : (block + 1) * tokens].astype(LOW)
            returned = lax.ppermute(term, "ctx", [((i + back) % n_ctx, i) for i in range(n_ctx)])
            grad_normed_own = grad_normed_own + returned.astype(FULL)
        _, norm_pull = jax.vjp(lambda rows: rms_norm(rows, norm_attn), own_rows)
        grad_input = (grad_after + norm_pull(grad_normed_own)[0])[None]

    if fast:
        shared_a, shared_b, token = plane_second(plane_2, token, (normed_other_grad,))
        shared_a, shared_b = swapped(shared_a, "ctx", 1), swapped(shared_b, "dp", 2)
        mixed, peak, token = mix(at, pick, out_home, gates[0].T, after, token)
        down_keep, down_send, token = down_last(at, down, down_a, down_b, token)
        down_got = swapped(down_send, "dp", 1)
        half_b, token = plane_sum(plane_2[2], plane_2[3], shared_b, token)
        in_a, in_b = hold(token, in_a, in_b)
        in_a, in_b = swapped(in_a, "ctx", 1), swapped(in_b, "dp", 2)
        plane, token = pair_last(plane_2[0], plane_2[1], shared_a, half_b, experts, token)
        plane = over_experts(plane)
        clipped, token = clip(w_query, w_key, peak, clip_level, token)
        expert_second, token = choose(at, down_keep, down_got, token)
        grad_input, token = input_grads(
            block_in[0], norm_attn.reshape(1, width), normed_own_grad, shared_a, grad_after, token
        )
        in_keep, in_send, token = in_last(at, first, in_a, in_b, token)
        in_got = swapped(in_send, "dp", 1)
        outs, token = last_rows(
            place_all, plane, own_gain, (w_query, w_key, w_value), norm_attn, token
        )
        expert_first, token = in_end(at, in_keep, in_got, token)
        shared_q, shared_k, shared_v, shared_o = outs[:4]
        small_attn, small_ffn = outs[4][0, :own_gain], outs[5][0, :own_gain]
        small_table = outs[6][0, :own_table]
    else:
        shared_q, shared_k, shared_v, shared_o = (
            lax.psum_scatter(grads, ("ctx", "exp", "dp"), scatter_dimension=0, tiled=True)
            for grads in (
                transpose_dot(normed_own, dq),
                transpose_dot(normed_all, dk),
                transpose_dot(normed_all, dv),
                transpose_dot(attended, grad_branch),
            )
        )
        small_ffn, small_table = (
            lax.dynamic_slice_in_dim(lax.psum(array, ("ctx", "exp", "dp")), place_all * own, own)
            for array, own in ((grad_gain_ffn[0], own_gain), (grad_table, own_table))
        )
        pairs = ((shared_q, w_query), (shared_k, w_key), (shared_v, w_value))
        row_sums = sum(
            jnp.sum(
                grads * lax.dynamic_slice_in_dim(weights, place_all * own_gain, own_gain).astype(FULL),
                axis=1,
            )
            for grads, weights in pairs
        )
        small_attn = row_sums / lax.dynamic_slice_in_dim(norm_attn, place_all * own_gain, own_gain)

    return (
        mixed,
        grad_input,
        small_attn,
        small_ffn,
        shared_q,
        shared_k,
        shared_v,
        shared_o,
        small_table,
        expert_first,
        expert_second,
        clipped[0],
        clipped[1],
        clipped[2][:, 0],
    )


def solution(mesh):
    tokens = P(("exp", "dp"), "ctx", None)
    everywhere = P(("ctx", "exp", "dp"))
    by_rows = P(("ctx", "exp", "dp"), None)
    by_expert = P("exp", None, None)
    expert_rows = P("exp", ("ctx", "dp"), None)
    in_specs = (tokens, P(("exp", "dp"), None), tokens, tokens) + (P(),) * 9
    in_specs = in_specs + (by_expert, by_expert, tokens)
    out_specs = (tokens, tokens, everywhere, everywhere) + (by_rows,) * 4
    out_specs = out_specs + (everywhere, expert_rows, expert_rows, P(), P(), P())
    return jax.shard_map(local, mesh=mesh, in_specs=in_specs, out_specs=out_specs, check_vma=False)
```

```python
import functools

import jax
import jax.numpy as jnp
from jax import lax
from jax.experimental import pallas as pl
from jax.experimental.pallas import tpu as pltpu
from jax.sharding import PartitionSpec as P

HDIM = 64
NB = 32
GROUP = 4
LANES = 128
EPSILON = 1e-06
FULL_PRECISION = lax.Precision.HIGHEST
LOW = jnp.bfloat16
FULL = jnp.float32
OUTSIDE = -1e30
GELU_SCALE = 0.7978845608028654
GELU_CUBE = 0.044715


def rms_norm(rows, gain):
    return rows * lax.rsqrt(jnp.mean(rows * rows, axis=-1, keepdims=True) + EPSILON) * gain


def dot_rows(left, right):
    return lax.dot_general(left, right, (((1,), (0,)), ((), ())), preferred_element_type=FULL)


def dot_back(left, right):
    return lax.dot_general(left, right, (((1,), (1,)), ((), ())), preferred_element_type=FULL)


def transpose_dot(left, right):
    return lax.dot_general(left, right, (((0,), (0,)), ((), ())), preferred_element_type=FULL)


def swapped(array, axis, bit):
    size = lax.axis_size(axis)
    return lax.ppermute(array, axis, [(i, i ^ bit) for i in range(size)])


def shifted(array, axis, shift):
    size = lax.axis_size(axis)
    return lax.ppermute(array, axis, [(i, (i + shift) % size) for i in range(size)])


def to_experts(blocks):
    return [blocks[0]] + [shifted(blocks[k], "exp", k) for k in range(1, len(blocks))]


def from_experts(blocks):
    return [blocks[0]] + [shifted(blocks[k], "exp", len(blocks) - k) for k in range(1, len(blocks))]


def over_experts(blocks):
    return lax.all_to_all(blocks, "exp", split_axis=0, concat_axis=0, tiled=True)


MICROSECOND = 1.15e9


def call(
    body, name, inputs, outputs, us, grid=None, token=None, prefetch=(), scratch=(), vmem=6,
    near_in=(), near_out=(), far_in=(), far_out=(), fetch=(),
    part_in=None,
):
    part_in = dict(part_in or {})
    far_in = tuple(far_in) + tuple(part_in)
    inputs = list(inputs) + [(array, None) for array in fetch]
    outputs = list(outputs) + [whole_out(array.shape, array.dtype) for array in fetch]
    n_pre, n_in, n_out = len(prefetch), len(inputs), len(outputs)
    held = [] if token is None else [token]
    n_far, n_scratch = len(far_in) + len(far_out), len(scratch)

    def kernel(*refs):
        split = n_pre + n_in
        outs = split + len(held)
        rest = refs[outs + n_out + 1 :]
        ins_here, outs_here = list(refs[:split]), list(refs[outs : outs + n_out])
        copies = []
        for number, at in enumerate(far_in):
            here = rest[n_scratch + number]
            source = refs[n_pre + at].at[part_in[at]] if at in part_in else refs[n_pre + at]
            copies.append(pltpu.make_async_copy(source, here, rest[-1].at[number]))
            ins_here[n_pre + at] = here
        for copy in copies:
            copy.start()
        fetches = [
            pltpu.make_async_copy(ins_here.pop(), outs_here.pop(), rest[-1].at[n_far + number])
            for number in range(len(fetch))
        ]
        for copy in fetches:
            copy.start()
        for copy in copies:
            copy.wait()
        copies = []
        for number, at in enumerate(far_out, len(far_in)):
            here = rest[n_scratch + number]
            copies.append(pltpu.make_async_copy(here, refs[outs + at], rest[-1].at[number]))
            outs_here[at] = here
        body(*ins_here, *outs_here, *rest[:n_scratch])
        for copy in fetches:
            copy.wait()
        for copy in copies:
            copy.start()
        for copy in copies:
            copy.wait()

    where = lambda at, near: pltpu.VMEM if at in near else pltpu.HBM
    arrays = [array for array, _ in inputs]
    shapes = [(shape, dtype) for shape, dtype, _ in outputs]
    anywhere = pl.BlockSpec(memory_space=pl.ANY)
    if grid is None:
        near = pl.BlockSpec(memory_space=pltpu.VMEM)
        far = [at in far_in or spec is None for at, (_, spec) in enumerate(inputs)]
        far_results = [at in far_out or spec is None for at, (_, _, spec) in enumerate(outputs)]
        left = lambda at: tuple(
            size if axis >= len(part_in.get(at, ())) else len(range(size)[part_in[at][axis]])
            for axis, size in enumerate(arrays[at].shape)
            if axis >= len(part_in.get(at, ())) or isinstance(part_in[at][axis], slice)
        )
        buffers = [pltpu.VMEM(left(at), arrays[at].dtype) for at in far_in]
        buffers += [pltpu.VMEM(*shapes[at]) for at in far_out]
        n_sems = n_far + len(fetch)
        buffers += [pltpu.SemaphoreType.DMA((n_sems,))] if n_sems else []
        form = dict(
            in_specs=[pl.BlockSpec(memory_space=pltpu.SMEM)] * n_pre
            + [anywhere if away else near for away in far]
            + [anywhere] * len(held),
            out_specs=[anywhere if away else near for away in far_results] + [anywhere],
            scratch_shapes=list(scratch) + buffers,
        )
        arrays = [
            pltpu.with_memory_space_constraint(array, pltpu.HBM) if away else array
            for array, away in zip(arrays, far)
        ]
        shapes = [
            pltpu.HBM(*one) if away else jax.ShapeDtypeStruct(*one)
            for away, one in zip(far_results, shapes)
        ]
    else:
        form = dict(
            grid_spec=pltpu.PrefetchScalarGridSpec(
                num_scalar_prefetch=n_pre,
                grid=grid,
                in_specs=[spec for _, spec in inputs] + [anywhere] * len(held),
                out_specs=[spec for _, _, spec in outputs] + [anywhere],
                scratch_shapes=list(scratch),
            )
        )
        arrays = [
            pltpu.with_memory_space_constraint(array, where(at, near_in))
            for at, array in enumerate(arrays)
        ]
        shapes = [where(at, near_out)(*one) for at, one in enumerate(shapes)]
    held = [pltpu.with_memory_space_constraint(array, pltpu.HBM) for array in held]
    results = pl.pallas_call(
        kernel,
        out_shape=shapes + [pltpu.HBM((8, LANES), FULL)],
        cost_estimate=pl.CostEstimate(
            flops=int(us * MICROSECOND), bytes_accessed=1, transcendentals=0
        ),
        compiler_params=pltpu.CompilerParams(vmem_limit_bytes=vmem * 2**20),
        name=name,
        **form,
    )(*prefetch, *arrays, *held)
    return list(results[:-1]), results[-1]


def whole(array):
    return array, pl.BlockSpec(array.shape, lambda *_: (0,) * array.ndim)


def whole_out(shape, dtype):
    return shape, dtype, pl.BlockSpec(shape, lambda *_: (0,) * len(shape))


def hold(token, *arrays):
    anywhere = pl.BlockSpec(memory_space=pl.ANY)
    return pl.pallas_call(
        lambda *refs: None,
        in_specs=[anywhere] * (len(arrays) + 1),
        out_specs=[anywhere] * len(arrays),
        out_shape=[jax.ShapeDtypeStruct(array.shape, array.dtype) for array in arrays],
        input_output_aliases={at + 1: at for at in range(len(arrays))},
        cost_estimate=pl.CostEstimate(flops=1, bytes_accessed=1, transcendentals=0),
        name="hold",
    )(token, *arrays)


def pass_kernel(*refs):
    half = len(refs) // 2
    for ref, out_ref in zip(refs[:half], refs[half:]):
        out_ref[...] = ref[...]


def bring(token, us, *arrays):
    return call(lambda *refs: None, "bring", [], [], token=token, fetch=arrays, us=us)


def pass_on(token, *arrays):
    return call(
        pass_kernel,
        "pass_on",
        [whole(array) for array in arrays],
        [whole_out(array.shape, array.dtype) for array in arrays],
        token=token,
        us=1,
    )


def eye(size):
    rows = lax.broadcasted_iota(jnp.int32, (size, size), 0)
    return rows == lax.broadcasted_iota(jnp.int32, (size, size), 1)


def to_column(row):
    size = row.shape[1]
    return jnp.sum(jnp.where(eye(size), row, jnp.zeros_like(row)), 1, keepdims=True)


def front_kernel(
    at_ref, routes_ref, gates_ref, grad_ref, seg_ref, rows_ref,
    spread_ref, pick_ref, mask_ref, copy_ref, *out_refs,
):
    top, tokens = routes_ref.shape
    experts, capacity = len(out_refs), out_refs[0].shape[0]
    routes = [routes_ref[r : r + 1, :] for r in range(top)]
    gates = [gates_ref[r : r + 1, :] for r in range(top)]
    before = lax.broadcasted_iota(jnp.int32, (tokens, tokens), 0)
    before = before < lax.broadcasted_iota(jnp.int32, (tokens, tokens), 1)
    slots = lax.broadcasted_iota(jnp.int32, (capacity, tokens), 0).astype(FULL)
    for e in range(experts):
        part = pl.ds(e * capacity, capacity)
        name = lax.rem(at_ref[3] + e, experts)
        hits = [jnp.where(route == name, 1.0, 0.0) for route in routes]
        named = functools.reduce(jnp.add, hits)
        slot = jnp.sum(jnp.where(before, to_column(named), 0.0), 0, keepdims=True)
        place = (slots == slot).astype(FULL)
        spread = place * named
        gate = functools.reduce(jnp.add, [hit * g for hit, g in zip(hits, gates)])
        spread_low = spread.astype(LOW)
        spread_ref[part, :] = spread_low
        for r in range(top):
            pick_ref[part, pl.ds(r * tokens, tokens)] = (place * hits[r]).astype(LOW)
        slot_gate = jnp.sum(spread * gate, 1, keepdims=True)
        out_refs[e][...] = (slot_gate * dot_rows(spread_low, grad_ref[...])).astype(LOW)
    length = mask_ref.shape[1]
    ctx = at_ref[0]
    seg = jnp.broadcast_to(seg_ref[...].astype(FULL), (8, length))
    keys = pltpu.roll(seg, length - (ctx + 1) * tokens, 1)[:1, :]
    at_row = lax.broadcasted_iota(jnp.int32, (tokens, length), 0) + (length - tokens)
    at_key = lax.broadcasted_iota(jnp.int32, (tokens, length), 1)
    own = jnp.sum(jnp.where(at_row == at_key, keys, 0.0), 1, keepdims=True)
    allowed = (at_key <= at_row) & (own == keys) & (at_key >= length - (ctx + 1) * tokens)
    mask_ref[...] = jnp.where(allowed, 0.0, OUTSIDE)
    copy_ref[...] = rows_ref[...]


def front(at, routes, gates, grad, seg, rows, experts, capacity):
    top, tokens = routes.shape
    slots = experts * capacity
    return call(
        front_kernel,
        "front",
        [whole(array) for array in (routes, gates, grad, seg, rows)],
        [
            whole_out((slots, tokens), LOW),
            whole_out((slots, top * tokens), LOW),
            whole_out((tokens, seg.shape[1]), FULL),
            whole_out(rows.shape, LOW),
        ]
        + [whole_out((capacity, grad.shape[1]), LOW)] * experts,
        prefetch=(at,),
        far_in=(0, 1, 2, 3, 4),
        far_out=(1,),
        us=1.5,
    )


def bias_kernel(buckets_ref, table_ref, hot_ref, bias_ref):
    heads, rows, keys = bias_ref.shape
    width = hot_ref.shape[1]
    buckets = buckets_ref[...].astype(FULL)
    column = jnp.sum(jnp.where(eye(keys), buckets, 0.0), 1, keepdims=True)
    distance = lax.broadcasted_iota(jnp.int32, (keys, width), 0)
    lane = lax.broadcasted_iota(jnp.int32, (keys, width), 1)
    turned = jnp.sum(jnp.where(distance + lane == keys - 1, column, 0.0), 0, keepdims=True)
    bucket = lax.broadcasted_iota(jnp.int32, (NB, width), 0).astype(FULL)
    hot = jnp.where(bucket == turned, 1.0, 0.0)
    hot_ref[...] = hot
    by_lane = lax.dot_general(
        table_ref[...], hot, (((0,), (0,)), ((), ())), precision=FULL_PRECISION,
        preferred_element_type=FULL,
    )
    for head in range(heads):
        line = jnp.broadcast_to(by_lane[head : head + 1, :], (8, width))
        line = pltpu.roll(line, keys + 1, 1, stride=1, stride_axis=0)
        for start in range(0, rows, 8):
            moved = line if start == 0 else pltpu.roll(line, start, 1)
            bias_ref[head, pl.ds(start, 8), :] = moved[:, :keys]


def bias_tiles(buckets, table, rows, fetch):
    heads, keys = table.shape[1], buckets.shape[1]
    return call(
        bias_kernel,
        "bias_tiles",
        [whole(buckets), whole(table)],
        [whole_out((NB, keys + rows), FULL), whole_out((heads, rows, keys), FULL)],
        us=2.5,
        vmem=16,
        fetch=fetch,
    )


def half_lanes(half, shape):
    lane = lax.broadcasted_iota(jnp.int32, shape, 1)
    return lane < HDIM if half == 0 else lane >= HDIM


def attention_kernel(q_ref, k_ref, v_ref, bias_ref, mask_ref, out_ref, probs_ref, peak_ref):
    groups = peak_ref.shape[0]

    def group(step, _):
        mask = mask_ref[...]
        for pair in range(GROUP // 2):
            lanes = pair_lanes(step, pair)
            queries, keys, values = q_ref[:, lanes], k_ref[:, lanes], v_ref[:, lanes]
            parts = []
            for half in range(2):
                at = 2 * pair + half
                own = half_lanes(half, queries.shape)
                raw = dot_back(jnp.where(own, queries, jnp.zeros_like(queries)), keys)
                raw = raw * HDIM**-0.5 + mask
                top = jnp.max(raw, axis=0, keepdims=True)
                best = top[:, :LANES]
                for start in range(LANES, top.shape[1], LANES):
                    best = jnp.maximum(best, top[:, start : start + LANES])
                peak_ref[step, at : at + 1, :] = best
                scores = raw + bias_ref[step * GROUP + at]
                raised = jnp.exp(scores - jnp.max(scores, axis=1, keepdims=True))
                probs = raised * (1.0 / jnp.sum(raised, axis=1, keepdims=True))
                probs_low = probs.astype(LOW)
                probs_ref[step * GROUP + at] = probs_low
                parts.append(dot_rows(probs_low, values))
            first = half_lanes(0, parts[0].shape)
            out_ref[:, lanes] = jnp.where(first, parts[0], parts[1]).astype(LOW)
        return 0

    lax.fori_loop(0, groups, group, 0)


def pair_lanes(step, pair):
    return pl.ds(pl.multiple_of(step * GROUP * HDIM + pair * LANES, LANES), LANES)


def attention(queries, keys, values, bias, mask, fetch):
    rows, width = queries.shape
    length = keys.shape[0]
    heads = width // HDIM
    (out, probs, peak, *fetched), _ = call(
        attention_kernel,
        "attention",
        [whole(array) for array in (queries, keys, values, bias, mask)],
        [
            whole_out((rows, width), LOW),
            whole_out((heads, rows, length), LOW),
            whole_out((heads // GROUP, 8, LANES), FULL),
        ],
        us=4.5,
        vmem=10,
        far_out=(1,),
        fetch=fetch,
    )
    return out, probs, peak, *fetched


def attention_back_kernel(
    q_ref, k_ref, v_ref, probs_ref, grad_ref, dq_ref, dk_ref, dv_ref, lines_ref
):
    groups = lines_ref.shape[0]
    rows, length = probs_ref.shape[1:]
    scale = HDIM**-0.5

    def group(step, _):
        for pair in range(GROUP // 2):
            lanes = pair_lanes(step, pair)
            queries, keys, values, grad = (
                ref[:, lanes] for ref in (q_ref, k_ref, v_ref, grad_ref)
            )
            dq, dk, dv = [], [], []
            for half in range(2):
                at = 2 * pair + half
                own = half_lanes(half, grad.shape)
                dp = dot_back(jnp.where(own, grad, jnp.zeros_like(grad)), values)
                probs_low = probs_ref[step * GROUP + at]
                probs = probs_low.astype(FULL)
                ds = probs * (dp - jnp.sum(probs * dp, axis=1, keepdims=True))
                ds_low = ds.astype(LOW)
                dq.append(dot_rows(ds_low, keys))
                dk.append(transpose_dot(ds_low, queries))
                dv.append(transpose_dot(probs_low, grad))
                wide = jnp.concatenate([ds, jnp.zeros((rows, rows), FULL)], axis=1)
                total = wide[rows - 8 :, :]
                for start in range(0, rows - 8, 8):
                    total = total + pltpu.roll(wide[start : start + 8, :], rows - 8 - start, 1)
                line = lax.broadcasted_iota(jnp.int32, total.shape, 0)
                for bit in (1, 2, 4):
                    total = jnp.where(((7 - line) & bit) != 0, pltpu.roll(total, bit, 1), total)
                lines_ref[step, at : at + 1, :] = jnp.sum(total, axis=0, keepdims=True)
            first = half_lanes(0, dq[0].shape)
            dq_ref[:, lanes] = (jnp.where(first, dq[0], dq[1]) * scale).astype(LOW)
            first = half_lanes(0, dk[0].shape)
            dk_ref[:, lanes] = (jnp.where(first, dk[0], dk[1]) * scale).astype(LOW)
            dv_ref[:, lanes] = jnp.where(first, dv[0], dv[1]).astype(LOW)
        return 0

    lax.fori_loop(0, groups, group, 0)


def packed_back_kernel(
    q_ref, k_ref, v_ref, probs_ref, grad_ref, branch_ref, hot_ref, gain_ref, out_ref, lines_ref
):
    rows, length = probs_ref.shape[1:]
    ends = [0, rows, rows + length, rows + 2 * length, 2 * rows + 2 * length]
    parts = [out_ref.at[pl.ds(a, b - a), :] for a, b in zip(ends, ends[1:])]
    attention_back_kernel(q_ref, k_ref, v_ref, probs_ref, grad_ref, *parts[:3], lines_ref)
    parts[3][...] = branch_ref[...]
    groups = lines_ref.shape[0]
    width = gain_ref.shape[1]
    devices = out_ref.shape[0] - ends[4]
    own, turns = width // devices, LANES * devices // width
    device = lax.broadcasted_iota(jnp.int32, (devices, width), 0)
    feature = lax.broadcasted_iota(jnp.int32, (devices, width), 1)
    spread = jnp.where(feature // own == device, gain_ref[...], 0.0)
    folded = functools.reduce(
        jnp.add, [spread[:, start : start + LANES] for start in range(0, width, LANES)]
    )
    device = lax.broadcasted_iota(jnp.int32, folded.shape, 0)
    small = folded
    for turn_by in range(1, turns):
        moved = pltpu.roll(folded, LANES - turn_by * own, 1)
        small = jnp.where(device % turns == turn_by, moved, small)
    lines = jnp.concatenate([lines_ref[g, :GROUP, :] for g in range(groups)], axis=0)
    blank = jnp.zeros((LANES - TABLE_LANE - lines.shape[0], lines.shape[1]), FULL)
    lines = jnp.concatenate([jnp.zeros((TABLE_LANE, lines.shape[1]), FULL), lines, blank], axis=0)
    upper = lines.astype(LOW)
    lower = (lines - upper.astype(FULL)).astype(LOW)
    hot = hot_ref[...].astype(LOW)
    small = small + dot_back(hot, upper) + dot_back(hot, lower)
    out_ref[pl.ds(ends[4], devices), :LANES] = small.astype(LOW)


def attention_back(queries, keys, values, probs, grad, token, packed=None):
    rows, width = queries.shape
    length = keys.shape[0]
    heads = width // HDIM
    lines = whole_out((heads // GROUP, 8, length + rows), FULL)
    inputs = [whole(array) for array in (queries, keys, values, probs, grad)]
    if packed is None:
        outs, token = call(
            attention_back_kernel,
            "attention_back",
            inputs,
            [whole_out((size, width), LOW) for size in (rows, length, length)] + [lines],
            token=token,
            us=6.6,
            vmem=16,
        )
        return *outs, token
    branch, hot, gain, devices = packed
    (out, _), token = call(
        packed_back_kernel,
        "attention_back",
        inputs + [whole(branch), whole(hot), whole(gain)],
        [whole_out((2 * rows + 2 * length + devices, width), LOW), lines],
        token=token,
        us=7,
        vmem=16,
    )
    return out, token


def post_kernel(attended_ref, weights_ref, rows_ref, gain_ref, spread_ref, after_ref, *out_refs):
    after = rows_ref[...].astype(FULL) + dot_rows(attended_ref[...], weights_ref[...])
    after_ref[...] = after
    sent = rms_norm(after, gain_ref[...]).astype(LOW)
    size = out_refs[0].shape[0]
    for at, out_ref in enumerate(out_refs):
        out_ref[...] = dot_rows(spread_ref[pl.ds(at * size, size), :], sent).astype(LOW)


def after_attention(attended, weights, rows, gain, spread, experts):
    tokens, width = rows.shape
    (after, *sent), _ = call(
        post_kernel,
        "post",
        [whole(array) for array in (attended, weights, rows, gain, spread)],
        [whole_out((tokens, width), FULL)]
        + [whole_out((spread.shape[0] // experts, width), LOW)] * experts,
        far_out=(0,),
        us=2,
    )
    return after, sent


def gather_kernel(*refs):
    size = refs[0].shape[0]
    for at, ref in enumerate(refs[:-1]):
        refs[-1][pl.ds(at * size, size), :] = ref[...]


def side_by_side(blocks, token):
    size, width = blocks[0].shape
    (out,), token = call(
        gather_kernel,
        "gather",
        [whole(block) for block in blocks],
        [whole_out((len(blocks) * size, width), LOW)],
        token=token,
        us=1,
    )
    return out, token


def expert_part(gate, up, dhid):
    square = gate * gate
    curve = jnp.tanh(GELU_SCALE * gate * (1.0 + GELU_CUBE * square))
    upper = 0.5 * (1.0 + curve)
    gelu = gate * upper
    slope = upper + 0.5 * gate * (1.0 - curve * curve) * (
        GELU_SCALE * (1.0 + 3.0 * GELU_CUBE * square)
    )
    hid = (gelu * up).astype(LOW)
    dgate = (dhid * up * slope).astype(LOW)
    dup = (dhid * gelu).astype(LOW)
    return hid, dgate, dup


def expert_kernel(
    rows_ref, grad_ref, gate_w_ref, up_w_ref, down_w_ref,
    out_ref, back_ref, dgate_ref, dup_ref, hid_ref, turned_ref, out_sum, back_sum,
):
    step = pl.program_id(0)

    @pl.when(step == 0)
    def _():
        out_sum[...] = jnp.zeros_like(out_sum)
        back_sum[...] = jnp.zeros_like(back_sum)

    rows, grad = rows_ref[...], grad_ref[...]
    gate_w, up_w, down_w = gate_w_ref[0], up_w_ref[0], down_w_ref[0]
    hid, dgate, dup = expert_part(
        dot_rows(rows, gate_w), dot_rows(rows, up_w), dot_back(grad, down_w)
    )
    dgate_ref[...] = dgate
    dup_ref[...] = dup
    hid_ref[...] = hid.T
    out_sum[...] += dot_rows(hid, down_w)
    back_sum[...] += dot_back(dgate, gate_w) + dot_back(dup, up_w)

    @pl.when(step == pl.num_programs(0) - 1)
    def _():
        out_ref[...] = out_sum[...].astype(LOW)
        back_ref[...] = back_sum[...].astype(LOW)
        turned_ref[...] = rows_ref[...].T


def expert(rows, grad, w_in, w_down, token):
    count, width = rows.shape
    hidden = w_down.shape[1]
    part = 256
    steps = hidden // part
    return call(
        expert_kernel,
        "expert",
        [
            whole(rows),
            whole(grad),
            (w_in, pl.BlockSpec((1, width, part), lambda i: (0, 0, i))),
            (w_in, pl.BlockSpec((1, width, part), lambda i: (0, 0, i + steps))),
            (w_down, pl.BlockSpec((1, part, width), lambda i: (0, i, 0))),
        ],
        [
            whole_out((count, width), LOW),
            whole_out((count, width), LOW),
            ((count, hidden), LOW, pl.BlockSpec((count, part), lambda i: (0, i))),
            ((count, hidden), LOW, pl.BlockSpec((count, part), lambda i: (0, i))),
            ((hidden, count), LOW, pl.BlockSpec((part, count), lambda i: (i, 0))),
            whole_out((width, count), LOW),
        ],
        grid=(steps,),
        token=token,
        scratch=[pltpu.VMEM((count, width), FULL), pltpu.VMEM((count, width), FULL)],
        vmem=24,
        us=20,
    )


CHUNK = 512
EXPERT_CHUNK = 768
EXPERT_VMEM = 40


def halves_kernel(
    at_ref, x0_ref, x1_ref, g0_ref, g1_ref, w_in_ref, w_down_ref,
    back_keep, back_send, dgate_ref, dup_ref, turned_ref, hid_out, a_send, a_keep, b_out,
    both_w, du, turned, hid_ref, down_ref, a_sum, b_ref, sems, out_sems,
):
    count, width = x0_ref.shape
    half = down_ref.shape[0]
    full, rest = half // EXPERT_CHUNK, half % EXPERT_CHUNK
    first = pl.multiple_of(at_ref[2] * half, LANES)

    def copies(i, units):
        start = pl.multiple_of(i * EXPERT_CHUNK, LANES)
        pairs = []
        for piece in range(4):
            rows = pl.ds(piece * (width // 4), width // 4)
            for part in range(2):
                one = pl.ds(pl.multiple_of(first + start + 2 * part * half, LANES), units)
                two = pl.ds(pl.multiple_of(start + part * half, LANES), units)
                pairs.append((w_in_ref.at[0, rows, one], both_w.at[rows, two]))
            size = units // 4
            one = pl.ds(pl.multiple_of(first + start + piece * size, 16), size)
            two = pl.ds(pl.multiple_of(start + piece * size, 16), size)
            pairs.append((w_down_ref.at[0, one, :], down_ref.at[two, :]))
        return [
            pltpu.make_async_copy(one, two, sems.at[i, at]) for at, (one, two) in enumerate(pairs)
        ]

    def results(i, units):
        copies = []
        for part, ref in enumerate((dgate_ref, dup_ref)):
            one = pl.ds(pl.multiple_of(part * half + i * EXPERT_CHUNK, LANES), units)
            two = pl.ds(pl.multiple_of(i * EXPERT_CHUNK, LANES), units)
            copies.append(pltpu.make_async_copy(du.at[:, one], ref.at[:, two], out_sems.at[i, part]))
        return copies

    sizes = [EXPERT_CHUNK] * full + ([rest] if rest else [])
    for copy in copies(0, sizes[0]):
        copy.start()
    turned[:, :count] = x0_ref[...].T
    turned[:, count:] = x1_ref[...].T
    turned_copy = pltpu.make_async_copy(turned, turned_ref, out_sems.at[len(sizes), 0])

    def chunk(i, units):
        for copy in copies(i, units):
            copy.wait()

        @pl.when(i == 0)
        def _():
            for later, size in enumerate(sizes[1:], 1):
                for copy in copies(later, size):
                    copy.start()

        start = pl.multiple_of(i * EXPERT_CHUNK, LANES)
        columns = pl.ds(start, units)
        other = pl.ds(pl.multiple_of(start + half, LANES), units)
        gate_w, up_w, down_w = both_w[:, columns], both_w[:, other], down_ref[columns, :]
        for side, (x_ref, g_ref) in enumerate(((x0_ref, g0_ref), (x1_ref, g1_ref))):
            rows = pl.ds(side * count, count)
            x = x_ref[...]
            hid, dgate, dup = expert_part(
                dot_rows(x, gate_w), dot_rows(x, up_w), dot_back(g_ref[...], down_w)
            )
            hid_ref[rows, columns] = hid
            du[rows, columns] = dgate
            du[rows, other] = dup
        for copy in results(i, units):
            copy.start()

    def step(i, _):
        chunk(i, EXPERT_CHUNK)
        return 0

    lax.fori_loop(0, full, step, 0)
    if rest:
        chunk(full, rest)
    turned_copy.start()
    kept = [
        pltpu.make_async_copy(ref, out, out_sems.at[len(sizes) + 1, at])
        for at, (ref, out) in enumerate(((hid_ref, hid_out),))
    ]
    for copy in kept:
        copy.start()
    terms = transpose_dot(hid_ref[:count, :], g0_ref[...])
    terms = terms + transpose_dot(hid_ref[count:, :], g1_ref[...])
    middle, size = width // 2, half // 2
    b_ref[...] = terms[:, middle:].astype(LOW)
    a_sum[...] = terms[:, :middle].astype(LOW)
    own = pl.ds(pl.multiple_of(at_ref[1] * size, 16), size)
    other = pl.ds(pl.multiple_of((1 - at_ref[1]) * size, 16), size)
    sent = [(b_ref, b_out), (a_sum.at[other, :], a_send), (a_sum.at[own, :], a_keep)]
    sent = [
        pltpu.make_async_copy(ref, out, out_sems.at[len(sizes) + 2 + at // 2, at % 2])
        for at, (ref, out) in enumerate(sent)
    ]
    for copy in sent:
        copy.start()
    back_send[...] = dot_back(du[count:, :], both_w[...]).astype(LOW)
    back_keep[...] = dot_back(du[:count, :], both_w[...])
    turned_copy.wait()
    for copy in kept + sent:
        copy.wait()
    for i, units in enumerate(sizes):
        for copy in results(i, units):
            copy.wait()


def expert_halves(at, rows, grads, w_in, w_down, token):
    count, width = rows[0].shape
    half = w_down.shape[1] // 2
    chunks = pl.cdiv(half, EXPERT_CHUNK)
    return call(
        halves_kernel,
        "expert_halves",
        [whole(array) for array in (*rows, *grads)] + [(w_in, None), (w_down, None)],
        [
            whole_out((count, width), FULL),
            whole_out((count, width), LOW),
            ((2 * count, half), LOW, None),
            ((2 * count, half), LOW, None),
            ((width, 2 * count), LOW, None),
            ((2 * count, half), LOW, None),
            ((half // 2, width // 2), LOW, None),
            ((half // 2, width // 2), LOW, None),
            ((half, width // 2), LOW, None),
        ],
        token=token,
        prefetch=(at,),
        scratch=[
            pltpu.VMEM((width, 2 * half), LOW),
            pltpu.VMEM((2 * count, 2 * half), LOW),
            pltpu.VMEM((width, 2 * count), LOW),
            pltpu.VMEM((2 * count, half), LOW),
            pltpu.VMEM((half, width), LOW),
            pltpu.VMEM((half, width // 2), LOW),
            pltpu.VMEM((half, width // 2), LOW),
            pltpu.SemaphoreType.DMA((chunks, 12)),
            pltpu.SemaphoreType.DMA((chunks + 4, 2)),
        ],
        vmem=EXPERT_VMEM,
        us=20,
    )


def results_kernel(at_ref, hid_out, w_down_ref, keep_out, send_out, hid_ref, down_ref, sum_ref, sems):
    half = down_ref.shape[0]
    size = half // 4
    count = sum_ref.shape[1]
    copies = []
    for side in range(2):
        rows = pl.ds(side * count, count)
        copies.append(pltpu.make_async_copy(hid_out.at[rows, :], hid_ref.at[rows, :], sems.at[4 + side]))
    for piece in range(4):
        rows = pl.ds(pl.multiple_of(at_ref[2] * half + piece * size, 16), size)
        here = down_ref.at[pl.ds(piece * size, size), :]
        copies.append(pltpu.make_async_copy(w_down_ref.at[0, rows, :], here, sems.at[piece]))
    for copy in copies:
        copy.start()
    for copy in copies:
        copy.wait()
    copies = []
    for side, out in ((1, send_out), (0, keep_out)):
        rows = pl.ds(side * count, count)
        sum_ref[side] = dot_rows(hid_ref[rows, :], down_ref[...]).astype(LOW)
        copies.append(pltpu.make_async_copy(sum_ref.at[side], out, sems.at[6 + side]))
        copies[-1].start()
    for copy in copies:
        copy.wait()


def expert_results(at, hid, w_down, token):
    half, width = hid.shape[1], w_down.shape[2]
    shape = (hid.shape[0] // 2, width)
    (keep, send), token = call(
        results_kernel,
        "expert_results",
        [(hid, None), (w_down, None)],
        [(shape, LOW, None)] * 2,
        token=token,
        prefetch=(at,),
        scratch=[
            pltpu.VMEM(hid.shape, LOW),
            pltpu.VMEM((half, width), LOW),
            pltpu.VMEM((2, *shape), LOW),
            pltpu.SemaphoreType.DMA((8,)),
        ],
        vmem=16,
        us=0.01,
    )
    return keep, send, token


def block_of(at_ref, k, blocks):
    return lax.rem(at_ref[3] + (blocks - k), blocks)


def join_kernel(at_ref, kept_ref, got_ref, out_ref):
    blocks, size, _ = out_ref.shape
    for k in range(blocks):
        rows = pl.ds(k * size, size)
        total = kept_ref[rows, :] + got_ref[rows, :].astype(FULL)
        out_ref[block_of(at_ref, k, blocks)] = total.astype(LOW)


def join(at, kept, got, blocks, token):
    rows, width = kept.shape
    (out,), token = call(
        join_kernel,
        "join",
        [whole(kept), whole(got)],
        [whole_out((blocks, rows // blocks, width), LOW)],
        token=token,
        prefetch=(at,),
        far_out=(0,),
        us=1,
    )
    return out, token


def join_peak_kernel(at_ref, kept_ref, got_ref, peak_ref, out_ref):
    blocks, size, width = out_ref.shape
    rows = kept_ref.shape[0] // blocks
    best = jnp.concatenate([peak_ref[g, :GROUP, :] for g in range(peak_ref.shape[0])], axis=0)
    best = jnp.broadcast_to(jnp.max(best, axis=1, keepdims=True), (size - rows, LANES))
    upper = best.astype(LOW)
    lower = (best - upper.astype(FULL)).astype(LOW)
    for k in range(blocks):
        part = pl.ds(k * rows, rows)
        to = block_of(at_ref, k, blocks)
        total = kept_ref[part, :].astype(FULL) + got_ref[part, :].astype(FULL)
        out_ref[to, :rows, :] = total.astype(LOW)
        out_ref[to, rows:, :] = jnp.zeros((size - rows, width), LOW)
        out_ref[to, rows:, :LANES] = upper
        out_ref[to, rows:, LANES : 2 * LANES] = lower


def join_peak(at, kept, got, peak, blocks, token):
    rows, width = kept.shape
    heads = peak.shape[0] * GROUP
    (out,), token = call(
        join_peak_kernel,
        "join_peak",
        [whole(kept), whole(got), whole(peak)],
        [whole_out((blocks, rows // blocks + heads, width), LOW)],
        token=token,
        prefetch=(at,),
        far_out=(0,),
        us=0.01,
        far_in=(0,),
    )
    return out, token


def larger_kernel(one_ref, two_ref, out_ref):
    out_ref[...] = jnp.maximum(one_ref[...], two_ref[...])


def larger(one, two, token):
    (out,), token = call(
        larger_kernel,
        "larger",
        [whole(one), whole(two)],
        [whole_out(one.shape, FULL)],
        token=token,
        us=0.5,
    )
    return out, token


def place():
    dp = lax.axis_index("dp")
    return lax.axis_index("ctx"), lax.axis_index("exp"), dp // 2, dp % 2


def to_down_plane(array):
    pairs = [
        ((1 - core) * 4 + x * 2 + core, core * 4 + x * 2 + core)
        for core in range(2)
        for x in range(2)
    ]
    return lax.ppermute(array, ("ctx", "dp"), pairs)


def in_down_plane(array):
    pairs = [
        (core * 4 + x * 2 + core, core * 4 + (1 - x) * 2 + core)
        for core in range(2)
        for x in range(2)
    ]
    return lax.ppermute(array, ("ctx", "dp"), pairs)


def in_kernel(
    at_ref, turned_ref, gate_ref, up_ref, *refs,
):
    out_refs, turned, near, results, sems, out_sems = refs[:4], *refs[4:]
    half = gate_ref.shape[1]
    starts = list(range(0, half, CHUNK))
    loads = []
    for at, (ref, to) in enumerate(((gate_ref, near.at[0]), (up_ref, near.at[1]))):
        for i, start in enumerate(starts):
            columns = pl.ds(start, min(CHUNK, half - start))
            loads.append(
                pltpu.make_async_copy(ref.at[:, columns], to.at[:, columns], sems.at[at, i])
            )
    whole_load = pltpu.make_async_copy(turned_ref, turned, sems.at[2, 0])
    whole_load.start()
    loads[0].start()
    loads[len(starts)].start()
    whole_load.wait()
    size = turned.shape[0] // 4
    stores = []
    for i, start in enumerate(starts):
        columns = pl.ds(start, min(CHUNK, half - start))
        loads[i].wait()
        loads[len(starts) + i].wait()
        if i + 1 < len(starts):
            loads[i + 1].start()
            loads[len(starts) + i + 1].start()
        for block in range(4):
            ry, rx = block // 2, block % 2
            chip = (at_ref[0] ^ ry) * 2 + (at_ref[1] ^ rx)
            rows = turned[pl.ds(pl.multiple_of(chip * size, size), size), :]
            a, b = 1 - rx, 2 + 1 - ry
            results[a, ry, :, columns] = dot_rows(rows, near[0, :, columns]).astype(LOW)
            results[b, rx, :, columns] = dot_rows(rows, near[1, :, columns]).astype(LOW)
        for at, ref in enumerate(out_refs):
            copy = pltpu.make_async_copy(
                results.at[at, :, :, columns], ref.at[:, :, columns], out_sems.at[at, i]
            )
            copy.start()
            stores.append(copy)
    for copy in stores:
        copy.wait()


def in_terms(at, turned, gate, up, token):
    width, count = turned.shape
    half = gate.shape[1]
    shape = (2, width // 4, half)
    chunks = pl.cdiv(half, CHUNK)
    return call(
        in_kernel,
        "in_terms",
        [(turned, None), (gate, None), (up, None)],
        [(shape, LOW, None)] * 4,
        token=token,
        prefetch=(at,),
        scratch=[
            pltpu.VMEM((width, count), LOW),
            pltpu.VMEM((2, count, half), LOW),
            pltpu.VMEM((4, *shape), LOW),
            pltpu.SemaphoreType.DMA((3, chunks)),
            pltpu.SemaphoreType.DMA((4, chunks)),
        ],
        vmem=20,
        us=0.01,
    )


def plane_first(parts):
    a_send, a_keep, b_send, b_keep = parts
    return swapped(a_send, "dp", 2), a_keep, swapped(b_send, "ctx", 1), b_keep


def second_kernel(*refs):
    (a_ref, a_keep_ref, b_ref, b_keep_ref), (a_send_ref, b_send_ref) = refs[:4], refs[-2:]
    rows = a_ref.shape[0]
    total = a_keep_ref[...].astype(FULL) + a_ref[...].astype(FULL)
    a_send_ref[pl.ds(0, rows), :] = total.astype(LOW)
    b_send_ref[...] = (b_keep_ref[...].astype(FULL) + b_ref[...].astype(FULL)).astype(LOW)
    for beside in refs[4:-2]:
        more, width = beside.shape
        a_send_ref[pl.ds(rows, more), pl.ds(0, width)] = beside[...]


def plane_second(parts, token, us, beside=()):
    extra = sum(part.shape[0] for part in beside)
    (_, a_rows, a_width), (_, b_rows, b_width) = parts[0].shape, parts[2].shape
    (a_send, b_send), token = call(
        second_kernel,
        "second_terms",
        [whole(part) for part in (*parts, *beside)],
        [whole_out((a_rows + extra, a_width), LOW), whole_out((b_rows, b_width), LOW)],
        token=token,
        us=us,
        far_in=tuple(range(4, 4 + len(beside))),
        part_in={at: (1,) for at in range(4)},
        far_out=(0, 1),
        vmem=10,
    )
    return a_send, b_send, token


def down_second_kernel(at_ref, a_ref, a_keep_ref, b_ref, b_keep_ref, a_send_ref, b_send_ref):
    size = b_send_ref.shape[0]
    rows = pl.ds(pl.multiple_of((1 - at_ref[1]) * size, 16), size)
    a_send_ref[...] = (a_keep_ref[...].astype(FULL) + a_ref[...].astype(FULL)).astype(LOW)
    b_send_ref[...] = (b_keep_ref[rows, :].astype(FULL) + b_ref[rows, :].astype(FULL)).astype(LOW)


def down_second(at, parts, token, us):
    shape = parts[0].shape
    (a_send, b_send), token = call(
        down_second_kernel,
        "down_second",
        [whole(part) for part in parts],
        [whole_out(shape, LOW)] * 2,
        token=token,
        prefetch=(at,),
        us=us,
        far_out=(0, 1),
    )
    return a_send, b_send, token


def sum_kernel(one_ref, two_ref, three_ref, out_ref):
    out_ref[...] = sum(ref[...].astype(FULL) for ref in (one_ref, two_ref, three_ref)).astype(LOW)


def plane_sum(got, kept, more, token):
    (out,), token = call(
        sum_kernel,
        "plane_sum",
        [whole(got), whole(kept), whole(more)],
        [whole_out(more.shape, LOW)],
        token=token,
        far_in=(2,),
        part_in={0: (0,), 1: (0,)},
        far_out=(0,),
        us=0.01,
    )
    return out, token


def pair_last_kernel(a_ref, a_keep_ref, a2_ref, b_ref, out_ref):
    blocks = out_ref.shape[0]
    a = sum(ref[...].astype(FULL) for ref in (a_keep_ref, a_ref, a2_ref))
    size = b_ref.shape[0] // blocks
    for z in range(blocks):
        here = slice(z * size, (z + 1) * size)
        out_ref[z, :size, :] = a[here].astype(LOW)
        small = jnp.broadcast_to(a[blocks * size + z : blocks * size + z + 1], (EXTRA, a.shape[1]))
        out_ref[z, size : size + EXTRA, :] = small.astype(LOW)
        out_ref[z, size + EXTRA :, :] = b_ref[here, :]


def pair_last(got, kept, more, b, blocks, token):
    rows, width = b.shape
    own = slice(0, rows + EXTRA)
    (out,), token = call(
        pair_last_kernel,
        "pair_last",
        [whole(got), whole(kept), whole(more), whole(b)],
        [whole_out((blocks, 2 * rows // blocks + EXTRA, width), LOW)],
        token=token,
        far_in=(3,),
        part_in={0: (0,), 1: (0,), 2: (own,)},
        far_out=(0,),
        us=1,
        vmem=12,
    )
    return out, token


def down_last_kernel(
    at_ref, a_ref, a_keep_ref, b_ref, b_keep_ref, a2_ref, b2_ref, keep_ref, send_ref
):
    size, width = keep_ref.shape
    half = width // 2
    for out_ref, core in ((send_ref, 1 - at_ref[2]), (keep_ref, at_ref[2])):
        rows = pl.ds(pl.multiple_of(core * size, 16), size)
        there = pl.ds(pl.multiple_of((at_ref[1] * 2 + core) * size, 16), size)
        for first, refs in (
            (0, ((a_ref, rows), (a_keep_ref, rows), (a2_ref, rows))),
            (half, ((b_ref, there), (b_keep_ref, there), (b2_ref, rows))),
        ):
            total = sum(ref[cut, :].astype(FULL) for ref, cut in refs)
            out_ref[:, first : first + half] = total.astype(out_ref.dtype)


def down_last(at, parts, a2, b2, token):
    rows, half = a2.shape
    shape = (rows // 2, 2 * half)
    (keep, send), token = call(
        down_last_kernel,
        "down_last",
        [whole(array) for array in (*parts, a2, b2)],
        [whole_out(shape, FULL), whole_out(shape, LOW)],
        token=token,
        prefetch=(at,),
        us=3,
        far_out=(0, 1),
    )
    return keep, send, token


def in_last_kernel(
    at_ref, a_ref, a_keep_ref, b_ref, b_keep_ref, a2_ref, b2_ref, down_ref, keep_ref, send_ref
):
    size = keep_ref.shape[1]
    start = down_ref.shape[0]
    send_ref[pl.ds(0, start), pl.ds(0, down_ref.shape[1])] = down_ref[...]
    for mine, core in ((False, 1 - at_ref[2]), (True, at_ref[2])):
        rows = pl.ds(pl.multiple_of(core * size, 16), size)
        for part, refs in enumerate(((a_ref, a_keep_ref, a2_ref), (b_ref, b_keep_ref, b2_ref))):
            total = sum(ref[rows, :].astype(FULL) for ref in refs)
            if mine:
                keep_ref[part] = total
            else:
                send_ref[pl.ds(start + part * size, size), :] = total.astype(LOW)


def in_last(at, parts, a2, b2, down_send, token):
    rows, half = b2.shape
    (keep, send), token = call(
        in_last_kernel,
        "in_last",
        [whole(array) for array in (*parts, a2, b2, down_send)],
        [
            whole_out((2, rows // 2, half), FULL),
            whole_out((down_send.shape[0] + rows, half), LOW),
        ],
        token=token,
        prefetch=(at,),
        us=0.01,
        far_in=(4, 5, 6),
        part_in={at: (0,) for at in range(4)},
        far_out=(0, 1),
        vmem=16,
    )
    return keep, send, token


def finish_kernel(at_ref, in_ref, down_ref, got_ref, in_out, down_out, in_near, down_near, sems):
    _, size, half = in_ref.shape
    start, width = down_ref.shape
    for part in range(2):
        other = got_ref[pl.ds(start + part * size, size), :].astype(FULL)
        for first, value in ((at_ref[2], in_ref[part]), (1 - at_ref[2], other)):
            column = pl.multiple_of((part * 2 + first) * half, LANES)
            in_near[:, pl.ds(column, half)] = value
    copies = [pltpu.make_async_copy(in_near, in_out.at[0], sems.at[0])]
    copies[0].start()
    mine = at_ref[0] == at_ref[2]
    down_near[...] = jnp.where(mine, down_ref[...], got_ref[pl.ds(0, start), :width].astype(FULL))
    copies.append(pltpu.make_async_copy(down_near, down_out.at[0], sems.at[1]))
    copies[1].start()
    for copy in copies:
        copy.wait()


def finish(at, in_keep, down_keep, got, token):
    _, size, half = in_keep.shape
    in_shape, down_shape = (size, 4 * half), down_keep.shape
    outs, token = call(
        finish_kernel,
        "finish",
        [whole(in_keep), whole(down_keep), whole(got)],
        [((1, *in_shape), FULL, None), ((1, *down_shape), FULL, None)],
        token=token,
        prefetch=(at,),
        scratch=[
            pltpu.VMEM(in_shape, FULL),
            pltpu.VMEM(down_shape, FULL),
            pltpu.SemaphoreType.DMA((2,)),
        ],
        us=0.01,
        far_in=(0, 1),
        vmem=16,
    )
    return *outs, token


EXTRA = 16
TABLE_LANE = 32


def turn_kernel(at_ref, *refs):
    out_ref, turned = refs[-2:]
    start = 0
    for ref in refs[:-2]:
        turned[:, start : start + ref.shape[0]] = ref[...].T
        start += ref.shape[0]
    size = out_ref.shape[0] // 16
    for to in range(16):
        device = device_at(to % 4, to // 4, at_ref)
        out_ref[pl.ds(to * size, size), :] = turned[pl.ds(device * size, size), :]


def device_at(block, z, at_ref):
    return (
        (at_ref[0] ^ (block // 2)) * 16 + z * 4 + (at_ref[1] ^ (block % 2)) * 2 + at_ref[2]
    )


def turn(at, parts, token):
    count, width = sum(part.shape[0] for part in parts), parts[0].shape[1]
    (out,), token = call(
        turn_kernel,
        "turn",
        [whole(part) for part in parts],
        [whole_out((width // 2, count), LOW)],
        token=token,
        prefetch=(at,),
        scratch=[pltpu.VMEM((width, count), LOW)],
        us=2,
        far_out=(0,),
    )
    return out, token


def shared_kernel(
    at_ref, left_ref, own_ref, other_ref, *refs, experts
):
    out_refs, near_refs, sems = refs[:4], refs[4:8], refs[8]
    a_send_ref, a_keep_ref, b_send_ref, b_keep_ref = near_refs
    copies = []

    def leave(step, rows):
        for at, (near, out) in enumerate(zip(near_refs, out_refs)):
            if rows.start < near.shape[1]:
                part = pl.ds(rows.start, rows.stop - rows.start)
                copy = pltpu.make_async_copy(
                    near.at[:, part, :], out.at[:, part, :], sems.at[at, step]
                )
                copy.start()
                copies.append(copy)

    rows, count = left_ref.shape[0] // experts, left_ref.shape[1] // 2
    width = own_ref.shape[1]
    tokens = count // 3
    size = rows // 4
    small = own_ref[6 * tokens :, :LANES].astype(FULL) + other_ref[6 * tokens :, :LANES].astype(FULL)
    place = lax.broadcasted_iota(jnp.int32, small.shape, 0)
    for z in range(experts):
        left = left_ref[pl.ds(z * rows, rows), :]

        def product(columns, start, length):
            right = slice(start, start + length)
            one = left[:, columns : columns + length]
            two = left[:, count + columns : count + columns + length]
            total = dot_rows(one, own_ref[right, :]) + dot_rows(two, other_ref[right, :])
            return total.astype(LOW)

        a_terms = product(2 * tokens, 5 * tokens, tokens), product(tokens, 0, tokens)
        b_terms = product(0, tokens, 2 * tokens), product(0, 3 * tokens, 2 * tokens)
        for block in range(4):
            ry, rx = block // 2, block % 2
            a_ref = (a_send_ref if rx else a_keep_ref).at[ry]
            b_ref = (b_send_ref if ry else b_keep_ref).at[rx]
            here = slice(block * size, (block + 1) * size)
            for at in range(2):
                to = pl.ds((2 * z + at) * size, size)
                a_ref[to, :] = a_terms[at][here]
                b_ref[to, :] = b_terms[at][here]
        leave(z, slice(2 * z * size, 2 * (z + 1) * size))
    line = lax.broadcasted_iota(jnp.int32, (EXTRA, LANES), 0)
    for block in range(4):
        ry, rx = block // 2, block % 2
        a_ref = (a_send_ref if rx else a_keep_ref).at[ry]
        rows_here = jnp.zeros((EXTRA, LANES), FULL)
        for z in range(experts):
            row = jnp.where(place == device_at(block, z, at_ref), small, 0.0)
            rows_here = jnp.where(line == z, jnp.sum(row, 0, keepdims=True), rows_here)
        a_ref[2 * size * experts :, :] = jnp.zeros((EXTRA, width), LOW)
        a_ref[2 * size * experts :, :LANES] = rows_here.astype(LOW)
    leave(experts, slice(2 * size * experts, 2 * size * experts + EXTRA))
    for copy in copies:
        copy.wait()


def shared_terms(at, left, own, other, experts, token):
    rows = left.shape[0]
    width = own.shape[1]
    b_shape = (2, rows // 2, width)
    a_shape = (2, rows // 2 + EXTRA, width)
    return call(
        functools.partial(shared_kernel, experts=experts),
        "shared_terms",
        [whole(array) for array in (left, own, other)],
        [(shape, LOW, None) for shape in (a_shape, a_shape, b_shape, b_shape)],
        token=token,
        prefetch=(at,),
        scratch=[pltpu.VMEM(shape, LOW) for shape in (a_shape, a_shape, b_shape, b_shape)]
        + [pltpu.SemaphoreType.DMA((4, experts + 1))],
        us=0.01,
        vmem=16,
    )


def rows_kernel(
    place_ref, plane_ref, w_query_ref, w_key_ref, w_value_ref, gain_ref,
    query_ref, key_ref, value_ref, out_ref, gain_grad_ref, ffn_ref, table_ref,
    near_query, near_key, near_value, sems,
):
    rows = query_ref.shape[0]
    at = pl.ds(pl.multiple_of(place_ref[0] * rows, rows), rows)
    pairs = ((w_query_ref, near_query), (w_key_ref, near_key), (w_value_ref, near_value))
    copies = [
        pltpu.make_async_copy(ref.at[at, :], near, sems.at[number])
        for number, (ref, near) in enumerate(pairs)
    ]
    for copy in copies:
        copy.start()
    total = sum(plane_ref[block].astype(FULL) for block in range(plane_ref.shape[0]))
    out_ref[...] = total[:rows]
    query = total[rows : 2 * rows]
    key, value = (
        total[start + EXTRA : start + EXTRA + rows] for start in (2 * rows, 3 * rows)
    )
    query_ref[...] = query
    key_ref[...] = key
    value_ref[...] = value
    small = total[2 * rows : 2 * rows + 1, :LANES]
    ffn_ref[...] = small
    table_ref[...] = pltpu.roll(jnp.broadcast_to(small, (8, LANES)), LANES - TABLE_LANE, 1)[:1]
    for copy in copies:
        copy.wait()
    sums = query * near_query[...].astype(FULL) + key * near_key[...].astype(FULL)
    sums = jnp.sum(sums + value * near_value[...].astype(FULL), axis=1, keepdims=True)
    lane = lax.broadcasted_iota(jnp.int32, (rows, LANES), 1)
    line = lax.broadcasted_iota(jnp.int32, (rows, LANES), 0)
    spread = jnp.sum(jnp.where(lane == line, sums, 0.0), 0, keepdims=True)
    device = place_ref[0]
    block = gain_ref[pl.ds(device * rows // LANES, 1), :]
    gain = pltpu.roll(jnp.broadcast_to(block, (8, LANES)), LANES - device * rows % LANES, 1)[:1]
    gain_grad_ref[...] = spread / gain


def last_rows(place_all, plane, rows, weights, gain, token):
    width = plane.shape[2]
    small = whole_out((1, LANES), FULL)
    outs, token = call(
        rows_kernel,
        "last_rows",
        [whole(plane)] + [(array, None) for array in weights] + [whole(gain.reshape(-1, LANES))],
        [whole_out((rows, width), FULL)] * 4 + [small] * 3,
        token=token,
        prefetch=(place_all.reshape(1),),
        scratch=[pltpu.VMEM((rows, width), LOW)] * 3 + [pltpu.SemaphoreType.DMA((3,))],
        us=0.01,
    )
    return outs, token


def clip_kernel(query_ref, key_ref, peak_ref, level_ref, query_out, key_out, factor_ref):
    heads = peak_ref.shape[0]
    width = query_ref.shape[1]
    level = jnp.sum(jnp.where(eye(heads), level_ref[...], 0.0), 1, keepdims=True)
    factor = level / jnp.maximum(peak_ref[:, :1], level)
    factor_ref[...] = jnp.broadcast_to(factor, (heads, LANES))
    head = lax.broadcasted_iota(jnp.int32, (heads, width), 0)
    lane = lax.broadcasted_iota(jnp.int32, (heads, width), 1)
    scale = jnp.sum(jnp.where(lane // HDIM == head, jnp.sqrt(factor), 0.0), 0, keepdims=True)
    query_out[...] = query_ref[...].astype(FULL) * scale
    key_out[...] = key_ref[...].astype(FULL) * scale


def clip(w_query, w_key, peak, level, token):
    rows, width = w_query.shape
    spec = pl.BlockSpec((rows // 4, width), lambda i: (i, 0))
    outs, token = call(
        clip_kernel,
        "clip",
        [(w_query, spec), (w_key, spec), whole(peak), whole(level.reshape(1, -1))],
        [((rows, width), FULL, spec)] * 2 + [whole_out(peak.shape, FULL)],
        grid=(4,),
        token=token,
        us=0.01,
        vmem=16,
    )
    return outs, token


def normed_kernel(
    packed_ref, w_query_ref, w_key_ref, w_value_ref, own_ref, other_ref, near, sems
):
    copies = [
        pltpu.make_async_copy(ref, near.at[at], sems.at[at])
        for at, ref in enumerate((w_key_ref, w_value_ref, w_query_ref))
    ]
    for copy in copies:
        copy.start()
    tokens = own_ref.shape[0]
    dq, dk, dv = (
        packed_ref[pl.ds(start * tokens, size * tokens), :]
        for start, size in ((0, 1), (1, 2), (3, 2))
    )
    copies[0].wait()
    total = dot_back(dk, near[0])
    copies[1].wait()
    total = total + dot_back(dv, near[1])
    other_ref[...] = total[:tokens].astype(LOW)
    copies[2].wait()
    own_ref[...] = total[tokens:] + dot_back(dq, near[2])


def normed_grads(packed, weights, tokens, token):
    width = packed.shape[1]
    (own, other), token = call(
        normed_kernel,
        "normed_grads",
        [whole(packed)] + [(array, None) for array in weights],
        [whole_out((tokens, width), FULL), whole_out((tokens, width), LOW)],
        token=token,
        scratch=[pltpu.VMEM((3, width, width), LOW), pltpu.SemaphoreType.DMA((3,))],
        far_in=(0,),
        far_out=(0, 1),
        us=0.01,
        vmem=14,
    )
    return own, other, token


def input_kernel(rows_ref, gain_ref, own_ref, got_ref, past_ref, out_ref):
    rows = rows_ref[...].astype(FULL)
    inverse = lax.rsqrt(jnp.mean(rows * rows, axis=1, keepdims=True) + EPSILON)
    scaled = rows * inverse
    grad = (own_ref[...] + got_ref[...].astype(FULL)) * gain_ref[...]
    along = jnp.mean(scaled * grad, axis=1, keepdims=True)
    out_ref[0] = past_ref[...] + inverse * (grad - scaled * along)


def input_grads(rows, gain, own, got, past, token):
    tokens, width = rows.shape
    start = got.shape[0] - tokens
    (out,), token = call(
        input_kernel,
        "input_grads",
        [whole(array) for array in (rows, gain, own, got, past)],
        [whole_out((1, tokens, width), FULL)],
        token=token,
        far_in=(0, 1, 2, 4),
        part_in={3: (slice(start, start + tokens), slice(0, width))},
        far_out=(0,),
        us=0.01,
    )
    return out, token


def back_kernel(
    at_ref, spread_ref, rows_ref, after_ref, gain_ref, grad_ref, weights_ref,
    total_ref, branch_ref, attended_ref, gain_grad_ref,
):
    rows = after_ref[...]
    inverse = lax.rsqrt(jnp.mean(rows * rows, axis=1, keepdims=True) + EPSILON)
    scaled = rows * inverse
    blocks, size, _ = rows_ref.shape
    grad = sum(
        transpose_dot(spread_ref[pl.ds(k * size, size), :], rows_ref[lax.rem(at_ref[3] + k, blocks)])
        for k in range(blocks)
    )
    gain_grad_ref[...] = jnp.sum(scaled * grad, axis=0, keepdims=True)
    grad = grad * gain_ref[...]
    along = jnp.mean(scaled * grad, axis=1, keepdims=True)
    total = grad_ref[...].astype(FULL) + inverse * (grad - scaled * along)
    total_ref[...] = total
    branch = total.astype(LOW)
    branch_ref[...] = branch
    attended_ref[...] = dot_back(branch, weights_ref[...]).astype(LOW)


def back_to_attention(at, spread, rows, after, gain, grad, weights, fetch, token):
    shape = after.shape
    inputs = (spread, rows, after, gain, grad, weights)
    return call(
        back_kernel,
        "back",
        [whole(array) for array in inputs],
        [
            whole_out(shape, FULL),
            whole_out(shape, LOW),
            whole_out(shape, LOW),
            whole_out((1, shape[1]), FULL),
        ],
        token=token,
        vmem=16,
        us=0.01,
        far_in=(0, 2, 4, 5),
        prefetch=(at,),
        fetch=fetch,
    )


def mix_kernel(at_ref, pick_ref, rows_ref, gates_ref, after_ref, out_ref, peak_ref):
    top, tokens = gates_ref.shape
    blocks = rows_ref.shape[0]
    size = pick_ref.shape[0] // blocks
    total = after_ref[...]
    gates = [to_column(gates_ref[r : r + 1, :]) for r in range(top)]
    for block in range(blocks):
        rows = rows_ref[lax.rem(at_ref[3] + block, blocks), :size, :]
        for r in range(top):
            pick = pick_ref[pl.ds(block * size, size), pl.ds(r * tokens, tokens)]
            total = total + gates[r] * transpose_dot(pick, rows)
    out_ref[0] = total.astype(LOW)
    if rows_ref.shape[1] > size:
        peaks = [
            rows_ref[block, size:, :LANES].astype(FULL)
            + rows_ref[block, size:, LANES : 2 * LANES].astype(FULL)
            for block in range(blocks)
        ]
        peak_ref[...] = functools.reduce(jnp.maximum, peaks)


def mix(at, pick, rows, gates, after, token):
    (out, peak), token = call(
        mix_kernel,
        "mix",
        [whole(pick), whole(rows), whole(gates), whole(after)],
        [whole_out((1, *after.shape), LOW), whole_out((16, LANES), FULL)],
        token=token,
        us=0.01,
        far_in=(0, 3),
        prefetch=(at,),
    )
    return out, peak, token


def local(
    block_in,
    seg_ids,
    routes,
    gates,
    buckets,
    norm_attn,
    norm_ffn,
    w_query,
    w_key,
    w_value,
    w_out_attn,
    rel_bias,
    clip_level,
    w_in,
    w_down,
    cotangent,
):
    tokens, width = block_in.shape[1:]
    heads = width // HDIM
    n_ctx, experts, n_dp = (lax.axis_size(axis) for axis in ("ctx", "exp", "dp"))
    fast = (n_ctx, experts, n_dp) == (2, 4, 4)
    devices = n_ctx * experts * n_dp
    length = n_ctx * tokens
    y, z, x, core = place()
    place_all = (y * experts + z) * n_dp + lax.axis_index("dp")
    top_count = routes.shape[-1]
    capacity = tokens * top_count * 3 // (2 * experts)
    at = jnp.stack([y, x, core, z])

    (spread, pick, mask, rows_copy, *grad_out), token = front(
        at, routes[0].T, gates[0].T, cotangent[0], seg_ids, block_in[0], experts, capacity
    )
    backs = list(range(n_ctx - 1, 0, -1))
    earlier = [
        lax.ppermute(block_in[0], "ctx", [(i, (i + back) % n_ctx) for i in range(n_ctx)])
        for back in backs
    ]
    grad_blocks = to_experts(grad_out)
    (bucket_hot, bias, w_key_near, w_value_near), _ = bias_tiles(
        buckets.reshape(1, length), rel_bias.reshape(NB, heads), tokens, (w_key, w_value)
    )

    own_rows = block_in[0].astype(FULL)
    normed_own = rms_norm(own_rows, norm_attn).astype(LOW)
    normed_all = jnp.concatenate(
        [rms_norm(rows.astype(FULL), norm_attn).astype(LOW) for rows in earlier] + [normed_own],
        axis=0,
    )
    queries = dot_rows(normed_own, w_query).astype(LOW)
    keys = dot_rows(normed_all, w_key_near).astype(LOW)
    values = dot_rows(normed_all, w_value_near).astype(LOW)
    attended, probs, peak_lanes, w_out_near = attention(
        queries, keys, values, bias, mask, (w_out_attn,)
    )
    after, sent = after_attention(
        attended, w_out_near, rows_copy, norm_ffn.reshape(1, width), spread, experts
    )

    row_blocks = to_experts(sent)
    own_gain, own_table = width // devices, NB * heads // devices
    if fast:
        expert_grad, token = side_by_side(grad_blocks, token)
        parts = (normed_all, attended)
        parts = parts + tuple(swapped(part, "dp", 1) for part in parts)
        left, token = turn(at, parts, token)
        peak, token = larger(peak_lanes, swapped(peak_lanes, "dp", 1), token)
        peak, token = larger(peak, swapped(peak, "dp", 2), token)
        peak, token = larger(peak, swapped(peak, "ctx", 1), token)
        expert_rows, token = side_by_side(row_blocks, token)
        both_rows = expert_rows, swapped(expert_rows, "dp", 1)
        both_grads = expert_grad, swapped(expert_grad, "dp", 1)
        outs, token = expert_halves(at, both_rows, both_grads, w_in, w_down, token)
        back_keep, back_send, dgate, dup, rows_turned, hid, *down = outs
        back_got = swapped(back_send, "dp", 1)
        down = swapped(down[0], "dp", 2), down[1], to_down_plane(down[2]), down[2]
        back_rows, token = join(at, back_keep, back_got, experts, token)
        back_home = over_experts(back_rows)
        first, token = in_terms(at, rows_turned, dgate, dup, token)
        first = plane_first(first)
        down_a, down_b, token = down_second(at, down, token, 5)
        out_keep, out_send, token = expert_results(at, hid, w_down, token)
    else:
        expert_rows = jnp.concatenate(row_blocks, axis=0)
        expert_grad = jnp.concatenate(grad_blocks, axis=0)
        (out_rows, back_rows, dgate, dup, hid_turned, rows_turned), token = expert(
            expert_rows, expert_grad, w_in, w_down, token
        )
        expert_first, expert_second = (
            lax.psum_scatter(grads, ("ctx", "dp"), scatter_dimension=0, tiled=True)[None]
            for grads in (
                dot_rows(rows_turned, jnp.concatenate([dgate, dup], axis=1)),
                dot_rows(hid_turned, expert_grad),
            )
        )
        back_home, out_home = (
            jnp.stack(from_experts(list(rows.reshape(experts, capacity, width))))
            for rows in (back_rows, out_rows)
        )

    home = at if fast else jnp.zeros_like(at)
    soon = (queries, keys, values, probs) + ((bucket_hot,) if fast else ())
    (grad_after, grad_branch, grad_attended, grad_gain_ffn, *soon), token = back_to_attention(
        home, spread, back_home, after, norm_ffn.reshape(1, width), cotangent[0], w_out_attn, soon, token
    )
    if fast:
        packed, token = attention_back(
            *soon[:4], grad_attended, token, (grad_branch, soon[4], grad_gain_ffn, devices),
        )
        packed_got = swapped(packed, "dp", 1)
        (left,), token = bring(token, 20, left)
        plane_2, token = shared_terms(at, left, packed, packed_got, experts, token)
        plane_2 = plane_first(plane_2)
        out_send, = hold(token, out_send)
        out_got = swapped(out_send, "dp", 1)
        out_rows, token = join_peak(at, out_keep, out_got, peak, experts, token)
        out_home = over_experts(out_rows)
        normed_own_grad, normed_other_grad, token = normed_grads(
            packed, (w_query, w_key, w_value), tokens, token
        )
        in_a, in_b, token = plane_second(first, token, 0.01)
    else:
        dq, dk, dv, lines, token = attention_back(
            *soon, grad_attended, token
        )
        lines = lines[:, :GROUP, :].reshape(heads, length + tokens)
        grad_table = lax.dot_general(
            bucket_hot, lines, (((1,), (1,)), ((), ())), precision=FULL_PRECISION
        ).reshape(-1)
        mixed, _, _ = mix(home, pick, out_home, gates[0].T, after, token)
        peak = jnp.max(peak_lanes[:, :GROUP, :], axis=-1).reshape(heads)
        peak = lax.pmax(peak, ("ctx", "exp", "dp"))
        peak = jnp.broadcast_to(peak[:, None], (heads, LANES))
        clipped, _ = clip(w_query, w_key, peak, clip_level, token)

        grad_normed = dot_back(dk, w_key) + dot_back(dv, w_value)
        grad_normed_own = grad_normed[length - tokens :] + dot_back(dq, w_query)
        for block, back in enumerate(backs):
            term = grad_normed[block * tokens : (block + 1) * tokens].astype(LOW)
            returned = lax.ppermute(term, "ctx", [((i + back) % n_ctx, i) for i in range(n_ctx)])
            grad_normed_own = grad_normed_own + returned.astype(FULL)
        _, norm_pull = jax.vjp(lambda rows: rms_norm(rows, norm_attn), own_rows)
        grad_input = (grad_after + norm_pull(grad_normed_own)[0])[None]

    if fast:
        shared_a, shared_b, token = plane_second(plane_2, token, 8, (normed_other_grad,))
        shared_a, shared_b = swapped(shared_a, "ctx", 1), swapped(shared_b, "dp", 2)
        down_a, down_b = hold(token, down_a, down_b)
        down_a, down_b = to_down_plane(down_a), in_down_plane(down_b)
        mixed, peak, token = mix(at, pick, out_home, gates[0].T, after, token)
        half_b, token = plane_sum(plane_2[2], plane_2[3], shared_b, token)
        in_a, in_b = hold(token, in_a, in_b)
        in_a, in_b = swapped(in_a, "ctx", 1), swapped(in_b, "dp", 2)
        plane, token = pair_last(plane_2[0], plane_2[1], shared_a, half_b, experts, token)
        plane = over_experts(plane)
        clipped, token = clip(w_query, w_key, peak, clip_level, token)
        down_keep, down_send, token = down_last(at, down, down_a, down_b, token)
        grad_input, token = input_grads(
            block_in[0], norm_attn.reshape(1, width), normed_own_grad, shared_a, grad_after, token
        )
        in_keep, last_send, token = in_last(at, first, in_a, in_b, down_send, token)
        last_got = swapped(last_send, "dp", 1)
        expert_first, expert_second, token = finish(at, in_keep, down_keep, last_got, token)
        outs, token = last_rows(
            place_all, plane, own_gain, (w_query, w_key, w_value), norm_attn, token
        )
        shared_q, shared_k, shared_v, shared_o = outs[:4]
        small_attn, small_ffn = outs[4][0, :own_gain], outs[5][0, :own_gain]
        small_table = outs[6][0, :own_table]
    else:
        shared_q, shared_k, shared_v, shared_o = (
            lax.psum_scatter(grads, ("ctx", "exp", "dp"), scatter_dimension=0, tiled=True)
            for grads in (
                transpose_dot(normed_own, dq),
                transpose_dot(normed_all, dk),
                transpose_dot(normed_all, dv),
                transpose_dot(attended, grad_branch),
            )
        )
        small_ffn, small_table = (
            lax.dynamic_slice_in_dim(lax.psum(array, ("ctx", "exp", "dp")), place_all * own, own)
            for array, own in ((grad_gain_ffn[0], own_gain), (grad_table, own_table))
        )
        pairs = ((shared_q, w_query), (shared_k, w_key), (shared_v, w_value))
        row_sums = sum(
            jnp.sum(
                grads * lax.dynamic_slice_in_dim(weights, place_all * own_gain, own_gain).astype(FULL),
                axis=1,
            )
            for grads, weights in pairs
        )
        small_attn = row_sums / lax.dynamic_slice_in_dim(norm_attn, place_all * own_gain, own_gain)

    return (
        mixed,
        grad_input,
        small_attn,
        small_ffn,
        shared_q,
        shared_k,
        shared_v,
        shared_o,
        small_table,
        expert_first,
        expert_second,
        clipped[0],
        clipped[1],
        clipped[2][:, 0],
    )


def solution(mesh):
    tokens = P(("exp", "dp"), "ctx", None)
    everywhere = P(("ctx", "exp", "dp"))
    by_rows = P(("ctx", "exp", "dp"), None)
    by_expert = P("exp", None, None)
    expert_rows = P("exp", ("ctx", "dp"), None)
    in_specs = (tokens, P(("exp", "dp"), None), tokens, tokens) + (P(),) * 9
    in_specs = in_specs + (by_expert, by_expert, tokens)
    out_specs = (tokens, tokens, everywhere, everywhere) + (by_rows,) * 4
    out_specs = out_specs + (everywhere, expert_rows, expert_rows, P(), P(), P())
    return jax.shard_map(local, mesh=mesh, in_specs=in_specs, out_specs=out_specs, check_vma=False)
```

```python
import functools

import jax
import jax.numpy as jnp
from jax import lax
from jax.experimental import pallas as pl
from jax.experimental.pallas import tpu as pltpu
from jax.sharding import PartitionSpec as P

HDIM = 64
NB = 32
GROUP = 4
LANES = 128
EPSILON = 1e-06
FULL_PRECISION = lax.Precision.HIGHEST
LOW = jnp.bfloat16
FULL = jnp.float32
OUTSIDE = -1e30
GELU_SCALE = 0.7978845608028654
GELU_CUBE = 0.044715


def rms_norm(rows, gain):
    return rows * lax.rsqrt(jnp.mean(rows * rows, axis=-1, keepdims=True) + EPSILON) * gain


def dot_rows(left, right):
    return lax.dot_general(left, right, (((1,), (0,)), ((), ())), preferred_element_type=FULL)


def dot_back(left, right):
    return lax.dot_general(left, right, (((1,), (1,)), ((), ())), preferred_element_type=FULL)


def transpose_dot(left, right):
    return lax.dot_general(left, right, (((0,), (0,)), ((), ())), preferred_element_type=FULL)


def swapped(array, axis, bit):
    size = lax.axis_size(axis)
    return lax.ppermute(array, axis, [(i, i ^ bit) for i in range(size)])


def shifted(array, axis, shift):
    size = lax.axis_size(axis)
    return lax.ppermute(array, axis, [(i, (i + shift) % size) for i in range(size)])


def to_experts(blocks):
    return [blocks[0]] + [shifted(blocks[k], "exp", k) for k in range(1, len(blocks))]


def from_experts(blocks):
    return [blocks[0]] + [shifted(blocks[k], "exp", len(blocks) - k) for k in range(1, len(blocks))]


def over_experts(blocks):
    return lax.all_to_all(blocks, "exp", split_axis=0, concat_axis=0, tiled=True)


MICROSECOND = 1.15e9


def call(
    body, name, inputs, outputs, us, grid=None, token=None, prefetch=(), scratch=(), vmem=6,
    near_in=(), near_out=(), far_in=(), far_out=(), fetch=(),
    part_in=None,
):
    part_in = dict(part_in or {})
    far_in = tuple(far_in) + tuple(part_in)
    inputs = list(inputs) + [(array, None) for array in fetch]
    outputs = list(outputs) + [whole_out(array.shape, array.dtype) for array in fetch]
    n_pre, n_in, n_out = len(prefetch), len(inputs), len(outputs)
    held = [] if token is None else [token]
    n_far, n_scratch = len(far_in) + len(far_out), len(scratch)

    def kernel(*refs):
        split = n_pre + n_in
        outs = split + len(held)
        rest = refs[outs + n_out + 1 :]
        ins_here, outs_here = list(refs[:split]), list(refs[outs : outs + n_out])
        copies = []
        for number, at in enumerate(far_in):
            here = rest[n_scratch + number]
            source = refs[n_pre + at].at[part_in[at]] if at in part_in else refs[n_pre + at]
            copies.append(pltpu.make_async_copy(source, here, rest[-1].at[number]))
            ins_here[n_pre + at] = here
        for copy in copies:
            copy.start()
        fetches = [
            pltpu.make_async_copy(ins_here.pop(), outs_here.pop(), rest[-1].at[n_far + number])
            for number in range(len(fetch))
        ]
        for copy in fetches:
            copy.start()
        for copy in copies:
            copy.wait()
        copies = []
        for number, at in enumerate(far_out, len(far_in)):
            here = rest[n_scratch + number]
            copies.append(pltpu.make_async_copy(here, refs[outs + at], rest[-1].at[number]))
            outs_here[at] = here
        body(*ins_here, *outs_here, *rest[:n_scratch])
        for copy in fetches:
            copy.wait()
        for copy in copies:
            copy.start()
        for copy in copies:
            copy.wait()

    where = lambda at, near: pltpu.VMEM if at in near else pltpu.HBM
    arrays = [array for array, _ in inputs]
    shapes = [(shape, dtype) for shape, dtype, _ in outputs]
    anywhere = pl.BlockSpec(memory_space=pl.ANY)
    if grid is None:
        near = pl.BlockSpec(memory_space=pltpu.VMEM)
        far = [at in far_in or spec is None for at, (_, spec) in enumerate(inputs)]
        far_results = [at in far_out or spec is None for at, (_, _, spec) in enumerate(outputs)]
        left = lambda at: tuple(
            size if axis >= len(part_in.get(at, ())) else len(range(size)[part_in[at][axis]])
            for axis, size in enumerate(arrays[at].shape)
            if axis >= len(part_in.get(at, ())) or isinstance(part_in[at][axis], slice)
        )
        buffers = [pltpu.VMEM(left(at), arrays[at].dtype) for at in far_in]
        buffers += [pltpu.VMEM(*shapes[at]) for at in far_out]
        n_sems = n_far + len(fetch)
        buffers += [pltpu.SemaphoreType.DMA((n_sems,))] if n_sems else []
        form = dict(
            in_specs=[pl.BlockSpec(memory_space=pltpu.SMEM)] * n_pre
            + [anywhere if away else near for away in far]
            + [anywhere] * len(held),
            out_specs=[anywhere if away else near for away in far_results] + [anywhere],
            scratch_shapes=list(scratch) + buffers,
        )
        arrays = [
            pltpu.with_memory_space_constraint(array, pltpu.HBM) if away else array
            for array, away in zip(arrays, far)
        ]
        shapes = [
            pltpu.HBM(*one) if away else jax.ShapeDtypeStruct(*one)
            for away, one in zip(far_results, shapes)
        ]
    else:
        form = dict(
            grid_spec=pltpu.PrefetchScalarGridSpec(
                num_scalar_prefetch=n_pre,
                grid=grid,
                in_specs=[spec for _, spec in inputs] + [anywhere] * len(held),
                out_specs=[spec for _, _, spec in outputs] + [anywhere],
                scratch_shapes=list(scratch),
            )
        )
        arrays = [
            pltpu.with_memory_space_constraint(array, where(at, near_in))
            for at, array in enumerate(arrays)
        ]
        shapes = [where(at, near_out)(*one) for at, one in enumerate(shapes)]
    held = [pltpu.with_memory_space_constraint(array, pltpu.HBM) for array in held]
    results = pl.pallas_call(
        kernel,
        out_shape=shapes + [pltpu.HBM((8, LANES), FULL)],
        cost_estimate=pl.CostEstimate(
            flops=int(us * MICROSECOND), bytes_accessed=1, transcendentals=0
        ),
        compiler_params=pltpu.CompilerParams(vmem_limit_bytes=vmem * 2**20),
        name=name,
        **form,
    )(*prefetch, *arrays, *held)
    return list(results[:-1]), results[-1]


def whole(array):
    return array, pl.BlockSpec(array.shape, lambda *_: (0,) * array.ndim)


def whole_out(shape, dtype):
    return shape, dtype, pl.BlockSpec(shape, lambda *_: (0,) * len(shape))


def hold(token, *arrays):
    anywhere = pl.BlockSpec(memory_space=pl.ANY)
    return pl.pallas_call(
        lambda *refs: None,
        in_specs=[anywhere] * (len(arrays) + 1),
        out_specs=[anywhere] * len(arrays),
        out_shape=[jax.ShapeDtypeStruct(array.shape, array.dtype) for array in arrays],
        input_output_aliases={at + 1: at for at in range(len(arrays))},
        cost_estimate=pl.CostEstimate(flops=1, bytes_accessed=1, transcendentals=0),
        name="hold",
    )(token, *arrays)


def pass_kernel(*refs):
    half = len(refs) // 2
    for ref, out_ref in zip(refs[:half], refs[half:]):
        out_ref[...] = ref[...]


def bring(token, us, *arrays):
    return call(lambda *refs: None, "bring", [], [], token=token, fetch=arrays, us=us)


def pass_on(token, *arrays):
    return call(
        pass_kernel,
        "pass_on",
        [whole(array) for array in arrays],
        [whole_out(array.shape, array.dtype) for array in arrays],
        token=token,
        us=1,
    )


def eye(size):
    rows = lax.broadcasted_iota(jnp.int32, (size, size), 0)
    return rows == lax.broadcasted_iota(jnp.int32, (size, size), 1)


def to_column(row):
    size = row.shape[1]
    return jnp.sum(jnp.where(eye(size), row, jnp.zeros_like(row)), 1, keepdims=True)


def front_kernel(
    at_ref, routes_ref, gates_ref, grad_ref, seg_ref, rows_ref,
    spread_ref, pick_ref, mask_ref, copy_ref, *out_refs,
):
    top, tokens = routes_ref.shape
    experts, capacity = len(out_refs), out_refs[0].shape[0]
    routes = [routes_ref[r : r + 1, :] for r in range(top)]
    gates = [gates_ref[r : r + 1, :] for r in range(top)]
    before = lax.broadcasted_iota(jnp.int32, (tokens, tokens), 0)
    before = before < lax.broadcasted_iota(jnp.int32, (tokens, tokens), 1)
    slots = lax.broadcasted_iota(jnp.int32, (capacity, tokens), 0).astype(FULL)
    for e in range(experts):
        part = pl.ds(e * capacity, capacity)
        name = lax.rem(at_ref[3] + e, experts)
        hits = [jnp.where(route == name, 1.0, 0.0) for route in routes]
        named = functools.reduce(jnp.add, hits)
        slot = jnp.sum(jnp.where(before, to_column(named), 0.0), 0, keepdims=True)
        place = (slots == slot).astype(FULL)
        spread = place * named
        gate = functools.reduce(jnp.add, [hit * g for hit, g in zip(hits, gates)])
        spread_low = spread.astype(LOW)
        spread_ref[part, :] = spread_low
        for r in range(top):
            pick_ref[part, pl.ds(r * tokens, tokens)] = (place * hits[r]).astype(LOW)
        slot_gate = jnp.sum(spread * gate, 1, keepdims=True)
        out_refs[e][...] = (slot_gate * dot_rows(spread_low, grad_ref[...])).astype(LOW)
    length = mask_ref.shape[1]
    ctx = at_ref[0]
    seg = jnp.broadcast_to(seg_ref[...].astype(FULL), (8, length))
    keys = pltpu.roll(seg, length - (ctx + 1) * tokens, 1)[:1, :]
    at_row = lax.broadcasted_iota(jnp.int32, (tokens, length), 0) + (length - tokens)
    at_key = lax.broadcasted_iota(jnp.int32, (tokens, length), 1)
    own = jnp.sum(jnp.where(at_row == at_key, keys, 0.0), 1, keepdims=True)
    allowed = (at_key <= at_row) & (own == keys) & (at_key >= length - (ctx + 1) * tokens)
    mask_ref[...] = jnp.where(allowed, 0.0, OUTSIDE)
    copy_ref[...] = rows_ref[...]


def front(at, routes, gates, grad, seg, rows, experts, capacity):
    top, tokens = routes.shape
    slots = experts * capacity
    return call(
        front_kernel,
        "front",
        [whole(array) for array in (routes, gates, grad, seg, rows)],
        [
            whole_out((slots, tokens), LOW),
            whole_out((slots, top * tokens), LOW),
            whole_out((tokens, seg.shape[1]), FULL),
            whole_out(rows.shape, LOW),
        ]
        + [whole_out((capacity, grad.shape[1]), LOW)] * experts,
        prefetch=(at,),
        far_in=(0, 1, 2, 3, 4),
        far_out=(1,),
        us=1.5,
    )


def bias_kernel(buckets_ref, table_ref, hot_ref, bias_ref):
    heads, rows, keys = bias_ref.shape
    width = hot_ref.shape[1]
    buckets = buckets_ref[...].astype(FULL)
    column = jnp.sum(jnp.where(eye(keys), buckets, 0.0), 1, keepdims=True)
    distance = lax.broadcasted_iota(jnp.int32, (keys, width), 0)
    lane = lax.broadcasted_iota(jnp.int32, (keys, width), 1)
    turned = jnp.sum(jnp.where(distance + lane == keys - 1, column, 0.0), 0, keepdims=True)
    bucket = lax.broadcasted_iota(jnp.int32, (NB, width), 0).astype(FULL)
    hot = jnp.where(bucket == turned, 1.0, 0.0)
    hot_ref[...] = hot
    by_lane = lax.dot_general(
        table_ref[...], hot, (((0,), (0,)), ((), ())), precision=FULL_PRECISION,
        preferred_element_type=FULL,
    )
    for head in range(heads):
        line = jnp.broadcast_to(by_lane[head : head + 1, :], (8, width))
        line = pltpu.roll(line, keys + 1, 1, stride=1, stride_axis=0)
        for start in range(0, rows, 8):
            moved = line if start == 0 else pltpu.roll(line, start, 1)
            bias_ref[head, pl.ds(start, 8), :] = moved[:, :keys]


def bias_tiles(buckets, table, rows, fetch):
    heads, keys = table.shape[1], buckets.shape[1]
    return call(
        bias_kernel,
        "bias_tiles",
        [whole(buckets), whole(table)],
        [whole_out((NB, keys + rows), FULL), whole_out((heads, rows, keys), FULL)],
        us=2.5,
        vmem=16,
        fetch=fetch,
    )


def half_lanes(half, shape):
    lane = lax.broadcasted_iota(jnp.int32, shape, 1)
    return lane < HDIM if half == 0 else lane >= HDIM


def attention_kernel(q_ref, k_ref, v_ref, bias_ref, mask_ref, out_ref, probs_ref, peak_ref):
    groups = peak_ref.shape[0]

    def group(step, _):
        mask = mask_ref[...]
        for pair in range(GROUP // 2):
            lanes = pair_lanes(step, pair)
            queries, keys, values = q_ref[:, lanes], k_ref[:, lanes], v_ref[:, lanes]
            parts = []
            for half in range(2):
                at = 2 * pair + half
                own = half_lanes(half, queries.shape)
                raw = dot_back(jnp.where(own, queries, jnp.zeros_like(queries)), keys)
                raw = raw * HDIM**-0.5 + mask
                top = jnp.max(raw, axis=0, keepdims=True)
                best = top[:, :LANES]
                for start in range(LANES, top.shape[1], LANES):
                    best = jnp.maximum(best, top[:, start : start + LANES])
                peak_ref[step, at : at + 1, :] = best
                scores = raw + bias_ref[step * GROUP + at]
                raised = jnp.exp(scores - jnp.max(scores, axis=1, keepdims=True))
                probs = raised * (1.0 / jnp.sum(raised, axis=1, keepdims=True))
                probs_low = probs.astype(LOW)
                probs_ref[step * GROUP + at] = probs_low
                parts.append(dot_rows(probs_low, values))
            first = half_lanes(0, parts[0].shape)
            out_ref[:, lanes] = jnp.where(first, parts[0], parts[1]).astype(LOW)
        return 0

    lax.fori_loop(0, groups, group, 0)


def pair_lanes(step, pair):
    return pl.ds(pl.multiple_of(step * GROUP * HDIM + pair * LANES, LANES), LANES)


def attention(queries, keys, values, bias, mask, fetch):
    rows, width = queries.shape
    length = keys.shape[0]
    heads = width // HDIM
    (out, probs, peak, *fetched), _ = call(
        attention_kernel,
        "attention",
        [whole(array) for array in (queries, keys, values, bias, mask)],
        [
            whole_out((rows, width), LOW),
            whole_out((heads, rows, length), LOW),
            whole_out((heads // GROUP, 8, LANES), FULL),
        ],
        us=4.5,
        vmem=10,
        far_out=(1,),
        fetch=fetch,
    )
    return out, probs, peak, *fetched


def attention_back_kernel(
    q_ref, k_ref, v_ref, probs_ref, grad_ref, dq_ref, dk_ref, dv_ref, lines_ref
):
    groups = lines_ref.shape[0]
    rows, length = probs_ref.shape[1:]
    scale = HDIM**-0.5

    def group(step, _):
        for pair in range(GROUP // 2):
            lanes = pair_lanes(step, pair)
            queries, keys, values, grad = (
                ref[:, lanes] for ref in (q_ref, k_ref, v_ref, grad_ref)
            )
            dq, dk, dv = [], [], []
            for half in range(2):
                at = 2 * pair + half
                own = half_lanes(half, grad.shape)
                dp = dot_back(jnp.where(own, grad, jnp.zeros_like(grad)), values)
                probs_low = probs_ref[step * GROUP + at]
                probs = probs_low.astype(FULL)
                ds = probs * (dp - jnp.sum(probs * dp, axis=1, keepdims=True))
                ds_low = ds.astype(LOW)
                dq.append(dot_rows(ds_low, keys))
                dk.append(transpose_dot(ds_low, queries))
                dv.append(transpose_dot(probs_low, grad))
                wide = jnp.concatenate([ds, jnp.zeros((rows, rows), FULL)], axis=1)
                total = wide[rows - 8 :, :]
                for start in range(0, rows - 8, 8):
                    total = total + pltpu.roll(wide[start : start + 8, :], rows - 8 - start, 1)
                line = lax.broadcasted_iota(jnp.int32, total.shape, 0)
                for bit in (1, 2, 4):
                    total = jnp.where(((7 - line) & bit) != 0, pltpu.roll(total, bit, 1), total)
                lines_ref[step, at : at + 1, :] = jnp.sum(total, axis=0, keepdims=True)
            first = half_lanes(0, dq[0].shape)
            dq_ref[:, lanes] = (jnp.where(first, dq[0], dq[1]) * scale).astype(LOW)
            first = half_lanes(0, dk[0].shape)
            dk_ref[:, lanes] = (jnp.where(first, dk[0], dk[1]) * scale).astype(LOW)
            dv_ref[:, lanes] = jnp.where(first, dv[0], dv[1]).astype(LOW)
        return 0

    lax.fori_loop(0, groups, group, 0)


def packed_back_kernel(
    q_ref, k_ref, v_ref, probs_ref, grad_ref, branch_ref, hot_ref, gain_ref, out_ref, lines_ref
):
    rows, length = probs_ref.shape[1:]
    ends = [0, rows, rows + length, rows + 2 * length, 2 * rows + 2 * length]
    parts = [out_ref.at[pl.ds(a, b - a), :] for a, b in zip(ends, ends[1:])]
    attention_back_kernel(q_ref, k_ref, v_ref, probs_ref, grad_ref, *parts[:3], lines_ref)
    parts[3][...] = branch_ref[...]
    groups = lines_ref.shape[0]
    width = gain_ref.shape[1]
    devices = out_ref.shape[0] - ends[4]
    own, turns = width // devices, LANES * devices // width
    device = lax.broadcasted_iota(jnp.int32, (devices, width), 0)
    feature = lax.broadcasted_iota(jnp.int32, (devices, width), 1)
    spread = jnp.where(feature // own == device, gain_ref[...], 0.0)
    folded = functools.reduce(
        jnp.add, [spread[:, start : start + LANES] for start in range(0, width, LANES)]
    )
    device = lax.broadcasted_iota(jnp.int32, folded.shape, 0)
    small = folded
    for turn_by in range(1, turns):
        moved = pltpu.roll(folded, LANES - turn_by * own, 1)
        small = jnp.where(device % turns == turn_by, moved, small)
    lines = jnp.concatenate([lines_ref[g, :GROUP, :] for g in range(groups)], axis=0)
    blank = jnp.zeros((LANES - TABLE_LANE - lines.shape[0], lines.shape[1]), FULL)
    lines = jnp.concatenate([jnp.zeros((TABLE_LANE, lines.shape[1]), FULL), lines, blank], axis=0)
    upper = lines.astype(LOW)
    lower = (lines - upper.astype(FULL)).astype(LOW)
    hot = hot_ref[...].astype(LOW)
    small = small + dot_back(hot, upper) + dot_back(hot, lower)
    out_ref[pl.ds(ends[4], devices), :LANES] = small.astype(LOW)


def attention_back(queries, keys, values, probs, grad, token, packed=None):
    rows, width = queries.shape
    length = keys.shape[0]
    heads = width // HDIM
    lines = whole_out((heads // GROUP, 8, length + rows), FULL)
    inputs = [whole(array) for array in (queries, keys, values, probs, grad)]
    if packed is None:
        outs, token = call(
            attention_back_kernel,
            "attention_back",
            inputs,
            [whole_out((size, width), LOW) for size in (rows, length, length)] + [lines],
            token=token,
            us=6.6,
            vmem=16,
        )
        return *outs, token
    branch, hot, gain, devices = packed
    (out, _), token = call(
        packed_back_kernel,
        "attention_back",
        inputs + [whole(branch), whole(hot), whole(gain)],
        [whole_out((2 * rows + 2 * length + devices, width), LOW), lines],
        token=token,
        us=7,
        vmem=16,
    )
    return out, token


def post_kernel(attended_ref, weights_ref, rows_ref, gain_ref, spread_ref, after_ref, *out_refs):
    after = rows_ref[...].astype(FULL) + dot_rows(attended_ref[...], weights_ref[...])
    after_ref[...] = after
    sent = rms_norm(after, gain_ref[...]).astype(LOW)
    size = out_refs[0].shape[0]
    for at, out_ref in enumerate(out_refs):
        out_ref[...] = dot_rows(spread_ref[pl.ds(at * size, size), :], sent).astype(LOW)


def after_attention(attended, weights, rows, gain, spread, experts):
    tokens, width = rows.shape
    (after, *sent), _ = call(
        post_kernel,
        "post",
        [whole(array) for array in (attended, weights, rows, gain, spread)],
        [whole_out((tokens, width), FULL)]
        + [whole_out((spread.shape[0] // experts, width), LOW)] * experts,
        far_out=(0,),
        us=2,
    )
    return after, sent


def gather_kernel(*refs):
    size = refs[0].shape[0]
    for at, ref in enumerate(refs[:-1]):
        refs[-1][pl.ds(at * size, size), :] = ref[...]


def side_by_side(blocks, token):
    size, width = blocks[0].shape
    (out,), token = call(
        gather_kernel,
        "gather",
        [whole(block) for block in blocks],
        [whole_out((len(blocks) * size, width), LOW)],
        token=token,
        us=1,
    )
    return out, token


def expert_part(gate, up, dhid):
    square = gate * gate
    curve = jnp.tanh(GELU_SCALE * gate * (1.0 + GELU_CUBE * square))
    upper = 0.5 * (1.0 + curve)
    gelu = gate * upper
    slope = upper + 0.5 * gate * (1.0 - curve * curve) * (
        GELU_SCALE * (1.0 + 3.0 * GELU_CUBE * square)
    )
    hid = (gelu * up).astype(LOW)
    dgate = (dhid * up * slope).astype(LOW)
    dup = (dhid * gelu).astype(LOW)
    return hid, dgate, dup


def expert_kernel(
    rows_ref, grad_ref, gate_w_ref, up_w_ref, down_w_ref,
    out_ref, back_ref, dgate_ref, dup_ref, hid_ref, turned_ref, out_sum, back_sum,
):
    step = pl.program_id(0)

    @pl.when(step == 0)
    def _():
        out_sum[...] = jnp.zeros_like(out_sum)
        back_sum[...] = jnp.zeros_like(back_sum)

    rows, grad = rows_ref[...], grad_ref[...]
    gate_w, up_w, down_w = gate_w_ref[0], up_w_ref[0], down_w_ref[0]
    hid, dgate, dup = expert_part(
        dot_rows(rows, gate_w), dot_rows(rows, up_w), dot_back(grad, down_w)
    )
    dgate_ref[...] = dgate
    dup_ref[...] = dup
    hid_ref[...] = hid.T
    out_sum[...] += dot_rows(hid, down_w)
    back_sum[...] += dot_back(dgate, gate_w) + dot_back(dup, up_w)

    @pl.when(step == pl.num_programs(0) - 1)
    def _():
        out_ref[...] = out_sum[...].astype(LOW)
        back_ref[...] = back_sum[...].astype(LOW)
        turned_ref[...] = rows_ref[...].T


def expert(rows, grad, w_in, w_down, token):
    count, width = rows.shape
    hidden = w_down.shape[1]
    part = 256
    steps = hidden // part
    return call(
        expert_kernel,
        "expert",
        [
            whole(rows),
            whole(grad),
            (w_in, pl.BlockSpec((1, width, part), lambda i: (0, 0, i))),
            (w_in, pl.BlockSpec((1, width, part), lambda i: (0, 0, i + steps))),
            (w_down, pl.BlockSpec((1, part, width), lambda i: (0, i, 0))),
        ],
        [
            whole_out((count, width), LOW),
            whole_out((count, width), LOW),
            ((count, hidden), LOW, pl.BlockSpec((count, part), lambda i: (0, i))),
            ((count, hidden), LOW, pl.BlockSpec((count, part), lambda i: (0, i))),
            ((hidden, count), LOW, pl.BlockSpec((part, count), lambda i: (i, 0))),
            whole_out((width, count), LOW),
        ],
        grid=(steps,),
        token=token,
        scratch=[pltpu.VMEM((count, width), FULL), pltpu.VMEM((count, width), FULL)],
        vmem=24,
        us=20,
    )


CHUNK = 512
EXPERT_CHUNK = 512
EXPERT_VMEM = 40


def weight_copies(at_ref, w_in_ref, w_down_ref, start, units, gate, up, down, sems):
    width, half = w_in_ref.shape[1], w_down_ref.shape[1] // 2
    first = pl.multiple_of(at_ref[2] * half, LANES) + start
    pairs = []
    for piece in range(4):
        rows = pl.ds(piece * (width // 4), width // 4)
        for part, ref in ((0, gate), (2 * half, up)):
            columns = pl.ds(pl.multiple_of(first + part, LANES), units)
            pairs.append((w_in_ref.at[0, rows, columns], ref.at[rows, :]))
        size = units // 4
        rows = pl.ds(pl.multiple_of(first + piece * size, 16), size)
        pairs.append((w_down_ref.at[0, rows, :], down.at[pl.ds(piece * size, size), :]))
    return [pltpu.make_async_copy(one, two, sems.at[at]) for at, (one, two) in enumerate(pairs)]


def ahead_kernel(at_ref, w_in_ref, w_down_ref, gate_ref, up_ref, down_ref, sems):
    copies = weight_copies(
        at_ref, w_in_ref, w_down_ref, 0, gate_ref.shape[1], gate_ref, up_ref, down_ref, sems
    )
    for copy in copies:
        copy.start()
    for copy in copies:
        copy.wait()


def weights_ahead(at, w_in, w_down, token):
    width = w_in.shape[1]
    return call(
        ahead_kernel,
        "weights_ahead",
        [(w_in, None), (w_down, None)],
        [whole_out((width, EXPERT_CHUNK), LOW)] * 2 + [whole_out((EXPERT_CHUNK, width), LOW)],
        token=token,
        prefetch=(at,),
        scratch=[pltpu.SemaphoreType.DMA((12,))],
        us=2,
    )


def halves_kernel(
    at_ref, x0_ref, x1_ref, g0_ref, g1_ref, gate0_ref, up0_ref, down0_ref, w_in_ref, w_down_ref,
    back_keep, back_send, dgate_ref, dup_ref, turned_ref, hid_out, a_send, a_keep, b_out,
    both_w, du, turned, hid_ref, down_ref, a_sum, b_ref, sems, out_sems,
):
    count, width = x0_ref.shape
    half = hid_ref.shape[1]
    starts = list(range(0, half, EXPERT_CHUNK))
    sizes = [min(EXPERT_CHUNK, half - start) for start in starts]
    loads = [
        weight_copies(
            at_ref, w_in_ref, w_down_ref, start, units,
            both_w.at[:, pl.ds(start, units)],
            both_w.at[:, pl.ds(half + start, units)],
            down_ref.at[pl.ds(start, units), :],
            sems.at[i],
        )
        for i, (start, units) in enumerate(zip(starts, sizes))
        if i > 0
    ]
    for copies in loads:
        for copy in copies:
            copy.start()
    firsts = [
        pltpu.make_async_copy(ref, both_w.at[:, pl.ds(start, sizes[0])], sems.at[0, at])
        for at, (ref, start) in enumerate(((gate0_ref, 0), (up0_ref, half)))
    ]
    for copy in firsts:
        copy.start()
    turned[:, :count] = x0_ref[...].T
    turned[:, count:] = x1_ref[...].T
    kept = [pltpu.make_async_copy(turned, turned_ref, out_sems.at[len(sizes), 0])]
    for i, (start, units) in enumerate(zip(starts, sizes)):
        columns, other = pl.ds(start, units), pl.ds(half + start, units)
        if i == 0:
            gate_w, up_w, down_w = gate0_ref[...], up0_ref[...], down0_ref[...]
        else:
            for copy in loads[i - 1]:
                copy.wait()
            gate_w, up_w, down_w = both_w[:, columns], both_w[:, other], down_ref[columns, :]
        for side, (x_ref, g_ref) in enumerate(((x0_ref, g0_ref), (x1_ref, g1_ref))):
            rows = pl.ds(side * count, count)
            x = x_ref[...]
            hid, dgate, dup = expert_part(
                dot_rows(x, gate_w), dot_rows(x, up_w), dot_back(g_ref[...], down_w)
            )
            hid_ref[rows, columns] = hid
            du[rows, columns] = dgate
            du[rows, other] = dup
        for part, (ref, from_columns) in enumerate(((dgate_ref, columns), (dup_ref, other))):
            copy = pltpu.make_async_copy(
                du.at[:, from_columns], ref.at[:, columns], out_sems.at[i, part]
            )
            copy.start()
            kept.append(copy)
    kept[0].start()
    kept.append(pltpu.make_async_copy(hid_ref, hid_out, out_sems.at[len(sizes), 1]))
    kept[-1].start()
    terms = transpose_dot(hid_ref[:count, :], g0_ref[...])
    terms = terms + transpose_dot(hid_ref[count:, :], g1_ref[...])
    middle, size = width // 2, half // 2
    b_ref[...] = terms[:, middle:].astype(LOW)
    a_sum[...] = terms[:, :middle].astype(LOW)
    own = pl.ds(pl.multiple_of(at_ref[1] * size, 16), size)
    other = pl.ds(pl.multiple_of((1 - at_ref[1]) * size, 16), size)
    sent = [(b_ref, b_out), (a_sum.at[other, :], a_send), (a_sum.at[own, :], a_keep)]
    sent = [
        pltpu.make_async_copy(ref, out, out_sems.at[len(sizes) + 1 + at // 2, at % 2])
        for at, (ref, out) in enumerate(sent)
    ]
    for copy in sent:
        copy.start()
    for copy in firsts:
        copy.wait()
    back_send[...] = dot_back(du[count:, :], both_w[...]).astype(LOW)
    back_keep[...] = dot_back(du[:count, :], both_w[...])
    for copy in kept + sent:
        copy.wait()


def expert_halves(at, rows, grads, firsts, w_in, w_down, token):
    count, width = rows[0].shape
    half = w_down.shape[1] // 2
    chunks = pl.cdiv(half, EXPERT_CHUNK)
    return call(
        halves_kernel,
        "expert_halves",
        [whole(array) for array in (*rows, *grads, *firsts)] + [(w_in, None), (w_down, None)],
        [
            whole_out((count, width), FULL),
            whole_out((count, width), LOW),
            ((2 * count, half), LOW, None),
            ((2 * count, half), LOW, None),
            ((width, 2 * count), LOW, None),
            ((2 * count, half), LOW, None),
            ((half // 2, width // 2), LOW, None),
            ((half // 2, width // 2), LOW, None),
            ((half, width // 2), LOW, None),
        ],
        token=token,
        prefetch=(at,),
        scratch=[
            pltpu.VMEM((width, 2 * half), LOW),
            pltpu.VMEM((2 * count, 2 * half), LOW),
            pltpu.VMEM((width, 2 * count), LOW),
            pltpu.VMEM((2 * count, half), LOW),
            pltpu.VMEM((half, width), LOW),
            pltpu.VMEM((half, width // 2), LOW),
            pltpu.VMEM((half, width // 2), LOW),
            pltpu.SemaphoreType.DMA((chunks, 12)),
            pltpu.SemaphoreType.DMA((chunks + 3, 2)),
        ],
        vmem=EXPERT_VMEM,
        us=20,
    )


def results_kernel(at_ref, hid_out, w_down_ref, keep_out, send_out, hid_ref, down_ref, sum_ref, sems):
    half = down_ref.shape[0]
    size = half // 4
    count = sum_ref.shape[1]
    copies = []
    for side in range(2):
        rows = pl.ds(side * count, count)
        copies.append(pltpu.make_async_copy(hid_out.at[rows, :], hid_ref.at[rows, :], sems.at[4 + side]))
    for piece in range(4):
        rows = pl.ds(pl.multiple_of(at_ref[2] * half + piece * size, 16), size)
        here = down_ref.at[pl.ds(piece * size, size), :]
        copies.append(pltpu.make_async_copy(w_down_ref.at[0, rows, :], here, sems.at[piece]))
    for copy in copies:
        copy.start()
    for copy in copies:
        copy.wait()
    copies = []
    for side, out in ((1, send_out), (0, keep_out)):
        rows = pl.ds(side * count, count)
        sum_ref[side] = dot_rows(hid_ref[rows, :], down_ref[...]).astype(LOW)
        copies.append(pltpu.make_async_copy(sum_ref.at[side], out, sems.at[6 + side]))
        copies[-1].start()
    for copy in copies:
        copy.wait()


def expert_results(at, hid, w_down, token):
    half, width = hid.shape[1], w_down.shape[2]
    shape = (hid.shape[0] // 2, width)
    (keep, send), token = call(
        results_kernel,
        "expert_results",
        [(hid, None), (w_down, None)],
        [(shape, LOW, None)] * 2,
        token=token,
        prefetch=(at,),
        scratch=[
            pltpu.VMEM(hid.shape, LOW),
            pltpu.VMEM((half, width), LOW),
            pltpu.VMEM((2, *shape), LOW),
            pltpu.SemaphoreType.DMA((8,)),
        ],
        vmem=16,
        us=0.01,
    )
    return keep, send, token


def block_of(at_ref, k, blocks):
    return lax.rem(at_ref[3] + (blocks - k), blocks)


def join_kernel(at_ref, kept_ref, got_ref, out_ref):
    blocks, size, _ = out_ref.shape
    for k in range(blocks):
        rows = pl.ds(k * size, size)
        total = kept_ref[rows, :] + got_ref[rows, :].astype(FULL)
        out_ref[block_of(at_ref, k, blocks)] = total.astype(LOW)


def join(at, kept, got, blocks, token):
    rows, width = kept.shape
    (out,), token = call(
        join_kernel,
        "join",
        [whole(kept), whole(got)],
        [whole_out((blocks, rows // blocks, width), LOW)],
        token=token,
        prefetch=(at,),
        far_out=(0,),
        us=1,
    )
    return out, token


def join_peak_kernel(at_ref, kept_ref, got_ref, peak_ref, out_ref):
    blocks, size, width = out_ref.shape
    rows = kept_ref.shape[0] // blocks
    best = jnp.concatenate([peak_ref[g, :GROUP, :] for g in range(peak_ref.shape[0])], axis=0)
    best = jnp.broadcast_to(jnp.max(best, axis=1, keepdims=True), (size - rows, LANES))
    upper = best.astype(LOW)
    lower = (best - upper.astype(FULL)).astype(LOW)
    for k in range(blocks):
        part = pl.ds(k * rows, rows)
        to = block_of(at_ref, k, blocks)
        total = kept_ref[part, :].astype(FULL) + got_ref[part, :].astype(FULL)
        out_ref[to, :rows, :] = total.astype(LOW)
        out_ref[to, rows:, :] = jnp.zeros((size - rows, width), LOW)
        out_ref[to, rows:, :LANES] = upper
        out_ref[to, rows:, LANES : 2 * LANES] = lower


def join_peak(at, kept, got, peak, blocks, token):
    rows, width = kept.shape
    heads = peak.shape[0] * GROUP
    (out,), token = call(
        join_peak_kernel,
        "join_peak",
        [whole(kept), whole(got), whole(peak)],
        [whole_out((blocks, rows // blocks + heads, width), LOW)],
        token=token,
        prefetch=(at,),
        far_out=(0,),
        us=0.01,
        far_in=(0,),
    )
    return out, token


def larger_kernel(one_ref, two_ref, out_ref):
    out_ref[...] = jnp.maximum(one_ref[...], two_ref[...])


def larger(one, two, token):
    (out,), token = call(
        larger_kernel,
        "larger",
        [whole(one), whole(two)],
        [whole_out(one.shape, FULL)],
        token=token,
        us=0.5,
    )
    return out, token


def place():
    dp = lax.axis_index("dp")
    return lax.axis_index("ctx"), lax.axis_index("exp"), dp // 2, dp % 2


def to_down_plane(array):
    pairs = [
        ((1 - core) * 4 + x * 2 + core, core * 4 + x * 2 + core)
        for core in range(2)
        for x in range(2)
    ]
    return lax.ppermute(array, ("ctx", "dp"), pairs)


def in_down_plane(array):
    pairs = [
        (core * 4 + x * 2 + core, core * 4 + (1 - x) * 2 + core)
        for core in range(2)
        for x in range(2)
    ]
    return lax.ppermute(array, ("ctx", "dp"), pairs)


def in_kernel(
    at_ref, turned_ref, gate_ref, up_ref, *refs,
):
    out_refs, turned, near, results, sems, out_sems = refs[:4], *refs[4:]
    half = gate_ref.shape[1]
    ends = [CHUNK // 2] + list(range(3 * CHUNK // 2, half, CHUNK)) + [half]
    starts = [0] + ends[:-1]
    loads = []
    for at, (ref, to) in enumerate(((gate_ref, near.at[0]), (up_ref, near.at[1]))):
        for i, start in enumerate(starts):
            columns = pl.ds(start, ends[i] - start)
            loads.append(
                pltpu.make_async_copy(ref.at[:, columns], to.at[:, columns], sems.at[at, i])
            )
    whole_load = pltpu.make_async_copy(turned_ref, turned, sems.at[2, 0])
    whole_load.start()
    loads[0].start()
    loads[len(starts)].start()
    whole_load.wait()
    size = turned.shape[0] // 4
    stores = []
    for i, start in enumerate(starts):
        columns = pl.ds(start, ends[i] - start)
        loads[i].wait()
        loads[len(starts) + i].wait()
        if i + 1 < len(starts):
            loads[i + 1].start()
            loads[len(starts) + i + 1].start()
        for block in range(4):
            ry, rx = block // 2, block % 2
            chip = (at_ref[0] ^ ry) * 2 + (at_ref[1] ^ rx)
            rows = turned[pl.ds(pl.multiple_of(chip * size, size), size), :]
            a, b = 1 - rx, 2 + 1 - ry
            results[a, ry, :, columns] = dot_rows(rows, near[0, :, columns]).astype(LOW)
            results[b, rx, :, columns] = dot_rows(rows, near[1, :, columns]).astype(LOW)
        for at, ref in enumerate(out_refs):
            copy = pltpu.make_async_copy(
                results.at[at, :, :, columns], ref.at[:, :, columns], out_sems.at[at, i]
            )
            copy.start()
            stores.append(copy)
    for copy in stores:
        copy.wait()


def in_terms(at, turned, gate, up, token):
    width, count = turned.shape
    half = gate.shape[1]
    shape = (2, width // 4, half)
    chunks = pl.cdiv(half, CHUNK) + 1
    return call(
        in_kernel,
        "in_terms",
        [(turned, None), (gate, None), (up, None)],
        [(shape, LOW, None)] * 4,
        token=token,
        prefetch=(at,),
        scratch=[
            pltpu.VMEM((width, count), LOW),
            pltpu.VMEM((2, count, half), LOW),
            pltpu.VMEM((4, *shape), LOW),
            pltpu.SemaphoreType.DMA((3, chunks)),
            pltpu.SemaphoreType.DMA((4, chunks)),
        ],
        vmem=20,
        us=0.01,
    )


def plane_first(parts):
    a_send, a_keep, b_send, b_keep = parts
    return swapped(a_send, "dp", 2), a_keep, swapped(b_send, "ctx", 1), b_keep


def second_kernel(*refs):
    (a_ref, a_keep_ref, b_ref, b_keep_ref), (a_send_ref, b_send_ref) = refs[:4], refs[-2:]
    rows = a_ref.shape[0]
    total = a_keep_ref[...].astype(FULL) + a_ref[...].astype(FULL)
    a_send_ref[pl.ds(0, rows), :] = total.astype(LOW)
    b_send_ref[...] = (b_keep_ref[...].astype(FULL) + b_ref[...].astype(FULL)).astype(LOW)
    for beside in refs[4:-2]:
        more, width = beside.shape
        a_send_ref[pl.ds(rows, more), pl.ds(0, width)] = beside[...]


def plane_second(parts, token, us, beside=()):
    extra = sum(part.shape[0] for part in beside)
    (_, a_rows, a_width), (_, b_rows, b_width) = parts[0].shape, parts[2].shape
    (a_send, b_send), token = call(
        second_kernel,
        "second_terms",
        [whole(part) for part in (*parts, *beside)],
        [whole_out((a_rows + extra, a_width), LOW), whole_out((b_rows, b_width), LOW)],
        token=token,
        us=us,
        far_in=tuple(range(4, 4 + len(beside))),
        part_in={at: (1,) for at in range(4)},
        far_out=(0, 1),
        vmem=10,
    )
    return a_send, b_send, token


def down_second_kernel(at_ref, a_ref, a_keep_ref, b_ref, b_keep_ref, a_send_ref, b_send_ref):
    size = b_send_ref.shape[0]
    rows = pl.ds(pl.multiple_of((1 - at_ref[1]) * size, 16), size)
    a_send_ref[...] = (a_keep_ref[...].astype(FULL) + a_ref[...].astype(FULL)).astype(LOW)
    b_send_ref[...] = (b_keep_ref[rows, :].astype(FULL) + b_ref[rows, :].astype(FULL)).astype(LOW)


def down_second(at, parts, token, us):
    shape = parts[0].shape
    (a_send, b_send), token = call(
        down_second_kernel,
        "down_second",
        [whole(part) for part in parts],
        [whole_out(shape, LOW)] * 2,
        token=token,
        prefetch=(at,),
        us=us,
        far_out=(0, 1),
    )
    return a_send, b_send, token


def sum_kernel(one_ref, two_ref, three_ref, out_ref):
    out_ref[...] = sum(ref[...].astype(FULL) for ref in (one_ref, two_ref, three_ref)).astype(LOW)


def plane_sum(got, kept, more, token):
    (out,), token = call(
        sum_kernel,
        "plane_sum",
        [whole(got), whole(kept), whole(more)],
        [whole_out(more.shape, LOW)],
        token=token,
        far_in=(2,),
        part_in={0: (0,), 1: (0,)},
        far_out=(0,),
        us=0.01,
    )
    return out, token


def pair_last_kernel(a_ref, a_keep_ref, a2_ref, b_ref, out_ref):
    blocks = out_ref.shape[0]
    a = sum(ref[...].astype(FULL) for ref in (a_keep_ref, a_ref, a2_ref))
    size = b_ref.shape[0] // blocks
    for z in range(blocks):
        here = slice(z * size, (z + 1) * size)
        out_ref[z, :size, :] = a[here].astype(LOW)
        small = jnp.broadcast_to(a[blocks * size + z : blocks * size + z + 1], (EXTRA, a.shape[1]))
        out_ref[z, size : size + EXTRA, :] = small.astype(LOW)
        out_ref[z, size + EXTRA :, :] = b_ref[here, :]


def pair_last(got, kept, more, b, blocks, token):
    rows, width = b.shape
    own = slice(0, rows + EXTRA)
    (out,), token = call(
        pair_last_kernel,
        "pair_last",
        [whole(got), whole(kept), whole(more), whole(b)],
        [whole_out((blocks, 2 * rows // blocks + EXTRA, width), LOW)],
        token=token,
        far_in=(3,),
        part_in={0: (0,), 1: (0,), 2: (own,)},
        far_out=(0,),
        us=1,
        vmem=12,
    )
    return out, token


def down_last_kernel(
    at_ref, a_ref, a_keep_ref, b_ref, b_keep_ref, a2_ref, b2_ref, keep_ref, send_ref
):
    size, width = keep_ref.shape
    half = width // 2
    for out_ref, core in ((send_ref, 1 - at_ref[2]), (keep_ref, at_ref[2])):
        rows = pl.ds(pl.multiple_of(core * size, 16), size)
        there = pl.ds(pl.multiple_of((at_ref[1] * 2 + core) * size, 16), size)
        for first, refs in (
            (0, ((a_ref, rows), (a_keep_ref, rows), (a2_ref, rows))),
            (half, ((b_ref, there), (b_keep_ref, there), (b2_ref, rows))),
        ):
            total = sum(ref[cut, :].astype(FULL) for ref, cut in refs)
            out_ref[:, first : first + half] = total.astype(out_ref.dtype)


def down_last(at, parts, a2, b2, token):
    rows, half = a2.shape
    shape = (rows // 2, 2 * half)
    (keep, send), token = call(
        down_last_kernel,
        "down_last",
        [whole(array) for array in (*parts, a2, b2)],
        [whole_out(shape, FULL), whole_out(shape, LOW)],
        token=token,
        prefetch=(at,),
        us=3,
        far_out=(0, 1),
    )
    return keep, send, token


def in_last_kernel(
    at_ref, a_ref, a_keep_ref, b_ref, b_keep_ref, a2_ref, b2_ref, down_ref, keep_ref, send_ref
):
    size = keep_ref.shape[1]
    start = down_ref.shape[0]
    send_ref[pl.ds(0, start), pl.ds(0, down_ref.shape[1])] = down_ref[...]
    for mine, core in ((False, 1 - at_ref[2]), (True, at_ref[2])):
        rows = pl.ds(pl.multiple_of(core * size, 16), size)
        for part, refs in enumerate(((a_ref, a_keep_ref, a2_ref), (b_ref, b_keep_ref, b2_ref))):
            total = sum(ref[rows, :].astype(FULL) for ref in refs)
            if mine:
                keep_ref[part] = total
            else:
                send_ref[pl.ds(start + part * size, size), :] = total.astype(LOW)


def in_last(at, parts, a2, b2, down_send, token):
    rows, half = b2.shape
    (keep, send), token = call(
        in_last_kernel,
        "in_last",
        [whole(array) for array in (*parts, a2, b2, down_send)],
        [
            whole_out((2, rows // 2, half), FULL),
            whole_out((down_send.shape[0] + rows, half), LOW),
        ],
        token=token,
        prefetch=(at,),
        us=0.01,
        far_in=(4, 5, 6),
        part_in={at: (0,) for at in range(4)},
        far_out=(0, 1),
        vmem=16,
    )
    return keep, send, token


def finish_kernel(at_ref, in_ref, down_ref, got_ref, in_out, down_out, in_near, down_near, sems):
    _, size, half = in_ref.shape
    start, width = down_ref.shape
    for part in range(2):
        other = got_ref[pl.ds(start + part * size, size), :].astype(FULL)
        for first, value in ((at_ref[2], in_ref[part]), (1 - at_ref[2], other)):
            column = pl.multiple_of((part * 2 + first) * half, LANES)
            in_near[:, pl.ds(column, half)] = value
    copies = [pltpu.make_async_copy(in_near, in_out.at[0], sems.at[0])]
    copies[0].start()
    mine = at_ref[0] == at_ref[2]
    down_near[...] = jnp.where(mine, down_ref[...], got_ref[pl.ds(0, start), :width].astype(FULL))
    copies.append(pltpu.make_async_copy(down_near, down_out.at[0], sems.at[1]))
    copies[1].start()
    for copy in copies:
        copy.wait()


def finish(at, in_keep, down_keep, got, token):
    _, size, half = in_keep.shape
    in_shape, down_shape = (size, 4 * half), down_keep.shape
    outs, token = call(
        finish_kernel,
        "finish",
        [whole(in_keep), whole(down_keep), whole(got)],
        [((1, *in_shape), FULL, None), ((1, *down_shape), FULL, None)],
        token=token,
        prefetch=(at,),
        scratch=[
            pltpu.VMEM(in_shape, FULL),
            pltpu.VMEM(down_shape, FULL),
            pltpu.SemaphoreType.DMA((2,)),
        ],
        us=0.01,
        vmem=16,
    )
    return *outs, token


EXTRA = 16
TABLE_LANE = 32


def turn_kernel(at_ref, *refs):
    out_ref, turned = refs[-2:]
    start = 0
    for ref in refs[:-2]:
        turned[:, start : start + ref.shape[0]] = ref[...].T
        start += ref.shape[0]
    size = out_ref.shape[0] // 16
    for to in range(16):
        device = device_at(to % 4, to // 4, at_ref)
        out_ref[pl.ds(to * size, size), :] = turned[pl.ds(device * size, size), :]


def device_at(block, z, at_ref):
    return (
        (at_ref[0] ^ (block // 2)) * 16 + z * 4 + (at_ref[1] ^ (block % 2)) * 2 + at_ref[2]
    )


def turn(at, parts, token):
    count, width = sum(part.shape[0] for part in parts), parts[0].shape[1]
    (out,), token = call(
        turn_kernel,
        "turn",
        [whole(part) for part in parts],
        [whole_out((width // 2, count), LOW)],
        token=token,
        prefetch=(at,),
        scratch=[pltpu.VMEM((width, count), LOW)],
        us=2,
        far_out=(0,),
    )
    return out, token


def shared_kernel(
    at_ref, left_ref, own_ref, other_ref, *refs, experts
):
    out_refs, near_refs, sems = refs[:4], refs[4:8], refs[8]
    a_send_ref, a_keep_ref, b_send_ref, b_keep_ref = near_refs
    copies = []

    def leave(step, rows):
        for at, (near, out) in enumerate(zip(near_refs, out_refs)):
            if rows.start < near.shape[1]:
                part = pl.ds(rows.start, rows.stop - rows.start)
                copy = pltpu.make_async_copy(
                    near.at[:, part, :], out.at[:, part, :], sems.at[at, step]
                )
                copy.start()
                copies.append(copy)

    rows, count = left_ref.shape[0] // experts, left_ref.shape[1] // 2
    width = own_ref.shape[1]
    tokens = count // 3
    size = rows // 4
    small = own_ref[6 * tokens :, :LANES].astype(FULL) + other_ref[6 * tokens :, :LANES].astype(FULL)
    place = lax.broadcasted_iota(jnp.int32, small.shape, 0)
    for z in range(experts):
        left = left_ref[pl.ds(z * rows, rows), :]

        def product(columns, start, length):
            right = slice(start, start + length)
            one = left[:, columns : columns + length]
            two = left[:, count + columns : count + columns + length]
            total = dot_rows(one, own_ref[right, :]) + dot_rows(two, other_ref[right, :])
            return total.astype(LOW)

        a_terms = product(2 * tokens, 5 * tokens, tokens), product(tokens, 0, tokens)
        b_terms = product(0, tokens, 2 * tokens), product(0, 3 * tokens, 2 * tokens)
        for block in range(4):
            ry, rx = block // 2, block % 2
            a_ref = (a_send_ref if rx else a_keep_ref).at[ry]
            b_ref = (b_send_ref if ry else b_keep_ref).at[rx]
            here = slice(block * size, (block + 1) * size)
            for at in range(2):
                to = pl.ds((2 * z + at) * size, size)
                a_ref[to, :] = a_terms[at][here]
                b_ref[to, :] = b_terms[at][here]
        leave(z, slice(2 * z * size, 2 * (z + 1) * size))
    line = lax.broadcasted_iota(jnp.int32, (EXTRA, LANES), 0)
    for block in range(4):
        ry, rx = block // 2, block % 2
        a_ref = (a_send_ref if rx else a_keep_ref).at[ry]
        rows_here = jnp.zeros((EXTRA, LANES), FULL)
        for z in range(experts):
            row = jnp.where(place == device_at(block, z, at_ref), small, 0.0)
            rows_here = jnp.where(line == z, jnp.sum(row, 0, keepdims=True), rows_here)
        a_ref[2 * size * experts :, :] = jnp.zeros((EXTRA, width), LOW)
        a_ref[2 * size * experts :, :LANES] = rows_here.astype(LOW)
    leave(experts, slice(2 * size * experts, 2 * size * experts + EXTRA))
    for copy in copies:
        copy.wait()


def shared_terms(at, left, own, other, experts, token):
    rows = left.shape[0]
    width = own.shape[1]
    b_shape = (2, rows // 2, width)
    a_shape = (2, rows // 2 + EXTRA, width)
    return call(
        functools.partial(shared_kernel, experts=experts),
        "shared_terms",
        [whole(array) for array in (left, own, other)],
        [(shape, LOW, None) for shape in (a_shape, a_shape, b_shape, b_shape)],
        token=token,
        prefetch=(at,),
        scratch=[pltpu.VMEM(shape, LOW) for shape in (a_shape, a_shape, b_shape, b_shape)]
        + [pltpu.SemaphoreType.DMA((4, experts + 1))],
        us=0.01,
        vmem=16,
    )


def rows_kernel(
    place_ref, plane_ref, w_query_ref, w_key_ref, w_value_ref, gain_ref,
    query_ref, key_ref, value_ref, out_ref, gain_grad_ref, ffn_ref, table_ref,
    near_query, near_key, near_value, sems,
):
    rows = query_ref.shape[0]
    at = pl.ds(pl.multiple_of(place_ref[0] * rows, rows), rows)
    pairs = ((w_query_ref, near_query), (w_key_ref, near_key), (w_value_ref, near_value))
    copies = [
        pltpu.make_async_copy(ref.at[at, :], near, sems.at[number])
        for number, (ref, near) in enumerate(pairs)
    ]
    for copy in copies:
        copy.start()
    total = sum(plane_ref[block].astype(FULL) for block in range(plane_ref.shape[0]))
    out_ref[...] = total[:rows]
    query = total[rows : 2 * rows]
    key, value = (
        total[start + EXTRA : start + EXTRA + rows] for start in (2 * rows, 3 * rows)
    )
    query_ref[...] = query
    key_ref[...] = key
    value_ref[...] = value
    small = total[2 * rows : 2 * rows + 1, :LANES]
    ffn_ref[...] = small
    table_ref[...] = pltpu.roll(jnp.broadcast_to(small, (8, LANES)), LANES - TABLE_LANE, 1)[:1]
    for copy in copies:
        copy.wait()
    sums = query * near_query[...].astype(FULL) + key * near_key[...].astype(FULL)
    sums = jnp.sum(sums + value * near_value[...].astype(FULL), axis=1, keepdims=True)
    lane = lax.broadcasted_iota(jnp.int32, (rows, LANES), 1)
    line = lax.broadcasted_iota(jnp.int32, (rows, LANES), 0)
    spread = jnp.sum(jnp.where(lane == line, sums, 0.0), 0, keepdims=True)
    device = place_ref[0]
    block = gain_ref[pl.ds(device * rows // LANES, 1), :]
    gain = pltpu.roll(jnp.broadcast_to(block, (8, LANES)), LANES - device * rows % LANES, 1)[:1]
    gain_grad_ref[...] = spread / gain


def last_rows(place_all, plane, rows, weights, gain, token):
    width = plane.shape[2]
    small = whole_out((1, LANES), FULL)
    outs, token = call(
        rows_kernel,
        "last_rows",
        [whole(plane)] + [(array, None) for array in weights] + [whole(gain.reshape(-1, LANES))],
        [whole_out((rows, width), FULL)] * 4 + [small] * 3,
        token=token,
        prefetch=(place_all.reshape(1),),
        scratch=[pltpu.VMEM((rows, width), LOW)] * 3 + [pltpu.SemaphoreType.DMA((3,))],
        us=0.01,
    )
    return outs, token


def clip_kernel(query_ref, key_ref, peak_ref, level_ref, query_out, key_out, factor_ref):
    heads = peak_ref.shape[0]
    width = query_ref.shape[1]
    level = jnp.sum(jnp.where(eye(heads), level_ref[...], 0.0), 1, keepdims=True)
    factor = level / jnp.maximum(peak_ref[:, :1], level)
    factor_ref[...] = jnp.broadcast_to(factor, (heads, LANES))
    head = lax.broadcasted_iota(jnp.int32, (heads, width), 0)
    lane = lax.broadcasted_iota(jnp.int32, (heads, width), 1)
    scale = jnp.sum(jnp.where(lane // HDIM == head, jnp.sqrt(factor), 0.0), 0, keepdims=True)
    query_out[...] = query_ref[...].astype(FULL) * scale
    key_out[...] = key_ref[...].astype(FULL) * scale


def clip(w_query, w_key, peak, level, token):
    rows, width = w_query.shape
    spec = pl.BlockSpec((rows // 4, width), lambda i: (i, 0))
    outs, token = call(
        clip_kernel,
        "clip",
        [(w_query, spec), (w_key, spec), whole(peak), whole(level.reshape(1, -1))],
        [((rows, width), FULL, spec)] * 2 + [whole_out(peak.shape, FULL)],
        grid=(4,),
        token=token,
        us=0.01,
        vmem=16,
    )
    return outs, token


def normed_kernel(
    packed_ref, w_query_ref, w_key_ref, w_value_ref, own_ref, other_ref, near, sems
):
    copies = [
        pltpu.make_async_copy(ref, near.at[at], sems.at[at])
        for at, ref in enumerate((w_key_ref, w_value_ref, w_query_ref))
    ]
    for copy in copies:
        copy.start()
    tokens = own_ref.shape[0]
    dq, dk, dv = (
        packed_ref[pl.ds(start * tokens, size * tokens), :]
        for start, size in ((0, 1), (1, 2), (3, 2))
    )
    copies[0].wait()
    total = dot_back(dk, near[0])
    copies[1].wait()
    total = total + dot_back(dv, near[1])
    other_ref[...] = total[:tokens].astype(LOW)
    copies[2].wait()
    own_ref[...] = total[tokens:] + dot_back(dq, near[2])


def normed_grads(packed, weights, tokens, token):
    width = packed.shape[1]
    (own, other), token = call(
        normed_kernel,
        "normed_grads",
        [whole(packed)] + [(array, None) for array in weights],
        [whole_out((tokens, width), FULL), whole_out((tokens, width), LOW)],
        token=token,
        scratch=[pltpu.VMEM((3, width, width), LOW), pltpu.SemaphoreType.DMA((3,))],
        far_in=(0,),
        far_out=(0, 1),
        us=0.01,
        vmem=14,
    )
    return own, other, token


def input_kernel(rows_ref, gain_ref, own_ref, got_ref, past_ref, out_ref):
    rows = rows_ref[...].astype(FULL)
    inverse = lax.rsqrt(jnp.mean(rows * rows, axis=1, keepdims=True) + EPSILON)
    scaled = rows * inverse
    grad = (own_ref[...] + got_ref[...].astype(FULL)) * gain_ref[...]
    along = jnp.mean(scaled * grad, axis=1, keepdims=True)
    out_ref[0] = past_ref[...] + inverse * (grad - scaled * along)


def input_grads(rows, gain, own, got, past, token):
    tokens, width = rows.shape
    start = got.shape[0] - tokens
    (out,), token = call(
        input_kernel,
        "input_grads",
        [whole(array) for array in (rows, gain, own, got, past)],
        [whole_out((1, tokens, width), FULL)],
        token=token,
        far_in=(0, 1, 2, 4),
        part_in={3: (slice(start, start + tokens), slice(0, width))},
        far_out=(0,),
        us=0.01,
    )
    return out, token


def back_kernel(
    at_ref, spread_ref, rows_ref, after_ref, gain_ref, grad_ref, weights_ref,
    total_ref, branch_ref, attended_ref, gain_grad_ref,
):
    rows = after_ref[...]
    inverse = lax.rsqrt(jnp.mean(rows * rows, axis=1, keepdims=True) + EPSILON)
    scaled = rows * inverse
    blocks, size, _ = rows_ref.shape
    grad = sum(
        transpose_dot(spread_ref[pl.ds(k * size, size), :], rows_ref[lax.rem(at_ref[3] + k, blocks)])
        for k in range(blocks)
    )
    gain_grad_ref[...] = jnp.sum(scaled * grad, axis=0, keepdims=True)
    grad = grad * gain_ref[...]
    along = jnp.mean(scaled * grad, axis=1, keepdims=True)
    total = grad_ref[...].astype(FULL) + inverse * (grad - scaled * along)
    total_ref[...] = total
    branch = total.astype(LOW)
    branch_ref[...] = branch
    attended_ref[...] = dot_back(branch, weights_ref[...]).astype(LOW)


def back_to_attention(at, spread, rows, after, gain, grad, weights, fetch, token):
    shape = after.shape
    inputs = (spread, rows, after, gain, grad, weights)
    return call(
        back_kernel,
        "back",
        [whole(array) for array in inputs],
        [
            whole_out(shape, FULL),
            whole_out(shape, LOW),
            whole_out(shape, LOW),
            whole_out((1, shape[1]), FULL),
        ],
        token=token,
        vmem=16,
        us=0.01,
        far_in=(0, 2, 4, 5),
        prefetch=(at,),
        fetch=fetch,
    )


def mix_kernel(at_ref, pick_ref, rows_ref, gates_ref, after_ref, out_ref, peak_ref):
    top, tokens = gates_ref.shape
    blocks = rows_ref.shape[0]
    size = pick_ref.shape[0] // blocks
    total = after_ref[...]
    gates = [to_column(gates_ref[r : r + 1, :]) for r in range(top)]
    for block in range(blocks):
        rows = rows_ref[lax.rem(at_ref[3] + block, blocks), :size, :]
        for r in range(top):
            pick = pick_ref[pl.ds(block * size, size), pl.ds(r * tokens, tokens)]
            total = total + gates[r] * transpose_dot(pick, rows)
    out_ref[0] = total.astype(LOW)
    if rows_ref.shape[1] > size:
        peaks = [
            rows_ref[block, size:, :LANES].astype(FULL)
            + rows_ref[block, size:, LANES : 2 * LANES].astype(FULL)
            for block in range(blocks)
        ]
        peak_ref[...] = functools.reduce(jnp.maximum, peaks)


def mix(at, pick, rows, gates, after, token):
    (out, peak), token = call(
        mix_kernel,
        "mix",
        [whole(pick), whole(rows), whole(gates), whole(after)],
        [whole_out((1, *after.shape), LOW), whole_out((16, LANES), FULL)],
        token=token,
        us=0.01,
        far_in=(0, 3),
        prefetch=(at,),
    )
    return out, peak, token


def local(
    block_in,
    seg_ids,
    routes,
    gates,
    buckets,
    norm_attn,
    norm_ffn,
    w_query,
    w_key,
    w_value,
    w_out_attn,
    rel_bias,
    clip_level,
    w_in,
    w_down,
    cotangent,
):
    tokens, width = block_in.shape[1:]
    heads = width // HDIM
    n_ctx, experts, n_dp = (lax.axis_size(axis) for axis in ("ctx", "exp", "dp"))
    fast = (n_ctx, experts, n_dp) == (2, 4, 4)
    devices = n_ctx * experts * n_dp
    length = n_ctx * tokens
    y, z, x, core = place()
    place_all = (y * experts + z) * n_dp + lax.axis_index("dp")
    top_count = routes.shape[-1]
    capacity = tokens * top_count * 3 // (2 * experts)
    at = jnp.stack([y, x, core, z])

    (spread, pick, mask, rows_copy, *grad_out), token = front(
        at, routes[0].T, gates[0].T, cotangent[0], seg_ids, block_in[0], experts, capacity
    )
    backs = list(range(n_ctx - 1, 0, -1))
    earlier = [
        lax.ppermute(block_in[0], "ctx", [(i, (i + back) % n_ctx) for i in range(n_ctx)])
        for back in backs
    ]
    grad_blocks = to_experts(grad_out)
    (bucket_hot, bias, w_key_near, w_value_near), _ = bias_tiles(
        buckets.reshape(1, length), rel_bias.reshape(NB, heads), tokens, (w_key, w_value)
    )

    own_rows = block_in[0].astype(FULL)
    normed_own = rms_norm(own_rows, norm_attn).astype(LOW)
    normed_all = jnp.concatenate(
        [rms_norm(rows.astype(FULL), norm_attn).astype(LOW) for rows in earlier] + [normed_own],
        axis=0,
    )
    queries = dot_rows(normed_own, w_query).astype(LOW)
    keys = dot_rows(normed_all, w_key_near).astype(LOW)
    values = dot_rows(normed_all, w_value_near).astype(LOW)
    attended, probs, peak_lanes, w_out_near = attention(
        queries, keys, values, bias, mask, (w_out_attn,)
    )
    after, sent = after_attention(
        attended, w_out_near, rows_copy, norm_ffn.reshape(1, width), spread, experts
    )

    row_blocks = to_experts(sent)
    own_gain, own_table = width // devices, NB * heads // devices
    if fast:
        expert_grad, token = side_by_side(grad_blocks, token)
        parts = (normed_all, attended)
        parts = parts + tuple(swapped(part, "dp", 1) for part in parts)
        left, token = turn(at, parts, token)
        peak, token = larger(peak_lanes, swapped(peak_lanes, "dp", 1), token)
        peak, token = larger(peak, swapped(peak, "dp", 2), token)
        peak, token = larger(peak, swapped(peak, "ctx", 1), token)
        expert_rows, token = side_by_side(row_blocks, token)
        both_rows = expert_rows, swapped(expert_rows, "dp", 1)
        both_grads = expert_grad, swapped(expert_grad, "dp", 1)
        firsts, token = weights_ahead(at, w_in, w_down, token)
        outs, token = expert_halves(at, both_rows, both_grads, firsts, w_in, w_down, token)
        back_keep, back_send, dgate, dup, rows_turned, hid, *down = outs
        back_got = swapped(back_send, "dp", 1)
        down = swapped(down[0], "dp", 2), down[1], to_down_plane(down[2]), down[2]
        back_rows, token = join(at, back_keep, back_got, experts, token)
        back_home = over_experts(back_rows)
        first, token = in_terms(at, rows_turned, dgate, dup, token)
        first = plane_first(first)
        down_a, down_b, token = down_second(at, down, token, 5)
        out_keep, out_send, token = expert_results(at, hid, w_down, token)
    else:
        expert_rows = jnp.concatenate(row_blocks, axis=0)
        expert_grad = jnp.concatenate(grad_blocks, axis=0)
        (out_rows, back_rows, dgate, dup, hid_turned, rows_turned), token = expert(
            expert_rows, expert_grad, w_in, w_down, token
        )
        expert_first, expert_second = (
            lax.psum_scatter(grads, ("ctx", "dp"), scatter_dimension=0, tiled=True)[None]
            for grads in (
                dot_rows(rows_turned, jnp.concatenate([dgate, dup], axis=1)),
                dot_rows(hid_turned, expert_grad),
            )
        )
        back_home, out_home = (
            jnp.stack(from_experts(list(rows.reshape(experts, capacity, width))))
            for rows in (back_rows, out_rows)
        )

    home = at if fast else jnp.zeros_like(at)
    soon = (queries, keys, values, probs) + ((bucket_hot,) if fast else ())
    (grad_after, grad_branch, grad_attended, grad_gain_ffn, *soon), token = back_to_attention(
        home, spread, back_home, after, norm_ffn.reshape(1, width), cotangent[0], w_out_attn, soon, token
    )
    if fast:
        packed, token = attention_back(
            *soon[:4], grad_attended, token, (grad_branch, soon[4], grad_gain_ffn, devices),
        )
        packed_got = swapped(packed, "dp", 1)
        (left,), token = bring(token, 20, left)
        plane_2, token = shared_terms(at, left, packed, packed_got, experts, token)
        plane_2 = plane_first(plane_2)
        out_send, = hold(token, out_send)
        out_got = swapped(out_send, "dp", 1)
        out_rows, token = join_peak(at, out_keep, out_got, peak, experts, token)
        out_home = over_experts(out_rows)
        normed_own_grad, normed_other_grad, token = normed_grads(
            packed, (w_query, w_key, w_value), tokens, token
        )
        in_a, in_b, token = plane_second(first, token, 0.01)
    else:
        dq, dk, dv, lines, token = attention_back(
            *soon, grad_attended, token
        )
        lines = lines[:, :GROUP, :].reshape(heads, length + tokens)
        grad_table = lax.dot_general(
            bucket_hot, lines, (((1,), (1,)), ((), ())), precision=FULL_PRECISION
        ).reshape(-1)
        mixed, _, _ = mix(home, pick, out_home, gates[0].T, after, token)
        peak = jnp.max(peak_lanes[:, :GROUP, :], axis=-1).reshape(heads)
        peak = lax.pmax(peak, ("ctx", "exp", "dp"))
        peak = jnp.broadcast_to(peak[:, None], (heads, LANES))
        clipped, _ = clip(w_query, w_key, peak, clip_level, token)

        grad_normed = dot_back(dk, w_key) + dot_back(dv, w_value)
        grad_normed_own = grad_normed[length - tokens :] + dot_back(dq, w_query)
        for block, back in enumerate(backs):
            term = grad_normed[block * tokens : (block + 1) * tokens].astype(LOW)
            returned = lax.ppermute(term, "ctx", [((i + back) % n_ctx, i) for i in range(n_ctx)])
            grad_normed_own = grad_normed_own + returned.astype(FULL)
        _, norm_pull = jax.vjp(lambda rows: rms_norm(rows, norm_attn), own_rows)
        grad_input = (grad_after + norm_pull(grad_normed_own)[0])[None]

    if fast:
        shared_a, shared_b, token = plane_second(plane_2, token, 8, (normed_other_grad,))
        shared_a, shared_b = swapped(shared_a, "ctx", 1), swapped(shared_b, "dp", 2)
        down_a, down_b = hold(token, down_a, down_b)
        down_a, down_b = to_down_plane(down_a), in_down_plane(down_b)
        mixed, peak, token = mix(at, pick, out_home, gates[0].T, after, token)
        half_b, token = plane_sum(plane_2[2], plane_2[3], shared_b, token)
        in_a, in_b = hold(token, in_a, in_b)
        in_a, in_b = swapped(in_a, "ctx", 1), swapped(in_b, "dp", 2)
        plane, token = pair_last(plane_2[0], plane_2[1], shared_a, half_b, experts, token)
        plane = over_experts(plane)
        clipped, token = clip(w_query, w_key, peak, clip_level, token)
        down_keep, down_send, token = down_last(at, down, down_a, down_b, token)
        grad_input, token = input_grads(
            block_in[0], norm_attn.reshape(1, width), normed_own_grad, shared_a, grad_after, token
        )
        in_keep, last_send, token = in_last(at, first, in_a, in_b, down_send, token)
        last_got = swapped(last_send, "dp", 1)
        (in_keep, down_keep), token = bring(token, 0.01, in_keep, down_keep)
        expert_first, expert_second, token = finish(at, in_keep, down_keep, last_got, token)
        outs, token = last_rows(
            place_all, plane, own_gain, (w_query, w_key, w_value), norm_attn, token
        )
        shared_q, shared_k, shared_v, shared_o = outs[:4]
        small_attn, small_ffn = outs[4][0, :own_gain], outs[5][0, :own_gain]
        small_table = outs[6][0, :own_table]
    else:
        shared_q, shared_k, shared_v, shared_o = (
            lax.psum_scatter(grads, ("ctx", "exp", "dp"), scatter_dimension=0, tiled=True)
            for grads in (
                transpose_dot(normed_own, dq),
                transpose_dot(normed_all, dk),
                transpose_dot(normed_all, dv),
                transpose_dot(attended, grad_branch),
            )
        )
        small_ffn, small_table = (
            lax.dynamic_slice_in_dim(lax.psum(array, ("ctx", "exp", "dp")), place_all * own, own)
            for array, own in ((grad_gain_ffn[0], own_gain), (grad_table, own_table))
        )
        pairs = ((shared_q, w_query), (shared_k, w_key), (shared_v, w_value))
        row_sums = sum(
            jnp.sum(
                grads * lax.dynamic_slice_in_dim(weights, place_all * own_gain, own_gain).astype(FULL),
                axis=1,
            )
            for grads, weights in pairs
        )
        small_attn = row_sums / lax.dynamic_slice_in_dim(norm_attn, place_all * own_gain, own_gain)

    return (
        mixed,
        grad_input,
        small_attn,
        small_ffn,
        shared_q,
        shared_k,
        shared_v,
        shared_o,
        small_table,
        expert_first,
        expert_second,
        clipped[0],
        clipped[1],
        clipped[2][:, 0],
    )


def solution(mesh):
    tokens = P(("exp", "dp"), "ctx", None)
    everywhere = P(("ctx", "exp", "dp"))
    by_rows = P(("ctx", "exp", "dp"), None)
    by_expert = P("exp", None, None)
    expert_rows = P("exp", ("ctx", "dp"), None)
    in_specs = (tokens, P(("exp", "dp"), None), tokens, tokens) + (P(),) * 9
    in_specs = in_specs + (by_expert, by_expert, tokens)
    out_specs = (tokens, tokens, everywhere, everywhere) + (by_rows,) * 4
    out_specs = out_specs + (everywhere, expert_rows, expert_rows, P(), P(), P())
    return jax.shard_map(local, mesh=mesh, in_specs=in_specs, out_specs=out_specs, check_vma=False)
```

```python
import functools

import jax
import jax.numpy as jnp
from jax import lax
from jax.experimental import pallas as pl
from jax.experimental.pallas import tpu as pltpu
from jax.sharding import PartitionSpec as P

HDIM = 64
NB = 32
GROUP = 4
LANES = 128
EPSILON = 1e-06
FULL_PRECISION = lax.Precision.HIGHEST
LOW = jnp.bfloat16
FULL = jnp.float32
OUTSIDE = -1e30
GELU_SCALE = 0.7978845608028654
GELU_CUBE = 0.044715


def rms_norm(rows, gain):
    return rows * lax.rsqrt(jnp.mean(rows * rows, axis=-1, keepdims=True) + EPSILON) * gain


def dot_rows(left, right):
    return lax.dot_general(left, right, (((1,), (0,)), ((), ())), preferred_element_type=FULL)


def dot_back(left, right):
    return lax.dot_general(left, right, (((1,), (1,)), ((), ())), preferred_element_type=FULL)


def transpose_dot(left, right):
    return lax.dot_general(left, right, (((0,), (0,)), ((), ())), preferred_element_type=FULL)


def swapped(array, axis, bit):
    size = lax.axis_size(axis)
    return lax.ppermute(array, axis, [(i, i ^ bit) for i in range(size)])


def shifted(array, axis, shift):
    size = lax.axis_size(axis)
    return lax.ppermute(array, axis, [(i, (i + shift) % size) for i in range(size)])


def to_experts(blocks):
    return [blocks[0]] + [shifted(blocks[k], "exp", k) for k in range(1, len(blocks))]


def from_experts(blocks):
    return [blocks[0]] + [shifted(blocks[k], "exp", len(blocks) - k) for k in range(1, len(blocks))]


def over_experts(blocks):
    return lax.all_to_all(blocks, "exp", split_axis=0, concat_axis=0, tiled=True)


MICROSECOND = 1.15e9


def call(
    body, name, inputs, outputs, us, grid=None, token=None, prefetch=(), scratch=(), vmem=6,
    near_in=(), near_out=(), far_in=(), far_out=(), fetch=(),
    part_in=None,
):
    part_in = dict(part_in or {})
    far_in = tuple(far_in) + tuple(part_in)
    inputs = list(inputs) + [(array, None) for array in fetch]
    outputs = list(outputs) + [whole_out(array.shape, array.dtype) for array in fetch]
    n_pre, n_in, n_out = len(prefetch), len(inputs), len(outputs)
    held = [] if token is None else [token]
    n_far, n_scratch = len(far_in) + len(far_out), len(scratch)

    def kernel(*refs):
        split = n_pre + n_in
        outs = split + len(held)
        rest = refs[outs + n_out + 1 :]
        ins_here, outs_here = list(refs[:split]), list(refs[outs : outs + n_out])
        copies = []
        for number, at in enumerate(far_in):
            here = rest[n_scratch + number]
            source = refs[n_pre + at].at[part_in[at]] if at in part_in else refs[n_pre + at]
            copies.append(pltpu.make_async_copy(source, here, rest[-1].at[number]))
            ins_here[n_pre + at] = here
        for copy in copies:
            copy.start()
        fetches = [
            pltpu.make_async_copy(ins_here.pop(), outs_here.pop(), rest[-1].at[n_far + number])
            for number in range(len(fetch))
        ]
        for copy in fetches:
            copy.start()
        for copy in copies:
            copy.wait()
        copies = []
        for number, at in enumerate(far_out, len(far_in)):
            here = rest[n_scratch + number]
            copies.append(pltpu.make_async_copy(here, refs[outs + at], rest[-1].at[number]))
            outs_here[at] = here
        body(*ins_here, *outs_here, *rest[:n_scratch])
        for copy in fetches:
            copy.wait()
        for copy in copies:
            copy.start()
        for copy in copies:
            copy.wait()

    where = lambda at, near: pltpu.VMEM if at in near else pltpu.HBM
    arrays = [array for array, _ in inputs]
    shapes = [(shape, dtype) for shape, dtype, _ in outputs]
    anywhere = pl.BlockSpec(memory_space=pl.ANY)
    if grid is None:
        near = pl.BlockSpec(memory_space=pltpu.VMEM)
        far = [at in far_in or spec is None for at, (_, spec) in enumerate(inputs)]
        far_results = [at in far_out or spec is None for at, (_, _, spec) in enumerate(outputs)]
        left = lambda at: tuple(
            size if axis >= len(part_in.get(at, ())) else len(range(size)[part_in[at][axis]])
            for axis, size in enumerate(arrays[at].shape)
            if axis >= len(part_in.get(at, ())) or isinstance(part_in[at][axis], slice)
        )
        buffers = [pltpu.VMEM(left(at), arrays[at].dtype) for at in far_in]
        buffers += [pltpu.VMEM(*shapes[at]) for at in far_out]
        n_sems = n_far + len(fetch)
        buffers += [pltpu.SemaphoreType.DMA((n_sems,))] if n_sems else []
        form = dict(
            in_specs=[pl.BlockSpec(memory_space=pltpu.SMEM)] * n_pre
            + [anywhere if away else near for away in far]
            + [anywhere] * len(held),
            out_specs=[anywhere if away else near for away in far_results] + [anywhere],
            scratch_shapes=list(scratch) + buffers,
        )
        arrays = [
            pltpu.with_memory_space_constraint(array, pltpu.HBM) if away else array
            for array, away in zip(arrays, far)
        ]
        shapes = [
            pltpu.HBM(*one) if away else jax.ShapeDtypeStruct(*one)
            for away, one in zip(far_results, shapes)
        ]
    else:
        form = dict(
            grid_spec=pltpu.PrefetchScalarGridSpec(
                num_scalar_prefetch=n_pre,
                grid=grid,
                in_specs=[spec for _, spec in inputs] + [anywhere] * len(held),
                out_specs=[spec for _, _, spec in outputs] + [anywhere],
                scratch_shapes=list(scratch),
            )
        )
        arrays = [
            pltpu.with_memory_space_constraint(array, where(at, near_in))
            for at, array in enumerate(arrays)
        ]
        shapes = [where(at, near_out)(*one) for at, one in enumerate(shapes)]
    held = [pltpu.with_memory_space_constraint(array, pltpu.HBM) for array in held]
    results = pl.pallas_call(
        kernel,
        out_shape=shapes + [pltpu.HBM((8, LANES), FULL)],
        cost_estimate=pl.CostEstimate(
            flops=int(us * MICROSECOND), bytes_accessed=1, transcendentals=0
        ),
        compiler_params=pltpu.CompilerParams(vmem_limit_bytes=vmem * 2**20),
        name=name,
        **form,
    )(*prefetch, *arrays, *held)
    return list(results[:-1]), results[-1]


def whole(array):
    return array, pl.BlockSpec(array.shape, lambda *_: (0,) * array.ndim)


def whole_out(shape, dtype):
    return shape, dtype, pl.BlockSpec(shape, lambda *_: (0,) * len(shape))


def hold(token, *arrays):
    anywhere = pl.BlockSpec(memory_space=pl.ANY)
    return pl.pallas_call(
        lambda *refs: None,
        in_specs=[anywhere] * (len(arrays) + 1),
        out_specs=[anywhere] * len(arrays),
        out_shape=[jax.ShapeDtypeStruct(array.shape, array.dtype) for array in arrays],
        input_output_aliases={at + 1: at for at in range(len(arrays))},
        cost_estimate=pl.CostEstimate(flops=1, bytes_accessed=1, transcendentals=0),
        name="hold",
    )(token, *arrays)


def pass_kernel(*refs):
    half = len(refs) // 2
    for ref, out_ref in zip(refs[:half], refs[half:]):
        out_ref[...] = ref[...]


def bring(token, us, *arrays):
    return call(lambda *refs: None, "bring", [], [], token=token, fetch=arrays, us=us)


def pass_on(token, *arrays):
    return call(
        pass_kernel,
        "pass_on",
        [whole(array) for array in arrays],
        [whole_out(array.shape, array.dtype) for array in arrays],
        token=token,
        us=1,
    )


def eye(size):
    rows = lax.broadcasted_iota(jnp.int32, (size, size), 0)
    return rows == lax.broadcasted_iota(jnp.int32, (size, size), 1)


def to_column(row):
    size = row.shape[1]
    return jnp.sum(jnp.where(eye(size), row, jnp.zeros_like(row)), 1, keepdims=True)


def front_kernel(
    at_ref, routes_ref, gates_ref, grad_ref, seg_ref, rows_ref,
    spread_ref, pick_ref, mask_ref, copy_ref, *out_refs,
):
    top, tokens = routes_ref.shape
    experts, capacity = len(out_refs), out_refs[0].shape[0]
    routes = [routes_ref[r : r + 1, :] for r in range(top)]
    gates = [gates_ref[r : r + 1, :] for r in range(top)]
    before = lax.broadcasted_iota(jnp.int32, (tokens, tokens), 0)
    before = before < lax.broadcasted_iota(jnp.int32, (tokens, tokens), 1)
    slots = lax.broadcasted_iota(jnp.int32, (capacity, tokens), 0).astype(FULL)
    for e in range(experts):
        part = pl.ds(e * capacity, capacity)
        name = lax.rem(at_ref[3] + e, experts)
        hits = [jnp.where(route == name, 1.0, 0.0) for route in routes]
        named = functools.reduce(jnp.add, hits)
        slot = jnp.sum(jnp.where(before, to_column(named), 0.0), 0, keepdims=True)
        place = (slots == slot).astype(FULL)
        spread = place * named
        gate = functools.reduce(jnp.add, [hit * g for hit, g in zip(hits, gates)])
        spread_low = spread.astype(LOW)
        spread_ref[part, :] = spread_low
        for r in range(top):
            pick_ref[part, pl.ds(r * tokens, tokens)] = (place * hits[r]).astype(LOW)
        slot_gate = jnp.sum(spread * gate, 1, keepdims=True)
        out_refs[e][...] = (slot_gate * dot_rows(spread_low, grad_ref[...])).astype(LOW)
    length = mask_ref.shape[1]
    ctx = at_ref[0]
    seg = jnp.broadcast_to(seg_ref[...].astype(FULL), (8, length))
    keys = pltpu.roll(seg, length - (ctx + 1) * tokens, 1)[:1, :]
    at_row = lax.broadcasted_iota(jnp.int32, (tokens, length), 0) + (length - tokens)
    at_key = lax.broadcasted_iota(jnp.int32, (tokens, length), 1)
    own = jnp.sum(jnp.where(at_row == at_key, keys, 0.0), 1, keepdims=True)
    allowed = (at_key <= at_row) & (own == keys) & (at_key >= length - (ctx + 1) * tokens)
    mask_ref[...] = jnp.where(allowed, 0.0, OUTSIDE)
    copy_ref[...] = rows_ref[...]


def front(at, routes, gates, grad, seg, rows, experts, capacity):
    top, tokens = routes.shape
    slots = experts * capacity
    return call(
        front_kernel,
        "front",
        [whole(array) for array in (routes, gates, grad, seg, rows)],
        [
            whole_out((slots, tokens), LOW),
            whole_out((slots, top * tokens), LOW),
            whole_out((tokens, seg.shape[1]), FULL),
            whole_out(rows.shape, LOW),
        ]
        + [whole_out((capacity, grad.shape[1]), LOW)] * experts,
        prefetch=(at,),
        far_in=(0, 1, 2, 3, 4),
        far_out=(1,),
        us=1.5,
    )


def project_kernel(buckets_ref, table_ref, gain_ref, *refs, blocks):
    x_refs, weights = refs[:blocks], refs[blocks : blocks + 3]
    hot_ref, bias_ref, normed_ref, q_ref, k_ref, v_ref, near, sems = refs[blocks + 3 :]
    copies = [
        pltpu.make_async_copy(ref, near.at[at], sems.at[at]) for at, ref in enumerate(weights)
    ]
    for copy in copies:
        copy.start()
    tokens = q_ref.shape[0]
    for at, x_ref in enumerate(x_refs):
        rows = rms_norm(x_ref[...].astype(FULL), gain_ref[...])
        normed_ref[pl.ds(at * tokens, tokens), :] = rows.astype(LOW)
    bias_part(buckets_ref, table_ref, hot_ref, bias_ref)
    own = pl.ds((blocks - 1) * tokens, tokens)
    for at, (out_ref, rows) in enumerate(
        ((q_ref, own), (k_ref, slice(None)), (v_ref, slice(None)))
    ):
        copies[at].wait()
        out_ref[...] = dot_rows(normed_ref[rows, :], near[at]).astype(LOW)


def bias_part(buckets_ref, table_ref, hot_ref, bias_ref):
    heads, rows, keys = bias_ref.shape
    width = hot_ref.shape[1]
    buckets = buckets_ref[...].astype(FULL)
    column = jnp.sum(jnp.where(eye(keys), buckets, 0.0), 1, keepdims=True)
    distance = lax.broadcasted_iota(jnp.int32, (keys, width), 0)
    lane = lax.broadcasted_iota(jnp.int32, (keys, width), 1)
    turned = jnp.sum(jnp.where(distance + lane == keys - 1, column, 0.0), 0, keepdims=True)
    bucket = lax.broadcasted_iota(jnp.int32, (NB, width), 0).astype(FULL)
    hot = jnp.where(bucket == turned, 1.0, 0.0)
    hot_ref[...] = hot
    by_lane = lax.dot_general(
        table_ref[...], hot, (((0,), (0,)), ((), ())), precision=FULL_PRECISION,
        preferred_element_type=FULL,
    )
    for head in range(heads):
        line = jnp.broadcast_to(by_lane[head : head + 1, :], (8, width))
        line = pltpu.roll(line, keys + 1, 1, stride=1, stride_axis=0)
        for start in range(0, rows, 8):
            moved = line if start == 0 else pltpu.roll(line, start, 1)
            bias_ref[head, pl.ds(start, 8), :] = moved[:, :keys]


def project(buckets, table, gain, parts, weights):
    heads, keys = table.shape[1], buckets.shape[1]
    tokens, width = parts[0].shape
    outs, _ = call(
        functools.partial(project_kernel, blocks=len(parts)),
        "project",
        [whole(array) for array in (buckets, table, gain, *parts)]
        + [(array, None) for array in weights],
        [
            whole_out((NB, keys + tokens), FULL),
            whole_out((heads, tokens, keys), FULL),
            whole_out((keys, width), LOW),
            whole_out((tokens, width), LOW),
            whole_out((keys, width), LOW),
            whole_out((keys, width), LOW),
        ],
        scratch=[pltpu.VMEM((3, width, width), LOW), pltpu.SemaphoreType.DMA((3,))],
        us=4.5,
        vmem=16,
    )
    return outs


def half_lanes(half, shape):
    lane = lax.broadcasted_iota(jnp.int32, shape, 1)
    return lane < HDIM if half == 0 else lane >= HDIM


def attention_kernel(q_ref, k_ref, v_ref, bias_ref, mask_ref, out_ref, probs_ref, peak_ref):
    groups = peak_ref.shape[0]

    def group(step, _):
        mask = mask_ref[...]
        for pair in range(GROUP // 2):
            lanes = pair_lanes(step, pair)
            queries, keys, values = q_ref[:, lanes], k_ref[:, lanes], v_ref[:, lanes]
            parts = []
            for half in range(2):
                at = 2 * pair + half
                own = half_lanes(half, queries.shape)
                raw = dot_back(jnp.where(own, queries, jnp.zeros_like(queries)), keys)
                raw = raw * HDIM**-0.5 + mask
                top = jnp.max(raw, axis=0, keepdims=True)
                best = top[:, :LANES]
                for start in range(LANES, top.shape[1], LANES):
                    best = jnp.maximum(best, top[:, start : start + LANES])
                peak_ref[step, at : at + 1, :] = best
                scores = raw + bias_ref[step * GROUP + at]
                raised = jnp.exp(scores - jnp.max(scores, axis=1, keepdims=True))
                probs = raised * (1.0 / jnp.sum(raised, axis=1, keepdims=True))
                probs_low = probs.astype(LOW)
                probs_ref[step * GROUP + at] = probs_low
                parts.append(dot_rows(probs_low, values))
            first = half_lanes(0, parts[0].shape)
            out_ref[:, lanes] = jnp.where(first, parts[0], parts[1]).astype(LOW)
        return 0

    lax.fori_loop(0, groups, group, 0)


def pair_lanes(step, pair):
    return pl.ds(pl.multiple_of(step * GROUP * HDIM + pair * LANES, LANES), LANES)


def attention(queries, keys, values, bias, mask, fetch):
    rows, width = queries.shape
    length = keys.shape[0]
    heads = width // HDIM
    (out, probs, peak, *fetched), _ = call(
        attention_kernel,
        "attention",
        [whole(array) for array in (queries, keys, values, bias, mask)],
        [
            whole_out((rows, width), LOW),
            whole_out((heads, rows, length), LOW),
            whole_out((heads // GROUP, 8, LANES), FULL),
        ],
        us=4.5,
        vmem=10,
        far_out=(1,),
        fetch=fetch,
    )
    return out, probs, peak, *fetched


def attention_back_kernel(
    q_ref, k_ref, v_ref, probs_ref, grad_ref, dq_ref, dk_ref, dv_ref, lines_ref
):
    groups = lines_ref.shape[0]
    rows, length = probs_ref.shape[1:]
    scale = HDIM**-0.5

    def group(step, _):
        for pair in range(GROUP // 2):
            lanes = pair_lanes(step, pair)
            queries, keys, values, grad = (
                ref[:, lanes] for ref in (q_ref, k_ref, v_ref, grad_ref)
            )
            dq, dk, dv = [], [], []
            for half in range(2):
                at = 2 * pair + half
                own = half_lanes(half, grad.shape)
                dp = dot_back(jnp.where(own, grad, jnp.zeros_like(grad)), values)
                probs_low = probs_ref[step * GROUP + at]
                probs = probs_low.astype(FULL)
                ds = probs * (dp - jnp.sum(probs * dp, axis=1, keepdims=True))
                ds_low = ds.astype(LOW)
                dq.append(dot_rows(ds_low, keys))
                dk.append(transpose_dot(ds_low, queries))
                dv.append(transpose_dot(probs_low, grad))
                wide = jnp.concatenate([ds, jnp.zeros((rows, rows), FULL)], axis=1)
                total = wide[rows - 8 :, :]
                for start in range(0, rows - 8, 8):
                    total = total + pltpu.roll(wide[start : start + 8, :], rows - 8 - start, 1)
                line = lax.broadcasted_iota(jnp.int32, total.shape, 0)
                for bit in (1, 2, 4):
                    total = jnp.where(((7 - line) & bit) != 0, pltpu.roll(total, bit, 1), total)
                lines_ref[step, at : at + 1, :] = jnp.sum(total, axis=0, keepdims=True)
            first = half_lanes(0, dq[0].shape)
            dq_ref[:, lanes] = (jnp.where(first, dq[0], dq[1]) * scale).astype(LOW)
            first = half_lanes(0, dk[0].shape)
            dk_ref[:, lanes] = (jnp.where(first, dk[0], dk[1]) * scale).astype(LOW)
            dv_ref[:, lanes] = jnp.where(first, dv[0], dv[1]).astype(LOW)
        return 0

    lax.fori_loop(0, groups, group, 0)


def packed_back_kernel(
    q_ref, k_ref, v_ref, probs_ref, grad_ref, branch_ref, hot_ref, gain_ref, out_ref, lines_ref
):
    rows, length = probs_ref.shape[1:]
    ends = [0, rows, rows + length, rows + 2 * length, 2 * rows + 2 * length]
    parts = [out_ref.at[pl.ds(a, b - a), :] for a, b in zip(ends, ends[1:])]
    attention_back_kernel(q_ref, k_ref, v_ref, probs_ref, grad_ref, *parts[:3], lines_ref)
    parts[3][...] = branch_ref[...]
    groups = lines_ref.shape[0]
    width = gain_ref.shape[1]
    devices = out_ref.shape[0] - ends[4]
    own, turns = width // devices, LANES * devices // width
    device = lax.broadcasted_iota(jnp.int32, (devices, width), 0)
    feature = lax.broadcasted_iota(jnp.int32, (devices, width), 1)
    spread = jnp.where(feature // own == device, gain_ref[...], 0.0)
    folded = functools.reduce(
        jnp.add, [spread[:, start : start + LANES] for start in range(0, width, LANES)]
    )
    device = lax.broadcasted_iota(jnp.int32, folded.shape, 0)
    small = folded
    for turn_by in range(1, turns):
        moved = pltpu.roll(folded, LANES - turn_by * own, 1)
        small = jnp.where(device % turns == turn_by, moved, small)
    lines = jnp.concatenate([lines_ref[g, :GROUP, :] for g in range(groups)], axis=0)
    blank = jnp.zeros((LANES - TABLE_LANE - lines.shape[0], lines.shape[1]), FULL)
    lines = jnp.concatenate([jnp.zeros((TABLE_LANE, lines.shape[1]), FULL), lines, blank], axis=0)
    upper = lines.astype(LOW)
    lower = (lines - upper.astype(FULL)).astype(LOW)
    hot = hot_ref[...].astype(LOW)
    small = small + dot_back(hot, upper) + dot_back(hot, lower)
    out_ref[pl.ds(ends[4], devices), :LANES] = small.astype(LOW)


def attention_back(queries, keys, values, probs, grad, token, packed=None):
    rows, width = queries.shape
    length = keys.shape[0]
    heads = width // HDIM
    lines = whole_out((heads // GROUP, 8, length + rows), FULL)
    inputs = [whole(array) for array in (queries, keys, values, probs, grad)]
    if packed is None:
        outs, token = call(
            attention_back_kernel,
            "attention_back",
            inputs,
            [whole_out((size, width), LOW) for size in (rows, length, length)] + [lines],
            token=token,
            us=6.6,
            vmem=16,
        )
        return *outs, token
    branch, hot, gain, devices = packed
    (out, _), token = call(
        packed_back_kernel,
        "attention_back",
        inputs + [whole(branch), whole(hot), whole(gain)],
        [whole_out((2 * rows + 2 * length + devices, width), LOW), lines],
        token=token,
        us=7,
        vmem=16,
    )
    return out, token


def post_kernel(attended_ref, weights_ref, rows_ref, gain_ref, spread_ref, after_ref, *out_refs):
    after = rows_ref[...].astype(FULL) + dot_rows(attended_ref[...], weights_ref[...])
    after_ref[...] = after
    sent = rms_norm(after, gain_ref[...]).astype(LOW)
    size = out_refs[0].shape[0]
    for at, out_ref in enumerate(out_refs):
        out_ref[...] = dot_rows(spread_ref[pl.ds(at * size, size), :], sent).astype(LOW)


def after_attention(attended, weights, rows, gain, spread, experts):
    tokens, width = rows.shape
    (after, *sent), _ = call(
        post_kernel,
        "post",
        [whole(array) for array in (attended, weights, rows, gain, spread)],
        [whole_out((tokens, width), FULL)]
        + [whole_out((spread.shape[0] // experts, width), LOW)] * experts,
        far_out=(0,),
        us=2,
    )
    return after, sent


def gather_kernel(*refs):
    size = refs[0].shape[0]
    for at, ref in enumerate(refs[:-1]):
        refs[-1][pl.ds(at * size, size), :] = ref[...]


def side_by_side(blocks, token):
    size, width = blocks[0].shape
    (out,), token = call(
        gather_kernel,
        "gather",
        [whole(block) for block in blocks],
        [whole_out((len(blocks) * size, width), LOW)],
        token=token,
        us=1,
    )
    return out, token


def expert_part(gate, up, dhid):
    square = gate * gate
    curve = jnp.tanh(GELU_SCALE * gate * (1.0 + GELU_CUBE * square))
    upper = 0.5 * (1.0 + curve)
    gelu = gate * upper
    slope = upper + 0.5 * gate * (1.0 - curve * curve) * (
        GELU_SCALE * (1.0 + 3.0 * GELU_CUBE * square)
    )
    hid = (gelu * up).astype(LOW)
    dgate = (dhid * up * slope).astype(LOW)
    dup = (dhid * gelu).astype(LOW)
    return hid, dgate, dup


def expert_kernel(
    rows_ref, grad_ref, gate_w_ref, up_w_ref, down_w_ref,
    out_ref, back_ref, dgate_ref, dup_ref, hid_ref, turned_ref, out_sum, back_sum,
):
    step = pl.program_id(0)

    @pl.when(step == 0)
    def _():
        out_sum[...] = jnp.zeros_like(out_sum)
        back_sum[...] = jnp.zeros_like(back_sum)

    rows, grad = rows_ref[...], grad_ref[...]
    gate_w, up_w, down_w = gate_w_ref[0], up_w_ref[0], down_w_ref[0]
    hid, dgate, dup = expert_part(
        dot_rows(rows, gate_w), dot_rows(rows, up_w), dot_back(grad, down_w)
    )
    dgate_ref[...] = dgate
    dup_ref[...] = dup
    hid_ref[...] = hid.T
    out_sum[...] += dot_rows(hid, down_w)
    back_sum[...] += dot_back(dgate, gate_w) + dot_back(dup, up_w)

    @pl.when(step == pl.num_programs(0) - 1)
    def _():
        out_ref[...] = out_sum[...].astype(LOW)
        back_ref[...] = back_sum[...].astype(LOW)
        turned_ref[...] = rows_ref[...].T


def expert(rows, grad, w_in, w_down, token):
    count, width = rows.shape
    hidden = w_down.shape[1]
    part = 256
    steps = hidden // part
    return call(
        expert_kernel,
        "expert",
        [
            whole(rows),
            whole(grad),
            (w_in, pl.BlockSpec((1, width, part), lambda i: (0, 0, i))),
            (w_in, pl.BlockSpec((1, width, part), lambda i: (0, 0, i + steps))),
            (w_down, pl.BlockSpec((1, part, width), lambda i: (0, i, 0))),
        ],
        [
            whole_out((count, width), LOW),
            whole_out((count, width), LOW),
            ((count, hidden), LOW, pl.BlockSpec((count, part), lambda i: (0, i))),
            ((count, hidden), LOW, pl.BlockSpec((count, part), lambda i: (0, i))),
            ((hidden, count), LOW, pl.BlockSpec((part, count), lambda i: (i, 0))),
            whole_out((width, count), LOW),
        ],
        grid=(steps,),
        token=token,
        scratch=[pltpu.VMEM((count, width), FULL), pltpu.VMEM((count, width), FULL)],
        vmem=24,
        us=20,
    )


CHUNK = 512
EXPERT_CHUNK = 512
EXPERT_VMEM = 40


def weight_copies(at_ref, w_in_ref, w_down_ref, start, units, gate, up, down, sems):
    width, half = w_in_ref.shape[1], w_down_ref.shape[1] // 2
    first = pl.multiple_of(at_ref[2] * half, LANES) + start
    pairs = []
    for piece in range(4):
        rows = pl.ds(piece * (width // 4), width // 4)
        for part, ref in ((0, gate), (2 * half, up)):
            columns = pl.ds(pl.multiple_of(first + part, LANES), units)
            pairs.append((w_in_ref.at[0, rows, columns], ref.at[rows, :]))
        size = units // 4
        rows = pl.ds(pl.multiple_of(first + piece * size, 16), size)
        pairs.append((w_down_ref.at[0, rows, :], down.at[pl.ds(piece * size, size), :]))
    return [pltpu.make_async_copy(one, two, sems.at[at]) for at, (one, two) in enumerate(pairs)]


def ahead_kernel(at_ref, w_in_ref, w_down_ref, gate_ref, up_ref, down_ref, sems):
    copies = weight_copies(
        at_ref, w_in_ref, w_down_ref, 0, gate_ref.shape[1], gate_ref, up_ref, down_ref, sems
    )
    for copy in copies:
        copy.start()
    for copy in copies:
        copy.wait()


def weights_ahead(at, w_in, w_down, token):
    width = w_in.shape[1]
    return call(
        ahead_kernel,
        "weights_ahead",
        [(w_in, None), (w_down, None)],
        [whole_out((width, EXPERT_CHUNK), LOW)] * 2 + [whole_out((EXPERT_CHUNK, width), LOW)],
        token=token,
        prefetch=(at,),
        scratch=[pltpu.SemaphoreType.DMA((12,))],
        us=2,
    )


def halves_kernel(
    at_ref, x0_ref, x1_ref, g0_ref, g1_ref, gate0_ref, up0_ref, down0_ref, w_in_ref, w_down_ref,
    back_keep, back_send, dgate_ref, dup_ref, turned_ref, hid_out, a_send, a_keep, b_out,
    both_w, du, turned, hid_ref, down_ref, a_sum, b_ref, sems, out_sems,
):
    count, width = x0_ref.shape
    half = hid_ref.shape[1]
    starts = list(range(0, half, EXPERT_CHUNK))
    sizes = [min(EXPERT_CHUNK, half - start) for start in starts]
    loads = [
        weight_copies(
            at_ref, w_in_ref, w_down_ref, start, units,
            both_w.at[:, pl.ds(start, units)],
            both_w.at[:, pl.ds(half + start, units)],
            down_ref.at[pl.ds(start, units), :],
            sems.at[i],
        )
        for i, (start, units) in enumerate(zip(starts, sizes))
        if i > 0
    ]
    for copies in loads:
        for copy in copies:
            copy.start()
    firsts = [
        pltpu.make_async_copy(ref, both_w.at[:, pl.ds(start, sizes[0])], sems.at[0, at])
        for at, (ref, start) in enumerate(((gate0_ref, 0), (up0_ref, half)))
    ]
    for copy in firsts:
        copy.start()
    turned[:, :count] = x0_ref[...].T
    turned[:, count:] = x1_ref[...].T
    kept = [pltpu.make_async_copy(turned, turned_ref, out_sems.at[len(sizes), 0])]
    for i, (start, units) in enumerate(zip(starts, sizes)):
        columns, other = pl.ds(start, units), pl.ds(half + start, units)
        if i == 0:
            gate_w, up_w, down_w = gate0_ref[...], up0_ref[...], down0_ref[...]
        else:
            for copy in loads[i - 1]:
                copy.wait()
            gate_w, up_w, down_w = both_w[:, columns], both_w[:, other], down_ref[columns, :]
        for side, (x_ref, g_ref) in enumerate(((x0_ref, g0_ref), (x1_ref, g1_ref))):
            rows = pl.ds(side * count, count)
            x = x_ref[...]
            hid, dgate, dup = expert_part(
                dot_rows(x, gate_w), dot_rows(x, up_w), dot_back(g_ref[...], down_w)
            )
            hid_ref[rows, columns] = hid
            du[rows, columns] = dgate
            du[rows, other] = dup
        for part, (ref, from_columns) in enumerate(((dgate_ref, columns), (dup_ref, other))):
            copy = pltpu.make_async_copy(
                du.at[:, from_columns], ref.at[:, columns], out_sems.at[i, part]
            )
            copy.start()
            kept.append(copy)
    kept[0].start()
    kept.append(pltpu.make_async_copy(hid_ref, hid_out, out_sems.at[len(sizes), 1]))
    kept[-1].start()
    terms = transpose_dot(hid_ref[:count, :], g0_ref[...])
    terms = terms + transpose_dot(hid_ref[count:, :], g1_ref[...])
    middle, size = width // 2, half // 2
    b_ref[...] = terms[:, middle:].astype(LOW)
    a_sum[...] = terms[:, :middle].astype(LOW)
    own = pl.ds(pl.multiple_of(at_ref[1] * size, 16), size)
    other = pl.ds(pl.multiple_of((1 - at_ref[1]) * size, 16), size)
    sent = [(b_ref, b_out), (a_sum.at[other, :], a_send), (a_sum.at[own, :], a_keep)]
    sent = [
        pltpu.make_async_copy(ref, out, out_sems.at[len(sizes) + 1 + at // 2, at % 2])
        for at, (ref, out) in enumerate(sent)
    ]
    for copy in sent:
        copy.start()
    for copy in firsts:
        copy.wait()
    back_send[...] = dot_back(du[count:, :], both_w[...]).astype(LOW)
    back_keep[...] = dot_back(du[:count, :], both_w[...])
    for copy in kept + sent:
        copy.wait()


def expert_halves(at, rows, grads, firsts, w_in, w_down, token):
    count, width = rows[0].shape
    half = w_down.shape[1] // 2
    chunks = pl.cdiv(half, EXPERT_CHUNK)
    return call(
        halves_kernel,
        "expert_halves",
        [whole(array) for array in (*rows, *grads, *firsts)] + [(w_in, None), (w_down, None)],
        [
            whole_out((count, width), FULL),
            whole_out((count, width), LOW),
            ((2 * count, half), LOW, None),
            ((2 * count, half), LOW, None),
            ((width, 2 * count), LOW, None),
            ((2 * count, half), LOW, None),
            ((half // 2, width // 2), LOW, None),
            ((half // 2, width // 2), LOW, None),
            ((half, width // 2), LOW, None),
        ],
        token=token,
        prefetch=(at,),
        scratch=[
            pltpu.VMEM((width, 2 * half), LOW),
            pltpu.VMEM((2 * count, 2 * half), LOW),
            pltpu.VMEM((width, 2 * count), LOW),
            pltpu.VMEM((2 * count, half), LOW),
            pltpu.VMEM((half, width), LOW),
            pltpu.VMEM((half, width // 2), LOW),
            pltpu.VMEM((half, width // 2), LOW),
            pltpu.SemaphoreType.DMA((chunks, 12)),
            pltpu.SemaphoreType.DMA((chunks + 3, 2)),
        ],
        vmem=EXPERT_VMEM,
        us=20,
    )


def results_kernel(at_ref, hid_out, w_down_ref, keep_out, send_out, hid_ref, down_ref, sum_ref, sems):
    half = down_ref.shape[0]
    size = half // 4
    count = sum_ref.shape[1]
    copies = []
    for side in range(2):
        rows = pl.ds(side * count, count)
        copies.append(pltpu.make_async_copy(hid_out.at[rows, :], hid_ref.at[rows, :], sems.at[4 + side]))
    for piece in range(4):
        rows = pl.ds(pl.multiple_of(at_ref[2] * half + piece * size, 16), size)
        here = down_ref.at[pl.ds(piece * size, size), :]
        copies.append(pltpu.make_async_copy(w_down_ref.at[0, rows, :], here, sems.at[piece]))
    for copy in copies:
        copy.start()
    for copy in copies:
        copy.wait()
    copies = []
    for side, out in ((1, send_out), (0, keep_out)):
        rows = pl.ds(side * count, count)
        sum_ref[side] = dot_rows(hid_ref[rows, :], down_ref[...]).astype(LOW)
        copies.append(pltpu.make_async_copy(sum_ref.at[side], out, sems.at[6 + side]))
        copies[-1].start()
    for copy in copies:
        copy.wait()


def expert_results(at, hid, w_down, fetch, token):
    half, width = hid.shape[1], w_down.shape[2]
    shape = (hid.shape[0] // 2, width)
    (keep, send, *fetched), token = call(
        results_kernel,
        "expert_results",
        [(hid, None), (w_down, None)],
        [(shape, LOW, None)] * 2,
        token=token,
        prefetch=(at,),
        scratch=[
            pltpu.VMEM(hid.shape, LOW),
            pltpu.VMEM((half, width), LOW),
            pltpu.VMEM((2, *shape), LOW),
            pltpu.SemaphoreType.DMA((8,)),
        ],
        vmem=16,
        us=0.01,
        fetch=fetch,
    )
    return keep, send, *fetched, token


def block_of(at_ref, k, blocks):
    return lax.rem(at_ref[3] + (blocks - k), blocks)


def join_kernel(at_ref, kept_ref, got_ref, out_ref):
    blocks, size, _ = out_ref.shape
    for k in range(blocks):
        rows = pl.ds(k * size, size)
        total = kept_ref[rows, :] + got_ref[rows, :].astype(FULL)
        out_ref[block_of(at_ref, k, blocks)] = total.astype(LOW)


def join(at, kept, got, blocks, token):
    rows, width = kept.shape
    (out,), token = call(
        join_kernel,
        "join",
        [whole(kept), whole(got)],
        [whole_out((blocks, rows // blocks, width), LOW)],
        token=token,
        prefetch=(at,),
        far_out=(0,),
        us=1,
    )
    return out, token


def join_peak_kernel(at_ref, kept_ref, got_ref, peak_ref, out_ref):
    blocks, size, width = out_ref.shape
    rows = kept_ref.shape[0] // blocks
    best = jnp.concatenate([peak_ref[g, :GROUP, :] for g in range(peak_ref.shape[0])], axis=0)
    best = jnp.broadcast_to(jnp.max(best, axis=1, keepdims=True), (size - rows, LANES))
    upper = best.astype(LOW)
    lower = (best - upper.astype(FULL)).astype(LOW)
    for k in range(blocks):
        part = pl.ds(k * rows, rows)
        to = block_of(at_ref, k, blocks)
        total = kept_ref[part, :].astype(FULL) + got_ref[part, :].astype(FULL)
        out_ref[to, :rows, :] = total.astype(LOW)
        out_ref[to, rows:, :] = jnp.zeros((size - rows, width), LOW)
        out_ref[to, rows:, :LANES] = upper
        out_ref[to, rows:, LANES : 2 * LANES] = lower


def join_peak(at, kept, got, peak, blocks, token):
    rows, width = kept.shape
    heads = peak.shape[0] * GROUP
    (out,), token = call(
        join_peak_kernel,
        "join_peak",
        [whole(kept), whole(got), whole(peak)],
        [whole_out((blocks, rows // blocks + heads, width), LOW)],
        token=token,
        prefetch=(at,),
        far_out=(0,),
        us=0.01,
        far_in=(0,),
    )
    return out, token


def larger_kernel(one_ref, two_ref, out_ref):
    out_ref[...] = jnp.maximum(one_ref[...], two_ref[...])


def larger(one, two, token):
    (out,), token = call(
        larger_kernel,
        "larger",
        [whole(one), whole(two)],
        [whole_out(one.shape, FULL)],
        token=token,
        us=0.5,
    )
    return out, token


def place():
    dp = lax.axis_index("dp")
    return lax.axis_index("ctx"), lax.axis_index("exp"), dp // 2, dp % 2


def to_down_plane(array):
    pairs = [
        ((1 - core) * 4 + x * 2 + core, core * 4 + x * 2 + core)
        for core in range(2)
        for x in range(2)
    ]
    return lax.ppermute(array, ("ctx", "dp"), pairs)


def in_down_plane(array):
    pairs = [
        (core * 4 + x * 2 + core, core * 4 + (1 - x) * 2 + core)
        for core in range(2)
        for x in range(2)
    ]
    return lax.ppermute(array, ("ctx", "dp"), pairs)


def in_kernel(
    at_ref, turned_ref, gate_ref, up_ref, *refs,
):
    out_refs, turned, near, results, sems, out_sems = refs[:4], *refs[4:]
    half = gate_ref.shape[1]
    ends = [CHUNK // 2] + list(range(3 * CHUNK // 2, half, CHUNK)) + [half]
    starts = [0] + ends[:-1]
    loads = []
    for at, (ref, to) in enumerate(((gate_ref, near.at[0]), (up_ref, near.at[1]))):
        for i, start in enumerate(starts):
            columns = pl.ds(start, ends[i] - start)
            loads.append(
                pltpu.make_async_copy(ref.at[:, columns], to.at[:, columns], sems.at[at, i])
            )
    whole_load = pltpu.make_async_copy(turned_ref, turned, sems.at[2, 0])
    whole_load.start()
    loads[0].start()
    loads[len(starts)].start()
    whole_load.wait()
    size = turned.shape[0] // 4
    stores = []
    for i, start in enumerate(starts):
        columns = pl.ds(start, ends[i] - start)
        loads[i].wait()
        loads[len(starts) + i].wait()
        if i + 1 < len(starts):
            loads[i + 1].start()
            loads[len(starts) + i + 1].start()
        for block in range(4):
            ry, rx = block // 2, block % 2
            chip = (at_ref[0] ^ ry) * 2 + (at_ref[1] ^ rx)
            rows = turned[pl.ds(pl.multiple_of(chip * size, size), size), :]
            a, b = 1 - rx, 2 + 1 - ry
            results[a, ry, :, columns] = dot_rows(rows, near[0, :, columns]).astype(LOW)
            results[b, rx, :, columns] = dot_rows(rows, near[1, :, columns]).astype(LOW)
        for at, ref in enumerate(out_refs):
            copy = pltpu.make_async_copy(
                results.at[at, :, :, columns], ref.at[:, :, columns], out_sems.at[at, i]
            )
            copy.start()
            stores.append(copy)
    for copy in stores:
        copy.wait()


def in_terms(at, turned, gate, up, token):
    width, count = turned.shape
    half = gate.shape[1]
    shape = (2, width // 4, half)
    chunks = pl.cdiv(half, CHUNK) + 1
    return call(
        in_kernel,
        "in_terms",
        [(turned, None), (gate, None), (up, None)],
        [(shape, LOW, None)] * 4,
        token=token,
        prefetch=(at,),
        scratch=[
            pltpu.VMEM((width, count), LOW),
            pltpu.VMEM((2, count, half), LOW),
            pltpu.VMEM((4, *shape), LOW),
            pltpu.SemaphoreType.DMA((3, chunks)),
            pltpu.SemaphoreType.DMA((4, chunks)),
        ],
        vmem=20,
        us=0.01,
    )


def plane_first(parts):
    a_send, a_keep, b_send, b_keep = parts
    return swapped(a_send, "dp", 2), a_keep, swapped(b_send, "ctx", 1), b_keep


def second_kernel(*refs):
    (a_ref, a_keep_ref, b_ref, b_keep_ref), (a_send_ref, b_send_ref) = refs[:4], refs[-2:]
    rows = a_ref.shape[0]
    total = a_keep_ref[...].astype(FULL) + a_ref[...].astype(FULL)
    a_send_ref[pl.ds(0, rows), :] = total.astype(LOW)
    b_send_ref[...] = (b_keep_ref[...].astype(FULL) + b_ref[...].astype(FULL)).astype(LOW)
    for beside in refs[4:-2]:
        more, width = beside.shape
        a_send_ref[pl.ds(rows, more), pl.ds(0, width)] = beside[...]


def plane_second(parts, token, us, beside=()):
    extra = sum(part.shape[0] for part in beside)
    (_, a_rows, a_width), (_, b_rows, b_width) = parts[0].shape, parts[2].shape
    (a_send, b_send), token = call(
        second_kernel,
        "second_terms",
        [whole(part) for part in (*parts, *beside)],
        [whole_out((a_rows + extra, a_width), LOW), whole_out((b_rows, b_width), LOW)],
        token=token,
        us=us,
        far_in=tuple(range(4, 4 + len(beside))),
        part_in={at: (1,) for at in range(4)},
        far_out=(0, 1),
        vmem=10,
    )
    return a_send, b_send, token


def down_second_kernel(at_ref, a_ref, a_keep_ref, b_ref, b_keep_ref, a_send_ref, b_send_ref):
    size = b_send_ref.shape[0]
    rows = pl.ds(pl.multiple_of((1 - at_ref[1]) * size, 16), size)
    a_send_ref[...] = (a_keep_ref[...].astype(FULL) + a_ref[...].astype(FULL)).astype(LOW)
    b_send_ref[...] = (b_keep_ref[rows, :].astype(FULL) + b_ref[rows, :].astype(FULL)).astype(LOW)


def down_second(at, parts, token, us):
    shape = parts[0].shape
    (a_send, b_send), token = call(
        down_second_kernel,
        "down_second",
        [whole(part) for part in parts],
        [whole_out(shape, LOW)] * 2,
        token=token,
        prefetch=(at,),
        us=us,
        far_out=(0, 1),
    )
    return a_send, b_send, token


def pair_last_kernel(a_ref, a_keep_ref, b_ref, b_keep_ref, a2_ref, b2_ref, out_ref):
    blocks = out_ref.shape[0]
    a, b = (
        sum(ref[...].astype(FULL) for ref in refs)
        for refs in ((a_keep_ref, a_ref, a2_ref), (b_keep_ref, b_ref, b2_ref))
    )
    size = b.shape[0] // blocks
    for z in range(blocks):
        here = slice(z * size, (z + 1) * size)
        out_ref[z, :size, :] = a[here].astype(LOW)
        small = jnp.broadcast_to(a[blocks * size + z : blocks * size + z + 1], (EXTRA, a.shape[1]))
        out_ref[z, size : size + EXTRA, :] = small.astype(LOW)
        out_ref[z, size + EXTRA :, :] = b[here].astype(LOW)


def pair_last(parts, a2, b2, blocks, token):
    rows, width = b2.shape
    (out,), token = call(
        pair_last_kernel,
        "pair_last",
        [whole(part) for part in (*parts, a2, b2)],
        [whole_out((blocks, 2 * rows // blocks + EXTRA, width), LOW)],
        token=token,
        part_in={at: (0,) for at in range(4)},
        far_out=(0,),
        us=8,
        vmem=12,
    )
    return out, token


def down_last_kernel(
    at_ref, a_ref, a_keep_ref, b_ref, b_keep_ref, a2_ref, b2_ref, keep_ref, send_ref
):
    size, width = keep_ref.shape
    half = width // 2
    for out_ref, core in ((send_ref, 1 - at_ref[2]), (keep_ref, at_ref[2])):
        rows = pl.ds(pl.multiple_of(core * size, 16), size)
        there = pl.ds(pl.multiple_of((at_ref[1] * 2 + core) * size, 16), size)
        for first, refs in (
            (0, ((a_ref, rows), (a_keep_ref, rows), (a2_ref, rows))),
            (half, ((b_ref, there), (b_keep_ref, there), (b2_ref, rows))),
        ):
            total = sum(ref[cut, :].astype(FULL) for ref, cut in refs)
            out_ref[:, first : first + half] = total.astype(out_ref.dtype)


def down_last(at, parts, a2, b2, token):
    rows, half = a2.shape
    shape = (rows // 2, 2 * half)
    (keep, send), token = call(
        down_last_kernel,
        "down_last",
        [whole(array) for array in (*parts, a2, b2)],
        [whole_out(shape, FULL), whole_out(shape, LOW)],
        token=token,
        prefetch=(at,),
        us=0.01,
        far_out=(0, 1),
    )
    return keep, send, token


def in_last_kernel(
    at_ref, a_ref, a_keep_ref, b_ref, b_keep_ref, a2_ref, b2_ref, keep_ref, send_ref
):
    size = keep_ref.shape[1]
    for out_ref, core in ((send_ref, 1 - at_ref[2]), (keep_ref, at_ref[2])):
        rows = pl.ds(pl.multiple_of(core * size, 16), size)
        for part, refs in enumerate(((a_ref, a_keep_ref, a2_ref), (b_ref, b_keep_ref, b2_ref))):
            total = sum(ref[rows, :].astype(FULL) for ref in refs)
            out_ref[part] = total.astype(out_ref.dtype)


def in_last(at, parts, a2, b2, token):
    rows, half = b2.shape
    shape = (2, rows // 2, half)
    (keep, send), token = call(
        in_last_kernel,
        "in_last",
        [whole(array) for array in (*parts, a2, b2)],
        [whole_out(shape, FULL), whole_out(shape, LOW)],
        token=token,
        prefetch=(at,),
        us=8,
        part_in={at: (0,) for at in range(4)},
        far_out=(0, 1),
        vmem=16,
    )
    return keep, send, token


def finish_kernel(
    at_ref, in_ref, down_ref, in_got_ref, down_got_ref, in_out, down_out, in_near, down_near, sems
):
    half = in_ref.shape[2]
    for part in range(2):
        other = in_got_ref[part].astype(FULL)
        for first, value in ((at_ref[2], in_ref[part]), (1 - at_ref[2], other)):
            column = pl.multiple_of((part * 2 + first) * half, LANES)
            in_near[:, pl.ds(column, half)] = value
    copies = [pltpu.make_async_copy(in_near, in_out.at[0], sems.at[0])]
    copies[0].start()
    mine = at_ref[0] == at_ref[2]
    down_near[...] = jnp.where(mine, down_ref[...], down_got_ref[...].astype(FULL))
    copies.append(pltpu.make_async_copy(down_near, down_out.at[0], sems.at[1]))
    copies[1].start()
    for copy in copies:
        copy.wait()


def finish(at, in_keep, down_keep, in_got, down_got, token):
    _, size, half = in_keep.shape
    in_shape, down_shape = (size, 4 * half), down_keep.shape
    outs, token = call(
        finish_kernel,
        "finish",
        [whole(array) for array in (in_keep, down_keep, in_got, down_got)],
        [((1, *in_shape), FULL, None), ((1, *down_shape), FULL, None)],
        token=token,
        prefetch=(at,),
        scratch=[
            pltpu.VMEM(in_shape, FULL),
            pltpu.VMEM(down_shape, FULL),
            pltpu.SemaphoreType.DMA((2,)),
        ],
        us=0.01,
        vmem=16,
    )
    return *outs, token


EXTRA = 16
TABLE_LANE = 32


def turn_kernel(at_ref, *refs):
    out_ref, turned = refs[-2:]
    start = 0
    for ref in refs[:-2]:
        turned[:, start : start + ref.shape[0]] = ref[...].T
        start += ref.shape[0]
    size = out_ref.shape[0] // 16
    for to in range(16):
        device = device_at(to % 4, to // 4, at_ref)
        out_ref[pl.ds(to * size, size), :] = turned[pl.ds(device * size, size), :]


def device_at(block, z, at_ref):
    return (
        (at_ref[0] ^ (block // 2)) * 16 + z * 4 + (at_ref[1] ^ (block % 2)) * 2 + at_ref[2]
    )


def turn(at, parts, token):
    count, width = sum(part.shape[0] for part in parts), parts[0].shape[1]
    (out,), token = call(
        turn_kernel,
        "turn",
        [whole(part) for part in parts],
        [whole_out((width // 2, count), LOW)],
        token=token,
        prefetch=(at,),
        scratch=[pltpu.VMEM((width, count), LOW)],
        us=2,
        far_out=(0,),
    )
    return out, token


def shared_kernel(
    at_ref, left_ref, own_ref, other_ref, *refs, experts
):
    out_refs, near_refs, sems = refs[:4], refs[4:8], refs[8]
    a_send_ref, a_keep_ref, b_send_ref, b_keep_ref = near_refs
    copies = []

    def leave(step, rows):
        for at, (near, out) in enumerate(zip(near_refs, out_refs)):
            if rows.start < near.shape[1]:
                part = pl.ds(rows.start, rows.stop - rows.start)
                copy = pltpu.make_async_copy(
                    near.at[:, part, :], out.at[:, part, :], sems.at[at, step]
                )
                copy.start()
                copies.append(copy)

    rows, count = left_ref.shape[0] // experts, left_ref.shape[1] // 2
    width = own_ref.shape[1]
    tokens = count // 3
    size = rows // 4
    small = own_ref[6 * tokens :, :LANES].astype(FULL) + other_ref[6 * tokens :, :LANES].astype(FULL)
    place = lax.broadcasted_iota(jnp.int32, small.shape, 0)
    for z in range(experts):
        left = left_ref[pl.ds(z * rows, rows), :]

        def product(columns, start, length):
            right = slice(start, start + length)
            one = left[:, columns : columns + length]
            two = left[:, count + columns : count + columns + length]
            total = dot_rows(one, own_ref[right, :]) + dot_rows(two, other_ref[right, :])
            return total.astype(LOW)

        a_terms = product(2 * tokens, 5 * tokens, tokens), product(tokens, 0, tokens)
        b_terms = product(0, tokens, 2 * tokens), product(0, 3 * tokens, 2 * tokens)
        for block in range(4):
            ry, rx = block // 2, block % 2
            a_ref = (a_send_ref if rx else a_keep_ref).at[ry]
            b_ref = (b_send_ref if ry else b_keep_ref).at[rx]
            here = slice(block * size, (block + 1) * size)
            for at in range(2):
                to = pl.ds((2 * z + at) * size, size)
                a_ref[to, :] = a_terms[at][here]
                b_ref[to, :] = b_terms[at][here]
        leave(z, slice(2 * z * size, 2 * (z + 1) * size))
    line = lax.broadcasted_iota(jnp.int32, (EXTRA, LANES), 0)
    for block in range(4):
        ry, rx = block // 2, block % 2
        a_ref = (a_send_ref if rx else a_keep_ref).at[ry]
        rows_here = jnp.zeros((EXTRA, LANES), FULL)
        for z in range(experts):
            row = jnp.where(place == device_at(block, z, at_ref), small, 0.0)
            rows_here = jnp.where(line == z, jnp.sum(row, 0, keepdims=True), rows_here)
        a_ref[2 * size * experts :, :] = jnp.zeros((EXTRA, width), LOW)
        a_ref[2 * size * experts :, :LANES] = rows_here.astype(LOW)
    leave(experts, slice(2 * size * experts, 2 * size * experts + EXTRA))
    for copy in copies:
        copy.wait()


def shared_terms(at, left, own, other, experts, token):
    rows = left.shape[0]
    width = own.shape[1]
    b_shape = (2, rows // 2, width)
    a_shape = (2, rows // 2 + EXTRA, width)
    return call(
        functools.partial(shared_kernel, experts=experts),
        "shared_terms",
        [whole(array) for array in (left, own, other)],
        [(shape, LOW, None) for shape in (a_shape, a_shape, b_shape, b_shape)],
        token=token,
        prefetch=(at,),
        scratch=[pltpu.VMEM(shape, LOW) for shape in (a_shape, a_shape, b_shape, b_shape)]
        + [pltpu.SemaphoreType.DMA((4, experts + 1))],
        us=0.01,
        vmem=16,
    )


def rows_kernel(
    place_ref, plane_ref, w_query_ref, w_key_ref, w_value_ref, gain_ref,
    query_ref, key_ref, value_ref, out_ref, gain_grad_ref, ffn_ref, table_ref,
    near_query, near_key, near_value, sems,
):
    rows = query_ref.shape[0]
    at = pl.ds(pl.multiple_of(place_ref[0] * rows, rows), rows)
    pairs = ((w_query_ref, near_query), (w_key_ref, near_key), (w_value_ref, near_value))
    copies = [
        pltpu.make_async_copy(ref.at[at, :], near, sems.at[number])
        for number, (ref, near) in enumerate(pairs)
    ]
    for copy in copies:
        copy.start()
    total = sum(plane_ref[block].astype(FULL) for block in range(plane_ref.shape[0]))
    out_ref[...] = total[:rows]
    query = total[rows : 2 * rows]
    key, value = (
        total[start + EXTRA : start + EXTRA + rows] for start in (2 * rows, 3 * rows)
    )
    query_ref[...] = query
    key_ref[...] = key
    value_ref[...] = value
    small = total[2 * rows : 2 * rows + 1, :LANES]
    ffn_ref[...] = small
    table_ref[...] = pltpu.roll(jnp.broadcast_to(small, (8, LANES)), LANES - TABLE_LANE, 1)[:1]
    for copy in copies:
        copy.wait()
    sums = query * near_query[...].astype(FULL) + key * near_key[...].astype(FULL)
    sums = jnp.sum(sums + value * near_value[...].astype(FULL), axis=1, keepdims=True)
    lane = lax.broadcasted_iota(jnp.int32, (rows, LANES), 1)
    line = lax.broadcasted_iota(jnp.int32, (rows, LANES), 0)
    spread = jnp.sum(jnp.where(lane == line, sums, 0.0), 0, keepdims=True)
    device = place_ref[0]
    block = gain_ref[pl.ds(device * rows // LANES, 1), :]
    gain = pltpu.roll(jnp.broadcast_to(block, (8, LANES)), LANES - device * rows % LANES, 1)[:1]
    gain_grad_ref[...] = spread / gain


def last_rows(place_all, plane, rows, weights, gain, token):
    width = plane.shape[2]
    small = whole_out((1, LANES), FULL)
    outs, token = call(
        rows_kernel,
        "last_rows",
        [whole(plane)] + [(array, None) for array in weights] + [whole(gain.reshape(-1, LANES))],
        [whole_out((rows, width), FULL)] * 4 + [small] * 3,
        token=token,
        prefetch=(place_all.reshape(1),),
        scratch=[pltpu.VMEM((rows, width), LOW)] * 3 + [pltpu.SemaphoreType.DMA((3,))],
        us=0.01,
    )
    return outs, token


def clip_kernel(query_ref, key_ref, peak_ref, level_ref, query_out, key_out, factor_ref):
    heads = peak_ref.shape[0]
    width = query_ref.shape[1]
    level = jnp.sum(jnp.where(eye(heads), level_ref[...], 0.0), 1, keepdims=True)
    factor = level / jnp.maximum(peak_ref[:, :1], level)
    factor_ref[...] = jnp.broadcast_to(factor, (heads, LANES))
    head = lax.broadcasted_iota(jnp.int32, (heads, width), 0)
    lane = lax.broadcasted_iota(jnp.int32, (heads, width), 1)
    scale = jnp.sum(jnp.where(lane // HDIM == head, jnp.sqrt(factor), 0.0), 0, keepdims=True)
    query_out[...] = query_ref[...].astype(FULL) * scale
    key_out[...] = key_ref[...].astype(FULL) * scale


def clip(w_query, w_key, peak, level, token):
    rows, width = w_query.shape
    spec = pl.BlockSpec((rows // 4, width), lambda i: (i, 0))
    outs, token = call(
        clip_kernel,
        "clip",
        [(w_query, spec), (w_key, spec), whole(peak), whole(level.reshape(1, -1))],
        [((rows, width), FULL, spec)] * 2 + [whole_out(peak.shape, FULL)],
        grid=(4,),
        token=token,
        us=0.01,
        vmem=16,
    )
    return outs, token


def normed_kernel(
    packed_ref, w_query_ref, w_key_ref, w_value_ref, own_ref, other_ref, near, sems
):
    copies = [
        pltpu.make_async_copy(ref, near.at[at], sems.at[at])
        for at, ref in enumerate((w_key_ref, w_value_ref, w_query_ref))
    ]
    for copy in copies:
        copy.start()
    tokens = own_ref.shape[0]
    dq, dk, dv = (
        packed_ref[pl.ds(start * tokens, size * tokens), :]
        for start, size in ((0, 1), (1, 2), (3, 2))
    )
    copies[0].wait()
    total = dot_back(dk, near[0])
    copies[1].wait()
    total = total + dot_back(dv, near[1])
    other_ref[...] = total[:tokens].astype(LOW)
    copies[2].wait()
    own_ref[...] = total[tokens:] + dot_back(dq, near[2])


def normed_grads(packed, weights, tokens, token):
    width = packed.shape[1]
    (own, other), token = call(
        normed_kernel,
        "normed_grads",
        [whole(packed)] + [(array, None) for array in weights],
        [whole_out((tokens, width), FULL), whole_out((tokens, width), LOW)],
        token=token,
        scratch=[pltpu.VMEM((3, width, width), LOW), pltpu.SemaphoreType.DMA((3,))],
        far_out=(0, 1),
        us=0.01,
        vmem=14,
    )
    return own, other, token


def input_kernel(rows_ref, gain_ref, own_ref, got_ref, past_ref, out_ref):
    rows = rows_ref[...].astype(FULL)
    inverse = lax.rsqrt(jnp.mean(rows * rows, axis=1, keepdims=True) + EPSILON)
    scaled = rows * inverse
    grad = (own_ref[...] + got_ref[...].astype(FULL)) * gain_ref[...]
    along = jnp.mean(scaled * grad, axis=1, keepdims=True)
    out_ref[0] = past_ref[...] + inverse * (grad - scaled * along)


def input_grads(rows, gain, own, got, past, token):
    tokens, width = rows.shape
    (out,), token = call(
        input_kernel,
        "input_grads",
        [whole(array) for array in (rows, gain, own, got, past)],
        [whole_out((1, tokens, width), FULL)],
        token=token,
        far_in=(0, 1, 2, 4),
        far_out=(0,),
        us=10,
    )
    return out, token


def back_kernel(
    at_ref, spread_ref, rows_ref, after_ref, gain_ref, grad_ref, weights_ref,
    total_ref, branch_ref, attended_ref, gain_grad_ref,
):
    rows = after_ref[...]
    inverse = lax.rsqrt(jnp.mean(rows * rows, axis=1, keepdims=True) + EPSILON)
    scaled = rows * inverse
    blocks, size, _ = rows_ref.shape
    grad = sum(
        transpose_dot(spread_ref[pl.ds(k * size, size), :], rows_ref[lax.rem(at_ref[3] + k, blocks)])
        for k in range(blocks)
    )
    gain_grad_ref[...] = jnp.sum(scaled * grad, axis=0, keepdims=True)
    grad = grad * gain_ref[...]
    along = jnp.mean(scaled * grad, axis=1, keepdims=True)
    total = grad_ref[...].astype(FULL) + inverse * (grad - scaled * along)
    total_ref[...] = total
    branch = total.astype(LOW)
    branch_ref[...] = branch
    attended_ref[...] = dot_back(branch, weights_ref[...]).astype(LOW)


def back_to_attention(at, spread, rows, after, gain, grad, weights, fetch, token):
    shape = after.shape
    inputs = (spread, rows, after, gain, grad, weights)
    return call(
        back_kernel,
        "back",
        [whole(array) for array in inputs],
        [
            whole_out(shape, FULL),
            whole_out(shape, LOW),
            whole_out(shape, LOW),
            whole_out((1, shape[1]), FULL),
        ],
        token=token,
        vmem=16,
        us=0.01,
        far_in=(0, 2, 4),
        far_out=(0,),
        prefetch=(at,),
        fetch=fetch,
    )


def mix_kernel(at_ref, pick_ref, rows_ref, gates_ref, after_ref, out_ref, peak_ref):
    top, tokens = gates_ref.shape
    blocks = rows_ref.shape[0]
    size = pick_ref.shape[0] // blocks
    total = after_ref[...]
    gates = [to_column(gates_ref[r : r + 1, :]) for r in range(top)]
    for block in range(blocks):
        rows = rows_ref[lax.rem(at_ref[3] + block, blocks), :size, :]
        for r in range(top):
            pick = pick_ref[pl.ds(block * size, size), pl.ds(r * tokens, tokens)]
            total = total + gates[r] * transpose_dot(pick, rows)
    out_ref[0] = total.astype(LOW)
    if rows_ref.shape[1] > size:
        peaks = [
            rows_ref[block, size:, :LANES].astype(FULL)
            + rows_ref[block, size:, LANES : 2 * LANES].astype(FULL)
            for block in range(blocks)
        ]
        peak_ref[...] = functools.reduce(jnp.maximum, peaks)


def mix(at, pick, rows, gates, after, token):
    (out, peak), token = call(
        mix_kernel,
        "mix",
        [whole(pick), whole(rows), whole(gates), whole(after)],
        [whole_out((1, *after.shape), LOW), whole_out((16, LANES), FULL)],
        token=token,
        us=0.01,
        far_in=(0, 3),
        prefetch=(at,),
    )
    return out, peak, token


def local(
    block_in,
    seg_ids,
    routes,
    gates,
    buckets,
    norm_attn,
    norm_ffn,
    w_query,
    w_key,
    w_value,
    w_out_attn,
    rel_bias,
    clip_level,
    w_in,
    w_down,
    cotangent,
):
    tokens, width = block_in.shape[1:]
    heads = width // HDIM
    n_ctx, experts, n_dp = (lax.axis_size(axis) for axis in ("ctx", "exp", "dp"))
    fast = (n_ctx, experts, n_dp) == (2, 4, 4)
    devices = n_ctx * experts * n_dp
    length = n_ctx * tokens
    y, z, x, core = place()
    place_all = (y * experts + z) * n_dp + lax.axis_index("dp")
    top_count = routes.shape[-1]
    capacity = tokens * top_count * 3 // (2 * experts)
    at = jnp.stack([y, x, core, z])

    (spread, pick, mask, rows_copy, *grad_out), token = front(
        at, routes[0].T, gates[0].T, cotangent[0], seg_ids, block_in[0], experts, capacity
    )
    backs = list(range(n_ctx - 1, 0, -1))
    earlier = [
        lax.ppermute(block_in[0], "ctx", [(i, (i + back) % n_ctx) for i in range(n_ctx)])
        for back in backs
    ]
    grad_blocks = to_experts(grad_out)
    bucket_hot, bias, normed_all, queries, keys, values = project(
        buckets.reshape(1, length),
        rel_bias.reshape(NB, heads),
        norm_attn.reshape(1, width),
        (*earlier, block_in[0]),
        (w_query, w_key, w_value),
    )

    attended, probs, peak_lanes, w_out_near = attention(
        queries, keys, values, bias, mask, (w_out_attn,)
    )
    after, sent = after_attention(
        attended, w_out_near, rows_copy, norm_ffn.reshape(1, width), spread, experts
    )

    row_blocks = to_experts(sent)
    own_gain, own_table = width // devices, NB * heads // devices
    if fast:
        expert_grad, token = side_by_side(grad_blocks, token)
        parts = (normed_all, attended)
        parts = parts + tuple(swapped(part, "dp", 1) for part in parts)
        left, token = turn(at, parts, token)
        peak, token = larger(peak_lanes, swapped(peak_lanes, "dp", 1), token)
        peak, token = larger(peak, swapped(peak, "dp", 2), token)
        peak, token = larger(peak, swapped(peak, "ctx", 1), token)
        expert_rows, token = side_by_side(row_blocks, token)
        both_rows = expert_rows, swapped(expert_rows, "dp", 1)
        both_grads = expert_grad, swapped(expert_grad, "dp", 1)
        firsts, token = weights_ahead(at, w_in, w_down, token)
        outs, token = expert_halves(at, both_rows, both_grads, firsts, w_in, w_down, token)
        back_keep, back_send, dgate, dup, rows_turned, hid, *down = outs
        back_got = swapped(back_send, "dp", 1)
        down = swapped(down[0], "dp", 2), down[1], to_down_plane(down[2]), down[2]
        back_rows, token = join(at, back_keep, back_got, experts, token)
        back_home = over_experts(back_rows)
        first, token = in_terms(at, rows_turned, dgate, dup, token)
        first = plane_first(first)
        down_a, down_b, token = down_second(at, down, token, 5)
        out_keep, out_send, w_out_near, token = expert_results(at, hid, w_down, (w_out_attn,), token)
    else:
        expert_rows = jnp.concatenate(row_blocks, axis=0)
        expert_grad = jnp.concatenate(grad_blocks, axis=0)
        (out_rows, back_rows, dgate, dup, hid_turned, rows_turned), token = expert(
            expert_rows, expert_grad, w_in, w_down, token
        )
        expert_first, expert_second = (
            lax.psum_scatter(grads, ("ctx", "dp"), scatter_dimension=0, tiled=True)[None]
            for grads in (
                dot_rows(rows_turned, jnp.concatenate([dgate, dup], axis=1)),
                dot_rows(hid_turned, expert_grad),
            )
        )
        back_home, out_home = (
            jnp.stack(from_experts(list(rows.reshape(experts, capacity, width))))
            for rows in (back_rows, out_rows)
        )

    home = at if fast else jnp.zeros_like(at)
    soon = (queries, keys, values, probs) + ((bucket_hot,) if fast else ())
    (grad_after, grad_branch, grad_attended, grad_gain_ffn, *soon), token = back_to_attention(
        home, spread, back_home, after, norm_ffn.reshape(1, width), cotangent[0], w_out_near, soon, token
    )
    if fast:
        packed, token = attention_back(
            *soon[:4], grad_attended, token, (grad_branch, soon[4], grad_gain_ffn, devices),
        )
        packed_got = swapped(packed, "dp", 1)
        (left,), token = bring(token, 20, left)
        plane_2, token = shared_terms(at, left, packed, packed_got, experts, token)
        plane_2 = plane_first(plane_2)
        out_send, = hold(token, out_send)
        out_got = swapped(out_send, "dp", 1)
        out_rows, token = join_peak(at, out_keep, out_got, peak, experts, token)
        out_home = over_experts(out_rows)
        normed_own_grad, normed_other_grad, token = normed_grads(
            packed, (w_query, w_key, w_value), tokens, token
        )
        normed_got = lax.ppermute(normed_other_grad, "ctx", [(1, 0)])
        in_a, in_b, token = plane_second(first, token, 0.01)
    else:
        dq, dk, dv, lines, token = attention_back(
            *soon, grad_attended, token
        )
        lines = lines[:, :GROUP, :].reshape(heads, length + tokens)
        grad_table = lax.dot_general(
            bucket_hot, lines, (((1,), (1,)), ((), ())), precision=FULL_PRECISION
        ).reshape(-1)
        mixed, _, _ = mix(home, pick, out_home, gates[0].T, after, token)
        peak = jnp.max(peak_lanes[:, :GROUP, :], axis=-1).reshape(heads)
        peak = lax.pmax(peak, ("ctx", "exp", "dp"))
        peak = jnp.broadcast_to(peak[:, None], (heads, LANES))
        clipped, _ = clip(w_query, w_key, peak, clip_level, token)

        grad_normed = dot_back(dk, w_key) + dot_back(dv, w_value)
        grad_normed_own = grad_normed[length - tokens :] + dot_back(dq, w_query)
        for block, back in enumerate(backs):
            term = grad_normed[block * tokens : (block + 1) * tokens].astype(LOW)
            returned = lax.ppermute(term, "ctx", [((i + back) % n_ctx, i) for i in range(n_ctx)])
            grad_normed_own = grad_normed_own + returned.astype(FULL)
        own_rows = block_in[0].astype(FULL)
        _, norm_pull = jax.vjp(lambda rows: rms_norm(rows, norm_attn), own_rows)
        grad_input = (grad_after + norm_pull(grad_normed_own)[0])[None]

    if fast:
        shared_a, shared_b, token = plane_second(plane_2, token, 10)
        shared_a, shared_b = swapped(shared_a, "ctx", 1), swapped(shared_b, "dp", 2)
        mixed, peak, token = mix(at, pick, out_home, gates[0].T, after, token)
        grad_input, token = input_grads(
            block_in[0], norm_attn.reshape(1, width), normed_own_grad, normed_got, grad_after, token
        )
        in_a, in_b = hold(token, in_a, in_b)
        in_a, in_b = swapped(in_a, "ctx", 1), swapped(in_b, "dp", 2)
        plane, token = pair_last(plane_2, shared_a, shared_b, experts, token)
        plane = over_experts(plane)
        down_a, down_b = hold(token, down_a, down_b)
        down_a, down_b = to_down_plane(down_a), in_down_plane(down_b)
        clipped, token = clip(w_query, w_key, peak, clip_level, token)
        in_keep, in_send, token = in_last(at, first, in_a, in_b, token)
        in_got = swapped(in_send, "dp", 1)
        down_keep, down_send, token = down_last(at, down, down_a, down_b, token)
        down_got = swapped(down_send, "dp", 1)
        (in_keep, down_keep), token = bring(token, 0.01, in_keep, down_keep)
        expert_first, expert_second, token = finish(
            at, in_keep, down_keep, in_got, down_got, token
        )
        outs, token = last_rows(
            place_all, plane, own_gain, (w_query, w_key, w_value), norm_attn, token
        )
        shared_q, shared_k, shared_v, shared_o = outs[:4]
        small_attn, small_ffn = outs[4][0, :own_gain], outs[5][0, :own_gain]
        small_table = outs[6][0, :own_table]
    else:
        shared_q, shared_k, shared_v, shared_o = (
            lax.psum_scatter(grads, ("ctx", "exp", "dp"), scatter_dimension=0, tiled=True)
            for grads in (
                transpose_dot(normed_all[length - tokens :], dq),
                transpose_dot(normed_all, dk),
                transpose_dot(normed_all, dv),
                transpose_dot(attended, grad_branch),
            )
        )
        small_ffn, small_table = (
            lax.dynamic_slice_in_dim(lax.psum(array, ("ctx", "exp", "dp")), place_all * own, own)
            for array, own in ((grad_gain_ffn[0], own_gain), (grad_table, own_table))
        )
        pairs = ((shared_q, w_query), (shared_k, w_key), (shared_v, w_value))
        row_sums = sum(
            jnp.sum(
                grads * lax.dynamic_slice_in_dim(weights, place_all * own_gain, own_gain).astype(FULL),
                axis=1,
            )
            for grads, weights in pairs
        )
        small_attn = row_sums / lax.dynamic_slice_in_dim(norm_attn, place_all * own_gain, own_gain)

    return (
        mixed,
        grad_input,
        small_attn,
        small_ffn,
        shared_q,
        shared_k,
        shared_v,
        shared_o,
        small_table,
        expert_first,
        expert_second,
        clipped[0],
        clipped[1],
        clipped[2][:, 0],
    )


def solution(mesh):
    tokens = P(("exp", "dp"), "ctx", None)
    everywhere = P(("ctx", "exp", "dp"))
    by_rows = P(("ctx", "exp", "dp"), None)
    by_expert = P("exp", None, None)
    expert_rows = P("exp", ("ctx", "dp"), None)
    in_specs = (tokens, P(("exp", "dp"), None), tokens, tokens) + (P(),) * 9
    in_specs = in_specs + (by_expert, by_expert, tokens)
    out_specs = (tokens, tokens, everywhere, everywhere) + (by_rows,) * 4
    out_specs = out_specs + (everywhere, expert_rows, expert_rows, P(), P(), P())
    return jax.shard_map(local, mesh=mesh, in_specs=in_specs, out_specs=out_specs, check_vma=False)
```

```python
import functools

import jax
import jax.numpy as jnp
from jax import lax
from jax.experimental import pallas as pl
from jax.experimental.pallas import tpu as pltpu
from jax.sharding import PartitionSpec as P

HDIM = 64
NB = 32
GROUP = 4
LANES = 128
EPSILON = 1e-06
FULL_PRECISION = lax.Precision.HIGHEST
LOW = jnp.bfloat16
FULL = jnp.float32
OUTSIDE = -1e30
GELU_SCALE = 0.7978845608028654
GELU_CUBE = 0.044715


def rms_norm(rows, gain):
    return rows * lax.rsqrt(jnp.mean(rows * rows, axis=-1, keepdims=True) + EPSILON) * gain


def dot_rows(left, right):
    return lax.dot_general(left, right, (((1,), (0,)), ((), ())), preferred_element_type=FULL)


def dot_back(left, right):
    return lax.dot_general(left, right, (((1,), (1,)), ((), ())), preferred_element_type=FULL)


def transpose_dot(left, right):
    return lax.dot_general(left, right, (((0,), (0,)), ((), ())), preferred_element_type=FULL)


def swapped(array, axis, bit):
    size = lax.axis_size(axis)
    return lax.ppermute(array, axis, [(i, i ^ bit) for i in range(size)])


def shifted(array, axis, shift):
    size = lax.axis_size(axis)
    return lax.ppermute(array, axis, [(i, (i + shift) % size) for i in range(size)])


def to_experts(blocks):
    return [blocks[0]] + [shifted(blocks[k], "exp", k) for k in range(1, len(blocks))]


def from_experts(blocks):
    return [blocks[0]] + [shifted(blocks[k], "exp", len(blocks) - k) for k in range(1, len(blocks))]


def over_experts(blocks):
    return lax.all_to_all(blocks, "exp", split_axis=0, concat_axis=0, tiled=True)


MICROSECOND = 1.15e9


def call(
    body, name, inputs, outputs, us, grid=None, token=None, prefetch=(), scratch=(), vmem=6,
    near_in=(), near_out=(), far_in=(), far_out=(), fetch=(),
    part_in=None, onto=(),
):
    part_in = dict(part_in or {})
    far_in = tuple(far_in) + tuple(part_in)
    inputs = list(inputs) + [(array, None) for array in fetch]
    outputs = list(outputs) + [whole_out(array.shape, array.dtype) for array in fetch]
    n_pre, n_in, n_out = len(prefetch), len(inputs), len(outputs)
    held = [] if token is None else [token]
    n_far, n_scratch = len(far_in) + len(far_out), len(scratch)

    def kernel(*refs):
        split = n_pre + n_in
        outs = split + len(held)
        rest = refs[outs + n_out + 1 :]
        ins_here, outs_here = list(refs[:split]), list(refs[outs : outs + n_out])
        copies = []
        for number, at in enumerate(far_in):
            here = rest[n_scratch + number]
            source = refs[n_pre + at].at[part_in[at]] if at in part_in else refs[n_pre + at]
            copies.append(pltpu.make_async_copy(source, here, rest[-1].at[number]))
            ins_here[n_pre + at] = here
        for copy in copies:
            copy.start()
        fetches = [
            pltpu.make_async_copy(ins_here.pop(), outs_here.pop(), rest[-1].at[n_far + number])
            for number in range(len(fetch))
        ]
        for copy in fetches:
            copy.start()
        for copy in copies:
            copy.wait()
        copies = []
        for number, at in enumerate(far_out, len(far_in)):
            here = rest[n_scratch + number]
            copies.append(pltpu.make_async_copy(here, refs[outs + at], rest[-1].at[number]))
            outs_here[at] = here
        body(*ins_here, *outs_here, *rest[:n_scratch])
        for copy in fetches:
            copy.wait()
        for copy in copies:
            copy.start()
        for copy in copies:
            copy.wait()

    where = lambda at, near: pltpu.VMEM if at in near else pltpu.HBM
    arrays = [array for array, _ in inputs]
    shapes = [(shape, dtype) for shape, dtype, _ in outputs]
    anywhere = pl.BlockSpec(memory_space=pl.ANY)
    if grid is None:
        near = pl.BlockSpec(memory_space=pltpu.VMEM)
        far = [at in far_in or spec is None for at, (_, spec) in enumerate(inputs)]
        far_results = [at in far_out or spec is None for at, (_, _, spec) in enumerate(outputs)]
        left = lambda at: tuple(
            size if axis >= len(part_in.get(at, ())) else len(range(size)[part_in[at][axis]])
            for axis, size in enumerate(arrays[at].shape)
            if axis >= len(part_in.get(at, ())) or isinstance(part_in[at][axis], slice)
        )
        buffers = [pltpu.VMEM(left(at), arrays[at].dtype) for at in far_in]
        buffers += [pltpu.VMEM(*shapes[at]) for at in far_out]
        n_sems = n_far + len(fetch)
        buffers += [pltpu.SemaphoreType.DMA((n_sems,))] if n_sems else []
        form = dict(
            in_specs=[pl.BlockSpec(memory_space=pltpu.SMEM)] * n_pre
            + [anywhere if away else near for away in far]
            + [anywhere] * len(held),
            out_specs=[anywhere if away else near for away in far_results] + [anywhere],
            scratch_shapes=list(scratch) + buffers,
        )
        arrays = [
            pltpu.with_memory_space_constraint(array, pltpu.HBM) if away else array
            for array, away in zip(arrays, far)
        ]
        shapes = [
            pltpu.HBM(*one) if away else jax.ShapeDtypeStruct(*one)
            for away, one in zip(far_results, shapes)
        ]
    else:
        form = dict(
            grid_spec=pltpu.PrefetchScalarGridSpec(
                num_scalar_prefetch=n_pre,
                grid=grid,
                in_specs=[spec for _, spec in inputs] + [anywhere] * len(held),
                out_specs=[spec for _, _, spec in outputs] + [anywhere],
                scratch_shapes=list(scratch),
            )
        )
        arrays = [
            pltpu.with_memory_space_constraint(array, where(at, near_in))
            for at, array in enumerate(arrays)
        ]
        shapes = [where(at, near_out)(*one) for at, one in enumerate(shapes)]
    held = [pltpu.with_memory_space_constraint(array, pltpu.HBM) for array in held]
    results = pl.pallas_call(
        kernel,
        out_shape=shapes + [pltpu.HBM((8, LANES), FULL)],
        cost_estimate=pl.CostEstimate(
            flops=int(us * MICROSECOND), bytes_accessed=1, transcendentals=0
        ),
        compiler_params=pltpu.CompilerParams(vmem_limit_bytes=vmem * 2**20),
        name=name,
        input_output_aliases={n_pre + one: other for one, other in onto},
        **form,
    )(*prefetch, *arrays, *held)
    return list(results[:-1]), results[-1]


def whole(array):
    return array, pl.BlockSpec(array.shape, lambda *_: (0,) * array.ndim)


def whole_out(shape, dtype):
    return shape, dtype, pl.BlockSpec(shape, lambda *_: (0,) * len(shape))


def hold(token, *arrays):
    anywhere = pl.BlockSpec(memory_space=pl.ANY)
    return pl.pallas_call(
        lambda *refs: None,
        in_specs=[anywhere] * (len(arrays) + 1),
        out_specs=[anywhere] * len(arrays),
        out_shape=[jax.ShapeDtypeStruct(array.shape, array.dtype) for array in arrays],
        input_output_aliases={at + 1: at for at in range(len(arrays))},
        cost_estimate=pl.CostEstimate(flops=1, bytes_accessed=1, transcendentals=0),
        name="hold",
    )(token, *arrays)


def pass_kernel(*refs):
    half = len(refs) // 2
    for ref, out_ref in zip(refs[:half], refs[half:]):
        out_ref[...] = ref[...]


def bring(token, us, *arrays):
    return call(lambda *refs: None, "bring", [], [], token=token, fetch=arrays, us=us)


def pass_on(token, *arrays):
    return call(
        pass_kernel,
        "pass_on",
        [whole(array) for array in arrays],
        [whole_out(array.shape, array.dtype) for array in arrays],
        token=token,
        us=1,
    )


def eye(size):
    rows = lax.broadcasted_iota(jnp.int32, (size, size), 0)
    return rows == lax.broadcasted_iota(jnp.int32, (size, size), 1)


def to_column(row):
    size = row.shape[1]
    return jnp.sum(jnp.where(eye(size), row, jnp.zeros_like(row)), 1, keepdims=True)


def front_kernel(
    at_ref, routes_ref, gates_ref, grad_ref, seg_ref, rows_ref,
    spread_ref, pick_ref, mask_ref, copy_ref, *out_refs,
):
    top, tokens = routes_ref.shape
    experts, capacity = len(out_refs), out_refs[0].shape[0]
    routes = [routes_ref[r : r + 1, :] for r in range(top)]
    gates = [gates_ref[r : r + 1, :] for r in range(top)]
    before = lax.broadcasted_iota(jnp.int32, (tokens, tokens), 0)
    before = before < lax.broadcasted_iota(jnp.int32, (tokens, tokens), 1)
    slots = lax.broadcasted_iota(jnp.int32, (capacity, tokens), 0).astype(FULL)
    for e in range(experts):
        part = pl.ds(e * capacity, capacity)
        name = lax.rem(at_ref[3] + e, experts)
        hits = [jnp.where(route == name, 1.0, 0.0) for route in routes]
        named = functools.reduce(jnp.add, hits)
        slot = jnp.sum(jnp.where(before, to_column(named), 0.0), 0, keepdims=True)
        place = (slots == slot).astype(FULL)
        spread = place * named
        gate = functools.reduce(jnp.add, [hit * g for hit, g in zip(hits, gates)])
        spread_low = spread.astype(LOW)
        spread_ref[part, :] = spread_low
        for r in range(top):
            pick_ref[part, pl.ds(r * tokens, tokens)] = (place * hits[r]).astype(LOW)
        slot_gate = jnp.sum(spread * gate, 1, keepdims=True)
        out_refs[e][...] = (slot_gate * dot_rows(spread_low, grad_ref[...])).astype(LOW)
    length = mask_ref.shape[1]
    ctx = at_ref[0]
    seg = jnp.broadcast_to(seg_ref[...].astype(FULL), (8, length))
    keys = pltpu.roll(seg, length - (ctx + 1) * tokens, 1)[:1, :]
    at_row = lax.broadcasted_iota(jnp.int32, (tokens, length), 0) + (length - tokens)
    at_key = lax.broadcasted_iota(jnp.int32, (tokens, length), 1)
    own = jnp.sum(jnp.where(at_row == at_key, keys, 0.0), 1, keepdims=True)
    allowed = (at_key <= at_row) & (own == keys) & (at_key >= length - (ctx + 1) * tokens)
    mask_ref[...] = jnp.where(allowed, 0.0, OUTSIDE)
    copy_ref[...] = rows_ref[...]


def front(at, routes, gates, grad, seg, rows, experts, capacity):
    top, tokens = routes.shape
    slots = experts * capacity
    return call(
        front_kernel,
        "front",
        [whole(array) for array in (routes, gates, grad, seg, rows)],
        [
            whole_out((slots, tokens), LOW),
            whole_out((slots, top * tokens), LOW),
            whole_out((tokens, seg.shape[1]), FULL),
            whole_out(rows.shape, LOW),
        ]
        + [whole_out((capacity, grad.shape[1]), LOW)] * experts,
        prefetch=(at,),
        far_in=(0, 1, 2, 3, 4),
        far_out=(1,),
        us=1.5,
    )


def project_kernel(buckets_ref, table_ref, gain_ref, *refs, blocks):
    x_refs, weights = refs[:blocks], refs[blocks : blocks + 3]
    hot_ref, bias_ref, normed_ref, q_ref, k_ref, v_ref, near, sems = refs[blocks + 3 :]
    copies = [
        pltpu.make_async_copy(ref, near.at[at], sems.at[at]) for at, ref in enumerate(weights)
    ]
    for copy in copies:
        copy.start()
    tokens = q_ref.shape[0]
    for at, x_ref in enumerate(x_refs):
        rows = rms_norm(x_ref[...].astype(FULL), gain_ref[...])
        normed_ref[pl.ds(at * tokens, tokens), :] = rows.astype(LOW)
    bias_part(buckets_ref, table_ref, hot_ref, bias_ref)
    own = pl.ds((blocks - 1) * tokens, tokens)
    for at, (out_ref, rows) in enumerate(
        ((q_ref, own), (k_ref, slice(None)), (v_ref, slice(None)))
    ):
        copies[at].wait()
        out_ref[...] = dot_rows(normed_ref[rows, :], near[at]).astype(LOW)


def bias_part(buckets_ref, table_ref, hot_ref, bias_ref):
    heads, rows, keys = bias_ref.shape
    width = hot_ref.shape[1]
    buckets = buckets_ref[...].astype(FULL)
    column = jnp.sum(jnp.where(eye(keys), buckets, 0.0), 1, keepdims=True)
    distance = lax.broadcasted_iota(jnp.int32, (keys, width), 0)
    lane = lax.broadcasted_iota(jnp.int32, (keys, width), 1)
    turned = jnp.sum(jnp.where(distance + lane == keys - 1, column, 0.0), 0, keepdims=True)
    bucket = lax.broadcasted_iota(jnp.int32, (NB, width), 0).astype(FULL)
    hot = jnp.where(bucket == turned, 1.0, 0.0)
    hot_ref[...] = hot
    by_lane = lax.dot_general(
        table_ref[...], hot, (((0,), (0,)), ((), ())), precision=FULL_PRECISION,
        preferred_element_type=FULL,
    )
    for head in range(heads):
        line = jnp.broadcast_to(by_lane[head : head + 1, :], (8, width))
        line = pltpu.roll(line, keys + 1, 1, stride=1, stride_axis=0)
        for start in range(0, rows, 8):
            moved = line if start == 0 else pltpu.roll(line, start, 1)
            bias_ref[head, pl.ds(start, 8), :] = moved[:, :keys]


def project(buckets, table, gain, parts, weights):
    heads, keys = table.shape[1], buckets.shape[1]
    tokens, width = parts[0].shape
    outs, _ = call(
        functools.partial(project_kernel, blocks=len(parts)),
        "project",
        [whole(array) for array in (buckets, table, gain, *parts)]
        + [(array, None) for array in weights],
        [
            whole_out((NB, keys + tokens), FULL),
            whole_out((heads, tokens, keys), FULL),
            whole_out((keys, width), LOW),
            whole_out((tokens, width), LOW),
            whole_out((keys, width), LOW),
            whole_out((keys, width), LOW),
        ],
        scratch=[pltpu.VMEM((3, width, width), LOW), pltpu.SemaphoreType.DMA((3,))],
        us=4.5,
        vmem=16,
    )
    return outs


def half_lanes(half, shape):
    lane = lax.broadcasted_iota(jnp.int32, shape, 1)
    return lane < HDIM if half == 0 else lane >= HDIM


def attention_kernel(q_ref, k_ref, v_ref, bias_ref, mask_ref, out_ref, probs_ref, peak_ref):
    groups = peak_ref.shape[0]

    def group(step, _):
        mask = mask_ref[...]
        for pair in range(GROUP // 2):
            lanes = pair_lanes(step, pair)
            queries, keys, values = q_ref[:, lanes], k_ref[:, lanes], v_ref[:, lanes]
            parts = []
            for half in range(2):
                at = 2 * pair + half
                own = half_lanes(half, queries.shape)
                raw = dot_back(jnp.where(own, queries, jnp.zeros_like(queries)), keys)
                raw = raw * HDIM**-0.5 + mask
                top = jnp.max(raw, axis=0, keepdims=True)
                best = top[:, :LANES]
                for start in range(LANES, top.shape[1], LANES):
                    best = jnp.maximum(best, top[:, start : start + LANES])
                peak_ref[step, at : at + 1, :] = best
                scores = raw + bias_ref[step * GROUP + at]
                raised = jnp.exp(scores - jnp.max(scores, axis=1, keepdims=True))
                probs = raised * (1.0 / jnp.sum(raised, axis=1, keepdims=True))
                probs_low = probs.astype(LOW)
                probs_ref[step * GROUP + at] = probs_low
                parts.append(dot_rows(probs_low, values))
            first = half_lanes(0, parts[0].shape)
            out_ref[:, lanes] = jnp.where(first, parts[0], parts[1]).astype(LOW)
        return 0

    lax.fori_loop(0, groups, group, 0)


def pair_lanes(step, pair):
    return pl.ds(pl.multiple_of(step * GROUP * HDIM + pair * LANES, LANES), LANES)


def attention(queries, keys, values, bias, mask, fetch):
    rows, width = queries.shape
    length = keys.shape[0]
    heads = width // HDIM
    (out, probs, peak, *fetched), _ = call(
        attention_kernel,
        "attention",
        [whole(array) for array in (queries, keys, values, bias, mask)],
        [
            whole_out((rows, width), LOW),
            whole_out((heads, rows, length), LOW),
            whole_out((heads // GROUP, 8, LANES), FULL),
        ],
        us=4.5,
        vmem=10,
        far_out=(1,),
        fetch=fetch,
    )
    return out, probs, peak, *fetched


def attention_back_kernel(
    q_ref, k_ref, v_ref, probs_ref, grad_ref, dq_ref, dk_ref, dv_ref, lines_ref
):
    groups = lines_ref.shape[0]
    rows, length = probs_ref.shape[1:]
    scale = HDIM**-0.5

    def group(step, _):
        for pair in range(GROUP // 2):
            lanes = pair_lanes(step, pair)
            queries, keys, values, grad = (
                ref[:, lanes] for ref in (q_ref, k_ref, v_ref, grad_ref)
            )
            dq, dk, dv = [], [], []
            for half in range(2):
                at = 2 * pair + half
                own = half_lanes(half, grad.shape)
                dp = dot_back(jnp.where(own, grad, jnp.zeros_like(grad)), values)
                probs_low = probs_ref[step * GROUP + at]
                probs = probs_low.astype(FULL)
                ds = probs * (dp - jnp.sum(probs * dp, axis=1, keepdims=True))
                ds_low = ds.astype(LOW)
                dq.append(dot_rows(ds_low, keys))
                dk.append(transpose_dot(ds_low, queries))
                dv.append(transpose_dot(probs_low, grad))
                wide = jnp.concatenate([ds, jnp.zeros((rows, rows), FULL)], axis=1)
                total = wide[rows - 8 :, :]
                for start in range(0, rows - 8, 8):
                    total = total + pltpu.roll(wide[start : start + 8, :], rows - 8 - start, 1)
                line = lax.broadcasted_iota(jnp.int32, total.shape, 0)
                for bit in (1, 2, 4):
                    total = jnp.where(((7 - line) & bit) != 0, pltpu.roll(total, bit, 1), total)
                lines_ref[step, at : at + 1, :] = jnp.sum(total, axis=0, keepdims=True)
            first = half_lanes(0, dq[0].shape)
            dq_ref[:, lanes] = (jnp.where(first, dq[0], dq[1]) * scale).astype(LOW)
            first = half_lanes(0, dk[0].shape)
            dk_ref[:, lanes] = (jnp.where(first, dk[0], dk[1]) * scale).astype(LOW)
            dv_ref[:, lanes] = jnp.where(first, dv[0], dv[1]).astype(LOW)
        return 0

    lax.fori_loop(0, groups, group, 0)


def packed_back_kernel(
    q_ref, k_ref, v_ref, probs_ref, grad_ref, branch_ref, hot_ref, gain_ref, out_ref, lines_ref
):
    rows, length = probs_ref.shape[1:]
    ends = [0, rows, rows + length, rows + 2 * length, 2 * rows + 2 * length]
    parts = [out_ref.at[pl.ds(a, b - a), :] for a, b in zip(ends, ends[1:])]
    attention_back_kernel(q_ref, k_ref, v_ref, probs_ref, grad_ref, *parts[:3], lines_ref)
    parts[3][...] = branch_ref[...]
    groups = lines_ref.shape[0]
    width = gain_ref.shape[1]
    devices = out_ref.shape[0] - ends[4]
    own, turns = width // devices, LANES * devices // width
    device = lax.broadcasted_iota(jnp.int32, (devices, width), 0)
    feature = lax.broadcasted_iota(jnp.int32, (devices, width), 1)
    spread = jnp.where(feature // own == device, gain_ref[...], 0.0)
    folded = functools.reduce(
        jnp.add, [spread[:, start : start + LANES] for start in range(0, width, LANES)]
    )
    device = lax.broadcasted_iota(jnp.int32, folded.shape, 0)
    small = folded
    for turn_by in range(1, turns):
        moved = pltpu.roll(folded, LANES - turn_by * own, 1)
        small = jnp.where(device % turns == turn_by, moved, small)
    lines = jnp.concatenate([lines_ref[g, :GROUP, :] for g in range(groups)], axis=0)
    blank = jnp.zeros((LANES - TABLE_LANE - lines.shape[0], lines.shape[1]), FULL)
    lines = jnp.concatenate([jnp.zeros((TABLE_LANE, lines.shape[1]), FULL), lines, blank], axis=0)
    upper = lines.astype(LOW)
    lower = (lines - upper.astype(FULL)).astype(LOW)
    hot = hot_ref[...].astype(LOW)
    small = small + dot_back(hot, upper) + dot_back(hot, lower)
    out_ref[pl.ds(ends[4], devices), :LANES] = small.astype(LOW)


def attention_back(queries, keys, values, probs, grad, token, packed=None):
    rows, width = queries.shape
    length = keys.shape[0]
    heads = width // HDIM
    lines = whole_out((heads // GROUP, 8, length + rows), FULL)
    inputs = [whole(array) for array in (queries, keys, values, probs, grad)]
    if packed is None:
        outs, token = call(
            attention_back_kernel,
            "attention_back",
            inputs,
            [whole_out((size, width), LOW) for size in (rows, length, length)] + [lines],
            token=token,
            us=6.6,
            vmem=16,
        )
        return *outs, token
    branch, hot, gain, devices = packed
    (out, _), token = call(
        packed_back_kernel,
        "attention_back",
        inputs + [whole(branch), whole(hot), whole(gain)],
        [whole_out((2 * rows + 2 * length + devices, width), LOW), lines],
        token=token,
        us=7,
        vmem=16,
    )
    return out, token


def post_kernel(attended_ref, weights_ref, rows_ref, gain_ref, spread_ref, after_ref, *out_refs):
    after = rows_ref[...].astype(FULL) + dot_rows(attended_ref[...], weights_ref[...])
    after_ref[...] = after
    sent = rms_norm(after, gain_ref[...]).astype(LOW)
    size = out_refs[0].shape[0]
    for at, out_ref in enumerate(out_refs):
        out_ref[...] = dot_rows(spread_ref[pl.ds(at * size, size), :], sent).astype(LOW)


def after_attention(attended, weights, rows, gain, spread, experts):
    tokens, width = rows.shape
    (after, *sent), _ = call(
        post_kernel,
        "post",
        [whole(array) for array in (attended, weights, rows, gain, spread)],
        [whole_out((tokens, width), FULL)]
        + [whole_out((spread.shape[0] // experts, width), LOW)] * experts,
        far_out=(0,),
        us=2,
    )
    return after, sent


def gather_kernel(*refs):
    size = refs[0].shape[0]
    for at, ref in enumerate(refs[:-1]):
        refs[-1][pl.ds(at * size, size), :] = ref[...]


def side_by_side(blocks, token):
    size, width = blocks[0].shape
    (out,), token = call(
        gather_kernel,
        "gather",
        [whole(block) for block in blocks],
        [whole_out((len(blocks) * size, width), LOW)],
        token=token,
        us=1,
    )
    return out, token


def expert_part(gate, up, dhid):
    square = gate * gate
    curve = jnp.tanh(GELU_SCALE * gate * (1.0 + GELU_CUBE * square))
    upper = 0.5 * (1.0 + curve)
    gelu = gate * upper
    slope = upper + 0.5 * gate * (1.0 - curve * curve) * (
        GELU_SCALE * (1.0 + 3.0 * GELU_CUBE * square)
    )
    hid = (gelu * up).astype(LOW)
    dgate = (dhid * up * slope).astype(LOW)
    dup = (dhid * gelu).astype(LOW)
    return hid, dgate, dup


def expert_kernel(
    rows_ref, grad_ref, gate_w_ref, up_w_ref, down_w_ref,
    out_ref, back_ref, dgate_ref, dup_ref, hid_ref, turned_ref, out_sum, back_sum,
):
    step = pl.program_id(0)

    @pl.when(step == 0)
    def _():
        out_sum[...] = jnp.zeros_like(out_sum)
        back_sum[...] = jnp.zeros_like(back_sum)

    rows, grad = rows_ref[...], grad_ref[...]
    gate_w, up_w, down_w = gate_w_ref[0], up_w_ref[0], down_w_ref[0]
    hid, dgate, dup = expert_part(
        dot_rows(rows, gate_w), dot_rows(rows, up_w), dot_back(grad, down_w)
    )
    dgate_ref[...] = dgate
    dup_ref[...] = dup
    hid_ref[...] = hid.T
    out_sum[...] += dot_rows(hid, down_w)
    back_sum[...] += dot_back(dgate, gate_w) + dot_back(dup, up_w)

    @pl.when(step == pl.num_programs(0) - 1)
    def _():
        out_ref[...] = out_sum[...].astype(LOW)
        back_ref[...] = back_sum[...].astype(LOW)
        turned_ref[...] = rows_ref[...].T


def expert(rows, grad, w_in, w_down, token):
    count, width = rows.shape
    hidden = w_down.shape[1]
    part = 256
    steps = hidden // part
    return call(
        expert_kernel,
        "expert",
        [
            whole(rows),
            whole(grad),
            (w_in, pl.BlockSpec((1, width, part), lambda i: (0, 0, i))),
            (w_in, pl.BlockSpec((1, width, part), lambda i: (0, 0, i + steps))),
            (w_down, pl.BlockSpec((1, part, width), lambda i: (0, i, 0))),
        ],
        [
            whole_out((count, width), LOW),
            whole_out((count, width), LOW),
            ((count, hidden), LOW, pl.BlockSpec((count, part), lambda i: (0, i))),
            ((count, hidden), LOW, pl.BlockSpec((count, part), lambda i: (0, i))),
            ((hidden, count), LOW, pl.BlockSpec((part, count), lambda i: (i, 0))),
            whole_out((width, count), LOW),
        ],
        grid=(steps,),
        token=token,
        scratch=[pltpu.VMEM((count, width), FULL), pltpu.VMEM((count, width), FULL)],
        vmem=24,
        us=20,
    )


CHUNK = 512
EXPERT_CHUNK = 512
EXPERT_VMEM = 40


def weight_copies(at_ref, w_in_ref, w_down_ref, start, units, gate, up, down, sems):
    width, half = w_in_ref.shape[1], w_down_ref.shape[1] // 2
    first = pl.multiple_of(at_ref[2] * half, LANES) + start
    pairs = []
    for piece in range(4):
        rows = pl.ds(piece * (width // 4), width // 4)
        for part, ref in ((0, gate), (2 * half, up)):
            columns = pl.ds(pl.multiple_of(first + part, LANES), units)
            pairs.append((w_in_ref.at[0, rows, columns], ref.at[rows, :]))
        size = units // 4
        rows = pl.ds(pl.multiple_of(first + piece * size, 16), size)
        pairs.append((w_down_ref.at[0, rows, :], down.at[pl.ds(piece * size, size), :]))
    return [pltpu.make_async_copy(one, two, sems.at[at]) for at, (one, two) in enumerate(pairs)]


def ahead_kernel(at_ref, w_in_ref, w_down_ref, gate_ref, up_ref, down_ref, sems):
    copies = weight_copies(
        at_ref, w_in_ref, w_down_ref, 0, gate_ref.shape[1], gate_ref, up_ref, down_ref, sems
    )
    for copy in copies:
        copy.start()
    for copy in copies:
        copy.wait()


def weights_ahead(at, w_in, w_down, token):
    width = w_in.shape[1]
    return call(
        ahead_kernel,
        "weights_ahead",
        [(w_in, None), (w_down, None)],
        [whole_out((width, EXPERT_CHUNK), LOW)] * 2 + [whole_out((EXPERT_CHUNK, width), LOW)],
        token=token,
        prefetch=(at,),
        scratch=[pltpu.SemaphoreType.DMA((12,))],
        us=2,
    )


def halves_kernel(
    at_ref, x0_ref, x1_ref, g0_ref, g1_ref, gate0_ref, up0_ref, down0_ref, w_in_ref, w_down_ref,
    back_keep, back_send, dgate_ref, dup_ref, turned_ref, hid_out, a_send, a_keep, b_out,
    both_w, du, turned, hid_ref, down_ref, a_sum, b_ref, sems, out_sems,
):
    count, width = x0_ref.shape
    half = hid_ref.shape[1]
    starts = list(range(0, half, EXPERT_CHUNK))
    sizes = [min(EXPERT_CHUNK, half - start) for start in starts]
    loads = [
        weight_copies(
            at_ref, w_in_ref, w_down_ref, start, units,
            both_w.at[:, pl.ds(start, units)],
            both_w.at[:, pl.ds(half + start, units)],
            down_ref.at[pl.ds(start, units), :],
            sems.at[i],
        )
        for i, (start, units) in enumerate(zip(starts, sizes))
        if i > 0
    ]
    for copies in loads:
        for copy in copies:
            copy.start()
    firsts = [
        pltpu.make_async_copy(ref, both_w.at[:, pl.ds(start, sizes[0])], sems.at[0, at])
        for at, (ref, start) in enumerate(((gate0_ref, 0), (up0_ref, half)))
    ]
    for copy in firsts:
        copy.start()
    turned[:, :count] = x0_ref[...].T
    turned[:, count:] = x1_ref[...].T
    kept = [pltpu.make_async_copy(turned, turned_ref, out_sems.at[len(sizes), 0])]
    for i, (start, units) in enumerate(zip(starts, sizes)):
        columns, other = pl.ds(start, units), pl.ds(half + start, units)
        if i == 0:
            gate_w, up_w, down_w = gate0_ref[...], up0_ref[...], down0_ref[...]
        else:
            for copy in loads[i - 1]:
                copy.wait()
            gate_w, up_w, down_w = both_w[:, columns], both_w[:, other], down_ref[columns, :]
        for side, (x_ref, g_ref) in enumerate(((x0_ref, g0_ref), (x1_ref, g1_ref))):
            rows = pl.ds(side * count, count)
            x = x_ref[...]
            hid, dgate, dup = expert_part(
                dot_rows(x, gate_w), dot_rows(x, up_w), dot_back(g_ref[...], down_w)
            )
            hid_ref[rows, columns] = hid
            du[rows, columns] = dgate
            du[rows, other] = dup
        for part, (ref, from_columns) in enumerate(((dgate_ref, columns), (dup_ref, other))):
            copy = pltpu.make_async_copy(
                du.at[:, from_columns], ref.at[:, columns], out_sems.at[i, part]
            )
            copy.start()
            kept.append(copy)
    kept[0].start()
    kept.append(pltpu.make_async_copy(hid_ref, hid_out, out_sems.at[len(sizes), 1]))
    kept[-1].start()
    terms = transpose_dot(hid_ref[:count, :], g0_ref[...])
    terms = terms + transpose_dot(hid_ref[count:, :], g1_ref[...])
    middle, size = width // 2, half // 2
    b_ref[...] = terms[:, middle:].astype(LOW)
    a_sum[...] = terms[:, :middle].astype(LOW)
    own = pl.ds(pl.multiple_of(at_ref[1] * size, 16), size)
    other = pl.ds(pl.multiple_of((1 - at_ref[1]) * size, 16), size)
    sent = [(b_ref, b_out), (a_sum.at[other, :], a_send), (a_sum.at[own, :], a_keep)]
    sent = [
        pltpu.make_async_copy(ref, out, out_sems.at[len(sizes) + 1 + at // 2, at % 2])
        for at, (ref, out) in enumerate(sent)
    ]
    for copy in sent:
        copy.start()
    for copy in firsts:
        copy.wait()
    back_send[...] = dot_back(du[count:, :], both_w[...]).astype(LOW)
    back_keep[...] = dot_back(du[:count, :], both_w[...])
    for copy in kept + sent:
        copy.wait()


def expert_halves(at, rows, grads, firsts, w_in, w_down, token):
    count, width = rows[0].shape
    half = w_down.shape[1] // 2
    chunks = pl.cdiv(half, EXPERT_CHUNK)
    return call(
        halves_kernel,
        "expert_halves",
        [whole(array) for array in (*rows, *grads, *firsts)] + [(w_in, None), (w_down, None)],
        [
            whole_out((count, width), FULL),
            whole_out((count, width), LOW),
            ((2 * count, half), LOW, None),
            ((2 * count, half), LOW, None),
            ((width, 2 * count), LOW, None),
            ((2 * count, half), LOW, None),
            ((half // 2, width // 2), LOW, None),
            ((half // 2, width // 2), LOW, None),
            ((half, width // 2), LOW, None),
        ],
        token=token,
        prefetch=(at,),
        scratch=[
            pltpu.VMEM((width, 2 * half), LOW),
            pltpu.VMEM((2 * count, 2 * half), LOW),
            pltpu.VMEM((width, 2 * count), LOW),
            pltpu.VMEM((2 * count, half), LOW),
            pltpu.VMEM((half, width), LOW),
            pltpu.VMEM((half, width // 2), LOW),
            pltpu.VMEM((half, width // 2), LOW),
            pltpu.SemaphoreType.DMA((chunks, 12)),
            pltpu.SemaphoreType.DMA((chunks + 3, 2)),
        ],
        vmem=EXPERT_VMEM,
        us=20,
    )


def results_kernel(at_ref, hid_out, w_down_ref, keep_out, send_out, hid_ref, down_ref, sum_ref, sems):
    half = down_ref.shape[0]
    size = half // 4
    count = sum_ref.shape[1]
    copies = []
    for side in range(2):
        rows = pl.ds(side * count, count)
        copies.append(pltpu.make_async_copy(hid_out.at[rows, :], hid_ref.at[rows, :], sems.at[4 + side]))
    for piece in range(4):
        rows = pl.ds(pl.multiple_of(at_ref[2] * half + piece * size, 16), size)
        here = down_ref.at[pl.ds(piece * size, size), :]
        copies.append(pltpu.make_async_copy(w_down_ref.at[0, rows, :], here, sems.at[piece]))
    for copy in copies:
        copy.start()
    for copy in copies:
        copy.wait()
    copies = []
    for side, out in ((1, send_out), (0, keep_out)):
        rows = pl.ds(side * count, count)
        sum_ref[side] = dot_rows(hid_ref[rows, :], down_ref[...]).astype(LOW)
        copies.append(pltpu.make_async_copy(sum_ref.at[side], out, sems.at[6 + side]))
        copies[-1].start()
    for copy in copies:
        copy.wait()


def expert_results(at, hid, w_down, fetch, token):
    half, width = hid.shape[1], w_down.shape[2]
    shape = (hid.shape[0] // 2, width)
    (keep, send, *fetched), token = call(
        results_kernel,
        "expert_results",
        [(hid, None), (w_down, None)],
        [(shape, LOW, None)] * 2,
        token=token,
        prefetch=(at,),
        scratch=[
            pltpu.VMEM(hid.shape, LOW),
            pltpu.VMEM((half, width), LOW),
            pltpu.VMEM((2, *shape), LOW),
            pltpu.SemaphoreType.DMA((8,)),
        ],
        vmem=16,
        us=0.01,
        fetch=fetch,
    )
    return keep, send, *fetched, token


def block_of(at_ref, k, blocks):
    return lax.rem(at_ref[3] + (blocks - k), blocks)


def join_kernel(at_ref, kept_ref, got_ref, out_ref):
    blocks, size, _ = out_ref.shape
    for k in range(blocks):
        rows = pl.ds(k * size, size)
        total = kept_ref[rows, :] + got_ref[rows, :].astype(FULL)
        out_ref[block_of(at_ref, k, blocks)] = total.astype(LOW)


def join(at, kept, got, blocks, token):
    rows, width = kept.shape
    (out,), token = call(
        join_kernel,
        "join",
        [whole(kept), whole(got)],
        [whole_out((blocks, rows // blocks, width), LOW)],
        token=token,
        prefetch=(at,),
        far_out=(0,),
        us=1,
    )
    return out, token


def join_peak_kernel(at_ref, kept_ref, got_ref, peak_ref, out_ref):
    blocks, size, width = out_ref.shape
    rows = kept_ref.shape[0] // blocks
    best = jnp.concatenate([peak_ref[g, :GROUP, :] for g in range(peak_ref.shape[0])], axis=0)
    best = jnp.broadcast_to(jnp.max(best, axis=1, keepdims=True), (size - rows, LANES))
    upper = best.astype(LOW)
    lower = (best - upper.astype(FULL)).astype(LOW)
    for k in range(blocks):
        part = pl.ds(k * rows, rows)
        to = block_of(at_ref, k, blocks)
        total = kept_ref[part, :].astype(FULL) + got_ref[part, :].astype(FULL)
        out_ref[to, :rows, :] = total.astype(LOW)
        out_ref[to, rows:, :] = jnp.zeros((size - rows, width), LOW)
        out_ref[to, rows:, :LANES] = upper
        out_ref[to, rows:, LANES : 2 * LANES] = lower


def join_peak(at, kept, got, peak, blocks, token):
    rows, width = kept.shape
    heads = peak.shape[0] * GROUP
    (out,), token = call(
        join_peak_kernel,
        "join_peak",
        [whole(kept), whole(got), whole(peak)],
        [whole_out((blocks, rows // blocks + heads, width), LOW)],
        token=token,
        prefetch=(at,),
        far_out=(0,),
        us=0.01,
        far_in=(0,),
    )
    return out, token


def larger_kernel(one_ref, two_ref, out_ref):
    out_ref[...] = jnp.maximum(one_ref[...], two_ref[...])


def larger(one, two, token):
    (out,), token = call(
        larger_kernel,
        "larger",
        [whole(one), whole(two)],
        [whole_out(one.shape, FULL)],
        token=token,
        us=0.5,
    )
    return out, token


def place():
    dp = lax.axis_index("dp")
    return lax.axis_index("ctx"), lax.axis_index("exp"), dp // 2, dp % 2


def to_down_plane(array):
    pairs = [
        ((1 - core) * 4 + x * 2 + core, core * 4 + x * 2 + core)
        for core in range(2)
        for x in range(2)
    ]
    return lax.ppermute(array, ("ctx", "dp"), pairs)


def in_down_plane(array):
    pairs = [
        (core * 4 + x * 2 + core, core * 4 + (1 - x) * 2 + core)
        for core in range(2)
        for x in range(2)
    ]
    return lax.ppermute(array, ("ctx", "dp"), pairs)


def in_kernel(
    at_ref, turned_ref, gate_ref, up_ref, *refs,
):
    out_refs, turned, near, results, sems, out_sems = refs[:4], *refs[4:]
    half = gate_ref.shape[1]
    ends = [CHUNK // 2] + list(range(3 * CHUNK // 2, half, CHUNK)) + [half]
    starts = [0] + ends[:-1]
    loads = []
    for at, (ref, to) in enumerate(((gate_ref, near.at[0]), (up_ref, near.at[1]))):
        for i, start in enumerate(starts):
            columns = pl.ds(start, ends[i] - start)
            loads.append(
                pltpu.make_async_copy(ref.at[:, columns], to.at[:, columns], sems.at[at, i])
            )
    whole_load = pltpu.make_async_copy(turned_ref, turned, sems.at[2, 0])
    whole_load.start()
    loads[0].start()
    loads[len(starts)].start()
    whole_load.wait()
    size = turned.shape[0] // 4
    stores = []
    for i, start in enumerate(starts):
        columns = pl.ds(start, ends[i] - start)
        loads[i].wait()
        loads[len(starts) + i].wait()
        if i + 1 < len(starts):
            loads[i + 1].start()
            loads[len(starts) + i + 1].start()
        for block in range(4):
            ry, rx = block // 2, block % 2
            chip = (at_ref[0] ^ ry) * 2 + (at_ref[1] ^ rx)
            rows = turned[pl.ds(pl.multiple_of(chip * size, size), size), :]
            a, b = 1 - rx, 2 + 1 - ry
            results[a, ry, :, columns] = dot_rows(rows, near[0, :, columns]).astype(LOW)
            results[b, rx, :, columns] = dot_rows(rows, near[1, :, columns]).astype(LOW)
        for at, ref in enumerate(out_refs):
            copy = pltpu.make_async_copy(
                results.at[at, :, :, columns], ref.at[:, :, columns], out_sems.at[at, i]
            )
            copy.start()
            stores.append(copy)
    for copy in stores:
        copy.wait()


def in_terms(at, turned, gate, up, token):
    width, count = turned.shape
    half = gate.shape[1]
    shape = (2, width // 4, half)
    chunks = pl.cdiv(half, CHUNK) + 1
    return call(
        in_kernel,
        "in_terms",
        [(turned, None), (gate, None), (up, None)],
        [(shape, LOW, None)] * 4,
        token=token,
        prefetch=(at,),
        scratch=[
            pltpu.VMEM((width, count), LOW),
            pltpu.VMEM((2, count, half), LOW),
            pltpu.VMEM((4, *shape), LOW),
            pltpu.SemaphoreType.DMA((3, chunks)),
            pltpu.SemaphoreType.DMA((4, chunks)),
        ],
        vmem=20,
        us=0.01,
    )


def plane_first(parts):
    a_send, a_keep, b_send, b_keep = parts
    return swapped(a_send, "dp", 2), a_keep, swapped(b_send, "ctx", 1), b_keep


def second_kernel(*refs):
    (a_ref, a_keep_ref, b_ref, b_keep_ref), (a_send_ref, b_send_ref) = refs[:4], refs[-2:]
    rows = a_ref.shape[0]
    total = a_keep_ref[...].astype(FULL) + a_ref[...].astype(FULL)
    a_send_ref[pl.ds(0, rows), :] = total.astype(LOW)
    b_send_ref[...] = (b_keep_ref[...].astype(FULL) + b_ref[...].astype(FULL)).astype(LOW)
    for beside in refs[4:-2]:
        more, width = beside.shape
        a_send_ref[pl.ds(rows, more), pl.ds(0, width)] = beside[...]


def plane_second(parts, token, us, beside=()):
    extra = sum(part.shape[0] for part in beside)
    (_, a_rows, a_width), (_, b_rows, b_width) = parts[0].shape, parts[2].shape
    (a_send, b_send), token = call(
        second_kernel,
        "second_terms",
        [whole(part) for part in (*parts, *beside)],
        [whole_out((a_rows + extra, a_width), LOW), whole_out((b_rows, b_width), LOW)],
        token=token,
        us=us,
        far_in=tuple(range(4, 4 + len(beside))),
        part_in={at: (1,) for at in range(4)},
        far_out=(0, 1),
        vmem=10,
    )
    return a_send, b_send, token


def down_second_kernel(at_ref, a_ref, a_keep_ref, b_ref, b_keep_ref, a_send_ref, b_send_ref):
    size = b_send_ref.shape[0]
    rows = pl.ds(pl.multiple_of((1 - at_ref[1]) * size, 16), size)
    a_send_ref[...] = (a_keep_ref[...].astype(FULL) + a_ref[...].astype(FULL)).astype(LOW)
    b_send_ref[...] = (b_keep_ref[rows, :].astype(FULL) + b_ref[rows, :].astype(FULL)).astype(LOW)


def down_second(at, parts, token, us):
    shape = parts[0].shape
    (a_send, b_send), token = call(
        down_second_kernel,
        "down_second",
        [whole(part) for part in parts],
        [whole_out(shape, LOW)] * 2,
        token=token,
        prefetch=(at,),
        us=us,
        far_out=(0, 1),
    )
    return a_send, b_send, token


def pair_last_kernel(a_ref, a_keep_ref, b_ref, b_keep_ref, a2_ref, b2_ref, out_ref):
    blocks = out_ref.shape[0]
    a, b = (
        sum(ref[...].astype(FULL) for ref in refs)
        for refs in ((a_keep_ref, a_ref, a2_ref), (b_keep_ref, b_ref, b2_ref))
    )
    size, columns = b.shape[0] // blocks, b.shape[1] // LANES
    count = size * columns
    for z in range(blocks):
        out_ref[z, :count, :] = a[z * count : (z + 1) * count].astype(LOW)
        small = jnp.broadcast_to(a[blocks * count + z : blocks * count + z + 1], (EXTRA, LANES))
        out_ref[z, count : count + EXTRA, :] = small.astype(LOW)
        for column in range(columns):
            part = b[z * size : (z + 1) * size, column * LANES : (column + 1) * LANES]
            out_ref[z, pl.ds(count + EXTRA + column * size, size), :] = part.astype(LOW)


def pair_last(parts, a2, b2, blocks, token):
    rows, width = b2.shape
    (out,), token = call(
        pair_last_kernel,
        "pair_last",
        [whole(part) for part in (*parts, a2, b2)],
        [whole_out((blocks, 2 * rows // blocks * (width // LANES) + EXTRA, LANES), LOW)],
        token=token,
        part_in={at: (0,) for at in range(4)},
        far_out=(0,),
        us=8,
        vmem=12,
    )
    return out, token


def down_last_kernel(
    at_ref, a_ref, a_keep_ref, b_ref, b_keep_ref, a2_ref, b2_ref, keep_ref, send_ref
):
    size, width = keep_ref.shape
    half = width // 2
    for out_ref, core in ((send_ref, 1 - at_ref[2]), (keep_ref, at_ref[2])):
        rows = pl.ds(pl.multiple_of(core * size, 16), size)
        there = pl.ds(pl.multiple_of((at_ref[1] * 2 + core) * size, 16), size)
        for first, refs in (
            (0, ((a_ref, rows), (a_keep_ref, rows), (a2_ref, rows))),
            (half, ((b_ref, there), (b_keep_ref, there), (b2_ref, rows))),
        ):
            total = sum(ref[cut, :].astype(FULL) for ref, cut in refs)
            out_ref[:, first : first + half] = total.astype(out_ref.dtype)


def down_last(at, parts, a2, b2, token):
    rows, half = a2.shape
    shape = (rows // 2, 2 * half)
    (keep, send), token = call(
        down_last_kernel,
        "down_last",
        [whole(array) for array in (*parts, a2, b2)],
        [whole_out(shape, FULL), whole_out(shape, LOW)],
        token=token,
        prefetch=(at,),
        us=0.01,
        far_out=(1,),
    )
    return keep, send, token


def in_last_kernel(
    at_ref, a_ref, a_keep_ref, b_ref, b_keep_ref, a2_ref, b2_ref, out_ref, send_ref,
    send_near, keep_near, sems,
):
    _, size, half = keep_near.shape
    copies = []
    for number, near in enumerate((send_near, keep_near)):
        core = at_ref[2] if number else 1 - at_ref[2]
        rows = pl.ds(pl.multiple_of(core * size, 16), size)
        for part, refs in enumerate(((a_ref, a_keep_ref, a2_ref), (b_ref, b_keep_ref, b2_ref))):
            total = sum(ref[rows, :].astype(FULL) for ref in refs)
            near[part] = total.astype(near.dtype)
            column = pl.multiple_of((part * 2 + core) * half, LANES)
            there = out_ref.at[0, :, pl.ds(column, half)] if number else send_ref.at[part]
            copies.append(pltpu.make_async_copy(near.at[part], there, sems.at[number, part]))
            copies[-1].start()
    for copy in copies:
        copy.wait()


def in_last(at, parts, a2, b2, token):
    rows, half = b2.shape
    shape = (2, rows // 2, half)
    (out, send), token = call(
        in_last_kernel,
        "in_last",
        [whole(array) for array in (*parts, a2, b2)],
        [((1, rows // 2, 4 * half), FULL, None), (shape, LOW, None)],
        token=token,
        prefetch=(at,),
        scratch=[
            pltpu.VMEM(shape, LOW), pltpu.VMEM(shape, FULL), pltpu.SemaphoreType.DMA((2, 2)),
        ],
        us=8,
        part_in={at: (0,) for at in range(4)},
        vmem=16,
    )
    return out, send, token


def in_finish_kernel(at_ref, _, got_ref, out_ref, near, sems):
    half = got_ref.shape[2]
    copies = []
    for part in range(2):
        near[part] = got_ref[part].astype(FULL)
        column = pl.multiple_of((part * 2 + 1 - at_ref[2]) * half, LANES)
        there = out_ref.at[0, :, pl.ds(column, half)]
        copies.append(pltpu.make_async_copy(near.at[part], there, sems.at[part]))
        copies[-1].start()
    for copy in copies:
        copy.wait()


def in_finish(at, out, got, token):
    (out,), token = call(
        in_finish_kernel,
        "in_finish",
        [(out, None), whole(got)],
        [(out.shape, FULL, None)],
        token=token,
        prefetch=(at,),
        scratch=[pltpu.VMEM(got.shape, FULL), pltpu.SemaphoreType.DMA((2,))],
        onto=((0, 0),),
        us=0.01,
    )
    return out, token


def down_finish_kernel(at_ref, kept_ref, got_ref, out_ref):
    mine = at_ref[0] == at_ref[2]
    out_ref[0] = jnp.where(mine, kept_ref[...], got_ref[...].astype(FULL))


def down_finish(at, kept, got, token):
    (out,), token = call(
        down_finish_kernel,
        "down_finish",
        [whole(kept), whole(got)],
        [whole_out((1, *kept.shape), FULL)],
        token=token,
        prefetch=(at,),
        far_out=(0,),
        us=0.01,
    )
    return out, token


EXTRA = 16
TABLE_LANE = 32


def turn_kernel(at_ref, *refs):
    out_ref, turned = refs[-2:]
    start = 0
    for ref in refs[:-2]:
        turned[:, start : start + ref.shape[0]] = ref[...].T
        start += ref.shape[0]
    size = out_ref.shape[0] // 16
    for to in range(16):
        device = device_at(to % 4, to // 4, at_ref)
        out_ref[pl.ds(to * size, size), :] = turned[pl.ds(device * size, size), :]


def device_at(block, z, at_ref):
    return (
        (at_ref[0] ^ (block // 2)) * 16 + z * 4 + (at_ref[1] ^ (block % 2)) * 2 + at_ref[2]
    )


def turn(at, parts, token):
    count, width = sum(part.shape[0] for part in parts), parts[0].shape[1]
    (out,), token = call(
        turn_kernel,
        "turn",
        [whole(part) for part in parts],
        [whole_out((width // 2, count), LOW)],
        token=token,
        prefetch=(at,),
        scratch=[pltpu.VMEM((width, count), LOW)],
        us=2,
        far_out=(0,),
    )
    return out, token


def shared_kernel(
    at_ref, left_ref, own_ref, other_ref, *refs, experts
):
    out_refs, near_refs, sems = refs[:4], refs[4:8], refs[8]
    a_send_ref, a_keep_ref, b_send_ref, b_keep_ref = near_refs
    copies = []

    def leave(step, parts):
        for number, rows in enumerate(parts):
            for at in (2 * number, 2 * number + 1):
                part = pl.ds(rows.start, rows.stop - rows.start)
                near, out = near_refs[at], out_refs[at]
                copy = pltpu.make_async_copy(
                    near.at[:, part, :], out.at[:, part, :], sems.at[at, step]
                )
                copy.start()
                copies.append(copy)

    rows, count = left_ref.shape[0] // experts, left_ref.shape[1] // 2
    columns = own_ref.shape[1] // LANES
    tokens = count // 3
    size = rows // 4
    small = own_ref[6 * tokens :, :LANES].astype(FULL) + other_ref[6 * tokens :, :LANES].astype(FULL)
    place = lax.broadcasted_iota(jnp.int32, small.shape, 0)
    for z in range(experts):
        left = left_ref[pl.ds(z * rows, rows), :]

        def product(first, start, length):
            right = slice(start, start + length)
            one = left[:, first : first + length]
            two = left[:, count + first : count + first + length]
            total = dot_rows(one, own_ref[right, :]) + dot_rows(two, other_ref[right, :])
            return total.astype(LOW)

        a_terms = product(2 * tokens, 5 * tokens, tokens), product(tokens, 0, tokens)
        b_terms = product(0, tokens, 2 * tokens), product(0, 3 * tokens, 2 * tokens)
        for block in range(4):
            ry, rx = block // 2, block % 2
            a_ref = (a_send_ref if rx else a_keep_ref).at[ry]
            b_ref = (b_send_ref if ry else b_keep_ref).at[rx]
            here = slice(block * size, (block + 1) * size)
            for at in range(2):
                to = pl.ds((2 * z + at) * size, size)
                b_ref[to, :] = b_terms[at][here]
                for column in range(columns):
                    to = pl.ds(((z * columns + column) * 2 + at) * size, size)
                    a_ref[to, :] = a_terms[at][here, column * LANES : (column + 1) * LANES]
        rows_left = slice(2 * z * size, 2 * (z + 1) * size)
        leave(z, (slice(rows_left.start * columns, rows_left.stop * columns), rows_left))
    line = lax.broadcasted_iota(jnp.int32, (EXTRA, LANES), 0)
    for block in range(4):
        ry, rx = block // 2, block % 2
        a_ref = (a_send_ref if rx else a_keep_ref).at[ry]
        rows_here = jnp.zeros((EXTRA, LANES), FULL)
        for z in range(experts):
            row = jnp.where(place == device_at(block, z, at_ref), small, 0.0)
            rows_here = jnp.where(line == z, jnp.sum(row, 0, keepdims=True), rows_here)
        a_ref[2 * size * experts * columns :, :] = rows_here.astype(LOW)
    end = 2 * size * experts * columns
    leave(experts, (slice(end, end + EXTRA),))
    for copy in copies:
        copy.wait()


def shared_terms(at, left, own, other, experts, token):
    rows = left.shape[0]
    width = own.shape[1]
    b_shape = (2, rows // 2, width)
    a_shape = (2, rows // 2 * (width // LANES) + EXTRA, LANES)
    return call(
        functools.partial(shared_kernel, experts=experts),
        "shared_terms",
        [whole(array) for array in (left, own, other)],
        [(shape, LOW, None) for shape in (a_shape, a_shape, b_shape, b_shape)],
        token=token,
        prefetch=(at,),
        scratch=[pltpu.VMEM(shape, LOW) for shape in (a_shape, a_shape, b_shape, b_shape)]
        + [pltpu.SemaphoreType.DMA((4, experts + 1))],
        us=0.01,
        vmem=16,
    )


def rows_kernel(
    place_ref, plane_ref, w_query_ref, w_key_ref, w_value_ref, gain_ref,
    query_ref, key_ref, value_ref, out_ref, gain_grad_ref, ffn_ref, table_ref,
    near_query, near_key, near_value, sems,
):
    rows = query_ref.shape[0]
    at = pl.ds(pl.multiple_of(place_ref[0] * rows, rows), rows)
    pairs = ((w_query_ref, near_query), (w_key_ref, near_key), (w_value_ref, near_value))
    copies = [
        pltpu.make_async_copy(ref.at[at, :], near, sems.at[number])
        for number, (ref, near) in enumerate(pairs)
    ]
    for copy in copies:
        copy.start()
    total = sum(plane_ref[block].astype(FULL) for block in range(plane_ref.shape[0]))
    columns = out_ref.shape[1] // LANES
    count = 2 * rows * columns

    def side_by_side_from(start):
        parts = [total[start + 2 * rows * at : start + 2 * rows * at + rows] for at in range(columns)]
        return jnp.concatenate(parts, axis=1)

    out_ref[...] = side_by_side_from(0)
    query = side_by_side_from(rows)
    key, value = (side_by_side_from(count + EXTRA + start) for start in (0, rows))
    query_ref[...] = query
    key_ref[...] = key
    value_ref[...] = value
    small = total[count : count + 1]
    ffn_ref[...] = small[:, : ffn_ref.shape[1]]
    small = pltpu.roll(jnp.broadcast_to(small, (8, LANES)), LANES - TABLE_LANE, 1)[:1]
    table_ref[...] = small[:, : table_ref.shape[1]]
    for copy in copies:
        copy.wait()
    sums = query * near_query[...].astype(FULL) + key * near_key[...].astype(FULL)
    sums = jnp.sum(sums + value * near_value[...].astype(FULL), axis=1, keepdims=True)
    lane = lax.broadcasted_iota(jnp.int32, (rows, LANES), 1)
    line = lax.broadcasted_iota(jnp.int32, (rows, LANES), 0)
    spread = jnp.sum(jnp.where(lane == line, sums, 0.0), 0, keepdims=True)
    device = place_ref[0]
    block = gain_ref[pl.ds(device * rows // LANES, 1), :]
    gain = pltpu.roll(jnp.broadcast_to(block, (8, LANES)), LANES - device * rows % LANES, 1)[:1]
    gain_grad_ref[...] = (spread / gain)[:, : gain_grad_ref.shape[1]]


def last_rows(place_all, plane, rows, table, weights, gain, token):
    width = weights[0].shape[1]
    small = [whole_out((1, size), FULL) for size in (rows, rows, table)]
    outs, token = call(
        rows_kernel,
        "last_rows",
        [whole(plane)] + [(array, None) for array in weights] + [whole(gain.reshape(-1, LANES))],
        [whole_out((rows, width), FULL)] * 4 + small,
        token=token,
        prefetch=(place_all.reshape(1),),
        scratch=[pltpu.VMEM((rows, width), LOW)] * 3 + [pltpu.SemaphoreType.DMA((3,))],
        us=0.01,
    )
    return outs, token


def clip_kernel(weight_ref, peak_ref, level_ref, out_ref, factor_ref):
    heads = peak_ref.shape[0]
    width = weight_ref.shape[1]
    level = jnp.sum(jnp.where(eye(heads), level_ref[...], 0.0), 1, keepdims=True)
    factor = level / jnp.maximum(peak_ref[:, :1], level)
    factor_ref[...] = jnp.sum(jnp.where(eye(heads), factor, 0.0), 0, keepdims=True)
    head = lax.broadcasted_iota(jnp.int32, (heads, width), 0)
    lane = lax.broadcasted_iota(jnp.int32, (heads, width), 1)
    scale = jnp.sum(jnp.where(lane // HDIM == head, jnp.sqrt(factor), 0.0), 0, keepdims=True)
    out_ref[...] = weight_ref[...].astype(FULL) * scale


def clip(weight, peak, level, token):
    rows, width = weight.shape
    spec = pl.BlockSpec((rows // 4, width), lambda i: (i, 0))
    outs, token = call(
        clip_kernel,
        "clip",
        [(weight, spec), whole(peak), whole(level.reshape(1, -1))],
        [((rows, width), FULL, spec), whole_out((1, level.size), FULL)],
        grid=(4,),
        token=token,
        us=0.01,
        vmem=16,
    )
    return outs, token


def normed_kernel(
    packed_ref, w_query_ref, w_key_ref, w_value_ref, own_ref, other_ref, near, sems
):
    copies = [
        pltpu.make_async_copy(ref, near.at[at], sems.at[at])
        for at, ref in enumerate((w_key_ref, w_value_ref, w_query_ref))
    ]
    for copy in copies:
        copy.start()
    tokens = own_ref.shape[0]
    dq, dk, dv = (
        packed_ref[pl.ds(start * tokens, size * tokens), :]
        for start, size in ((0, 1), (1, 2), (3, 2))
    )
    copies[0].wait()
    total = dot_back(dk, near[0])
    copies[1].wait()
    total = total + dot_back(dv, near[1])
    other_ref[...] = total[:tokens].astype(LOW)
    copies[2].wait()
    own_ref[...] = total[tokens:] + dot_back(dq, near[2])


def normed_grads(packed, weights, tokens, token):
    width = packed.shape[1]
    (own, other), token = call(
        normed_kernel,
        "normed_grads",
        [whole(packed)] + [(array, None) for array in weights],
        [whole_out((tokens, width), FULL), whole_out((tokens, width), LOW)],
        token=token,
        scratch=[pltpu.VMEM((3, width, width), LOW), pltpu.SemaphoreType.DMA((3,))],
        far_out=(0, 1),
        us=0.01,
        vmem=14,
    )
    return own, other, token


def input_kernel(rows_ref, gain_ref, own_ref, got_ref, past_ref, out_ref):
    rows = rows_ref[...].astype(FULL)
    inverse = lax.rsqrt(jnp.mean(rows * rows, axis=1, keepdims=True) + EPSILON)
    scaled = rows * inverse
    grad = (own_ref[...] + got_ref[...].astype(FULL)) * gain_ref[...]
    along = jnp.mean(scaled * grad, axis=1, keepdims=True)
    out_ref[0] = past_ref[...] + inverse * (grad - scaled * along)


def input_grads(rows, gain, own, got, past, token):
    tokens, width = rows.shape
    (out,), token = call(
        input_kernel,
        "input_grads",
        [whole(array) for array in (rows, gain, own, got, past)],
        [whole_out((1, tokens, width), FULL)],
        token=token,
        far_in=(0, 1, 2, 4),
        far_out=(0,),
        us=10,
    )
    return out, token


def back_kernel(
    at_ref, spread_ref, rows_ref, after_ref, gain_ref, grad_ref, weights_ref,
    total_ref, branch_ref, attended_ref, gain_grad_ref,
):
    rows = after_ref[...]
    inverse = lax.rsqrt(jnp.mean(rows * rows, axis=1, keepdims=True) + EPSILON)
    scaled = rows * inverse
    blocks, size, _ = rows_ref.shape
    grad = sum(
        transpose_dot(spread_ref[pl.ds(k * size, size), :], rows_ref[lax.rem(at_ref[3] + k, blocks)])
        for k in range(blocks)
    )
    gain_grad_ref[...] = jnp.sum(scaled * grad, axis=0, keepdims=True)
    grad = grad * gain_ref[...]
    along = jnp.mean(scaled * grad, axis=1, keepdims=True)
    total = grad_ref[...].astype(FULL) + inverse * (grad - scaled * along)
    total_ref[...] = total
    branch = total.astype(LOW)
    branch_ref[...] = branch
    attended_ref[...] = dot_back(branch, weights_ref[...]).astype(LOW)


def back_to_attention(at, spread, rows, after, gain, grad, weights, fetch, token):
    shape = after.shape
    inputs = (spread, rows, after, gain, grad, weights)
    return call(
        back_kernel,
        "back",
        [whole(array) for array in inputs],
        [
            whole_out(shape, FULL),
            whole_out(shape, LOW),
            whole_out(shape, LOW),
            whole_out((1, shape[1]), FULL),
        ],
        token=token,
        vmem=16,
        us=0.01,
        far_in=(0, 2, 4),
        far_out=(0,),
        prefetch=(at,),
        fetch=fetch,
    )


def mix_kernel(at_ref, pick_ref, rows_ref, gates_ref, after_ref, out_ref, peak_ref):
    top, tokens = gates_ref.shape
    blocks = rows_ref.shape[0]
    size = pick_ref.shape[0] // blocks
    total = after_ref[...]
    gates = [to_column(gates_ref[r : r + 1, :]) for r in range(top)]
    for block in range(blocks):
        rows = rows_ref[lax.rem(at_ref[3] + block, blocks), :size, :]
        for r in range(top):
            pick = pick_ref[pl.ds(block * size, size), pl.ds(r * tokens, tokens)]
            total = total + gates[r] * transpose_dot(pick, rows)
    out_ref[0] = total.astype(LOW)
    if rows_ref.shape[1] > size:
        peaks = [
            rows_ref[block, size:, :LANES].astype(FULL)
            + rows_ref[block, size:, LANES : 2 * LANES].astype(FULL)
            for block in range(blocks)
        ]
        peak_ref[...] = functools.reduce(jnp.maximum, peaks)


def mix(at, pick, rows, gates, after, token):
    (out, peak), token = call(
        mix_kernel,
        "mix",
        [whole(pick), whole(rows), whole(gates), whole(after)],
        [whole_out((1, *after.shape), LOW), whole_out((16, LANES), FULL)],
        token=token,
        us=0.01,
        far_in=(0, 3),
        prefetch=(at,),
    )
    return out, peak, token


def local(
    block_in,
    seg_ids,
    routes,
    gates,
    buckets,
    norm_attn,
    norm_ffn,
    w_query,
    w_key,
    w_value,
    w_out_attn,
    rel_bias,
    clip_level,
    w_in,
    w_down,
    cotangent,
):
    tokens, width = block_in.shape[1:]
    heads = width // HDIM
    n_ctx, experts, n_dp = (lax.axis_size(axis) for axis in ("ctx", "exp", "dp"))
    fast = (n_ctx, experts, n_dp) == (2, 4, 4)
    devices = n_ctx * experts * n_dp
    length = n_ctx * tokens
    y, z, x, core = place()
    place_all = (y * experts + z) * n_dp + lax.axis_index("dp")
    top_count = routes.shape[-1]
    capacity = tokens * top_count * 3 // (2 * experts)
    at = jnp.stack([y, x, core, z])

    (spread, pick, mask, rows_copy, *grad_out), token = front(
        at, routes[0].T, gates[0].T, cotangent[0], seg_ids, block_in[0], experts, capacity
    )
    backs = list(range(n_ctx - 1, 0, -1))
    earlier = [
        lax.ppermute(block_in[0], "ctx", [(i, (i + back) % n_ctx) for i in range(n_ctx)])
        for back in backs
    ]
    grad_blocks = to_experts(grad_out)
    bucket_hot, bias, normed_all, queries, keys, values = project(
        buckets.reshape(1, length),
        rel_bias.reshape(NB, heads),
        norm_attn.reshape(1, width),
        (*earlier, block_in[0]),
        (w_query, w_key, w_value),
    )

    attended, probs, peak_lanes, w_out_near = attention(
        queries, keys, values, bias, mask, (w_out_attn,)
    )
    after, sent = after_attention(
        attended, w_out_near, rows_copy, norm_ffn.reshape(1, width), spread, experts
    )

    row_blocks = to_experts(sent)
    own_gain, own_table = width // devices, NB * heads // devices
    if fast:
        expert_grad, token = side_by_side(grad_blocks, token)
        parts = (normed_all, attended)
        parts = parts + tuple(swapped(part, "dp", 1) for part in parts)
        left, token = turn(at, parts, token)
        peak, token = larger(peak_lanes, swapped(peak_lanes, "dp", 1), token)
        peak, token = larger(peak, swapped(peak, "dp", 2), token)
        peak, token = larger(peak, swapped(peak, "ctx", 1), token)
        expert_rows, token = side_by_side(row_blocks, token)
        both_rows = expert_rows, swapped(expert_rows, "dp", 1)
        both_grads = expert_grad, swapped(expert_grad, "dp", 1)
        firsts, token = weights_ahead(at, w_in, w_down, token)
        outs, token = expert_halves(at, both_rows, both_grads, firsts, w_in, w_down, token)
        back_keep, back_send, dgate, dup, rows_turned, hid, *down = outs
        back_got = swapped(back_send, "dp", 1)
        down = swapped(down[0], "dp", 2), down[1], to_down_plane(down[2]), down[2]
        back_rows, token = join(at, back_keep, back_got, experts, token)
        back_home = over_experts(back_rows)
        first, token = in_terms(at, rows_turned, dgate, dup, token)
        first = plane_first(first)
        down_a, down_b, token = down_second(at, down, token, 5)
        out_keep, out_send, w_out_near, token = expert_results(at, hid, w_down, (w_out_attn,), token)
    else:
        expert_rows = jnp.concatenate(row_blocks, axis=0)
        expert_grad = jnp.concatenate(grad_blocks, axis=0)
        (out_rows, back_rows, dgate, dup, hid_turned, rows_turned), token = expert(
            expert_rows, expert_grad, w_in, w_down, token
        )
        expert_first, expert_second = (
            lax.psum_scatter(grads, ("ctx", "dp"), scatter_dimension=0, tiled=True)[None]
            for grads in (
                dot_rows(rows_turned, jnp.concatenate([dgate, dup], axis=1)),
                dot_rows(hid_turned, expert_grad),
            )
        )
        back_home, out_home = (
            jnp.stack(from_experts(list(rows.reshape(experts, capacity, width))))
            for rows in (back_rows, out_rows)
        )

    home = at if fast else jnp.zeros_like(at)
    soon = (queries, keys, values, probs) + ((bucket_hot,) if fast else ())
    (grad_after, grad_branch, grad_attended, grad_gain_ffn, *soon), token = back_to_attention(
        home, spread, back_home, after, norm_ffn.reshape(1, width), cotangent[0], w_out_near, soon, token
    )
    if fast:
        packed, token = attention_back(
            *soon[:4], grad_attended, token, (grad_branch, soon[4], grad_gain_ffn, devices),
        )
        packed_got = swapped(packed, "dp", 1)
        (left,), token = bring(token, 20, left)
        plane_2, token = shared_terms(at, left, packed, packed_got, experts, token)
        plane_2 = plane_first(plane_2)
        out_send, = hold(token, out_send)
        out_got = swapped(out_send, "dp", 1)
        out_rows, token = join_peak(at, out_keep, out_got, peak, experts, token)
        out_home = over_experts(out_rows)
        normed_own_grad, normed_other_grad, token = normed_grads(
            packed, (w_query, w_key, w_value), tokens, token
        )
        normed_got = lax.ppermute(normed_other_grad, "ctx", [(1, 0)])
        in_a, in_b, token = plane_second(first, token, 0.01)
    else:
        dq, dk, dv, lines, token = attention_back(
            *soon, grad_attended, token
        )
        lines = lines[:, :GROUP, :].reshape(heads, length + tokens)
        grad_table = lax.dot_general(
            bucket_hot, lines, (((1,), (1,)), ((), ())), precision=FULL_PRECISION
        ).reshape(-1)
        mixed, _, _ = mix(home, pick, out_home, gates[0].T, after, token)
        peak = jnp.max(peak_lanes[:, :GROUP, :], axis=-1).reshape(heads)
        peak = lax.pmax(peak, ("ctx", "exp", "dp"))
        peak = jnp.broadcast_to(peak[:, None], (heads, LANES))
        (clipped_query, factor), token = clip(w_query, peak, clip_level, token)
        (clipped_key, _), _ = clip(w_key, peak, clip_level, token)

        grad_normed = dot_back(dk, w_key) + dot_back(dv, w_value)
        grad_normed_own = grad_normed[length - tokens :] + dot_back(dq, w_query)
        for block, back in enumerate(backs):
            term = grad_normed[block * tokens : (block + 1) * tokens].astype(LOW)
            returned = lax.ppermute(term, "ctx", [((i + back) % n_ctx, i) for i in range(n_ctx)])
            grad_normed_own = grad_normed_own + returned.astype(FULL)
        own_rows = block_in[0].astype(FULL)
        _, norm_pull = jax.vjp(lambda rows: rms_norm(rows, norm_attn), own_rows)
        grad_input = (grad_after + norm_pull(grad_normed_own)[0])[None]

    if fast:
        shared_a, shared_b, token = plane_second(plane_2, token, 10)
        shared_a, shared_b = swapped(shared_a, "ctx", 1), swapped(shared_b, "dp", 2)
        mixed, peak, token = mix(at, pick, out_home, gates[0].T, after, token)
        grad_input, token = input_grads(
            block_in[0], norm_attn.reshape(1, width), normed_own_grad, normed_got, grad_after, token
        )
        in_a, in_b = hold(token, in_a, in_b)
        in_a, in_b = swapped(in_a, "ctx", 1), swapped(in_b, "dp", 2)
        (clipped_query, factor), token = clip(w_query, peak, clip_level, token)
        plane, token = pair_last(plane_2, shared_a, shared_b, experts, token)
        plane = over_experts(plane)
        down_a, down_b = hold(token, down_a, down_b)
        down_a, down_b = to_down_plane(down_a), in_down_plane(down_b)
        (clipped_key, _), token = clip(w_key, peak, clip_level, token)
        in_own, in_send, token = in_last(at, first, in_a, in_b, token)
        in_got = swapped(in_send, "dp", 1)
        down_keep, down_send, token = down_last(at, down, down_a, down_b, token)
        down_got = swapped(down_send, "dp", 1)
        expert_first, token = in_finish(at, in_own, in_got, token)
        expert_second, token = down_finish(at, down_keep, down_got, token)
        outs, token = last_rows(
            place_all, plane, own_gain, own_table, (w_query, w_key, w_value), norm_attn, token
        )
        shared_q, shared_k, shared_v, shared_o = outs[:4]
        small_attn, small_ffn, small_table = (out.reshape(-1) for out in outs[4:])
    else:
        shared_q, shared_k, shared_v, shared_o = (
            lax.psum_scatter(grads, ("ctx", "exp", "dp"), scatter_dimension=0, tiled=True)
            for grads in (
                transpose_dot(normed_all[length - tokens :], dq),
                transpose_dot(normed_all, dk),
                transpose_dot(normed_all, dv),
                transpose_dot(attended, grad_branch),
            )
        )
        small_ffn, small_table = (
            lax.dynamic_slice_in_dim(lax.psum(array, ("ctx", "exp", "dp")), place_all * own, own)
            for array, own in ((grad_gain_ffn[0], own_gain), (grad_table, own_table))
        )
        pairs = ((shared_q, w_query), (shared_k, w_key), (shared_v, w_value))
        row_sums = sum(
            jnp.sum(
                grads * lax.dynamic_slice_in_dim(weights, place_all * own_gain, own_gain).astype(FULL),
                axis=1,
            )
            for grads, weights in pairs
        )
        small_attn = row_sums / lax.dynamic_slice_in_dim(norm_attn, place_all * own_gain, own_gain)

    return (
        mixed,
        grad_input,
        small_attn,
        small_ffn,
        shared_q,
        shared_k,
        shared_v,
        shared_o,
        small_table,
        expert_first,
        expert_second,
        clipped_query,
        clipped_key,
        factor.reshape(-1),
    )


def solution(mesh):
    tokens = P(("exp", "dp"), "ctx", None)
    everywhere = P(("ctx", "exp", "dp"))
    by_rows = P(("ctx", "exp", "dp"), None)
    by_expert = P("exp", None, None)
    expert_rows = P("exp", ("ctx", "dp"), None)
    in_specs = (tokens, P(("exp", "dp"), None), tokens, tokens) + (P(),) * 9
    in_specs = in_specs + (by_expert, by_expert, tokens)
    out_specs = (tokens, tokens, everywhere, everywhere) + (by_rows,) * 4
    out_specs = out_specs + (everywhere, expert_rows, expert_rows, P(), P(), P())
    return jax.shard_map(local, mesh=mesh, in_specs=in_specs, out_specs=out_specs, check_vma=False)
```

```python
import functools

import jax
import jax.numpy as jnp
from jax import lax
from jax.experimental import pallas as pl
from jax.experimental.pallas import tpu as pltpu
from jax.sharding import PartitionSpec as P

HDIM = 64
NB = 32
GROUP = 4
LANES = 128
EPSILON = 1e-06
FULL_PRECISION = lax.Precision.HIGHEST
LOW = jnp.bfloat16
FULL = jnp.float32
OUTSIDE = -1e30
GELU_SCALE = 0.7978845608028654
GELU_CUBE = 0.044715


def rms_norm(rows, gain):
    return rows * lax.rsqrt(jnp.mean(rows * rows, axis=-1, keepdims=True) + EPSILON) * gain


def dot_rows(left, right):
    return lax.dot_general(left, right, (((1,), (0,)), ((), ())), preferred_element_type=FULL)


def dot_back(left, right):
    return lax.dot_general(left, right, (((1,), (1,)), ((), ())), preferred_element_type=FULL)


def transpose_dot(left, right):
    return lax.dot_general(left, right, (((0,), (0,)), ((), ())), preferred_element_type=FULL)


def swapped(array, axis, bit):
    size = lax.axis_size(axis)
    return lax.ppermute(array, axis, [(i, i ^ bit) for i in range(size)])


def shifted(array, axis, shift):
    size = lax.axis_size(axis)
    return lax.ppermute(array, axis, [(i, (i + shift) % size) for i in range(size)])


def to_experts(blocks):
    return [blocks[0]] + [shifted(blocks[k], "exp", k) for k in range(1, len(blocks))]


def from_experts(blocks):
    return [blocks[0]] + [shifted(blocks[k], "exp", len(blocks) - k) for k in range(1, len(blocks))]


def over_experts(blocks):
    return lax.all_to_all(blocks, "exp", split_axis=0, concat_axis=0, tiled=True)


MICROSECOND = 1.15e9


def call(
    body, name, inputs, outputs, us, grid=None, token=None, prefetch=(), scratch=(), vmem=6,
    near_in=(), near_out=(), far_in=(), far_out=(), fetch=(),
    part_in=None, onto=(),
):
    part_in = dict(part_in or {})
    far_in = tuple(far_in) + tuple(part_in)
    inputs = list(inputs) + [(array, None) for array in fetch]
    outputs = list(outputs) + [whole_out(array.shape, array.dtype) for array in fetch]
    n_pre, n_in, n_out = len(prefetch), len(inputs), len(outputs)
    held = [] if token is None else [token]
    n_far, n_scratch = len(far_in) + len(far_out), len(scratch)

    def kernel(*refs):
        split = n_pre + n_in
        outs = split + len(held)
        rest = refs[outs + n_out + 1 :]
        ins_here, outs_here = list(refs[:split]), list(refs[outs : outs + n_out])
        copies = []
        for number, at in enumerate(far_in):
            here = rest[n_scratch + number]
            source = refs[n_pre + at].at[part_in[at]] if at in part_in else refs[n_pre + at]
            copies.append(pltpu.make_async_copy(source, here, rest[-1].at[number]))
            ins_here[n_pre + at] = here
        for copy in copies:
            copy.start()
        fetches = [
            pltpu.make_async_copy(ins_here.pop(), outs_here.pop(), rest[-1].at[n_far + number])
            for number in range(len(fetch))
        ]
        for copy in fetches:
            copy.start()
        for copy in copies:
            copy.wait()
        copies = []
        for number, at in enumerate(far_out, len(far_in)):
            here = rest[n_scratch + number]
            copies.append(pltpu.make_async_copy(here, refs[outs + at], rest[-1].at[number]))
            outs_here[at] = here
        body(*ins_here, *outs_here, *rest[:n_scratch])
        for copy in fetches:
            copy.wait()
        for copy in copies:
            copy.start()
        for copy in copies:
            copy.wait()

    where = lambda at, near: pltpu.VMEM if at in near else pltpu.HBM
    arrays = [array for array, _ in inputs]
    shapes = [(shape, dtype) for shape, dtype, _ in outputs]
    anywhere = pl.BlockSpec(memory_space=pl.ANY)
    if grid is None:
        near = pl.BlockSpec(memory_space=pltpu.VMEM)
        far = [at in far_in or spec is None for at, (_, spec) in enumerate(inputs)]
        far_results = [at in far_out or spec is None for at, (_, _, spec) in enumerate(outputs)]
        left = lambda at: tuple(
            size if axis >= len(part_in.get(at, ())) else len(range(size)[part_in[at][axis]])
            for axis, size in enumerate(arrays[at].shape)
            if axis >= len(part_in.get(at, ())) or isinstance(part_in[at][axis], slice)
        )
        buffers = [pltpu.VMEM(left(at), arrays[at].dtype) for at in far_in]
        buffers += [pltpu.VMEM(*shapes[at]) for at in far_out]
        n_sems = n_far + len(fetch)
        buffers += [pltpu.SemaphoreType.DMA((n_sems,))] if n_sems else []
        form = dict(
            in_specs=[pl.BlockSpec(memory_space=pltpu.SMEM)] * n_pre
            + [anywhere if away else near for away in far]
            + [anywhere] * len(held),
            out_specs=[anywhere if away else near for away in far_results] + [anywhere],
            scratch_shapes=list(scratch) + buffers,
        )
        arrays = [
            pltpu.with_memory_space_constraint(array, pltpu.HBM) if away else array
            for array, away in zip(arrays, far)
        ]
        shapes = [
            pltpu.HBM(*one) if away else jax.ShapeDtypeStruct(*one)
            for away, one in zip(far_results, shapes)
        ]
    else:
        form = dict(
            grid_spec=pltpu.PrefetchScalarGridSpec(
                num_scalar_prefetch=n_pre,
                grid=grid,
                in_specs=[spec for _, spec in inputs] + [anywhere] * len(held),
                out_specs=[spec for _, _, spec in outputs] + [anywhere],
                scratch_shapes=list(scratch),
            )
        )
        arrays = [
            pltpu.with_memory_space_constraint(array, where(at, near_in))
            for at, array in enumerate(arrays)
        ]
        shapes = [where(at, near_out)(*one) for at, one in enumerate(shapes)]
    held = [pltpu.with_memory_space_constraint(array, pltpu.HBM) for array in held]
    results = pl.pallas_call(
        kernel,
        out_shape=shapes + [pltpu.HBM((8, LANES), FULL)],
        cost_estimate=pl.CostEstimate(
            flops=int(us * MICROSECOND), bytes_accessed=1, transcendentals=0
        ),
        compiler_params=pltpu.CompilerParams(vmem_limit_bytes=vmem * 2**20),
        name=name,
        input_output_aliases={n_pre + one: other for one, other in onto},
        **form,
    )(*prefetch, *arrays, *held)
    return list(results[:-1]), results[-1]


def whole(array):
    return array, pl.BlockSpec(array.shape, lambda *_: (0,) * array.ndim)


def whole_out(shape, dtype):
    return shape, dtype, pl.BlockSpec(shape, lambda *_: (0,) * len(shape))


def hold(token, *arrays):
    anywhere = pl.BlockSpec(memory_space=pl.ANY)
    return pl.pallas_call(
        lambda *refs: None,
        in_specs=[anywhere] * (len(arrays) + 1),
        out_specs=[anywhere] * len(arrays),
        out_shape=[jax.ShapeDtypeStruct(array.shape, array.dtype) for array in arrays],
        input_output_aliases={at + 1: at for at in range(len(arrays))},
        cost_estimate=pl.CostEstimate(flops=1, bytes_accessed=1, transcendentals=0),
        name="hold",
    )(token, *arrays)


def pass_kernel(*refs):
    half = len(refs) // 2
    for ref, out_ref in zip(refs[:half], refs[half:]):
        out_ref[...] = ref[...]


def bring(token, us, *arrays):
    return call(lambda *refs: None, "bring", [], [], token=token, fetch=arrays, us=us)


def pass_on(token, *arrays):
    return call(
        pass_kernel,
        "pass_on",
        [whole(array) for array in arrays],
        [whole_out(array.shape, array.dtype) for array in arrays],
        token=token,
        us=1,
    )


def eye(size):
    rows = lax.broadcasted_iota(jnp.int32, (size, size), 0)
    return rows == lax.broadcasted_iota(jnp.int32, (size, size), 1)


def to_column(row):
    size = row.shape[1]
    return jnp.sum(jnp.where(eye(size), row, jnp.zeros_like(row)), 1, keepdims=True)


def front_kernel(
    at_ref, routes_ref, gates_ref, grad_ref, seg_ref, rows_ref,
    spread_ref, pick_ref, mask_ref, copy_ref, *out_refs,
):
    top, tokens = routes_ref.shape
    experts, capacity = len(out_refs), out_refs[0].shape[0]
    routes = [routes_ref[r : r + 1, :] for r in range(top)]
    gates = [gates_ref[r : r + 1, :] for r in range(top)]
    before = lax.broadcasted_iota(jnp.int32, (tokens, tokens), 0)
    before = before < lax.broadcasted_iota(jnp.int32, (tokens, tokens), 1)
    slots = lax.broadcasted_iota(jnp.int32, (capacity, tokens), 0).astype(FULL)
    for e in range(experts):
        part = pl.ds(e * capacity, capacity)
        name = lax.rem(at_ref[3] + e, experts)
        hits = [jnp.where(route == name, 1.0, 0.0) for route in routes]
        named = functools.reduce(jnp.add, hits)
        slot = jnp.sum(jnp.where(before, to_column(named), 0.0), 0, keepdims=True)
        place = (slots == slot).astype(FULL)
        spread = place * named
        gate = functools.reduce(jnp.add, [hit * g for hit, g in zip(hits, gates)])
        spread_low = spread.astype(LOW)
        spread_ref[part, :] = spread_low
        for r in range(top):
            pick_ref[part, pl.ds(r * tokens, tokens)] = (place * hits[r]).astype(LOW)
        slot_gate = jnp.sum(spread * gate, 1, keepdims=True)
        out_refs[e][...] = (slot_gate * dot_rows(spread_low, grad_ref[...])).astype(LOW)
    length = mask_ref.shape[1]
    ctx = at_ref[0]
    seg = jnp.broadcast_to(seg_ref[...].astype(FULL), (8, length))
    keys = pltpu.roll(seg, length - (ctx + 1) * tokens, 1)[:1, :]
    at_row = lax.broadcasted_iota(jnp.int32, (tokens, length), 0) + (length - tokens)
    at_key = lax.broadcasted_iota(jnp.int32, (tokens, length), 1)
    own = jnp.sum(jnp.where(at_row == at_key, keys, 0.0), 1, keepdims=True)
    allowed = (at_key <= at_row) & (own == keys) & (at_key >= length - (ctx + 1) * tokens)
    mask_ref[...] = jnp.where(allowed, 0.0, OUTSIDE)
    copy_ref[...] = rows_ref[...]


def front(at, routes, gates, grad, seg, rows, experts, capacity):
    top, tokens = routes.shape
    slots = experts * capacity
    return call(
        front_kernel,
        "front",
        [whole(array) for array in (routes, gates, grad, seg, rows)],
        [
            whole_out((slots, tokens), LOW),
            whole_out((slots, top * tokens), LOW),
            whole_out((tokens, seg.shape[1]), FULL),
            whole_out(rows.shape, LOW),
        ]
        + [whole_out((capacity, grad.shape[1]), LOW)] * experts,
        prefetch=(at,),
        far_in=(0, 1, 2, 3, 4),
        far_out=(1,),
        us=1.5,
    )


def project_kernel(buckets_ref, table_ref, gain_ref, *refs, blocks):
    x_refs, weights = refs[:blocks], refs[blocks : blocks + 3]
    hot_ref, bias_ref, normed_ref, q_ref, k_ref, v_ref, near, sems = refs[blocks + 3 :]
    copies = [
        pltpu.make_async_copy(ref, near.at[at], sems.at[at]) for at, ref in enumerate(weights)
    ]
    for copy in copies:
        copy.start()
    tokens = q_ref.shape[0]
    for at, x_ref in enumerate(x_refs):
        rows = rms_norm(x_ref[...].astype(FULL), gain_ref[...])
        normed_ref[pl.ds(at * tokens, tokens), :] = rows.astype(LOW)
    bias_part(buckets_ref, table_ref, hot_ref, bias_ref)
    own = pl.ds((blocks - 1) * tokens, tokens)
    for at, (out_ref, rows) in enumerate(
        ((q_ref, own), (k_ref, slice(None)), (v_ref, slice(None)))
    ):
        copies[at].wait()
        out_ref[...] = dot_rows(normed_ref[rows, :], near[at]).astype(LOW)


def bias_part(buckets_ref, table_ref, hot_ref, bias_ref):
    heads, rows, keys = bias_ref.shape
    width = hot_ref.shape[1]
    buckets = buckets_ref[...].astype(FULL)
    column = jnp.sum(jnp.where(eye(keys), buckets, 0.0), 1, keepdims=True)
    distance = lax.broadcasted_iota(jnp.int32, (keys, width), 0)
    lane = lax.broadcasted_iota(jnp.int32, (keys, width), 1)
    turned = jnp.sum(jnp.where(distance + lane == keys - 1, column, 0.0), 0, keepdims=True)
    bucket = lax.broadcasted_iota(jnp.int32, (NB, width), 0).astype(FULL)
    hot = jnp.where(bucket == turned, 1.0, 0.0)
    hot_ref[...] = hot
    by_lane = lax.dot_general(
        table_ref[...], hot, (((0,), (0,)), ((), ())), precision=FULL_PRECISION,
        preferred_element_type=FULL,
    )
    for head in range(heads):
        line = jnp.broadcast_to(by_lane[head : head + 1, :], (8, width))
        line = pltpu.roll(line, keys + 1, 1, stride=1, stride_axis=0)
        for start in range(0, rows, 8):
            moved = line if start == 0 else pltpu.roll(line, start, 1)
            bias_ref[head, pl.ds(start, 8), :] = moved[:, :keys]


def project(buckets, table, gain, parts, weights):
    heads, keys = table.shape[1], buckets.shape[1]
    tokens, width = parts[0].shape
    outs, _ = call(
        functools.partial(project_kernel, blocks=len(parts)),
        "project",
        [whole(array) for array in (buckets, table, gain, *parts)]
        + [(array, None) for array in weights],
        [
            whole_out((NB, keys + tokens), FULL),
            whole_out((heads, tokens, keys), FULL),
            whole_out((keys, width), LOW),
            whole_out((tokens, width), LOW),
            whole_out((keys, width), LOW),
            whole_out((keys, width), LOW),
        ],
        scratch=[pltpu.VMEM((3, width, width), LOW), pltpu.SemaphoreType.DMA((3,))],
        us=4.5,
        vmem=16,
    )
    return outs


def half_lanes(half, shape):
    lane = lax.broadcasted_iota(jnp.int32, shape, 1)
    return lane < HDIM if half == 0 else lane >= HDIM


def attention_kernel(q_ref, k_ref, v_ref, bias_ref, mask_ref, out_ref, probs_ref, peak_ref):
    groups = peak_ref.shape[0]

    def group(step, _):
        mask = mask_ref[...]
        for pair in range(GROUP // 2):
            lanes = pair_lanes(step, pair)
            queries, keys, values = q_ref[:, lanes], k_ref[:, lanes], v_ref[:, lanes]
            parts = []
            for half in range(2):
                at = 2 * pair + half
                own = half_lanes(half, queries.shape)
                raw = dot_back(jnp.where(own, queries, jnp.zeros_like(queries)), keys)
                raw = raw * HDIM**-0.5 + mask
                top = jnp.max(raw, axis=0, keepdims=True)
                best = top[:, :LANES]
                for start in range(LANES, top.shape[1], LANES):
                    best = jnp.maximum(best, top[:, start : start + LANES])
                peak_ref[step, at : at + 1, :] = best
                scores = raw + bias_ref[step * GROUP + at]
                raised = jnp.exp(scores - jnp.max(scores, axis=1, keepdims=True))
                probs = raised * (1.0 / jnp.sum(raised, axis=1, keepdims=True))
                probs_low = probs.astype(LOW)
                probs_ref[step * GROUP + at] = probs_low
                parts.append(dot_rows(probs_low, values))
            first = half_lanes(0, parts[0].shape)
            out_ref[:, lanes] = jnp.where(first, parts[0], parts[1]).astype(LOW)
        return 0

    lax.fori_loop(0, groups, group, 0)


def pair_lanes(step, pair):
    return pl.ds(pl.multiple_of(step * GROUP * HDIM + pair * LANES, LANES), LANES)


def attention(queries, keys, values, bias, mask, fetch):
    rows, width = queries.shape
    length = keys.shape[0]
    heads = width // HDIM
    (out, probs, peak, *fetched), _ = call(
        attention_kernel,
        "attention",
        [whole(array) for array in (queries, keys, values, bias, mask)],
        [
            whole_out((rows, width), LOW),
            whole_out((heads, rows, length), LOW),
            whole_out((heads // GROUP, 8, LANES), FULL),
        ],
        us=4.5,
        vmem=10,
        far_out=(1,),
        fetch=fetch,
    )
    return out, probs, peak, *fetched


def attention_back_kernel(
    q_ref, k_ref, v_ref, probs_ref, grad_ref, dq_ref, dk_ref, dv_ref, lines_ref
):
    groups = lines_ref.shape[0]
    rows, length = probs_ref.shape[1:]
    scale = HDIM**-0.5

    def group(step, _):
        for pair in range(GROUP // 2):
            lanes = pair_lanes(step, pair)
            queries, keys, values, grad = (
                ref[:, lanes] for ref in (q_ref, k_ref, v_ref, grad_ref)
            )
            dq, dk, dv = [], [], []
            for half in range(2):
                at = 2 * pair + half
                own = half_lanes(half, grad.shape)
                dp = dot_back(jnp.where(own, grad, jnp.zeros_like(grad)), values)
                probs_low = probs_ref[step * GROUP + at]
                probs = probs_low.astype(FULL)
                ds = probs * (dp - jnp.sum(probs * dp, axis=1, keepdims=True))
                ds_low = ds.astype(LOW)
                dq.append(dot_rows(ds_low, keys))
                dk.append(transpose_dot(ds_low, queries))
                dv.append(transpose_dot(probs_low, grad))
                wide = jnp.concatenate([ds, jnp.zeros((rows, rows), FULL)], axis=1)
                total = wide[rows - 8 :, :]
                for start in range(0, rows - 8, 8):
                    total = total + pltpu.roll(wide[start : start + 8, :], rows - 8 - start, 1)
                line = lax.broadcasted_iota(jnp.int32, total.shape, 0)
                for bit in (1, 2, 4):
                    total = jnp.where(((7 - line) & bit) != 0, pltpu.roll(total, bit, 1), total)
                lines_ref[step, at : at + 1, :] = jnp.sum(total, axis=0, keepdims=True)
            first = half_lanes(0, dq[0].shape)
            dq_ref[:, lanes] = (jnp.where(first, dq[0], dq[1]) * scale).astype(LOW)
            first = half_lanes(0, dk[0].shape)
            dk_ref[:, lanes] = (jnp.where(first, dk[0], dk[1]) * scale).astype(LOW)
            dv_ref[:, lanes] = jnp.where(first, dv[0], dv[1]).astype(LOW)
        return 0

    lax.fori_loop(0, groups, group, 0)


def packed_back_kernel(
    q_ref, k_ref, v_ref, probs_ref, grad_ref, branch_ref, hot_ref, gain_ref, out_ref, lines_ref
):
    rows, length = probs_ref.shape[1:]
    ends = [0, rows, rows + length, rows + 2 * length, 2 * rows + 2 * length]
    parts = [out_ref.at[pl.ds(a, b - a), :] for a, b in zip(ends, ends[1:])]
    attention_back_kernel(q_ref, k_ref, v_ref, probs_ref, grad_ref, *parts[:3], lines_ref)
    parts[3][...] = branch_ref[...]
    groups = lines_ref.shape[0]
    width = gain_ref.shape[1]
    devices = out_ref.shape[0] - ends[4]
    own, turns = width // devices, LANES * devices // width
    device = lax.broadcasted_iota(jnp.int32, (devices, width), 0)
    feature = lax.broadcasted_iota(jnp.int32, (devices, width), 1)
    spread = jnp.where(feature // own == device, gain_ref[...], 0.0)
    folded = functools.reduce(
        jnp.add, [spread[:, start : start + LANES] for start in range(0, width, LANES)]
    )
    device = lax.broadcasted_iota(jnp.int32, folded.shape, 0)
    small = folded
    for turn_by in range(1, turns):
        moved = pltpu.roll(folded, LANES - turn_by * own, 1)
        small = jnp.where(device % turns == turn_by, moved, small)
    lines = jnp.concatenate([lines_ref[g, :GROUP, :] for g in range(groups)], axis=0)
    blank = jnp.zeros((LANES - TABLE_LANE - lines.shape[0], lines.shape[1]), FULL)
    lines = jnp.concatenate([jnp.zeros((TABLE_LANE, lines.shape[1]), FULL), lines, blank], axis=0)
    upper = lines.astype(LOW)
    lower = (lines - upper.astype(FULL)).astype(LOW)
    hot = hot_ref[...].astype(LOW)
    small = small + dot_back(hot, upper) + dot_back(hot, lower)
    out_ref[pl.ds(ends[4], devices), :LANES] = small.astype(LOW)


def attention_back(queries, keys, values, probs, grad, token, packed=None):
    rows, width = queries.shape
    length = keys.shape[0]
    heads = width // HDIM
    lines = whole_out((heads // GROUP, 8, length + rows), FULL)
    inputs = [whole(array) for array in (queries, keys, values, probs, grad)]
    if packed is None:
        outs, token = call(
            attention_back_kernel,
            "attention_back",
            inputs,
            [whole_out((size, width), LOW) for size in (rows, length, length)] + [lines],
            token=token,
            us=6.6,
            vmem=16,
        )
        return *outs, token
    branch, hot, gain, devices = packed
    (out, _), token = call(
        packed_back_kernel,
        "attention_back",
        inputs + [whole(branch), whole(hot), whole(gain)],
        [whole_out((2 * rows + 2 * length + devices, width), LOW), lines],
        token=token,
        us=7,
        vmem=16,
    )
    return out, token


def post_kernel(attended_ref, weights_ref, rows_ref, gain_ref, spread_ref, after_ref, *out_refs):
    after = rows_ref[...].astype(FULL) + dot_rows(attended_ref[...], weights_ref[...])
    after_ref[...] = after
    sent = rms_norm(after, gain_ref[...]).astype(LOW)
    size = out_refs[0].shape[0]
    for at, out_ref in enumerate(out_refs):
        out_ref[...] = dot_rows(spread_ref[pl.ds(at * size, size), :], sent).astype(LOW)


def after_attention(attended, weights, rows, gain, spread, experts, token):
    tokens, width = rows.shape
    (after, *sent), token = call(
        post_kernel,
        "post",
        [whole(array) for array in (attended, weights, rows, gain, spread)],
        [whole_out((tokens, width), FULL)]
        + [whole_out((spread.shape[0] // experts, width), LOW)] * experts,
        token=token,
        far_out=(0,),
        us=2,
    )
    return after, sent, token


def gather_kernel(*refs):
    size = refs[0].shape[0]
    for at, ref in enumerate(refs[:-1]):
        refs[-1][pl.ds(at * size, size), :] = ref[...]


def side_by_side(blocks, token):
    size, width = blocks[0].shape
    (out,), token = call(
        gather_kernel,
        "gather",
        [whole(block) for block in blocks],
        [whole_out((len(blocks) * size, width), LOW)],
        token=token,
        us=1,
    )
    return out, token


def expert_part(gate, up, dhid):
    square = gate * gate
    curve = jnp.tanh(GELU_SCALE * gate * (1.0 + GELU_CUBE * square))
    upper = 0.5 * (1.0 + curve)
    gelu = gate * upper
    slope = upper + 0.5 * gate * (1.0 - curve * curve) * (
        GELU_SCALE * (1.0 + 3.0 * GELU_CUBE * square)
    )
    hid = (gelu * up).astype(LOW)
    dgate = (dhid * up * slope).astype(LOW)
    dup = (dhid * gelu).astype(LOW)
    return hid, dgate, dup


def expert_kernel(
    rows_ref, grad_ref, gate_w_ref, up_w_ref, down_w_ref,
    out_ref, back_ref, dgate_ref, dup_ref, hid_ref, turned_ref, out_sum, back_sum,
):
    step = pl.program_id(0)

    @pl.when(step == 0)
    def _():
        out_sum[...] = jnp.zeros_like(out_sum)
        back_sum[...] = jnp.zeros_like(back_sum)

    rows, grad = rows_ref[...], grad_ref[...]
    gate_w, up_w, down_w = gate_w_ref[0], up_w_ref[0], down_w_ref[0]
    hid, dgate, dup = expert_part(
        dot_rows(rows, gate_w), dot_rows(rows, up_w), dot_back(grad, down_w)
    )
    dgate_ref[...] = dgate
    dup_ref[...] = dup
    hid_ref[...] = hid.T
    out_sum[...] += dot_rows(hid, down_w)
    back_sum[...] += dot_back(dgate, gate_w) + dot_back(dup, up_w)

    @pl.when(step == pl.num_programs(0) - 1)
    def _():
        out_ref[...] = out_sum[...].astype(LOW)
        back_ref[...] = back_sum[...].astype(LOW)
        turned_ref[...] = rows_ref[...].T


def expert(rows, grad, w_in, w_down, token):
    count, width = rows.shape
    hidden = w_down.shape[1]
    part = 256
    steps = hidden // part
    return call(
        expert_kernel,
        "expert",
        [
            whole(rows),
            whole(grad),
            (w_in, pl.BlockSpec((1, width, part), lambda i: (0, 0, i))),
            (w_in, pl.BlockSpec((1, width, part), lambda i: (0, 0, i + steps))),
            (w_down, pl.BlockSpec((1, part, width), lambda i: (0, i, 0))),
        ],
        [
            whole_out((count, width), LOW),
            whole_out((count, width), LOW),
            ((count, hidden), LOW, pl.BlockSpec((count, part), lambda i: (0, i))),
            ((count, hidden), LOW, pl.BlockSpec((count, part), lambda i: (0, i))),
            ((hidden, count), LOW, pl.BlockSpec((part, count), lambda i: (i, 0))),
            whole_out((width, count), LOW),
        ],
        grid=(steps,),
        token=token,
        scratch=[pltpu.VMEM((count, width), FULL), pltpu.VMEM((count, width), FULL)],
        vmem=24,
        us=20,
    )


CHUNK = 512
EXPERT_CHUNK = 512
EXPERT_VMEM = 40


def weight_copies(at_ref, w_in_ref, w_down_ref, start, units, gate, up, down, sems):
    width, half = w_in_ref.shape[1], w_down_ref.shape[1] // 2
    first = pl.multiple_of(at_ref[2] * half, LANES) + start
    pairs = []
    for piece in range(4):
        rows = pl.ds(piece * (width // 4), width // 4)
        for part, ref in ((0, gate), (2 * half, up)):
            columns = pl.ds(pl.multiple_of(first + part, LANES), units)
            pairs.append((w_in_ref.at[0, rows, columns], ref.at[rows, :]))
        size = units // 4
        rows = pl.ds(pl.multiple_of(first + piece * size, 16), size)
        pairs.append((w_down_ref.at[0, rows, :], down.at[pl.ds(piece * size, size), :]))
    return [pltpu.make_async_copy(one, two, sems.at[at]) for at, (one, two) in enumerate(pairs)]


def ahead_kernel(at_ref, w_in_ref, w_down_ref, gate_ref, up_ref, down_ref, sems):
    copies = weight_copies(
        at_ref, w_in_ref, w_down_ref, 0, gate_ref.shape[1], gate_ref, up_ref, down_ref, sems
    )
    for copy in copies:
        copy.start()
    for copy in copies:
        copy.wait()


def weights_ahead(at, w_in, w_down, token):
    width = w_in.shape[1]
    return call(
        ahead_kernel,
        "weights_ahead",
        [(w_in, None), (w_down, None)],
        [whole_out((width, EXPERT_CHUNK), LOW)] * 2 + [whole_out((EXPERT_CHUNK, width), LOW)],
        token=token,
        prefetch=(at,),
        scratch=[pltpu.SemaphoreType.DMA((12,))],
        us=2,
    )


def halves_kernel(
    at_ref, x0_ref, x1_ref, g0_ref, g1_ref, gate0_ref, up0_ref, down0_ref, w_in_ref, w_down_ref,
    back_keep, back_send, dgate_ref, dup_ref, turned_ref, hid_out, a_send, a_keep, b_out,
    both_w, du, turned, hid_ref, down_ref, a_sum, b_ref, sems, out_sems,
):
    count, width = x0_ref.shape
    half = hid_ref.shape[1]
    starts = list(range(0, half, EXPERT_CHUNK))
    sizes = [min(EXPERT_CHUNK, half - start) for start in starts]
    loads = [
        weight_copies(
            at_ref, w_in_ref, w_down_ref, start, units,
            both_w.at[:, pl.ds(start, units)],
            both_w.at[:, pl.ds(half + start, units)],
            down_ref.at[pl.ds(start, units), :],
            sems.at[i],
        )
        for i, (start, units) in enumerate(zip(starts, sizes))
        if i > 0
    ]
    for copies in loads:
        for copy in copies:
            copy.start()
    firsts = [
        pltpu.make_async_copy(ref, both_w.at[:, pl.ds(start, sizes[0])], sems.at[0, at])
        for at, (ref, start) in enumerate(((gate0_ref, 0), (up0_ref, half)))
    ]
    for copy in firsts:
        copy.start()
    turned[:, :count] = x0_ref[...].T
    turned[:, count:] = x1_ref[...].T
    kept = [pltpu.make_async_copy(turned, turned_ref, out_sems.at[len(sizes), 0])]
    for i, (start, units) in enumerate(zip(starts, sizes)):
        columns, other = pl.ds(start, units), pl.ds(half + start, units)
        if i == 0:
            gate_w, up_w, down_w = gate0_ref[...], up0_ref[...], down0_ref[...]
        else:
            for copy in loads[i - 1]:
                copy.wait()
            gate_w, up_w, down_w = both_w[:, columns], both_w[:, other], down_ref[columns, :]
        for side, (x_ref, g_ref) in enumerate(((x0_ref, g0_ref), (x1_ref, g1_ref))):
            rows = pl.ds(side * count, count)
            x = x_ref[...]
            hid, dgate, dup = expert_part(
                dot_rows(x, gate_w), dot_rows(x, up_w), dot_back(g_ref[...], down_w)
            )
            hid_ref[rows, columns] = hid
            du[rows, columns] = dgate
            du[rows, other] = dup
        for part, (ref, from_columns) in enumerate(((dgate_ref, columns), (dup_ref, other))):
            copy = pltpu.make_async_copy(
                du.at[:, from_columns], ref.at[:, columns], out_sems.at[i, part]
            )
            copy.start()
            kept.append(copy)
    kept[0].start()
    kept.append(pltpu.make_async_copy(hid_ref, hid_out, out_sems.at[len(sizes), 1]))
    kept[-1].start()
    terms = transpose_dot(hid_ref[:count, :], g0_ref[...])
    terms = terms + transpose_dot(hid_ref[count:, :], g1_ref[...])
    middle, size = width // 2, half // 2
    b_ref[...] = terms[:, middle:].astype(LOW)
    a_sum[...] = terms[:, :middle].astype(LOW)
    own = pl.ds(pl.multiple_of(at_ref[1] * size, 16), size)
    other = pl.ds(pl.multiple_of((1 - at_ref[1]) * size, 16), size)
    sent = [(b_ref, b_out), (a_sum.at[other, :], a_send), (a_sum.at[own, :], a_keep)]
    sent = [
        pltpu.make_async_copy(ref, out, out_sems.at[len(sizes) + 1 + at // 2, at % 2])
        for at, (ref, out) in enumerate(sent)
    ]
    for copy in sent:
        copy.start()
    for copy in firsts:
        copy.wait()
    back_send[...] = dot_back(du[count:, :], both_w[...]).astype(LOW)
    back_keep[...] = dot_back(du[:count, :], both_w[...])
    for copy in kept + sent:
        copy.wait()


def expert_halves(at, rows, grads, firsts, w_in, w_down, token):
    count, width = rows[0].shape
    half = w_down.shape[1] // 2
    chunks = pl.cdiv(half, EXPERT_CHUNK)
    return call(
        halves_kernel,
        "expert_halves",
        [whole(array) for array in (*rows, *grads, *firsts)] + [(w_in, None), (w_down, None)],
        [
            whole_out((count, width), FULL),
            whole_out((count, width), LOW),
            ((2 * count, half), LOW, None),
            ((2 * count, half), LOW, None),
            ((width, 2 * count), LOW, None),
            ((2 * count, half), LOW, None),
            ((half // 2, width // 2), LOW, None),
            ((half // 2, width // 2), LOW, None),
            ((half, width // 2), LOW, None),
        ],
        token=token,
        prefetch=(at,),
        scratch=[
            pltpu.VMEM((width, 2 * half), LOW),
            pltpu.VMEM((2 * count, 2 * half), LOW),
            pltpu.VMEM((width, 2 * count), LOW),
            pltpu.VMEM((2 * count, half), LOW),
            pltpu.VMEM((half, width), LOW),
            pltpu.VMEM((half, width // 2), LOW),
            pltpu.VMEM((half, width // 2), LOW),
            pltpu.SemaphoreType.DMA((chunks, 12)),
            pltpu.SemaphoreType.DMA((chunks + 3, 2)),
        ],
        vmem=EXPERT_VMEM,
        us=20,
    )


def results_kernel(at_ref, hid_out, w_down_ref, keep_out, send_out, hid_ref, down_ref, sum_ref, sems):
    half = down_ref.shape[0]
    size = half // 4
    count = sum_ref.shape[1]
    copies = []
    for side in range(2):
        rows = pl.ds(side * count, count)
        copies.append(pltpu.make_async_copy(hid_out.at[rows, :], hid_ref.at[rows, :], sems.at[4 + side]))
    for piece in range(4):
        rows = pl.ds(pl.multiple_of(at_ref[2] * half + piece * size, 16), size)
        here = down_ref.at[pl.ds(piece * size, size), :]
        copies.append(pltpu.make_async_copy(w_down_ref.at[0, rows, :], here, sems.at[piece]))
    for copy in copies:
        copy.start()
    for copy in copies:
        copy.wait()
    copies = []
    for side, out in ((1, send_out), (0, keep_out)):
        rows = pl.ds(side * count, count)
        sum_ref[side] = dot_rows(hid_ref[rows, :], down_ref[...]).astype(LOW)
        copies.append(pltpu.make_async_copy(sum_ref.at[side], out, sems.at[6 + side]))
        copies[-1].start()
    for copy in copies:
        copy.wait()


def expert_results(at, hid, w_down, fetch, token):
    half, width = hid.shape[1], w_down.shape[2]
    shape = (hid.shape[0] // 2, width)
    (keep, send, *fetched), token = call(
        results_kernel,
        "expert_results",
        [(hid, None), (w_down, None)],
        [(shape, LOW, None)] * 2,
        token=token,
        prefetch=(at,),
        scratch=[
            pltpu.VMEM(hid.shape, LOW),
            pltpu.VMEM((half, width), LOW),
            pltpu.VMEM((2, *shape), LOW),
            pltpu.SemaphoreType.DMA((8,)),
        ],
        vmem=16,
        us=0.01,
        fetch=fetch,
    )
    return keep, send, *fetched, token


def block_of(at_ref, k, blocks):
    return lax.rem(at_ref[3] + (blocks - k), blocks)


def join_kernel(at_ref, kept_ref, got_ref, out_ref):
    blocks, size, _ = out_ref.shape
    for k in range(blocks):
        rows = pl.ds(k * size, size)
        total = kept_ref[rows, :] + got_ref[rows, :].astype(FULL)
        out_ref[block_of(at_ref, k, blocks)] = total.astype(LOW)


def join(at, kept, got, blocks, token):
    rows, width = kept.shape
    (out,), token = call(
        join_kernel,
        "join",
        [whole(kept), whole(got)],
        [whole_out((blocks, rows // blocks, width), LOW)],
        token=token,
        prefetch=(at,),
        far_out=(0,),
        us=1,
    )
    return out, token


def join_peak_kernel(at_ref, kept_ref, got_ref, peak_ref, out_ref):
    blocks, size, width = out_ref.shape
    rows = kept_ref.shape[0] // blocks
    best = jnp.concatenate([peak_ref[g, :GROUP, :] for g in range(peak_ref.shape[0])], axis=0)
    best = jnp.broadcast_to(jnp.max(best, axis=1, keepdims=True), (size - rows, LANES))
    upper = best.astype(LOW)
    lower = (best - upper.astype(FULL)).astype(LOW)
    for k in range(blocks):
        part = pl.ds(k * rows, rows)
        to = block_of(at_ref, k, blocks)
        total = kept_ref[part, :].astype(FULL) + got_ref[part, :].astype(FULL)
        out_ref[to, :rows, :] = total.astype(LOW)
        out_ref[to, rows:, :] = jnp.zeros((size - rows, width), LOW)
        out_ref[to, rows:, :LANES] = upper
        out_ref[to, rows:, LANES : 2 * LANES] = lower


def join_peak(at, kept, got, peak, blocks, token):
    rows, width = kept.shape
    heads = peak.shape[0] * GROUP
    (out,), token = call(
        join_peak_kernel,
        "join_peak",
        [whole(kept), whole(got), whole(peak)],
        [whole_out((blocks, rows // blocks + heads, width), LOW)],
        token=token,
        prefetch=(at,),
        far_out=(0,),
        us=0.01,
        far_in=(0,),
    )
    return out, token


def larger_kernel(one_ref, two_ref, out_ref):
    out_ref[...] = jnp.maximum(one_ref[...], two_ref[...])


def larger(one, two, token):
    (out,), token = call(
        larger_kernel,
        "larger",
        [whole(one), whole(two)],
        [whole_out(one.shape, FULL)],
        token=token,
        us=0.5,
    )
    return out, token


def place():
    dp = lax.axis_index("dp")
    return lax.axis_index("ctx"), lax.axis_index("exp"), dp // 2, dp % 2


def to_down_plane(array):
    pairs = [
        ((1 - core) * 4 + x * 2 + core, core * 4 + x * 2 + core)
        for core in range(2)
        for x in range(2)
    ]
    return lax.ppermute(array, ("ctx", "dp"), pairs)


def in_down_plane(array):
    pairs = [
        (core * 4 + x * 2 + core, core * 4 + (1 - x) * 2 + core)
        for core in range(2)
        for x in range(2)
    ]
    return lax.ppermute(array, ("ctx", "dp"), pairs)


def in_kernel(
    at_ref, turned_ref, gate_ref, up_ref, *refs,
):
    out_refs, turned, near, results, sems, out_sems = refs[:4], *refs[4:]
    half = gate_ref.shape[1]
    ends = [CHUNK // 2] + list(range(3 * CHUNK // 2, half, CHUNK)) + [half]
    starts = [0] + ends[:-1]
    loads = []
    for at, (ref, to) in enumerate(((gate_ref, near.at[0]), (up_ref, near.at[1]))):
        for i, start in enumerate(starts):
            columns = pl.ds(start, ends[i] - start)
            loads.append(
                pltpu.make_async_copy(ref.at[:, columns], to.at[:, columns], sems.at[at, i])
            )
    whole_load = pltpu.make_async_copy(turned_ref, turned, sems.at[2, 0])
    whole_load.start()
    loads[0].start()
    loads[len(starts)].start()
    whole_load.wait()
    size = turned.shape[0] // 4
    stores = []
    for i, start in enumerate(starts):
        columns = pl.ds(start, ends[i] - start)
        loads[i].wait()
        loads[len(starts) + i].wait()
        if i + 1 < len(starts):
            loads[i + 1].start()
            loads[len(starts) + i + 1].start()
        for block in range(4):
            ry, rx = block // 2, block % 2
            chip = (at_ref[0] ^ ry) * 2 + (at_ref[1] ^ rx)
            rows = turned[pl.ds(pl.multiple_of(chip * size, size), size), :]
            a, b = 1 - rx, 2 + 1 - ry
            results[a, ry, :, columns] = dot_rows(rows, near[0, :, columns]).astype(LOW)
            results[b, rx, :, columns] = dot_rows(rows, near[1, :, columns]).astype(LOW)
        for at, ref in enumerate(out_refs):
            copy = pltpu.make_async_copy(
                results.at[at, :, :, columns], ref.at[:, :, columns], out_sems.at[at, i]
            )
            copy.start()
            stores.append(copy)
    for copy in stores:
        copy.wait()


def in_terms(at, turned, gate, up, token):
    width, count = turned.shape
    half = gate.shape[1]
    shape = (2, width // 4, half)
    chunks = pl.cdiv(half, CHUNK) + 1
    return call(
        in_kernel,
        "in_terms",
        [(turned, None), (gate, None), (up, None)],
        [(shape, LOW, None)] * 4,
        token=token,
        prefetch=(at,),
        scratch=[
            pltpu.VMEM((width, count), LOW),
            pltpu.VMEM((2, count, half), LOW),
            pltpu.VMEM((4, *shape), LOW),
            pltpu.SemaphoreType.DMA((3, chunks)),
            pltpu.SemaphoreType.DMA((4, chunks)),
        ],
        vmem=20,
        us=0.01,
    )


def plane_first(parts):
    a_send, a_keep, b_send, b_keep = parts
    return swapped(a_send, "dp", 2), a_keep, swapped(b_send, "ctx", 1), b_keep


def second_kernel(*refs):
    (a_ref, a_keep_ref, b_ref, b_keep_ref), (a_send_ref, b_send_ref) = refs[:4], refs[-2:]
    rows = a_ref.shape[0]
    total = a_keep_ref[...].astype(FULL) + a_ref[...].astype(FULL)
    a_send_ref[pl.ds(0, rows), :] = total.astype(LOW)
    b_send_ref[...] = (b_keep_ref[...].astype(FULL) + b_ref[...].astype(FULL)).astype(LOW)
    for beside in refs[4:-2]:
        more, width = beside.shape
        a_send_ref[pl.ds(rows, more), pl.ds(0, width)] = beside[...]


def plane_second(parts, token, us, beside=()):
    extra = sum(part.shape[0] for part in beside)
    (_, a_rows, a_width), (_, b_rows, b_width) = parts[0].shape, parts[2].shape
    (a_send, b_send), token = call(
        second_kernel,
        "second_terms",
        [whole(part) for part in (*parts, *beside)],
        [whole_out((a_rows + extra, a_width), LOW), whole_out((b_rows, b_width), LOW)],
        token=token,
        us=us,
        far_in=tuple(range(4, 4 + len(beside))),
        part_in={at: (1,) for at in range(4)},
        far_out=(0, 1),
        vmem=10,
    )
    return a_send, b_send, token


def down_second_kernel(at_ref, a_ref, a_keep_ref, b_ref, b_keep_ref, a_send_ref, b_send_ref):
    size = b_send_ref.shape[0]
    rows = pl.ds(pl.multiple_of((1 - at_ref[1]) * size, 16), size)
    a_send_ref[...] = (a_keep_ref[...].astype(FULL) + a_ref[...].astype(FULL)).astype(LOW)
    b_send_ref[...] = (b_keep_ref[rows, :].astype(FULL) + b_ref[rows, :].astype(FULL)).astype(LOW)


def down_second(at, parts, token, us):
    shape = parts[0].shape
    (a_send, b_send), token = call(
        down_second_kernel,
        "down_second",
        [whole(part) for part in parts],
        [whole_out(shape, LOW)] * 2,
        token=token,
        prefetch=(at,),
        us=us,
        far_out=(0, 1),
    )
    return a_send, b_send, token


def pair_last_kernel(a_ref, a_keep_ref, b_ref, b_keep_ref, a2_ref, b2_ref, out_ref):
    blocks = out_ref.shape[0]
    a, b = (
        sum(ref[...].astype(FULL) for ref in refs)
        for refs in ((a_keep_ref, a_ref, a2_ref), (b_keep_ref, b_ref, b2_ref))
    )
    size, columns = b.shape[0] // blocks, b.shape[1] // LANES
    count = size * columns
    for z in range(blocks):
        out_ref[z, :count, :] = a[z * count : (z + 1) * count].astype(LOW)
        small = jnp.broadcast_to(a[blocks * count + z : blocks * count + z + 1], (EXTRA, LANES))
        out_ref[z, count : count + EXTRA, :] = small.astype(LOW)
        for column in range(columns):
            part = b[z * size : (z + 1) * size, column * LANES : (column + 1) * LANES]
            out_ref[z, pl.ds(count + EXTRA + column * size, size), :] = part.astype(LOW)


def pair_last(parts, a2, b2, blocks, token):
    rows, width = b2.shape
    (out,), token = call(
        pair_last_kernel,
        "pair_last",
        [whole(part) for part in (*parts, a2, b2)],
        [whole_out((blocks, 2 * rows // blocks * (width // LANES) + EXTRA, LANES), LOW)],
        token=token,
        part_in={at: (0,) for at in range(4)},
        far_out=(0,),
        us=8,
        vmem=12,
    )
    return out, token


def down_last_kernel(
    at_ref, a_ref, a_keep_ref, b_ref, b_keep_ref, a2_ref, b2_ref, keep_ref, send_ref
):
    size, width = keep_ref.shape
    half = width // 2
    for out_ref, core in ((send_ref, 1 - at_ref[2]), (keep_ref, at_ref[2])):
        rows = pl.ds(pl.multiple_of(core * size, 16), size)
        there = pl.ds(pl.multiple_of((at_ref[1] * 2 + core) * size, 16), size)
        for first, refs in (
            (0, ((a_ref, rows), (a_keep_ref, rows), (a2_ref, rows))),
            (half, ((b_ref, there), (b_keep_ref, there), (b2_ref, rows))),
        ):
            total = sum(ref[cut, :].astype(FULL) for ref, cut in refs)
            out_ref[:, first : first + half] = total.astype(out_ref.dtype)


def down_last(at, parts, a2, b2, token):
    rows, half = a2.shape
    shape = (rows // 2, 2 * half)
    (keep, send), token = call(
        down_last_kernel,
        "down_last",
        [whole(array) for array in (*parts, a2, b2)],
        [whole_out(shape, FULL), whole_out(shape, LOW)],
        token=token,
        prefetch=(at,),
        us=0.01,
        far_out=(1,),
    )
    return keep, send, token


def in_last_kernel(
    at_ref, a_ref, a_keep_ref, b_ref, b_keep_ref, a2_ref, b2_ref, out_ref, send_ref,
    send_near, keep_near, sems,
):
    _, size, half = keep_near.shape
    copies = []
    for number, near in enumerate((send_near, keep_near)):
        core = at_ref[2] if number else 1 - at_ref[2]
        rows = pl.ds(pl.multiple_of(core * size, 16), size)
        for part, refs in enumerate(((a_ref, a_keep_ref, a2_ref), (b_ref, b_keep_ref, b2_ref))):
            total = sum(ref[rows, :].astype(FULL) for ref in refs)
            near[part] = total.astype(near.dtype)
            column = pl.multiple_of((part * 2 + core) * half, LANES)
            there = out_ref.at[0, :, pl.ds(column, half)] if number else send_ref.at[part]
            copies.append(pltpu.make_async_copy(near.at[part], there, sems.at[number, part]))
            copies[-1].start()
    for copy in copies:
        copy.wait()


def in_last(at, parts, a2, b2, token):
    rows, half = b2.shape
    shape = (2, rows // 2, half)
    (out, send), token = call(
        in_last_kernel,
        "in_last",
        [whole(array) for array in (*parts, a2, b2)],
        [((1, rows // 2, 4 * half), FULL, None), (shape, LOW, None)],
        token=token,
        prefetch=(at,),
        scratch=[
            pltpu.VMEM(shape, LOW), pltpu.VMEM(shape, FULL), pltpu.SemaphoreType.DMA((2, 2)),
        ],
        us=8,
        part_in={at: (0,) for at in range(4)},
        vmem=16,
    )
    return out, send, token


def in_finish_kernel(at_ref, _, got_ref, out_ref, near, sems):
    half = got_ref.shape[2]
    copies = []
    for part in range(2):
        near[part] = got_ref[part].astype(FULL)
        column = pl.multiple_of((part * 2 + 1 - at_ref[2]) * half, LANES)
        there = out_ref.at[0, :, pl.ds(column, half)]
        copies.append(pltpu.make_async_copy(near.at[part], there, sems.at[part]))
        copies[-1].start()
    for copy in copies:
        copy.wait()


def in_finish(at, out, got, token):
    (out,), token = call(
        in_finish_kernel,
        "in_finish",
        [(out, None), whole(got)],
        [(out.shape, FULL, None)],
        token=token,
        prefetch=(at,),
        scratch=[pltpu.VMEM(got.shape, FULL), pltpu.SemaphoreType.DMA((2,))],
        onto=((0, 0),),
        us=0.01,
    )
    return out, token


def down_finish_kernel(at_ref, kept_ref, got_ref, out_ref):
    mine = at_ref[0] == at_ref[2]
    out_ref[0] = jnp.where(mine, kept_ref[...], got_ref[...].astype(FULL))


def down_finish(at, kept, got, token):
    (out,), token = call(
        down_finish_kernel,
        "down_finish",
        [whole(kept), whole(got)],
        [whole_out((1, *kept.shape), FULL)],
        token=token,
        prefetch=(at,),
        far_out=(0,),
        us=0.01,
    )
    return out, token


EXTRA = 16
TABLE_LANE = 32


def turn_kernel(at_ref, *refs):
    out_ref, turned = refs[-2:]
    start = 0
    for ref in refs[:-2]:
        turned[:, start : start + ref.shape[0]] = ref[...].T
        start += ref.shape[0]
    size = out_ref.shape[0] // 16
    for to in range(16):
        device = device_at(to % 4, to // 4, at_ref)
        out_ref[pl.ds(to * size, size), :] = turned[pl.ds(device * size, size), :]


def device_at(block, z, at_ref):
    return (
        (at_ref[0] ^ (block // 2)) * 16 + z * 4 + (at_ref[1] ^ (block % 2)) * 2 + at_ref[2]
    )


def turn(at, parts, token):
    count, width = sum(part.shape[0] for part in parts), parts[0].shape[1]
    (out,), token = call(
        turn_kernel,
        "turn",
        [whole(part) for part in parts],
        [whole_out((width // 2, count), LOW)],
        token=token,
        prefetch=(at,),
        scratch=[pltpu.VMEM((width, count), LOW)],
        us=2,
        far_out=(0,),
    )
    return out, token


def shared_kernel(
    at_ref, left_ref, own_ref, other_ref, *refs, experts
):
    out_refs, near_refs, sems = refs[:4], refs[4:8], refs[8]
    a_send_ref, a_keep_ref, b_send_ref, b_keep_ref = near_refs
    copies = []

    def leave(step, parts):
        for number, rows in enumerate(parts):
            for at in (2 * number, 2 * number + 1):
                part = pl.ds(rows.start, rows.stop - rows.start)
                near, out = near_refs[at], out_refs[at]
                copy = pltpu.make_async_copy(
                    near.at[:, part, :], out.at[:, part, :], sems.at[at, step]
                )
                copy.start()
                copies.append(copy)

    rows, count = left_ref.shape[0] // experts, left_ref.shape[1] // 2
    columns = own_ref.shape[1] // LANES
    tokens = count // 3
    size = rows // 4
    small = own_ref[6 * tokens :, :LANES].astype(FULL) + other_ref[6 * tokens :, :LANES].astype(FULL)
    place = lax.broadcasted_iota(jnp.int32, small.shape, 0)
    for z in range(experts):
        left = left_ref[pl.ds(z * rows, rows), :]

        def product(first, start, length):
            right = slice(start, start + length)
            one = left[:, first : first + length]
            two = left[:, count + first : count + first + length]
            total = dot_rows(one, own_ref[right, :]) + dot_rows(two, other_ref[right, :])
            return total.astype(LOW)

        a_terms = product(2 * tokens, 5 * tokens, tokens), product(tokens, 0, tokens)
        b_terms = product(0, tokens, 2 * tokens), product(0, 3 * tokens, 2 * tokens)
        for block in range(4):
            ry, rx = block // 2, block % 2
            a_ref = (a_send_ref if rx else a_keep_ref).at[ry]
            b_ref = (b_send_ref if ry else b_keep_ref).at[rx]
            here = slice(block * size, (block + 1) * size)
            for at in range(2):
                to = pl.ds((2 * z + at) * size, size)
                b_ref[to, :] = b_terms[at][here]
                for column in range(columns):
                    to = pl.ds(((z * columns + column) * 2 + at) * size, size)
                    a_ref[to, :] = a_terms[at][here, column * LANES : (column + 1) * LANES]
        rows_left = slice(2 * z * size, 2 * (z + 1) * size)
        leave(z, (slice(rows_left.start * columns, rows_left.stop * columns), rows_left))
    line = lax.broadcasted_iota(jnp.int32, (EXTRA, LANES), 0)
    for block in range(4):
        ry, rx = block // 2, block % 2
        a_ref = (a_send_ref if rx else a_keep_ref).at[ry]
        rows_here = jnp.zeros((EXTRA, LANES), FULL)
        for z in range(experts):
            row = jnp.where(place == device_at(block, z, at_ref), small, 0.0)
            rows_here = jnp.where(line == z, jnp.sum(row, 0, keepdims=True), rows_here)
        a_ref[2 * size * experts * columns :, :] = rows_here.astype(LOW)
    end = 2 * size * experts * columns
    leave(experts, (slice(end, end + EXTRA),))
    for copy in copies:
        copy.wait()


def shared_terms(at, left, own, other, experts, token):
    rows = left.shape[0]
    width = own.shape[1]
    b_shape = (2, rows // 2, width)
    a_shape = (2, rows // 2 * (width // LANES) + EXTRA, LANES)
    return call(
        functools.partial(shared_kernel, experts=experts),
        "shared_terms",
        [whole(array) for array in (left, own, other)],
        [(shape, LOW, None) for shape in (a_shape, a_shape, b_shape, b_shape)],
        token=token,
        prefetch=(at,),
        scratch=[pltpu.VMEM(shape, LOW) for shape in (a_shape, a_shape, b_shape, b_shape)]
        + [pltpu.SemaphoreType.DMA((4, experts + 1))],
        us=0.01,
        vmem=16,
    )


def rows_kernel(
    place_ref, plane_ref, w_query_ref, w_key_ref, w_value_ref, gain_ref,
    query_ref, key_ref, value_ref, out_ref, gain_grad_ref, ffn_ref, table_ref,
    near_query, near_key, near_value, sems,
):
    rows = query_ref.shape[0]
    at = pl.ds(pl.multiple_of(place_ref[0] * rows, rows), rows)
    pairs = ((w_query_ref, near_query), (w_key_ref, near_key), (w_value_ref, near_value))
    copies = [
        pltpu.make_async_copy(ref.at[at, :], near, sems.at[number])
        for number, (ref, near) in enumerate(pairs)
    ]
    for copy in copies:
        copy.start()
    total = sum(plane_ref[block].astype(FULL) for block in range(plane_ref.shape[0]))
    columns = out_ref.shape[1] // LANES
    count = 2 * rows * columns

    def side_by_side_from(start):
        parts = [total[start + 2 * rows * at : start + 2 * rows * at + rows] for at in range(columns)]
        return jnp.concatenate(parts, axis=1)

    out_ref[...] = side_by_side_from(0)
    query = side_by_side_from(rows)
    key, value = (side_by_side_from(count + EXTRA + start) for start in (0, rows))
    query_ref[...] = query
    key_ref[...] = key
    value_ref[...] = value
    small = total[count : count + 1]
    ffn_ref[...] = small[:, : ffn_ref.shape[1]]
    small = pltpu.roll(jnp.broadcast_to(small, (8, LANES)), LANES - TABLE_LANE, 1)[:1]
    table_ref[...] = small[:, : table_ref.shape[1]]
    for copy in copies:
        copy.wait()
    sums = query * near_query[...].astype(FULL) + key * near_key[...].astype(FULL)
    sums = jnp.sum(sums + value * near_value[...].astype(FULL), axis=1, keepdims=True)
    lane = lax.broadcasted_iota(jnp.int32, (rows, LANES), 1)
    line = lax.broadcasted_iota(jnp.int32, (rows, LANES), 0)
    spread = jnp.sum(jnp.where(lane == line, sums, 0.0), 0, keepdims=True)
    device = place_ref[0]
    block = gain_ref[pl.ds(device * rows // LANES, 1), :]
    gain = pltpu.roll(jnp.broadcast_to(block, (8, LANES)), LANES - device * rows % LANES, 1)[:1]
    gain_grad_ref[...] = (spread / gain)[:, : gain_grad_ref.shape[1]]


def last_rows(place_all, plane, rows, table, weights, gain, token):
    width = weights[0].shape[1]
    small = [whole_out((1, size), FULL) for size in (rows, rows, table)]
    outs, token = call(
        rows_kernel,
        "last_rows",
        [whole(plane)] + [(array, None) for array in weights] + [whole(gain.reshape(-1, LANES))],
        [whole_out((rows, width), FULL)] * 4 + small,
        token=token,
        prefetch=(place_all.reshape(1),),
        scratch=[pltpu.VMEM((rows, width), LOW)] * 3 + [pltpu.SemaphoreType.DMA((3,))],
        us=0.01,
    )
    return outs, token


def clip_kernel(weight_ref, peak_ref, level_ref, out_ref, factor_ref):
    heads = peak_ref.shape[0]
    width = weight_ref.shape[1]
    level = jnp.sum(jnp.where(eye(heads), level_ref[...], 0.0), 1, keepdims=True)
    factor = level / jnp.maximum(peak_ref[:, :1], level)
    factor_ref[...] = jnp.sum(jnp.where(eye(heads), factor, 0.0), 0, keepdims=True)
    head = lax.broadcasted_iota(jnp.int32, (heads, width), 0)
    lane = lax.broadcasted_iota(jnp.int32, (heads, width), 1)
    scale = jnp.sum(jnp.where(lane // HDIM == head, jnp.sqrt(factor), 0.0), 0, keepdims=True)
    out_ref[...] = weight_ref[...].astype(FULL) * scale


def clip(weight, peak, level, token):
    rows, width = weight.shape
    spec = pl.BlockSpec((rows // 4, width), lambda i: (i, 0))
    outs, token = call(
        clip_kernel,
        "clip",
        [(weight, spec), whole(peak), whole(level.reshape(1, -1))],
        [((rows, width), FULL, spec), whole_out((1, level.size), FULL)],
        grid=(4,),
        token=token,
        us=0.01,
        vmem=16,
    )
    return outs, token


def normed_kernel(
    packed_ref, w_query_ref, w_key_ref, w_value_ref, own_ref, other_ref, near, sems
):
    copies = [
        pltpu.make_async_copy(ref, near.at[at], sems.at[at])
        for at, ref in enumerate((w_key_ref, w_value_ref, w_query_ref))
    ]
    for copy in copies:
        copy.start()
    tokens = own_ref.shape[0]
    dq, dk, dv = (
        packed_ref[pl.ds(start * tokens, size * tokens), :]
        for start, size in ((0, 1), (1, 2), (3, 2))
    )
    copies[0].wait()
    total = dot_back(dk, near[0])
    copies[1].wait()
    total = total + dot_back(dv, near[1])
    other_ref[...] = total[:tokens].astype(LOW)
    copies[2].wait()
    own_ref[...] = total[tokens:] + dot_back(dq, near[2])


def normed_grads(packed, weights, tokens, token):
    width = packed.shape[1]
    (own, other), token = call(
        normed_kernel,
        "normed_grads",
        [whole(packed)] + [(array, None) for array in weights],
        [whole_out((tokens, width), FULL), whole_out((tokens, width), LOW)],
        token=token,
        scratch=[pltpu.VMEM((3, width, width), LOW), pltpu.SemaphoreType.DMA((3,))],
        far_out=(0, 1),
        us=0.01,
        vmem=14,
    )
    return own, other, token


def input_kernel(rows_ref, gain_ref, own_ref, got_ref, past_ref, out_ref):
    rows = rows_ref[...].astype(FULL)
    inverse = lax.rsqrt(jnp.mean(rows * rows, axis=1, keepdims=True) + EPSILON)
    scaled = rows * inverse
    grad = (own_ref[...] + got_ref[...].astype(FULL)) * gain_ref[...]
    along = jnp.mean(scaled * grad, axis=1, keepdims=True)
    out_ref[0] = past_ref[...] + inverse * (grad - scaled * along)


def input_grads(rows, gain, own, got, past, token):
    tokens, width = rows.shape
    (out,), token = call(
        input_kernel,
        "input_grads",
        [whole(array) for array in (rows, gain, own, got, past)],
        [whole_out((1, tokens, width), FULL)],
        token=token,
        far_in=(0, 1, 2, 4),
        far_out=(0,),
        us=10,
    )
    return out, token


def back_kernel(
    at_ref, spread_ref, rows_ref, after_ref, gain_ref, grad_ref, weights_ref,
    total_ref, branch_ref, attended_ref, gain_grad_ref,
):
    rows = after_ref[...]
    inverse = lax.rsqrt(jnp.mean(rows * rows, axis=1, keepdims=True) + EPSILON)
    scaled = rows * inverse
    blocks, size, _ = rows_ref.shape
    grad = sum(
        transpose_dot(spread_ref[pl.ds(k * size, size), :], rows_ref[lax.rem(at_ref[3] + k, blocks)])
        for k in range(blocks)
    )
    gain_grad_ref[...] = jnp.sum(scaled * grad, axis=0, keepdims=True)
    grad = grad * gain_ref[...]
    along = jnp.mean(scaled * grad, axis=1, keepdims=True)
    total = grad_ref[...].astype(FULL) + inverse * (grad - scaled * along)
    total_ref[...] = total
    branch = total.astype(LOW)
    branch_ref[...] = branch
    attended_ref[...] = dot_back(branch, weights_ref[...]).astype(LOW)


def back_to_attention(at, spread, rows, after, gain, grad, weights, fetch, token):
    shape = after.shape
    inputs = (spread, rows, after, gain, grad, weights)
    return call(
        back_kernel,
        "back",
        [whole(array) for array in inputs],
        [
            whole_out(shape, FULL),
            whole_out(shape, LOW),
            whole_out(shape, LOW),
            whole_out((1, shape[1]), FULL),
        ],
        token=token,
        vmem=16,
        us=0.01,
        far_in=(0, 2, 4),
        far_out=(0,),
        prefetch=(at,),
        fetch=fetch,
    )


def mix_kernel(at_ref, pick_ref, rows_ref, gates_ref, after_ref, out_ref, peak_ref):
    top, tokens = gates_ref.shape
    blocks = rows_ref.shape[0]
    size = pick_ref.shape[0] // blocks
    total = after_ref[...]
    gates = [to_column(gates_ref[r : r + 1, :]) for r in range(top)]
    for block in range(blocks):
        rows = rows_ref[lax.rem(at_ref[3] + block, blocks), :size, :]
        for r in range(top):
            pick = pick_ref[pl.ds(block * size, size), pl.ds(r * tokens, tokens)]
            total = total + gates[r] * transpose_dot(pick, rows)
    out_ref[0] = total.astype(LOW)
    if rows_ref.shape[1] > size:
        peaks = [
            rows_ref[block, size:, :LANES].astype(FULL)
            + rows_ref[block, size:, LANES : 2 * LANES].astype(FULL)
            for block in range(blocks)
        ]
        peak_ref[...] = functools.reduce(jnp.maximum, peaks)


def mix(at, pick, rows, gates, after, token):
    (out, peak), token = call(
        mix_kernel,
        "mix",
        [whole(pick), whole(rows), whole(gates), whole(after)],
        [whole_out((1, *after.shape), LOW), whole_out((16, LANES), FULL)],
        token=token,
        us=0.01,
        far_in=(0, 3),
        prefetch=(at,),
    )
    return out, peak, token


def local(
    block_in,
    seg_ids,
    routes,
    gates,
    buckets,
    norm_attn,
    norm_ffn,
    w_query,
    w_key,
    w_value,
    w_out_attn,
    rel_bias,
    clip_level,
    w_in,
    w_down,
    cotangent,
):
    tokens, width = block_in.shape[1:]
    heads = width // HDIM
    n_ctx, experts, n_dp = (lax.axis_size(axis) for axis in ("ctx", "exp", "dp"))
    fast = (n_ctx, experts, n_dp) == (2, 4, 4)
    devices = n_ctx * experts * n_dp
    length = n_ctx * tokens
    y, z, x, core = place()
    place_all = (y * experts + z) * n_dp + lax.axis_index("dp")
    top_count = routes.shape[-1]
    capacity = tokens * top_count * 3 // (2 * experts)
    at = jnp.stack([y, x, core, z])

    (spread, pick, mask, rows_copy, *grad_out), token = front(
        at, routes[0].T, gates[0].T, cotangent[0], seg_ids, block_in[0], experts, capacity
    )
    backs = list(range(n_ctx - 1, 0, -1))
    earlier = [
        lax.ppermute(block_in[0], "ctx", [(i, (i + back) % n_ctx) for i in range(n_ctx)])
        for back in backs
    ]
    grad_blocks = to_experts(grad_out)
    bucket_hot, bias, normed_all, queries, keys, values = project(
        buckets.reshape(1, length),
        rel_bias.reshape(NB, heads),
        norm_attn.reshape(1, width),
        (*earlier, block_in[0]),
        (w_query, w_key, w_value),
    )

    attended, probs, peak_lanes, w_out_near = attention(
        queries, keys, values, bias, mask, (w_out_attn,)
    )
    after, sent, token = after_attention(
        attended, w_out_near, rows_copy, norm_ffn.reshape(1, width), spread, experts, token
    )

    row_blocks = to_experts(sent)
    own_gain, own_table = width // devices, NB * heads // devices
    if fast:
        expert_grad, token = side_by_side(grad_blocks, token)
        parts = (normed_all, attended)
        parts = parts + tuple(swapped(part, "dp", 1) for part in parts)
        left, token = turn(at, parts, token)
        peak, token = larger(peak_lanes, swapped(peak_lanes, "dp", 1), token)
        peak, token = larger(peak, swapped(peak, "dp", 2), token)
        peak, token = larger(peak, swapped(peak, "ctx", 1), token)
        expert_rows, token = side_by_side(row_blocks, token)
        both_rows = expert_rows, swapped(expert_rows, "dp", 1)
        both_grads = expert_grad, swapped(expert_grad, "dp", 1)
        firsts, token = weights_ahead(at, w_in, w_down, token)
        outs, token = expert_halves(at, both_rows, both_grads, firsts, w_in, w_down, token)
        back_keep, back_send, dgate, dup, rows_turned, hid, *down = outs
        back_got = swapped(back_send, "dp", 1)
        down = swapped(down[0], "dp", 2), down[1], to_down_plane(down[2]), down[2]
        back_rows, token = join(at, back_keep, back_got, experts, token)
        back_home = over_experts(back_rows)
        first, token = in_terms(at, rows_turned, dgate, dup, token)
        first = plane_first(first)
        down_a, down_b, token = down_second(at, down, token, 5)
        out_keep, out_send, w_out_near, token = expert_results(at, hid, w_down, (w_out_attn,), token)
    else:
        expert_rows = jnp.concatenate(row_blocks, axis=0)
        expert_grad = jnp.concatenate(grad_blocks, axis=0)
        (out_rows, back_rows, dgate, dup, hid_turned, rows_turned), token = expert(
            expert_rows, expert_grad, w_in, w_down, token
        )
        expert_first, expert_second = (
            lax.psum_scatter(grads, ("ctx", "dp"), scatter_dimension=0, tiled=True)[None]
            for grads in (
                dot_rows(rows_turned, jnp.concatenate([dgate, dup], axis=1)),
                dot_rows(hid_turned, expert_grad),
            )
        )
        back_home, out_home = (
            jnp.stack(from_experts(list(rows.reshape(experts, capacity, width))))
            for rows in (back_rows, out_rows)
        )

    home = at if fast else jnp.zeros_like(at)
    soon = (queries, keys, values, probs) + ((bucket_hot,) if fast else ())
    (grad_after, grad_branch, grad_attended, grad_gain_ffn, *soon), token = back_to_attention(
        home, spread, back_home, after, norm_ffn.reshape(1, width), cotangent[0], w_out_near, soon, token
    )
    if fast:
        packed, token = attention_back(
            *soon[:4], grad_attended, token, (grad_branch, soon[4], grad_gain_ffn, devices),
        )
        packed_got = swapped(packed, "dp", 1)
        (left,), token = bring(token, 20, left)
        plane_2, token = shared_terms(at, left, packed, packed_got, experts, token)
        plane_2 = plane_first(plane_2)
        out_send, = hold(token, out_send)
        out_got = swapped(out_send, "dp", 1)
        out_rows, token = join_peak(at, out_keep, out_got, peak, experts, token)
        out_home = over_experts(out_rows)
        normed_own_grad, normed_other_grad, token = normed_grads(
            packed, (w_query, w_key, w_value), tokens, token
        )
        normed_got = lax.ppermute(normed_other_grad, "ctx", [(1, 0)])
        in_a, in_b, token = plane_second(first, token, 0.01)
    else:
        dq, dk, dv, lines, token = attention_back(
            *soon, grad_attended, token
        )
        lines = lines[:, :GROUP, :].reshape(heads, length + tokens)
        grad_table = lax.dot_general(
            bucket_hot, lines, (((1,), (1,)), ((), ())), precision=FULL_PRECISION
        ).reshape(-1)
        mixed, _, _ = mix(home, pick, out_home, gates[0].T, after, token)
        peak = jnp.max(peak_lanes[:, :GROUP, :], axis=-1).reshape(heads)
        peak = lax.pmax(peak, ("ctx", "exp", "dp"))
        peak = jnp.broadcast_to(peak[:, None], (heads, LANES))
        (clipped_query, factor), token = clip(w_query, peak, clip_level, token)
        (clipped_key, _), _ = clip(w_key, peak, clip_level, token)

        grad_normed = dot_back(dk, w_key) + dot_back(dv, w_value)
        grad_normed_own = grad_normed[length - tokens :] + dot_back(dq, w_query)
        for block, back in enumerate(backs):
            term = grad_normed[block * tokens : (block + 1) * tokens].astype(LOW)
            returned = lax.ppermute(term, "ctx", [((i + back) % n_ctx, i) for i in range(n_ctx)])
            grad_normed_own = grad_normed_own + returned.astype(FULL)
        own_rows = block_in[0].astype(FULL)
        _, norm_pull = jax.vjp(lambda rows: rms_norm(rows, norm_attn), own_rows)
        grad_input = (grad_after + norm_pull(grad_normed_own)[0])[None]

    if fast:
        shared_a, shared_b, token = plane_second(plane_2, token, 10)
        shared_a, shared_b = swapped(shared_a, "ctx", 1), swapped(shared_b, "dp", 2)
        mixed, peak, token = mix(at, pick, out_home, gates[0].T, after, token)
        grad_input, token = input_grads(
            block_in[0], norm_attn.reshape(1, width), normed_own_grad, normed_got, grad_after, token
        )
        in_a, in_b = hold(token, in_a, in_b)
        in_a, in_b = swapped(in_a, "ctx", 1), swapped(in_b, "dp", 2)
        (clipped_query, factor), token = clip(w_query, peak, clip_level, token)
        plane, token = pair_last(plane_2, shared_a, shared_b, experts, token)
        plane = over_experts(plane)
        down_a, down_b = hold(token, down_a, down_b)
        down_a, down_b = to_down_plane(down_a), in_down_plane(down_b)
        (clipped_key, _), token = clip(w_key, peak, clip_level, token)
        in_own, in_send, token = in_last(at, first, in_a, in_b, token)
        in_got = swapped(in_send, "dp", 1)
        down_keep, down_send, token = down_last(at, down, down_a, down_b, token)
        down_got = swapped(down_send, "dp", 1)
        expert_first, token = in_finish(at, in_own, in_got, token)
        expert_second, token = down_finish(at, down_keep, down_got, token)
        outs, token = last_rows(
            place_all, plane, own_gain, own_table, (w_query, w_key, w_value), norm_attn, token
        )
        shared_q, shared_k, shared_v, shared_o = outs[:4]
        small_attn, small_ffn, small_table = (out.reshape(-1) for out in outs[4:])
    else:
        shared_q, shared_k, shared_v, shared_o = (
            lax.psum_scatter(grads, ("ctx", "exp", "dp"), scatter_dimension=0, tiled=True)
            for grads in (
                transpose_dot(normed_all[length - tokens :], dq),
                transpose_dot(normed_all, dk),
                transpose_dot(normed_all, dv),
                transpose_dot(attended, grad_branch),
            )
        )
        small_ffn, small_table = (
            lax.dynamic_slice_in_dim(lax.psum(array, ("ctx", "exp", "dp")), place_all * own, own)
            for array, own in ((grad_gain_ffn[0], own_gain), (grad_table, own_table))
        )
        pairs = ((shared_q, w_query), (shared_k, w_key), (shared_v, w_value))
        row_sums = sum(
            jnp.sum(
                grads * lax.dynamic_slice_in_dim(weights, place_all * own_gain, own_gain).astype(FULL),
                axis=1,
            )
            for grads, weights in pairs
        )
        small_attn = row_sums / lax.dynamic_slice_in_dim(norm_attn, place_all * own_gain, own_gain)

    return (
        mixed,
        grad_input,
        small_attn,
        small_ffn,
        shared_q,
        shared_k,
        shared_v,
        shared_o,
        small_table,
        expert_first,
        expert_second,
        clipped_query,
        clipped_key,
        factor.reshape(-1),
    )


def solution(mesh):
    tokens = P(("exp", "dp"), "ctx", None)
    everywhere = P(("ctx", "exp", "dp"))
    by_rows = P(("ctx", "exp", "dp"), None)
    by_expert = P("exp", None, None)
    expert_rows = P("exp", ("ctx", "dp"), None)
    in_specs = (tokens, P(("exp", "dp"), None), tokens, tokens) + (P(),) * 9
    in_specs = in_specs + (by_expert, by_expert, tokens)
    out_specs = (tokens, tokens, everywhere, everywhere) + (by_rows,) * 4
    out_specs = out_specs + (everywhere, expert_rows, expert_rows, P(), P(), P())
    return jax.shard_map(local, mesh=mesh, in_specs=in_specs, out_specs=out_specs, check_vma=False)
```

```python
import functools

import jax
import jax.numpy as jnp
from jax import lax
from jax.experimental import pallas as pl
from jax.experimental.pallas import tpu as pltpu
from jax.sharding import PartitionSpec as P

HDIM = 64
NB = 32
GROUP = 4
LANES = 128
EPSILON = 1e-06
FULL_PRECISION = lax.Precision.HIGHEST
LOW = jnp.bfloat16
FULL = jnp.float32
OUTSIDE = -1e30
GELU_SCALE = 0.7978845608028654
GELU_CUBE = 0.044715


def rms_norm(rows, gain):
    return rows * lax.rsqrt(jnp.mean(rows * rows, axis=-1, keepdims=True) + EPSILON) * gain


def dot_rows(left, right):
    return lax.dot_general(left, right, (((1,), (0,)), ((), ())), preferred_element_type=FULL)


def dot_back(left, right):
    return lax.dot_general(left, right, (((1,), (1,)), ((), ())), preferred_element_type=FULL)


def transpose_dot(left, right):
    return lax.dot_general(left, right, (((0,), (0,)), ((), ())), preferred_element_type=FULL)


def swapped(array, axis, bit):
    size = lax.axis_size(axis)
    return lax.ppermute(array, axis, [(i, i ^ bit) for i in range(size)])


def shifted(array, axis, shift):
    size = lax.axis_size(axis)
    return lax.ppermute(array, axis, [(i, (i + shift) % size) for i in range(size)])


def to_experts(blocks):
    return [blocks[0]] + [shifted(blocks[k], "exp", k) for k in range(1, len(blocks))]


def from_experts(blocks):
    return [blocks[0]] + [shifted(blocks[k], "exp", len(blocks) - k) for k in range(1, len(blocks))]


def over_experts(blocks):
    return lax.all_to_all(blocks, "exp", split_axis=0, concat_axis=0, tiled=True)


MICROSECOND = 1.15e9


def call(
    body, name, inputs, outputs, us, grid=None, token=None, prefetch=(), scratch=(), vmem=6,
    near_in=(), near_out=(), far_in=(), far_out=(), fetch=(),
    part_in=None, onto=(),
):
    part_in = dict(part_in or {})
    far_in = tuple(far_in) + tuple(part_in)
    inputs = list(inputs) + [(array, None) for array in fetch]
    outputs = list(outputs) + [whole_out(array.shape, array.dtype) for array in fetch]
    n_pre, n_in, n_out = len(prefetch), len(inputs), len(outputs)
    held = [] if token is None else [token]
    n_far, n_scratch = len(far_in) + len(far_out), len(scratch)

    def kernel(*refs):
        split = n_pre + n_in
        outs = split + len(held)
        rest = refs[outs + n_out + 1 :]
        ins_here, outs_here = list(refs[:split]), list(refs[outs : outs + n_out])
        copies = []
        for number, at in enumerate(far_in):
            here = rest[n_scratch + number]
            source = refs[n_pre + at].at[part_in[at]] if at in part_in else refs[n_pre + at]
            copies.append(pltpu.make_async_copy(source, here, rest[-1].at[number]))
            ins_here[n_pre + at] = here
        for copy in copies:
            copy.start()
        fetches = [
            pltpu.make_async_copy(ins_here.pop(), outs_here.pop(), rest[-1].at[n_far + number])
            for number in range(len(fetch))
        ]
        for copy in fetches:
            copy.start()
        for copy in copies:
            copy.wait()
        copies = []
        for number, at in enumerate(far_out, len(far_in)):
            here = rest[n_scratch + number]
            copies.append(pltpu.make_async_copy(here, refs[outs + at], rest[-1].at[number]))
            outs_here[at] = here
        body(*ins_here, *outs_here, *rest[:n_scratch])
        for copy in fetches:
            copy.wait()
        for copy in copies:
            copy.start()
        for copy in copies:
            copy.wait()

    where = lambda at, near: pltpu.VMEM if at in near else pltpu.HBM
    arrays = [array for array, _ in inputs]
    shapes = [(shape, dtype) for shape, dtype, _ in outputs]
    anywhere = pl.BlockSpec(memory_space=pl.ANY)
    if grid is None:
        near = pl.BlockSpec(memory_space=pltpu.VMEM)
        far = [at in far_in or spec is None for at, (_, spec) in enumerate(inputs)]
        far_results = [at in far_out or spec is None for at, (_, _, spec) in enumerate(outputs)]
        left = lambda at: tuple(
            size if axis >= len(part_in.get(at, ())) else len(range(size)[part_in[at][axis]])
            for axis, size in enumerate(arrays[at].shape)
            if axis >= len(part_in.get(at, ())) or isinstance(part_in[at][axis], slice)
        )
        buffers = [pltpu.VMEM(left(at), arrays[at].dtype) for at in far_in]
        buffers += [pltpu.VMEM(*shapes[at]) for at in far_out]
        n_sems = n_far + len(fetch)
        buffers += [pltpu.SemaphoreType.DMA((n_sems,))] if n_sems else []
        form = dict(
            in_specs=[pl.BlockSpec(memory_space=pltpu.SMEM)] * n_pre
            + [anywhere if away else near for away in far]
            + [anywhere] * len(held),
            out_specs=[anywhere if away else near for away in far_results] + [anywhere],
            scratch_shapes=list(scratch) + buffers,
        )
        arrays = [
            pltpu.with_memory_space_constraint(array, pltpu.HBM) if away else array
            for array, away in zip(arrays, far)
        ]
        shapes = [
            pltpu.HBM(*one) if away else jax.ShapeDtypeStruct(*one)
            for away, one in zip(far_results, shapes)
        ]
    else:
        form = dict(
            grid_spec=pltpu.PrefetchScalarGridSpec(
                num_scalar_prefetch=n_pre,
                grid=grid,
                in_specs=[spec for _, spec in inputs] + [anywhere] * len(held),
                out_specs=[spec for _, _, spec in outputs] + [anywhere],
                scratch_shapes=list(scratch),
            )
        )
        arrays = [
            pltpu.with_memory_space_constraint(array, where(at, near_in))
            for at, array in enumerate(arrays)
        ]
        shapes = [where(at, near_out)(*one) for at, one in enumerate(shapes)]
    held = [pltpu.with_memory_space_constraint(array, pltpu.HBM) for array in held]
    results = pl.pallas_call(
        kernel,
        out_shape=shapes + [pltpu.HBM((8, LANES), FULL)],
        cost_estimate=pl.CostEstimate(
            flops=int(us * MICROSECOND), bytes_accessed=1, transcendentals=0
        ),
        compiler_params=pltpu.CompilerParams(vmem_limit_bytes=vmem * 2**20),
        name=name,
        input_output_aliases={n_pre + one: other for one, other in onto},
        **form,
    )(*prefetch, *arrays, *held)
    return list(results[:-1]), results[-1]


def whole(array):
    return array, pl.BlockSpec(array.shape, lambda *_: (0,) * array.ndim)


def whole_out(shape, dtype):
    return shape, dtype, pl.BlockSpec(shape, lambda *_: (0,) * len(shape))


def hold(token, *arrays):
    anywhere = pl.BlockSpec(memory_space=pl.ANY)
    return pl.pallas_call(
        lambda *refs: None,
        in_specs=[anywhere] * (len(arrays) + 1),
        out_specs=[anywhere] * len(arrays),
        out_shape=[jax.ShapeDtypeStruct(array.shape, array.dtype) for array in arrays],
        input_output_aliases={at + 1: at for at in range(len(arrays))},
        cost_estimate=pl.CostEstimate(flops=1, bytes_accessed=1, transcendentals=0),
        name="hold",
    )(token, *arrays)


def pass_kernel(*refs):
    half = len(refs) // 2
    for ref, out_ref in zip(refs[:half], refs[half:]):
        out_ref[...] = ref[...]


def bring(token, us, *arrays):
    return call(lambda *refs: None, "bring", [], [], token=token, fetch=arrays, us=us)


def pass_on(token, *arrays):
    return call(
        pass_kernel,
        "pass_on",
        [whole(array) for array in arrays],
        [whole_out(array.shape, array.dtype) for array in arrays],
        token=token,
        us=1,
    )


def eye(size):
    rows = lax.broadcasted_iota(jnp.int32, (size, size), 0)
    return rows == lax.broadcasted_iota(jnp.int32, (size, size), 1)


def to_column(row):
    size = row.shape[1]
    return jnp.sum(jnp.where(eye(size), row, jnp.zeros_like(row)), 1, keepdims=True)


def front_kernel(
    at_ref, routes_ref, gates_ref, grad_ref, seg_ref, rows_ref,
    spread_ref, pick_ref, mask_ref, copy_ref, *out_refs,
):
    top, tokens = routes_ref.shape
    experts, capacity = len(out_refs), out_refs[0].shape[0]
    routes = [routes_ref[r : r + 1, :] for r in range(top)]
    gates = [gates_ref[r : r + 1, :] for r in range(top)]
    before = lax.broadcasted_iota(jnp.int32, (tokens, tokens), 0)
    before = before < lax.broadcasted_iota(jnp.int32, (tokens, tokens), 1)
    slots = lax.broadcasted_iota(jnp.int32, (capacity, tokens), 0).astype(FULL)
    for e in range(experts):
        part = pl.ds(e * capacity, capacity)
        name = lax.rem(at_ref[3] + e, experts)
        hits = [jnp.where(route == name, 1.0, 0.0) for route in routes]
        named = functools.reduce(jnp.add, hits)
        slot = jnp.sum(jnp.where(before, to_column(named), 0.0), 0, keepdims=True)
        place = (slots == slot).astype(FULL)
        spread = place * named
        gate = functools.reduce(jnp.add, [hit * g for hit, g in zip(hits, gates)])
        spread_low = spread.astype(LOW)
        spread_ref[part, :] = spread_low
        for r in range(top):
            pick_ref[part, pl.ds(r * tokens, tokens)] = (place * hits[r]).astype(LOW)
        slot_gate = jnp.sum(spread * gate, 1, keepdims=True)
        out_refs[e][...] = (slot_gate * dot_rows(spread_low, grad_ref[...])).astype(LOW)
    length = mask_ref.shape[1]
    ctx = at_ref[0]
    seg = jnp.broadcast_to(seg_ref[...].astype(FULL), (8, length))
    keys = pltpu.roll(seg, length - (ctx + 1) * tokens, 1)[:1, :]
    at_row = lax.broadcasted_iota(jnp.int32, (tokens, length), 0) + (length - tokens)
    at_key = lax.broadcasted_iota(jnp.int32, (tokens, length), 1)
    own = jnp.sum(jnp.where(at_row == at_key, keys, 0.0), 1, keepdims=True)
    allowed = (at_key <= at_row) & (own == keys) & (at_key >= length - (ctx + 1) * tokens)
    mask_ref[...] = jnp.where(allowed, 0.0, OUTSIDE)
    copy_ref[...] = rows_ref[...]


def front(at, routes, gates, grad, seg, rows, experts, capacity):
    top, tokens = routes.shape
    slots = experts * capacity
    return call(
        front_kernel,
        "front",
        [whole(array) for array in (routes, gates, grad, seg, rows)],
        [
            whole_out((slots, tokens), LOW),
            whole_out((slots, top * tokens), LOW),
            whole_out((tokens, seg.shape[1]), FULL),
            whole_out(rows.shape, LOW),
        ]
        + [whole_out((capacity, grad.shape[1]), LOW)] * experts,
        prefetch=(at,),
        far_in=(0, 1, 2, 3, 4),
        far_out=(1,),
        us=1.5,
    )


def project_kernel(buckets_ref, table_ref, gain_ref, *refs, blocks):
    x_refs, weights = refs[:blocks], refs[blocks : blocks + 3]
    hot_ref, bias_ref, normed_ref, q_ref, k_ref, v_ref, near, sems = refs[blocks + 3 :]
    copies = [
        pltpu.make_async_copy(ref, near.at[at], sems.at[at]) for at, ref in enumerate(weights)
    ]
    for copy in copies:
        copy.start()
    tokens = q_ref.shape[0]
    for at, x_ref in enumerate(x_refs):
        rows = rms_norm(x_ref[...].astype(FULL), gain_ref[...])
        normed_ref[pl.ds(at * tokens, tokens), :] = rows.astype(LOW)
    bias_part(buckets_ref, table_ref, hot_ref, bias_ref)
    own = pl.ds((blocks - 1) * tokens, tokens)
    for at, (out_ref, rows) in enumerate(
        ((q_ref, own), (k_ref, slice(None)), (v_ref, slice(None)))
    ):
        copies[at].wait()
        out_ref[...] = dot_rows(normed_ref[rows, :], near[at]).astype(LOW)


def bias_part(buckets_ref, table_ref, hot_ref, bias_ref):
    heads, rows, keys = bias_ref.shape
    width = hot_ref.shape[1]
    buckets = buckets_ref[...].astype(FULL)
    column = jnp.sum(jnp.where(eye(keys), buckets, 0.0), 1, keepdims=True)
    distance = lax.broadcasted_iota(jnp.int32, (keys, width), 0)
    lane = lax.broadcasted_iota(jnp.int32, (keys, width), 1)
    turned = jnp.sum(jnp.where(distance + lane == keys - 1, column, 0.0), 0, keepdims=True)
    bucket = lax.broadcasted_iota(jnp.int32, (NB, width), 0).astype(FULL)
    hot = jnp.where(bucket == turned, 1.0, 0.0)
    hot_ref[...] = hot
    by_lane = lax.dot_general(
        table_ref[...], hot, (((0,), (0,)), ((), ())), precision=FULL_PRECISION,
        preferred_element_type=FULL,
    )
    for head in range(heads):
        line = jnp.broadcast_to(by_lane[head : head + 1, :], (8, width))
        line = pltpu.roll(line, keys + 1, 1, stride=1, stride_axis=0)
        for start in range(0, rows, 8):
            moved = line if start == 0 else pltpu.roll(line, start, 1)
            bias_ref[head, pl.ds(start, 8), :] = moved[:, :keys]


def project(buckets, table, gain, parts, weights):
    heads, keys = table.shape[1], buckets.shape[1]
    tokens, width = parts[0].shape
    outs, _ = call(
        functools.partial(project_kernel, blocks=len(parts)),
        "project",
        [whole(array) for array in (buckets, table, gain, *parts)]
        + [(array, None) for array in weights],
        [
            whole_out((NB, keys + tokens), FULL),
            whole_out((heads, tokens, keys), FULL),
            whole_out((keys, width), LOW),
            whole_out((tokens, width), LOW),
            whole_out((keys, width), LOW),
            whole_out((keys, width), LOW),
        ],
        scratch=[pltpu.VMEM((3, width, width), LOW), pltpu.SemaphoreType.DMA((3,))],
        us=4.5,
        vmem=16,
    )
    return outs


def half_lanes(half, shape):
    lane = lax.broadcasted_iota(jnp.int32, shape, 1)
    return lane < HDIM if half == 0 else lane >= HDIM


def attention_kernel(q_ref, k_ref, v_ref, bias_ref, mask_ref, out_ref, probs_ref, peak_ref):
    groups = peak_ref.shape[0]

    def group(step, _):
        mask = mask_ref[...]
        for pair in range(GROUP // 2):
            lanes = pair_lanes(step, pair)
            queries, keys, values = q_ref[:, lanes], k_ref[:, lanes], v_ref[:, lanes]
            parts = []
            for half in range(2):
                at = 2 * pair + half
                own = half_lanes(half, queries.shape)
                raw = dot_back(jnp.where(own, queries, jnp.zeros_like(queries)), keys)
                raw = raw * HDIM**-0.5 + mask
                top = jnp.max(raw, axis=0, keepdims=True)
                best = top[:, :LANES]
                for start in range(LANES, top.shape[1], LANES):
                    best = jnp.maximum(best, top[:, start : start + LANES])
                peak_ref[step, at : at + 1, :] = best
                scores = raw + bias_ref[step * GROUP + at]
                raised = jnp.exp(scores - jnp.max(scores, axis=1, keepdims=True))
                probs = raised * (1.0 / jnp.sum(raised, axis=1, keepdims=True))
                probs_low = probs.astype(LOW)
                probs_ref[step * GROUP + at] = probs_low
                parts.append(dot_rows(probs_low, values))
            first = half_lanes(0, parts[0].shape)
            out_ref[:, lanes] = jnp.where(first, parts[0], parts[1]).astype(LOW)
        return 0

    lax.fori_loop(0, groups, group, 0)


def pair_lanes(step, pair):
    return pl.ds(pl.multiple_of(step * GROUP * HDIM + pair * LANES, LANES), LANES)


def attention(queries, keys, values, bias, mask, fetch):
    rows, width = queries.shape
    length = keys.shape[0]
    heads = width // HDIM
    (out, probs, peak, *fetched), _ = call(
        attention_kernel,
        "attention",
        [whole(array) for array in (queries, keys, values, bias, mask)],
        [
            whole_out((rows, width), LOW),
            whole_out((heads, rows, length), LOW),
            whole_out((heads // GROUP, 8, LANES), FULL),
        ],
        us=4.5,
        vmem=10,
        far_out=(1,),
        fetch=fetch,
    )
    return out, probs, peak, *fetched


def attention_back_kernel(
    q_ref, k_ref, v_ref, probs_ref, grad_ref, dq_ref, dk_ref, dv_ref, lines_ref
):
    groups = lines_ref.shape[0]
    rows, length = probs_ref.shape[1:]
    scale = HDIM**-0.5

    def group(step, _):
        for pair in range(GROUP // 2):
            lanes = pair_lanes(step, pair)
            queries, keys, values, grad = (
                ref[:, lanes] for ref in (q_ref, k_ref, v_ref, grad_ref)
            )
            dq, dk, dv = [], [], []
            for half in range(2):
                at = 2 * pair + half
                own = half_lanes(half, grad.shape)
                dp = dot_back(jnp.where(own, grad, jnp.zeros_like(grad)), values)
                probs_low = probs_ref[step * GROUP + at]
                probs = probs_low.astype(FULL)
                ds = probs * (dp - jnp.sum(probs * dp, axis=1, keepdims=True))
                ds_low = ds.astype(LOW)
                dq.append(dot_rows(ds_low, keys))
                dk.append(transpose_dot(ds_low, queries))
                dv.append(transpose_dot(probs_low, grad))
                wide = jnp.concatenate([ds, jnp.zeros((rows, rows), FULL)], axis=1)
                total = wide[rows - 8 :, :]
                for start in range(0, rows - 8, 8):
                    total = total + pltpu.roll(wide[start : start + 8, :], rows - 8 - start, 1)
                line = lax.broadcasted_iota(jnp.int32, total.shape, 0)
                for bit in (1, 2, 4):
                    total = jnp.where(((7 - line) & bit) != 0, pltpu.roll(total, bit, 1), total)
                lines_ref[step, at : at + 1, :] = jnp.sum(total, axis=0, keepdims=True)
            first = half_lanes(0, dq[0].shape)
            dq_ref[:, lanes] = (jnp.where(first, dq[0], dq[1]) * scale).astype(LOW)
            first = half_lanes(0, dk[0].shape)
            dk_ref[:, lanes] = (jnp.where(first, dk[0], dk[1]) * scale).astype(LOW)
            dv_ref[:, lanes] = jnp.where(first, dv[0], dv[1]).astype(LOW)
        return 0

    lax.fori_loop(0, groups, group, 0)


def packed_back_kernel(
    q_ref, k_ref, v_ref, probs_ref, grad_ref, branch_ref, hot_ref, gain_ref, out_ref, lines_ref
):
    rows, length = probs_ref.shape[1:]
    ends = [0, rows, rows + length, rows + 2 * length, 2 * rows + 2 * length]
    parts = [out_ref.at[pl.ds(a, b - a), :] for a, b in zip(ends, ends[1:])]
    attention_back_kernel(q_ref, k_ref, v_ref, probs_ref, grad_ref, *parts[:3], lines_ref)
    parts[3][...] = branch_ref[...]
    groups = lines_ref.shape[0]
    width = gain_ref.shape[1]
    devices = out_ref.shape[0] - ends[4]
    own, turns = width // devices, LANES * devices // width
    device = lax.broadcasted_iota(jnp.int32, (devices, width), 0)
    feature = lax.broadcasted_iota(jnp.int32, (devices, width), 1)
    spread = jnp.where(feature // own == device, gain_ref[...], 0.0)
    folded = functools.reduce(
        jnp.add, [spread[:, start : start + LANES] for start in range(0, width, LANES)]
    )
    device = lax.broadcasted_iota(jnp.int32, folded.shape, 0)
    small = folded
    for turn_by in range(1, turns):
        moved = pltpu.roll(folded, LANES - turn_by * own, 1)
        small = jnp.where(device % turns == turn_by, moved, small)
    lines = jnp.concatenate([lines_ref[g, :GROUP, :] for g in range(groups)], axis=0)
    blank = jnp.zeros((LANES - TABLE_LANE - lines.shape[0], lines.shape[1]), FULL)
    lines = jnp.concatenate([jnp.zeros((TABLE_LANE, lines.shape[1]), FULL), lines, blank], axis=0)
    upper = lines.astype(LOW)
    lower = (lines - upper.astype(FULL)).astype(LOW)
    hot = hot_ref[...].astype(LOW)
    small = small + dot_back(hot, upper) + dot_back(hot, lower)
    out_ref[pl.ds(ends[4], devices), :LANES] = small.astype(LOW)


def attention_back(queries, keys, values, probs, grad, token, packed=None):
    rows, width = queries.shape
    length = keys.shape[0]
    heads = width // HDIM
    lines = whole_out((heads // GROUP, 8, length + rows), FULL)
    inputs = [whole(array) for array in (queries, keys, values, probs, grad)]
    if packed is None:
        outs, token = call(
            attention_back_kernel,
            "attention_back",
            inputs,
            [whole_out((size, width), LOW) for size in (rows, length, length)] + [lines],
            token=token,
            us=6.6,
            vmem=16,
        )
        return *outs, token
    branch, hot, gain, devices = packed
    (out, _), token = call(
        packed_back_kernel,
        "attention_back",
        inputs + [whole(branch), whole(hot), whole(gain)],
        [whole_out((2 * rows + 2 * length + devices, width), LOW), lines],
        token=token,
        us=7,
        vmem=16,
    )
    return out, token


def post_kernel(attended_ref, weights_ref, rows_ref, gain_ref, spread_ref, after_ref, *out_refs):
    after = rows_ref[...].astype(FULL) + dot_rows(attended_ref[...], weights_ref[...])
    after_ref[...] = after
    sent = rms_norm(after, gain_ref[...]).astype(LOW)
    size = out_refs[0].shape[0]
    for at, out_ref in enumerate(out_refs):
        out_ref[...] = dot_rows(spread_ref[pl.ds(at * size, size), :], sent).astype(LOW)


def after_attention(attended, weights, rows, gain, spread, experts, token):
    tokens, width = rows.shape
    (after, *sent), token = call(
        post_kernel,
        "post",
        [whole(array) for array in (attended, weights, rows, gain, spread)],
        [whole_out((tokens, width), FULL)]
        + [whole_out((spread.shape[0] // experts, width), LOW)] * experts,
        token=token,
        far_out=(0,),
        us=2,
    )
    return after, sent, token


def gather_kernel(*refs):
    size = refs[0].shape[0]
    for at, ref in enumerate(refs[:-1]):
        refs[-1][pl.ds(at * size, size), :] = ref[...]


def side_by_side(blocks, token):
    size, width = blocks[0].shape
    (out,), token = call(
        gather_kernel,
        "gather",
        [whole(block) for block in blocks],
        [whole_out((len(blocks) * size, width), LOW)],
        token=token,
        us=1,
    )
    return out, token


def expert_part(gate, up, dhid):
    square = gate * gate
    curve = jnp.tanh(GELU_SCALE * gate * (1.0 + GELU_CUBE * square))
    upper = 0.5 * (1.0 + curve)
    gelu = gate * upper
    slope = upper + 0.5 * gate * (1.0 - curve * curve) * (
        GELU_SCALE * (1.0 + 3.0 * GELU_CUBE * square)
    )
    hid = (gelu * up).astype(LOW)
    dgate = (dhid * up * slope).astype(LOW)
    dup = (dhid * gelu).astype(LOW)
    return hid, dgate, dup


def expert_kernel(
    rows_ref, grad_ref, gate_w_ref, up_w_ref, down_w_ref,
    out_ref, back_ref, dgate_ref, dup_ref, hid_ref, turned_ref, out_sum, back_sum,
):
    step = pl.program_id(0)

    @pl.when(step == 0)
    def _():
        out_sum[...] = jnp.zeros_like(out_sum)
        back_sum[...] = jnp.zeros_like(back_sum)

    rows, grad = rows_ref[...], grad_ref[...]
    gate_w, up_w, down_w = gate_w_ref[0], up_w_ref[0], down_w_ref[0]
    hid, dgate, dup = expert_part(
        dot_rows(rows, gate_w), dot_rows(rows, up_w), dot_back(grad, down_w)
    )
    dgate_ref[...] = dgate
    dup_ref[...] = dup
    hid_ref[...] = hid.T
    out_sum[...] += dot_rows(hid, down_w)
    back_sum[...] += dot_back(dgate, gate_w) + dot_back(dup, up_w)

    @pl.when(step == pl.num_programs(0) - 1)
    def _():
        out_ref[...] = out_sum[...].astype(LOW)
        back_ref[...] = back_sum[...].astype(LOW)
        turned_ref[...] = rows_ref[...].T


def expert(rows, grad, w_in, w_down, token):
    count, width = rows.shape
    hidden = w_down.shape[1]
    part = 256
    steps = hidden // part
    return call(
        expert_kernel,
        "expert",
        [
            whole(rows),
            whole(grad),
            (w_in, pl.BlockSpec((1, width, part), lambda i: (0, 0, i))),
            (w_in, pl.BlockSpec((1, width, part), lambda i: (0, 0, i + steps))),
            (w_down, pl.BlockSpec((1, part, width), lambda i: (0, i, 0))),
        ],
        [
            whole_out((count, width), LOW),
            whole_out((count, width), LOW),
            ((count, hidden), LOW, pl.BlockSpec((count, part), lambda i: (0, i))),
            ((count, hidden), LOW, pl.BlockSpec((count, part), lambda i: (0, i))),
            ((hidden, count), LOW, pl.BlockSpec((part, count), lambda i: (i, 0))),
            whole_out((width, count), LOW),
        ],
        grid=(steps,),
        token=token,
        scratch=[pltpu.VMEM((count, width), FULL), pltpu.VMEM((count, width), FULL)],
        vmem=24,
        us=20,
    )


CHUNK = 512
EXPERT_CHUNK = 512
EXPERT_VMEM = 40


def weight_copies(at_ref, w_in_ref, w_down_ref, start, units, gate, up, down, sems):
    width, half = w_in_ref.shape[1], w_down_ref.shape[1] // 2
    first = pl.multiple_of(at_ref[2] * half, LANES) + start
    pairs = []
    for piece in range(4):
        rows = pl.ds(piece * (width // 4), width // 4)
        for part, ref in ((0, gate), (2 * half, up)):
            columns = pl.ds(pl.multiple_of(first + part, LANES), units)
            pairs.append((w_in_ref.at[0, rows, columns], ref.at[rows, :]))
        size = units // 4
        rows = pl.ds(pl.multiple_of(first + piece * size, 16), size)
        pairs.append((w_down_ref.at[0, rows, :], down.at[pl.ds(piece * size, size), :]))
    return [pltpu.make_async_copy(one, two, sems.at[at]) for at, (one, two) in enumerate(pairs)]


def ahead_kernel(at_ref, w_in_ref, w_down_ref, gate_ref, up_ref, down_ref, sems):
    copies = weight_copies(
        at_ref, w_in_ref, w_down_ref, 0, gate_ref.shape[1], gate_ref, up_ref, down_ref, sems
    )
    for copy in copies:
        copy.start()
    for copy in copies:
        copy.wait()


def weights_ahead(at, w_in, w_down, token):
    width = w_in.shape[1]
    return call(
        ahead_kernel,
        "weights_ahead",
        [(w_in, None), (w_down, None)],
        [whole_out((width, EXPERT_CHUNK), LOW)] * 2 + [whole_out((EXPERT_CHUNK, width), LOW)],
        token=token,
        prefetch=(at,),
        scratch=[pltpu.SemaphoreType.DMA((12,))],
        us=2,
    )


def halves_kernel(
    at_ref, x0_ref, x1_ref, g0_ref, g1_ref, gate0_ref, up0_ref, down0_ref, w_in_ref, w_down_ref,
    back_keep, back_send, dgate_ref, dup_ref, turned_ref, hid_out, a_send, a_keep, b_out,
    both_w, du, turned, hid_ref, down_ref, a_sum, b_ref, sems, out_sems,
):
    count, width = x0_ref.shape
    half = hid_ref.shape[1]
    starts = list(range(0, half, EXPERT_CHUNK))
    sizes = [min(EXPERT_CHUNK, half - start) for start in starts]
    loads = [
        weight_copies(
            at_ref, w_in_ref, w_down_ref, start, units,
            both_w.at[:, pl.ds(start, units)],
            both_w.at[:, pl.ds(half + start, units)],
            down_ref.at[pl.ds(start, units), :],
            sems.at[i],
        )
        for i, (start, units) in enumerate(zip(starts, sizes))
        if i > 0
    ]
    for copies in loads:
        for copy in copies:
            copy.start()
    firsts = [
        pltpu.make_async_copy(ref, both_w.at[:, pl.ds(start, sizes[0])], sems.at[0, at])
        for at, (ref, start) in enumerate(((gate0_ref, 0), (up0_ref, half)))
    ]
    for copy in firsts:
        copy.start()
    turned[:, :count] = x0_ref[...].T
    turned[:, count:] = x1_ref[...].T
    kept = [pltpu.make_async_copy(turned, turned_ref, out_sems.at[len(sizes), 0])]
    for i, (start, units) in enumerate(zip(starts, sizes)):
        columns, other = pl.ds(start, units), pl.ds(half + start, units)
        if i == 0:
            gate_w, up_w, down_w = gate0_ref[...], up0_ref[...], down0_ref[...]
        else:
            for copy in loads[i - 1]:
                copy.wait()
            gate_w, up_w, down_w = both_w[:, columns], both_w[:, other], down_ref[columns, :]
        for side, (x_ref, g_ref) in enumerate(((x0_ref, g0_ref), (x1_ref, g1_ref))):
            rows = pl.ds(side * count, count)
            x = x_ref[...]
            hid, dgate, dup = expert_part(
                dot_rows(x, gate_w), dot_rows(x, up_w), dot_back(g_ref[...], down_w)
            )
            hid_ref[rows, columns] = hid
            du[rows, columns] = dgate
            du[rows, other] = dup
        for part, (ref, from_columns) in enumerate(((dgate_ref, columns), (dup_ref, other))):
            copy = pltpu.make_async_copy(
                du.at[:, from_columns], ref.at[:, columns], out_sems.at[i, part]
            )
            copy.start()
            kept.append(copy)
    kept[0].start()
    kept.append(pltpu.make_async_copy(hid_ref, hid_out, out_sems.at[len(sizes), 1]))
    kept[-1].start()
    terms = transpose_dot(hid_ref[:count, :], g0_ref[...])
    terms = terms + transpose_dot(hid_ref[count:, :], g1_ref[...])
    middle, size = width // 2, half // 2
    b_ref[...] = terms[:, middle:].astype(LOW)
    a_sum[...] = terms[:, :middle].astype(LOW)
    own = pl.ds(pl.multiple_of(at_ref[1] * size, 16), size)
    other = pl.ds(pl.multiple_of((1 - at_ref[1]) * size, 16), size)
    sent = [(b_ref, b_out), (a_sum.at[other, :], a_send), (a_sum.at[own, :], a_keep)]
    sent = [
        pltpu.make_async_copy(ref, out, out_sems.at[len(sizes) + 1 + at // 2, at % 2])
        for at, (ref, out) in enumerate(sent)
    ]
    for copy in sent:
        copy.start()
    for copy in firsts:
        copy.wait()
    back_send[...] = dot_back(du[count:, :], both_w[...]).astype(LOW)
    back_keep[...] = dot_back(du[:count, :], both_w[...])
    for copy in kept + sent:
        copy.wait()


def expert_halves(at, rows, grads, firsts, w_in, w_down, token):
    count, width = rows[0].shape
    half = w_down.shape[1] // 2
    chunks = pl.cdiv(half, EXPERT_CHUNK)
    return call(
        halves_kernel,
        "expert_halves",
        [whole(array) for array in (*rows, *grads, *firsts)] + [(w_in, None), (w_down, None)],
        [
            whole_out((count, width), FULL),
            whole_out((count, width), LOW),
            ((2 * count, half), LOW, None),
            ((2 * count, half), LOW, None),
            ((width, 2 * count), LOW, None),
            ((2 * count, half), LOW, None),
            ((half // 2, width // 2), LOW, None),
            ((half // 2, width // 2), LOW, None),
            ((half, width // 2), LOW, None),
        ],
        token=token,
        prefetch=(at,),
        scratch=[
            pltpu.VMEM((width, 2 * half), LOW),
            pltpu.VMEM((2 * count, 2 * half), LOW),
            pltpu.VMEM((width, 2 * count), LOW),
            pltpu.VMEM((2 * count, half), LOW),
            pltpu.VMEM((half, width), LOW),
            pltpu.VMEM((half, width // 2), LOW),
            pltpu.VMEM((half, width // 2), LOW),
            pltpu.SemaphoreType.DMA((chunks, 12)),
            pltpu.SemaphoreType.DMA((chunks + 3, 2)),
        ],
        vmem=EXPERT_VMEM,
        us=20,
    )


def results_kernel(at_ref, hid_out, w_down_ref, keep_out, send_out, hid_ref, down_ref, sum_ref, sems):
    half = down_ref.shape[0]
    size = half // 4
    count = sum_ref.shape[1]
    copies = []
    for side in range(2):
        rows = pl.ds(side * count, count)
        copies.append(pltpu.make_async_copy(hid_out.at[rows, :], hid_ref.at[rows, :], sems.at[4 + side]))
    for piece in range(4):
        rows = pl.ds(pl.multiple_of(at_ref[2] * half + piece * size, 16), size)
        here = down_ref.at[pl.ds(piece * size, size), :]
        copies.append(pltpu.make_async_copy(w_down_ref.at[0, rows, :], here, sems.at[piece]))
    for copy in copies:
        copy.start()
    for copy in copies:
        copy.wait()
    copies = []
    for side, out in ((1, send_out), (0, keep_out)):
        rows = pl.ds(side * count, count)
        sum_ref[side] = dot_rows(hid_ref[rows, :], down_ref[...]).astype(LOW)
        copies.append(pltpu.make_async_copy(sum_ref.at[side], out, sems.at[6 + side]))
        copies[-1].start()
    for copy in copies:
        copy.wait()


def expert_results(at, hid, w_down, fetch, token):
    half, width = hid.shape[1], w_down.shape[2]
    shape = (hid.shape[0] // 2, width)
    (keep, send, *fetched), token = call(
        results_kernel,
        "expert_results",
        [(hid, None), (w_down, None)],
        [(shape, LOW, None)] * 2,
        token=token,
        prefetch=(at,),
        scratch=[
            pltpu.VMEM(hid.shape, LOW),
            pltpu.VMEM((half, width), LOW),
            pltpu.VMEM((2, *shape), LOW),
            pltpu.SemaphoreType.DMA((8,)),
        ],
        vmem=16,
        us=0.01,
        fetch=fetch,
    )
    return keep, send, *fetched, token


def block_of(at_ref, k, blocks):
    return lax.rem(at_ref[3] + (blocks - k), blocks)


def join_kernel(at_ref, kept_ref, got_ref, out_ref):
    blocks, size, _ = out_ref.shape
    for k in range(blocks):
        rows = pl.ds(k * size, size)
        total = kept_ref[rows, :] + got_ref[rows, :].astype(FULL)
        out_ref[block_of(at_ref, k, blocks)] = total.astype(LOW)


def join(at, kept, got, blocks, token):
    rows, width = kept.shape
    (out,), token = call(
        join_kernel,
        "join",
        [whole(kept), whole(got)],
        [whole_out((blocks, rows // blocks, width), LOW)],
        token=token,
        prefetch=(at,),
        far_out=(0,),
        us=1,
    )
    return out, token


def join_peak_kernel(at_ref, kept_ref, got_ref, peak_ref, out_ref):
    blocks, size, width = out_ref.shape
    rows = kept_ref.shape[0] // blocks
    best = jnp.concatenate([peak_ref[g, :GROUP, :] for g in range(peak_ref.shape[0])], axis=0)
    best = jnp.broadcast_to(jnp.max(best, axis=1, keepdims=True), (size - rows, LANES))
    upper = best.astype(LOW)
    lower = (best - upper.astype(FULL)).astype(LOW)
    for k in range(blocks):
        part = pl.ds(k * rows, rows)
        to = block_of(at_ref, k, blocks)
        total = kept_ref[part, :].astype(FULL) + got_ref[part, :].astype(FULL)
        out_ref[to, :rows, :] = total.astype(LOW)
        out_ref[to, rows:, :] = jnp.zeros((size - rows, width), LOW)
        out_ref[to, rows:, :LANES] = upper
        out_ref[to, rows:, LANES : 2 * LANES] = lower


def join_peak(at, kept, got, peak, blocks, token):
    rows, width = kept.shape
    heads = peak.shape[0] * GROUP
    (out,), token = call(
        join_peak_kernel,
        "join_peak",
        [whole(kept), whole(got), whole(peak)],
        [whole_out((blocks, rows // blocks + heads, width), LOW)],
        token=token,
        prefetch=(at,),
        far_out=(0,),
        us=0.01,
        far_in=(0,),
    )
    return out, token


def larger_kernel(one_ref, two_ref, out_ref):
    out_ref[...] = jnp.maximum(one_ref[...], two_ref[...])


def larger(one, two, token):
    (out,), token = call(
        larger_kernel,
        "larger",
        [whole(one), whole(two)],
        [whole_out(one.shape, FULL)],
        token=token,
        us=0.5,
    )
    return out, token


def place():
    dp = lax.axis_index("dp")
    return lax.axis_index("ctx"), lax.axis_index("exp"), dp // 2, dp % 2


def to_down_plane(array):
    pairs = [
        ((1 - core) * 4 + x * 2 + core, core * 4 + x * 2 + core)
        for core in range(2)
        for x in range(2)
    ]
    return lax.ppermute(array, ("ctx", "dp"), pairs)


def in_down_plane(array):
    pairs = [
        (core * 4 + x * 2 + core, core * 4 + (1 - x) * 2 + core)
        for core in range(2)
        for x in range(2)
    ]
    return lax.ppermute(array, ("ctx", "dp"), pairs)


def in_kernel(
    at_ref, turned_ref, gate_ref, up_ref, *refs,
):
    out_refs, turned, near, results, sems, out_sems = refs[:4], *refs[4:]
    half = gate_ref.shape[1]
    ends = [CHUNK // 2] + list(range(3 * CHUNK // 2, half - CHUNK // 2, CHUNK))
    ends += [half - CHUNK // 2, half]
    starts = [0] + ends[:-1]
    loads = []
    for at, (ref, to) in enumerate(((gate_ref, near.at[0]), (up_ref, near.at[1]))):
        for i, start in enumerate(starts):
            columns = pl.ds(start, ends[i] - start)
            loads.append(
                pltpu.make_async_copy(ref.at[:, columns], to.at[:, columns], sems.at[at, i])
            )
    whole_load = pltpu.make_async_copy(turned_ref, turned, sems.at[2, 0])
    whole_load.start()
    loads[0].start()
    loads[len(starts)].start()
    loads[1].start()
    loads[len(starts) + 1].start()
    whole_load.wait()
    size = turned.shape[0] // 4
    stores = []
    for i, start in enumerate(starts):
        columns = pl.ds(start, ends[i] - start)
        loads[i].wait()
        loads[len(starts) + i].wait()
        if i + 2 < len(starts):
            loads[i + 2].start()
            loads[len(starts) + i + 2].start()
        for block in range(4):
            ry, rx = block // 2, block % 2
            chip = (at_ref[0] ^ ry) * 2 + (at_ref[1] ^ rx)
            rows = turned[pl.ds(pl.multiple_of(chip * size, size), size), :]
            a, b = 1 - rx, 2 + 1 - ry
            results[a, ry, :, columns] = dot_rows(rows, near[0, :, columns]).astype(LOW)
            results[b, rx, :, columns] = dot_rows(rows, near[1, :, columns]).astype(LOW)
        for at, ref in enumerate(out_refs):
            copy = pltpu.make_async_copy(
                results.at[at, :, :, columns], ref.at[:, :, columns], out_sems.at[at, i]
            )
            copy.start()
            stores.append(copy)
    for copy in stores:
        copy.wait()


def in_terms(at, turned, gate, up, token):
    width, count = turned.shape
    half = gate.shape[1]
    shape = (2, width // 4, half)
    chunks = pl.cdiv(half, CHUNK) + 1
    return call(
        in_kernel,
        "in_terms",
        [(turned, None), (gate, None), (up, None)],
        [(shape, LOW, None)] * 4,
        token=token,
        prefetch=(at,),
        scratch=[
            pltpu.VMEM((width, count), LOW),
            pltpu.VMEM((2, count, half), LOW),
            pltpu.VMEM((4, *shape), LOW),
            pltpu.SemaphoreType.DMA((3, chunks)),
            pltpu.SemaphoreType.DMA((4, chunks)),
        ],
        vmem=20,
        us=0.01,
    )


def plane_first(parts):
    a_send, a_keep, b_send, b_keep = parts
    return swapped(a_send, "dp", 2), a_keep, swapped(b_send, "ctx", 1), b_keep


def second_kernel(*refs):
    (a_ref, a_keep_ref, b_ref, b_keep_ref), (a_send_ref, b_send_ref) = refs[:4], refs[-2:]
    rows = a_ref.shape[0]
    total = a_keep_ref[...].astype(FULL) + a_ref[...].astype(FULL)
    a_send_ref[pl.ds(0, rows), :] = total.astype(LOW)
    b_send_ref[...] = (b_keep_ref[...].astype(FULL) + b_ref[...].astype(FULL)).astype(LOW)
    for beside in refs[4:-2]:
        more, width = beside.shape
        a_send_ref[pl.ds(rows, more), pl.ds(0, width)] = beside[...]


def plane_second(parts, token, us, beside=()):
    extra = sum(part.shape[0] for part in beside)
    (_, a_rows, a_width), (_, b_rows, b_width) = parts[0].shape, parts[2].shape
    (a_send, b_send), token = call(
        second_kernel,
        "second_terms",
        [whole(part) for part in (*parts, *beside)],
        [whole_out((a_rows + extra, a_width), LOW), whole_out((b_rows, b_width), LOW)],
        token=token,
        us=us,
        far_in=tuple(range(4, 4 + len(beside))),
        part_in={at: (1,) for at in range(4)},
        far_out=(0, 1),
        vmem=10,
    )
    return a_send, b_send, token


def down_second_kernel(at_ref, a_ref, a_keep_ref, b_ref, b_keep_ref, a_send_ref, b_send_ref):
    size = b_send_ref.shape[0]
    rows = pl.ds(pl.multiple_of((1 - at_ref[1]) * size, 16), size)
    a_send_ref[...] = (a_keep_ref[...].astype(FULL) + a_ref[...].astype(FULL)).astype(LOW)
    b_send_ref[...] = (b_keep_ref[rows, :].astype(FULL) + b_ref[rows, :].astype(FULL)).astype(LOW)


def down_second(at, parts, token, us):
    shape = parts[0].shape
    (a_send, b_send), token = call(
        down_second_kernel,
        "down_second",
        [whole(part) for part in parts],
        [whole_out(shape, LOW)] * 2,
        token=token,
        prefetch=(at,),
        us=us,
        far_out=(0, 1),
    )
    return a_send, b_send, token


def pair_last_kernel(a_ref, a_keep_ref, b_ref, b_keep_ref, a2_ref, b2_ref, out_ref):
    blocks = out_ref.shape[0]
    a, b = (
        sum(ref[...].astype(FULL) for ref in refs)
        for refs in ((a_keep_ref, a_ref, a2_ref), (b_keep_ref, b_ref, b2_ref))
    )
    size, columns = b.shape[0] // blocks, b.shape[1] // LANES
    count = size * columns
    for z in range(blocks):
        out_ref[z, :count, :] = a[z * count : (z + 1) * count].astype(LOW)
        small = jnp.broadcast_to(a[blocks * count + z : blocks * count + z + 1], (EXTRA, LANES))
        out_ref[z, count : count + EXTRA, :] = small.astype(LOW)
        for column in range(columns):
            part = b[z * size : (z + 1) * size, column * LANES : (column + 1) * LANES]
            out_ref[z, pl.ds(count + EXTRA + column * size, size), :] = part.astype(LOW)


def pair_last(parts, a2, b2, blocks, token):
    rows, width = b2.shape
    (out,), token = call(
        pair_last_kernel,
        "pair_last",
        [whole(part) for part in (*parts, a2, b2)],
        [whole_out((blocks, 2 * rows // blocks * (width // LANES) + EXTRA, LANES), LOW)],
        token=token,
        part_in={at: (0,) for at in range(4)},
        far_out=(0,),
        us=8,
        vmem=12,
    )
    return out, token


def down_last_kernel(
    at_ref, a_ref, a_keep_ref, b_ref, b_keep_ref, a2_ref, b2_ref, keep_ref, send_ref
):
    size, width = keep_ref.shape
    half = width // 2
    for out_ref, core in ((send_ref, 1 - at_ref[2]), (keep_ref, at_ref[2])):
        rows = pl.ds(pl.multiple_of(core * size, 16), size)
        there = pl.ds(pl.multiple_of((at_ref[1] * 2 + core) * size, 16), size)
        for first, refs in (
            (0, ((a_ref, rows), (a_keep_ref, rows), (a2_ref, rows))),
            (half, ((b_ref, there), (b_keep_ref, there), (b2_ref, rows))),
        ):
            total = sum(ref[cut, :].astype(FULL) for ref, cut in refs)
            out_ref[:, first : first + half] = total.astype(out_ref.dtype)


def down_last(at, parts, a2, b2, token):
    rows, half = a2.shape
    shape = (rows // 2, 2 * half)
    (keep, send), token = call(
        down_last_kernel,
        "down_last",
        [whole(array) for array in (*parts, a2, b2)],
        [whole_out(shape, FULL), whole_out(shape, LOW)],
        token=token,
        prefetch=(at,),
        us=0.01,
        far_out=(1,),
    )
    return keep, send, token


def in_last_kernel(
    at_ref, a_ref, a_keep_ref, b_ref, b_keep_ref, a2_ref, b2_ref, out_ref, send_ref,
    send_near, keep_near, sems,
):
    _, size, half = keep_near.shape
    copies = []
    for number, near in enumerate((send_near, keep_near)):
        core = at_ref[2] if number else 1 - at_ref[2]
        rows = pl.ds(pl.multiple_of(core * size, 16), size)
        for part, refs in enumerate(((a_ref, a_keep_ref, a2_ref), (b_ref, b_keep_ref, b2_ref))):
            total = sum(ref[rows, :].astype(FULL) for ref in refs)
            near[part] = total.astype(near.dtype)
            column = pl.multiple_of((part * 2 + core) * half, LANES)
            there = out_ref.at[0, :, pl.ds(column, half)] if number else send_ref.at[part]
            copies.append(pltpu.make_async_copy(near.at[part], there, sems.at[number, part]))
            copies[-1].start()
    for copy in copies:
        copy.wait()


def in_last(at, parts, a2, b2, token):
    rows, half = b2.shape
    shape = (2, rows // 2, half)
    (out, send), token = call(
        in_last_kernel,
        "in_last",
        [whole(array) for array in (*parts, a2, b2)],
        [((1, rows // 2, 4 * half), FULL, None), (shape, LOW, None)],
        token=token,
        prefetch=(at,),
        scratch=[
            pltpu.VMEM(shape, LOW), pltpu.VMEM(shape, FULL), pltpu.SemaphoreType.DMA((2, 2)),
        ],
        us=8,
        part_in={at: (0,) for at in range(4)},
        vmem=16,
    )
    return out, send, token


def in_finish_kernel(at_ref, _, got_ref, out_ref, near, sems):
    half = got_ref.shape[2]
    copies = []
    for part in range(2):
        near[part] = got_ref[part].astype(FULL)
        column = pl.multiple_of((part * 2 + 1 - at_ref[2]) * half, LANES)
        there = out_ref.at[0, :, pl.ds(column, half)]
        copies.append(pltpu.make_async_copy(near.at[part], there, sems.at[part]))
        copies[-1].start()
    for copy in copies:
        copy.wait()


def in_finish(at, out, got, token):
    (out,), token = call(
        in_finish_kernel,
        "in_finish",
        [(out, None), whole(got)],
        [(out.shape, FULL, None)],
        token=token,
        prefetch=(at,),
        scratch=[pltpu.VMEM(got.shape, FULL), pltpu.SemaphoreType.DMA((2,))],
        onto=((0, 0),),
        us=0.01,
    )
    return out, token


def down_finish_kernel(at_ref, kept_ref, got_ref, out_ref):
    mine = at_ref[0] == at_ref[2]
    out_ref[0] = jnp.where(mine, kept_ref[...], got_ref[...].astype(FULL))


def down_finish(at, kept, got, token):
    (out,), token = call(
        down_finish_kernel,
        "down_finish",
        [whole(kept), whole(got)],
        [whole_out((1, *kept.shape), FULL)],
        token=token,
        prefetch=(at,),
        far_out=(0,),
        us=0.01,
    )
    return out, token


EXTRA = 16
TABLE_LANE = 32


def turn_kernel(at_ref, *refs):
    out_ref, turned = refs[-2:]
    start = 0
    for ref in refs[:-2]:
        turned[:, start : start + ref.shape[0]] = ref[...].T
        start += ref.shape[0]
    size = out_ref.shape[0] // 16
    for to in range(16):
        device = device_at(to % 4, to // 4, at_ref)
        out_ref[pl.ds(to * size, size), :] = turned[pl.ds(device * size, size), :]


def device_at(block, z, at_ref):
    return (
        (at_ref[0] ^ (block // 2)) * 16 + z * 4 + (at_ref[1] ^ (block % 2)) * 2 + at_ref[2]
    )


def turn(at, parts, token):
    count, width = sum(part.shape[0] for part in parts), parts[0].shape[1]
    (out,), token = call(
        turn_kernel,
        "turn",
        [whole(part) for part in parts],
        [whole_out((width // 2, count), LOW)],
        token=token,
        prefetch=(at,),
        scratch=[pltpu.VMEM((width, count), LOW)],
        us=2,
        far_out=(0,),
    )
    return out, token


def shared_kernel(
    at_ref, left_ref, own_ref, other_ref, *refs, experts
):
    out_refs, near_refs, sems = refs[:4], refs[4:8], refs[8]
    a_send_ref, a_keep_ref, b_send_ref, b_keep_ref = near_refs
    copies = []

    def leave(step, parts):
        for number, rows in enumerate(parts):
            for at in (2 * number, 2 * number + 1):
                part = pl.ds(rows.start, rows.stop - rows.start)
                near, out = near_refs[at], out_refs[at]
                copy = pltpu.make_async_copy(
                    near.at[:, part, :], out.at[:, part, :], sems.at[at, step]
                )
                copy.start()
                copies.append(copy)

    rows, count = left_ref.shape[0] // experts, left_ref.shape[1] // 2
    columns = own_ref.shape[1] // LANES
    tokens = count // 3
    size = rows // 4
    small = own_ref[6 * tokens :, :LANES].astype(FULL) + other_ref[6 * tokens :, :LANES].astype(FULL)
    place = lax.broadcasted_iota(jnp.int32, small.shape, 0)
    for z in range(experts):
        left = left_ref[pl.ds(z * rows, rows), :]

        def product(first, start, length):
            right = slice(start, start + length)
            one = left[:, first : first + length]
            two = left[:, count + first : count + first + length]
            total = dot_rows(one, own_ref[right, :]) + dot_rows(two, other_ref[right, :])
            return total.astype(LOW)

        a_terms = product(2 * tokens, 5 * tokens, tokens), product(tokens, 0, tokens)
        b_terms = product(0, tokens, 2 * tokens), product(0, 3 * tokens, 2 * tokens)
        for block in range(4):
            ry, rx = block // 2, block % 2
            a_ref = (a_send_ref if rx else a_keep_ref).at[ry]
            b_ref = (b_send_ref if ry else b_keep_ref).at[rx]
            here = slice(block * size, (block + 1) * size)
            for at in range(2):
                to = pl.ds((2 * z + at) * size, size)
                b_ref[to, :] = b_terms[at][here]
                for column in range(columns):
                    to = pl.ds(((z * columns + column) * 2 + at) * size, size)
                    a_ref[to, :] = a_terms[at][here, column * LANES : (column + 1) * LANES]
        rows_left = slice(2 * z * size, 2 * (z + 1) * size)
        leave(z, (slice(rows_left.start * columns, rows_left.stop * columns), rows_left))
    line = lax.broadcasted_iota(jnp.int32, (EXTRA, LANES), 0)
    for block in range(4):
        ry, rx = block // 2, block % 2
        a_ref = (a_send_ref if rx else a_keep_ref).at[ry]
        rows_here = jnp.zeros((EXTRA, LANES), FULL)
        for z in range(experts):
            row = jnp.where(place == device_at(block, z, at_ref), small, 0.0)
            rows_here = jnp.where(line == z, jnp.sum(row, 0, keepdims=True), rows_here)
        a_ref[2 * size * experts * columns :, :] = rows_here.astype(LOW)
    end = 2 * size * experts * columns
    leave(experts, (slice(end, end + EXTRA),))
    for copy in copies:
        copy.wait()


def shared_terms(at, left, own, other, experts, token):
    rows = left.shape[0]
    width = own.shape[1]
    b_shape = (2, rows // 2, width)
    a_shape = (2, rows // 2 * (width // LANES) + EXTRA, LANES)
    return call(
        functools.partial(shared_kernel, experts=experts),
        "shared_terms",
        [whole(array) for array in (left, own, other)],
        [(shape, LOW, None) for shape in (a_shape, a_shape, b_shape, b_shape)],
        token=token,
        prefetch=(at,),
        scratch=[pltpu.VMEM(shape, LOW) for shape in (a_shape, a_shape, b_shape, b_shape)]
        + [pltpu.SemaphoreType.DMA((4, experts + 1))],
        us=0.01,
        vmem=16,
    )


def rows_kernel(
    place_ref, plane_ref, w_query_ref, w_key_ref, w_value_ref, gain_ref,
    query_ref, key_ref, value_ref, out_ref, gain_grad_ref, ffn_ref, table_ref,
    near_query, near_key, near_value, sems,
):
    rows = query_ref.shape[0]
    at = pl.ds(pl.multiple_of(place_ref[0] * rows, rows), rows)
    pairs = ((w_query_ref, near_query), (w_key_ref, near_key), (w_value_ref, near_value))
    copies = [
        pltpu.make_async_copy(ref.at[at, :], near, sems.at[number])
        for number, (ref, near) in enumerate(pairs)
    ]
    for copy in copies:
        copy.start()
    total = sum(plane_ref[block].astype(FULL) for block in range(plane_ref.shape[0]))
    columns = out_ref.shape[1] // LANES
    count = 2 * rows * columns

    def side_by_side_from(start):
        parts = [total[start + 2 * rows * at : start + 2 * rows * at + rows] for at in range(columns)]
        return jnp.concatenate(parts, axis=1)

    out_ref[...] = side_by_side_from(0)
    query = side_by_side_from(rows)
    key, value = (side_by_side_from(count + EXTRA + start) for start in (0, rows))
    query_ref[...] = query
    key_ref[...] = key
    value_ref[...] = value
    small = total[count : count + 1]
    ffn_ref[...] = small[:, : ffn_ref.shape[1]]
    small = pltpu.roll(jnp.broadcast_to(small, (8, LANES)), LANES - TABLE_LANE, 1)[:1]
    table_ref[...] = small[:, : table_ref.shape[1]]
    for copy in copies:
        copy.wait()
    sums = query * near_query[...].astype(FULL) + key * near_key[...].astype(FULL)
    sums = jnp.sum(sums + value * near_value[...].astype(FULL), axis=1, keepdims=True)
    lane = lax.broadcasted_iota(jnp.int32, (rows, LANES), 1)
    line = lax.broadcasted_iota(jnp.int32, (rows, LANES), 0)
    spread = jnp.sum(jnp.where(lane == line, sums, 0.0), 0, keepdims=True)
    device = place_ref[0]
    block = gain_ref[pl.ds(device * rows // LANES, 1), :]
    gain = pltpu.roll(jnp.broadcast_to(block, (8, LANES)), LANES - device * rows % LANES, 1)[:1]
    gain_grad_ref[...] = (spread / gain)[:, : gain_grad_ref.shape[1]]


def last_rows(place_all, plane, rows, table, weights, gain, token):
    width = weights[0].shape[1]
    small = [whole_out((1, size), FULL) for size in (rows, rows, table)]
    outs, token = call(
        rows_kernel,
        "last_rows",
        [whole(plane)] + [(array, None) for array in weights] + [whole(gain.reshape(-1, LANES))],
        [whole_out((rows, width), FULL)] * 4 + small,
        token=token,
        prefetch=(place_all.reshape(1),),
        scratch=[pltpu.VMEM((rows, width), LOW)] * 3 + [pltpu.SemaphoreType.DMA((3,))],
        us=0.01,
    )
    return outs, token


def clip_kernel(weight_ref, peak_ref, level_ref, out_ref, factor_ref):
    heads = peak_ref.shape[0]
    width = weight_ref.shape[1]
    level = jnp.sum(jnp.where(eye(heads), level_ref[...], 0.0), 1, keepdims=True)
    factor = level / jnp.maximum(peak_ref[:, :1], level)
    factor_ref[...] = jnp.sum(jnp.where(eye(heads), factor, 0.0), 0, keepdims=True)
    head = lax.broadcasted_iota(jnp.int32, (heads, width), 0)
    lane = lax.broadcasted_iota(jnp.int32, (heads, width), 1)
    scale = jnp.sum(jnp.where(lane // HDIM == head, jnp.sqrt(factor), 0.0), 0, keepdims=True)
    out_ref[...] = weight_ref[...].astype(FULL) * scale


def clip(weight, peak, level, token):
    rows, width = weight.shape
    spec = pl.BlockSpec((rows // 4, width), lambda i: (i, 0))
    outs, token = call(
        clip_kernel,
        "clip",
        [(weight, spec), whole(peak), whole(level.reshape(1, -1))],
        [((rows, width), FULL, spec), whole_out((1, level.size), FULL)],
        grid=(4,),
        token=token,
        us=0.01,
        vmem=16,
    )
    return outs, token


def normed_kernel(
    packed_ref, w_query_ref, w_key_ref, w_value_ref, own_ref, other_ref, near, sems
):
    copies = [
        pltpu.make_async_copy(ref, near.at[at], sems.at[at])
        for at, ref in enumerate((w_key_ref, w_value_ref, w_query_ref))
    ]
    for copy in copies:
        copy.start()
    tokens = own_ref.shape[0]
    dq, dk, dv = (
        packed_ref[pl.ds(start * tokens, size * tokens), :]
        for start, size in ((0, 1), (1, 2), (3, 2))
    )
    copies[0].wait()
    total = dot_back(dk, near[0])
    copies[1].wait()
    total = total + dot_back(dv, near[1])
    other_ref[...] = total[:tokens].astype(LOW)
    copies[2].wait()
    own_ref[...] = total[tokens:] + dot_back(dq, near[2])


def normed_grads(packed, weights, tokens, token):
    width = packed.shape[1]
    (own, other), token = call(
        normed_kernel,
        "normed_grads",
        [whole(packed)] + [(array, None) for array in weights],
        [whole_out((tokens, width), FULL), whole_out((tokens, width), LOW)],
        token=token,
        scratch=[pltpu.VMEM((3, width, width), LOW), pltpu.SemaphoreType.DMA((3,))],
        far_out=(0, 1),
        us=0.01,
        vmem=14,
    )
    return own, other, token


def input_kernel(rows_ref, gain_ref, own_ref, got_ref, past_ref, out_ref):
    rows = rows_ref[...].astype(FULL)
    inverse = lax.rsqrt(jnp.mean(rows * rows, axis=1, keepdims=True) + EPSILON)
    scaled = rows * inverse
    grad = (own_ref[...] + got_ref[...].astype(FULL)) * gain_ref[...]
    along = jnp.mean(scaled * grad, axis=1, keepdims=True)
    out_ref[0] = past_ref[...] + inverse * (grad - scaled * along)


def input_grads(rows, gain, own, got, past, token):
    tokens, width = rows.shape
    (out,), token = call(
        input_kernel,
        "input_grads",
        [whole(array) for array in (rows, gain, own, got, past)],
        [whole_out((1, tokens, width), FULL)],
        token=token,
        far_in=(0, 1, 2, 4),
        far_out=(0,),
        us=10,
    )
    return out, token


def back_kernel(
    at_ref, spread_ref, rows_ref, after_ref, gain_ref, grad_ref, weights_ref,
    total_ref, branch_ref, attended_ref, gain_grad_ref,
):
    rows = after_ref[...]
    inverse = lax.rsqrt(jnp.mean(rows * rows, axis=1, keepdims=True) + EPSILON)
    scaled = rows * inverse
    blocks, size, _ = rows_ref.shape
    grad = sum(
        transpose_dot(spread_ref[pl.ds(k * size, size), :], rows_ref[lax.rem(at_ref[3] + k, blocks)])
        for k in range(blocks)
    )
    gain_grad_ref[...] = jnp.sum(scaled * grad, axis=0, keepdims=True)
    grad = grad * gain_ref[...]
    along = jnp.mean(scaled * grad, axis=1, keepdims=True)
    total = grad_ref[...].astype(FULL) + inverse * (grad - scaled * along)
    total_ref[...] = total
    branch = total.astype(LOW)
    branch_ref[...] = branch
    attended_ref[...] = dot_back(branch, weights_ref[...]).astype(LOW)


def back_to_attention(at, spread, rows, after, gain, grad, weights, fetch, token):
    shape = after.shape
    inputs = (spread, rows, after, gain, grad, weights)
    return call(
        back_kernel,
        "back",
        [whole(array) for array in inputs],
        [
            whole_out(shape, FULL),
            whole_out(shape, LOW),
            whole_out(shape, LOW),
            whole_out((1, shape[1]), FULL),
        ],
        token=token,
        vmem=16,
        us=0.01,
        far_in=(0, 2, 4),
        far_out=(0,),
        prefetch=(at,),
        fetch=fetch,
    )


def mix_kernel(at_ref, pick_ref, rows_ref, gates_ref, after_ref, out_ref, peak_ref):
    top, tokens = gates_ref.shape
    blocks = rows_ref.shape[0]
    size = pick_ref.shape[0] // blocks
    total = after_ref[...]
    gates = [to_column(gates_ref[r : r + 1, :]) for r in range(top)]
    for block in range(blocks):
        rows = rows_ref[lax.rem(at_ref[3] + block, blocks), :size, :]
        for r in range(top):
            pick = pick_ref[pl.ds(block * size, size), pl.ds(r * tokens, tokens)]
            total = total + gates[r] * transpose_dot(pick, rows)
    out_ref[0] = total.astype(LOW)
    if rows_ref.shape[1] > size:
        peaks = [
            rows_ref[block, size:, :LANES].astype(FULL)
            + rows_ref[block, size:, LANES : 2 * LANES].astype(FULL)
            for block in range(blocks)
        ]
        peak_ref[...] = functools.reduce(jnp.maximum, peaks)


def mix(at, pick, rows, gates, after, token):
    (out, peak), token = call(
        mix_kernel,
        "mix",
        [whole(pick), whole(rows), whole(gates), whole(after)],
        [whole_out((1, *after.shape), LOW), whole_out((16, LANES), FULL)],
        token=token,
        us=0.01,
        far_in=(0, 3),
        prefetch=(at,),
    )
    return out, peak, token


def local(
    block_in,
    seg_ids,
    routes,
    gates,
    buckets,
    norm_attn,
    norm_ffn,
    w_query,
    w_key,
    w_value,
    w_out_attn,
    rel_bias,
    clip_level,
    w_in,
    w_down,
    cotangent,
):
    tokens, width = block_in.shape[1:]
    heads = width // HDIM
    n_ctx, experts, n_dp = (lax.axis_size(axis) for axis in ("ctx", "exp", "dp"))
    fast = (n_ctx, experts, n_dp) == (2, 4, 4)
    devices = n_ctx * experts * n_dp
    length = n_ctx * tokens
    y, z, x, core = place()
    place_all = (y * experts + z) * n_dp + lax.axis_index("dp")
    top_count = routes.shape[-1]
    capacity = tokens * top_count * 3 // (2 * experts)
    at = jnp.stack([y, x, core, z])

    (spread, pick, mask, rows_copy, *grad_out), token = front(
        at, routes[0].T, gates[0].T, cotangent[0], seg_ids, block_in[0], experts, capacity
    )
    backs = list(range(n_ctx - 1, 0, -1))
    earlier = [
        lax.ppermute(block_in[0], "ctx", [(i, (i + back) % n_ctx) for i in range(n_ctx)])
        for back in backs
    ]
    grad_blocks = to_experts(grad_out)
    bucket_hot, bias, normed_all, queries, keys, values = project(
        buckets.reshape(1, length),
        rel_bias.reshape(NB, heads),
        norm_attn.reshape(1, width),
        (*earlier, block_in[0]),
        (w_query, w_key, w_value),
    )

    attended, probs, peak_lanes, w_out_near = attention(
        queries, keys, values, bias, mask, (w_out_attn,)
    )
    after, sent, token = after_attention(
        attended, w_out_near, rows_copy, norm_ffn.reshape(1, width), spread, experts, token
    )

    row_blocks = to_experts(sent)
    own_gain, own_table = width // devices, NB * heads // devices
    if fast:
        expert_grad, token = side_by_side(grad_blocks, token)
        parts = (normed_all, attended)
        parts = parts + tuple(swapped(part, "dp", 1) for part in parts)
        left, token = turn(at, parts, token)
        peak, token = larger(peak_lanes, swapped(peak_lanes, "dp", 1), token)
        peak, token = larger(peak, swapped(peak, "dp", 2), token)
        peak, token = larger(peak, swapped(peak, "ctx", 1), token)
        expert_rows, token = side_by_side(row_blocks, token)
        both_rows = expert_rows, swapped(expert_rows, "dp", 1)
        both_grads = expert_grad, swapped(expert_grad, "dp", 1)
        firsts, token = weights_ahead(at, w_in, w_down, token)
        outs, token = expert_halves(at, both_rows, both_grads, firsts, w_in, w_down, token)
        back_keep, back_send, dgate, dup, rows_turned, hid, *down = outs
        back_got = swapped(back_send, "dp", 1)
        down = swapped(down[0], "dp", 2), down[1], to_down_plane(down[2]), down[2]
        back_rows, token = join(at, back_keep, back_got, experts, token)
        back_home = over_experts(back_rows)
        first, token = in_terms(at, rows_turned, dgate, dup, token)
        first = plane_first(first)
        down_a, down_b, token = down_second(at, down, token, 5)
        out_keep, out_send, w_out_near, token = expert_results(at, hid, w_down, (w_out_attn,), token)
    else:
        expert_rows = jnp.concatenate(row_blocks, axis=0)
        expert_grad = jnp.concatenate(grad_blocks, axis=0)
        (out_rows, back_rows, dgate, dup, hid_turned, rows_turned), token = expert(
            expert_rows, expert_grad, w_in, w_down, token
        )
        expert_first, expert_second = (
            lax.psum_scatter(grads, ("ctx", "dp"), scatter_dimension=0, tiled=True)[None]
            for grads in (
                dot_rows(rows_turned, jnp.concatenate([dgate, dup], axis=1)),
                dot_rows(hid_turned, expert_grad),
            )
        )
        back_home, out_home = (
            jnp.stack(from_experts(list(rows.reshape(experts, capacity, width))))
            for rows in (back_rows, out_rows)
        )

    home = at if fast else jnp.zeros_like(at)
    soon = (queries, keys, values, probs) + ((bucket_hot,) if fast else ())
    (grad_after, grad_branch, grad_attended, grad_gain_ffn, *soon), token = back_to_attention(
        home, spread, back_home, after, norm_ffn.reshape(1, width), cotangent[0], w_out_near, soon, token
    )
    if fast:
        packed, token = attention_back(
            *soon[:4], grad_attended, token, (grad_branch, soon[4], grad_gain_ffn, devices),
        )
        packed_got = swapped(packed, "dp", 1)
        (left,), token = bring(token, 20, left)
        plane_2, token = shared_terms(at, left, packed, packed_got, experts, token)
        plane_2 = plane_first(plane_2)
        out_send, = hold(token, out_send)
        out_got = swapped(out_send, "dp", 1)
        out_rows, token = join_peak(at, out_keep, out_got, peak, experts, token)
        out_home = over_experts(out_rows)
        normed_own_grad, normed_other_grad, token = normed_grads(
            packed, (w_query, w_key, w_value), tokens, token
        )
        normed_got = lax.ppermute(normed_other_grad, "ctx", [(1, 0)])
        in_a, in_b, token = plane_second(first, token, 0.01)
    else:
        dq, dk, dv, lines, token = attention_back(
            *soon, grad_attended, token
        )
        lines = lines[:, :GROUP, :].reshape(heads, length + tokens)
        grad_table = lax.dot_general(
            bucket_hot, lines, (((1,), (1,)), ((), ())), precision=FULL_PRECISION
        ).reshape(-1)
        mixed, _, _ = mix(home, pick, out_home, gates[0].T, after, token)
        peak = jnp.max(peak_lanes[:, :GROUP, :], axis=-1).reshape(heads)
        peak = lax.pmax(peak, ("ctx", "exp", "dp"))
        peak = jnp.broadcast_to(peak[:, None], (heads, LANES))
        (clipped_query, factor), token = clip(w_query, peak, clip_level, token)
        (clipped_key, _), _ = clip(w_key, peak, clip_level, token)

        grad_normed = dot_back(dk, w_key) + dot_back(dv, w_value)
        grad_normed_own = grad_normed[length - tokens :] + dot_back(dq, w_query)
        for block, back in enumerate(backs):
            term = grad_normed[block * tokens : (block + 1) * tokens].astype(LOW)
            returned = lax.ppermute(term, "ctx", [((i + back) % n_ctx, i) for i in range(n_ctx)])
            grad_normed_own = grad_normed_own + returned.astype(FULL)
        own_rows = block_in[0].astype(FULL)
        _, norm_pull = jax.vjp(lambda rows: rms_norm(rows, norm_attn), own_rows)
        grad_input = (grad_after + norm_pull(grad_normed_own)[0])[None]

    if fast:
        shared_a, shared_b, token = plane_second(plane_2, token, 10)
        shared_a, shared_b = swapped(shared_a, "ctx", 1), swapped(shared_b, "dp", 2)
        mixed, peak, token = mix(at, pick, out_home, gates[0].T, after, token)
        grad_input, token = input_grads(
            block_in[0], norm_attn.reshape(1, width), normed_own_grad, normed_got, grad_after, token
        )
        in_a, in_b = hold(token, in_a, in_b)
        in_a, in_b = swapped(in_a, "ctx", 1), swapped(in_b, "dp", 2)
        (clipped_query, factor), token = clip(w_query, peak, clip_level, token)
        plane, token = pair_last(plane_2, shared_a, shared_b, experts, token)
        plane = over_experts(plane)
        down_a, down_b = hold(token, down_a, down_b)
        down_a, down_b = to_down_plane(down_a), in_down_plane(down_b)
        (clipped_key, _), token = clip(w_key, peak, clip_level, token)
        in_own, in_send, token = in_last(at, first, in_a, in_b, token)
        in_got = swapped(in_send, "dp", 1)
        down_keep, down_send, token = down_last(at, down, down_a, down_b, token)
        down_got = swapped(down_send, "dp", 1)
        expert_first, token = in_finish(at, in_own, in_got, token)
        expert_second, token = down_finish(at, down_keep, down_got, token)
        outs, token = last_rows(
            place_all, plane, own_gain, own_table, (w_query, w_key, w_value), norm_attn, token
        )
        shared_q, shared_k, shared_v, shared_o = outs[:4]
        small_attn, small_ffn, small_table = (out.reshape(-1) for out in outs[4:])
    else:
        shared_q, shared_k, shared_v, shared_o = (
            lax.psum_scatter(grads, ("ctx", "exp", "dp"), scatter_dimension=0, tiled=True)
            for grads in (
                transpose_dot(normed_all[length - tokens :], dq),
                transpose_dot(normed_all, dk),
                transpose_dot(normed_all, dv),
                transpose_dot(attended, grad_branch),
            )
        )
        small_ffn, small_table = (
            lax.dynamic_slice_in_dim(lax.psum(array, ("ctx", "exp", "dp")), place_all * own, own)
            for array, own in ((grad_gain_ffn[0], own_gain), (grad_table, own_table))
        )
        pairs = ((shared_q, w_query), (shared_k, w_key), (shared_v, w_value))
        row_sums = sum(
            jnp.sum(
                grads * lax.dynamic_slice_in_dim(weights, place_all * own_gain, own_gain).astype(FULL),
                axis=1,
            )
            for grads, weights in pairs
        )
        small_attn = row_sums / lax.dynamic_slice_in_dim(norm_attn, place_all * own_gain, own_gain)

    return (
        mixed,
        grad_input,
        small_attn,
        small_ffn,
        shared_q,
        shared_k,
        shared_v,
        shared_o,
        small_table,
        expert_first,
        expert_second,
        clipped_query,
        clipped_key,
        factor.reshape(-1),
    )


def solution(mesh):
    tokens = P(("exp", "dp"), "ctx", None)
    everywhere = P(("ctx", "exp", "dp"))
    by_rows = P(("ctx", "exp", "dp"), None)
    by_expert = P("exp", None, None)
    expert_rows = P("exp", ("ctx", "dp"), None)
    in_specs = (tokens, P(("exp", "dp"), None), tokens, tokens) + (P(),) * 9
    in_specs = in_specs + (by_expert, by_expert, tokens)
    out_specs = (tokens, tokens, everywhere, everywhere) + (by_rows,) * 4
    out_specs = out_specs + (everywhere, expert_rows, expert_rows, P(), P(), P())
    return jax.shard_map(local, mesh=mesh, in_specs=in_specs, out_specs=out_specs, check_vma=False)
```
